32 devices in a mesh: groups: 2 (over x), pair: 16 (over z, y, core).
Axes of the slice: x: 2, y: 2, z: 4, core: 2. Of those that a mesh axis runs over, the one named last changes fastest.
Arguments:
- ray_blocks: bfloat16 [256, 16, 128, 128], P(('groups', 'pair')), parts along dimension 0, may hold values from -0.125 to 0.125
- block_cells: int32 [256, 16], P(('groups', 'pair')), parts along dimension 0, may hold values from 0 to 1023, as said below
- block_counts: int32 [256], P(('groups', 'pair')), parts along dimension 0, may hold values from 1 to 16
- travel_times: float32 [32768, 64], P(('groups', 'pair')), parts along dimension 0, may hold values from -6 to 6
Outputs:
- estimate: float32 [262144, 64], P(('groups', 'pair')), parts along dimension 0
- model_vec: float32 [262144, 64], P(('groups', 'pair')), parts along dimension 0
The draws below stay inside these ranges and needn't reach their ends.
There are 2 independent parts, one for each index of `groups`. The reference program is written for one: setup_inputs(seed, part) draws one part's arguments, and reference() takes and returns one part's arrays. A program takes and returns all parts, laid end to end along the dimension named above; each array names one. Nothing has to cross between parts.
Inputs may be any that keep to these rules, and one draw needn't show every extreme that they name: Slots of pair block p at or past block_counts[p] are ignored. `block_cells`: cell block b belongs to the device holding output rows b * 128 to b * 128 + 127, that is device b // 64; among all slots of the pair blocks on one device, at most 8 name cell blocks of one owning device, and these name at most 4 distinct cell blocks.
All inputs are finite; a program needn't handle non-finite values.
Results may differ from the reference program's by a relative error of at most 0.0075.
Values may be sent and summed in bfloat16 or wider, within the bound.
No kernel may reach another device: no remote copies, remote signals or barrier semaphores. Data moves between devices by JAX's collectives and lax.ppermute only.
A program may use at most 128 MiB of HBM per device.

```python
import jax
import jax.numpy as jnp
from jax import lax

PB_DEV = 8
CELL_DEV = 8192
BS = 128
NB = 16
SCAP = 8
BCAP = 4
COLS = 64
ITERS = 2
PAIR_BLOCKS = 128
PAIRS = 16384
CELLS = 131072
CELL_BLOCKS = 1024


def draw_block_cells(key, part):
    key = jax.random.fold_in(key, 11)
    devices = PAIR_BLOCKS // PB_DEV
    owned_blocks = CELL_DEV // BS
    slot_total = PB_DEV * NB
    key_forced, key_devices = jax.random.split(key, 2)
    forced = jax.random.randint(key_forced, (), 0, devices)
    pool_owner = jnp.repeat(jnp.arange(devices, dtype=jnp.int32), SCAP)
    copy_index = jnp.tile(jnp.arange(SCAP, dtype=jnp.int32), devices)

    def one_device(device_key):
        key_order, key_base, key_offset = jax.random.split(device_key, 3)
        scores = jax.random.permutation(key_order, devices * SCAP).astype(jnp.int32)
        scores = jnp.where(pool_owner == forced, copy_index - SCAP, scores)
        ordering = jnp.argsort(scores, stable=True)
        chosen = pool_owner[ordering][:slot_total]
        base_block = jax.random.randint(key_base, (devices,), 0, owned_blocks)
        offset = jax.random.randint(key_offset, (slot_total,), 0, BCAP)
        position = jnp.arange(slot_total, dtype=jnp.int32)
        offset = jnp.where(position < SCAP, position % BCAP, offset)
        local_block = (base_block[chosen] + offset) % owned_blocks
        cell_ids = chosen * owned_blocks + local_block
        return cell_ids.reshape(NB, PB_DEV).T
    device_keys = jax.random.split(key_devices, devices)
    return jax.vmap(one_device)(device_keys).reshape(PAIR_BLOCKS, NB).astype(jnp.int32)


def plant(array, rng, smallest, high):
    spot = [jax.random.randint(jax.random.fold_in(rng, axis), (), 0, length) for axis, length in enumerate(array.shape)]
    main_axis = array.shape.index(max(array.shape))
    neighbour = spot[:main_axis] + [(spot[main_axis] + 1) % array.shape[main_axis]] + spot[main_axis + 1:]
    return array.at[tuple(spot)].set(smallest).at[tuple(neighbour)].set(high)


def steps_of(rng, dims, pieces, least, high):
    factor_of, own = 1.0, jax.random.fold_in(rng, 6)
    for dim, blocks in pieces:
        heights = jnp.exp(jax.random.uniform(jax.random.fold_in(own, dim), (blocks,), jnp.float32, least / len(pieces), high / len(pieces)))
        factor_of = factor_of * jnp.repeat(heights, dims[dim] // blocks).reshape([-1 if axis == dim else 1 for axis in range(len(dims))])
    return factor_of


def bell_draw(key, dims, spread, limit, shards=(), held_as=jnp.bfloat16):
    factor_of = steps_of(key, dims, shards, -0.22, 0.18) if shards else 1.0
    values = jax.random.normal(key, dims, jnp.float32) * spread * factor_of
    return jnp.minimum(jnp.maximum(values, -limit), limit).astype(held_as)


def setup_inputs(seed: int = 0, part: int = 0) -> dict:
    keys = jax.random.split(jax.random.key(seed), 5)
    own_keys = jax.random.split(jax.random.fold_in(keys[4], part), 5)
    return {
        "ray_blocks": bell_draw(own_keys[0], (PAIR_BLOCKS, NB, BS, BS), (NB * BS) ** -0.5, 0.125, ((0, 16),)),
        "block_cells": draw_block_cells(jax.random.fold_in(jax.random.fold_in(keys[4], part), 71), part),
        "block_counts": plant(jax.random.randint(own_keys[2], (PAIR_BLOCKS,), 1, NB + 1), jax.random.fold_in(own_keys[2], 1), 1, NB).astype(jnp.int32),
        "travel_times": bell_draw(own_keys[3], (PAIRS, COLS), 1.0, 6.0, ((0, 16),), jnp.float32),
    }


def rounded(values):
    return lax.optimization_barrier(values.astype(jnp.bfloat16)).astype(jnp.float32)

def live_slots(block_counts):
    return (jnp.arange(NB)[None, :] < block_counts[:, None]).astype(jnp.float32)

def apply_forward(ray_blocks, block_cells, block_counts, model_full):
    tiles = rounded(model_full).reshape(CELL_BLOCKS, BS, COLS)
    live = live_slots(block_counts)
    group_count = PAIR_BLOCKS // PB_DEV

    def one_group(parts):
        block_part, index_part, live_part = parts
        chosen = tiles[index_part] * live_part[:, :, None, None]
        return jnp.einsum('pkij,pkjc->pic', block_part.astype(jnp.float32), chosen, precision=lax.Precision.HIGHEST)
    result = lax.map(one_group, (ray_blocks.reshape(group_count, PB_DEV, NB, BS, BS), block_cells.reshape(group_count, PB_DEV, NB), live.reshape(group_count, PB_DEV, NB)))
    return result.reshape(PAIRS, COLS)

def apply_transpose(ray_blocks, block_cells, block_counts, data_vec):
    group_count = PAIR_BLOCKS // PB_DEV
    data_tiles = rounded(data_vec).reshape(group_count, PB_DEV, BS, COLS)
    live = live_slots(block_counts)

    def one_group(total, parts):
        block_part, index_part, live_part, data_part = parts
        contrib = jnp.einsum('pkij,pic->pkjc', block_part.astype(jnp.float32), data_part, precision=lax.Precision.HIGHEST)
        contrib = contrib * live_part[:, :, None, None]
        total = total.at[index_part.reshape(-1)].add(contrib.reshape(-1, BS, COLS))
        return (total, None)
    start = jnp.zeros((CELL_BLOCKS, BS, COLS), jnp.float32)
    total, unused = lax.scan(one_group, start, (ray_blocks.reshape(group_count, PB_DEV, NB, BS, BS), block_cells.reshape(group_count, PB_DEV, NB), live.reshape(group_count, PB_DEV, NB), data_tiles))
    return total.reshape(CELLS, COLS)

def column_norm(values):
    return jnp.sqrt(lax.optimization_barrier(jnp.sum(values * values, axis=0)) + 1e-12)

def reference(ray_blocks, block_cells, block_counts, travel_times):
    beta_norm = column_norm(travel_times)
    data_vec = travel_times / beta_norm
    raw = apply_transpose(ray_blocks, block_cells, block_counts, data_vec)
    alpha_norm = column_norm(raw)
    model_vec = raw / alpha_norm
    search = model_vec
    estimate = jnp.zeros((CELLS, COLS), jnp.float32)
    phi_bar = beta_norm
    rho_bar = alpha_norm
    for step in range(ITERS):
        raw = apply_forward(ray_blocks, block_cells, block_counts, model_vec) - alpha_norm * data_vec
        beta_norm = column_norm(raw)
        data_vec = raw / beta_norm
        raw = apply_transpose(ray_blocks, block_cells, block_counts, data_vec) - beta_norm * model_vec
        alpha_norm = column_norm(raw)
        model_vec = raw / alpha_norm
        rho_next = jnp.sqrt(rho_bar * rho_bar + beta_norm * beta_norm)
        cosine = rho_bar / rho_next
        sine_value = beta_norm / rho_next
        theta_step = sine_value * alpha_norm
        rho_bar = -cosine * alpha_norm
        phi_step = cosine * phi_bar
        phi_bar = sine_value * phi_bar
        estimate = estimate + phi_step / rho_next * search
        search = model_vec - theta_step / rho_next * search
    return (estimate, model_vec)
```

```python
import functools

import jax
import jax.numpy as jnp
from jax import lax
from jax.experimental import pallas as pl
from jax.experimental.pallas import tpu as pltpu
from jax.sharding import PartitionSpec as P

CELL_DEV = 8192
BCAP = 4
BS = 128
TAIL = 16
ITERS = 2
EPS = 1e-12
F32 = jnp.float32
BF16 = jnp.bfloat16
VMEM = pltpu.VMEM
SMEM = pltpu.SMEM


def diagonal(cols):
    shape = (cols, BS)
    return lax.broadcasted_iota(jnp.int32, shape, 0) == lax.broadcasted_iota(jnp.int32, shape, 1)


def squares_tail(squares):
    cols = squares.shape[0]
    total = jnp.sum(squares, axis=1, keepdims=True)
    row = jnp.sum(jnp.where(diagonal(cols), total, 0.0), axis=0, keepdims=True)
    high = row.astype(BF16).astype(F32)
    middle = (row - high).astype(BF16).astype(F32)
    low = row - high - middle
    place = lax.broadcasted_iota(jnp.int32, (TAIL, BS), 0)
    return jnp.where(
        place == 0, high, jnp.where(place == 1, middle, jnp.where(place == 2, low, 0.0))
    )


def norm_of_tails(message_ref, cols):
    tails = message_ref[:, BCAP * cols :, :].astype(F32)
    summed = jnp.sum(tails, axis=0)
    row = summed[0:1] + summed[1:2] + summed[2:3]
    column = jnp.sum(jnp.where(diagonal(cols), row, 0.0), axis=1, keepdims=True)
    return jnp.broadcast_to(jnp.sqrt(column + EPS), (cols, BS))


def lanes(block):
    return pl.ds(pl.multiple_of(block * BS, BS), BS)


def transposed(data_ref, rays_ref, target_ref, total_ref, message_ref):
    pair_count, slot_count = rays_ref.shape[:2]
    cols = data_ref.shape[0]
    peers = message_ref.shape[0]
    spots = peers * BCAP

    def clear(index, carry):
        total_ref[index] = jnp.zeros((cols, BS), F32)
        return carry

    lax.fori_loop(0, spots, clear, 0, unroll=8)

    def one_pair(pair, carry):
        data = data_ref[:, lanes(pair)].astype(BF16)
        for slot in range(0, slot_count, 2):
            rays = jnp.concatenate([rays_ref[pair, slot], rays_ref[pair, slot + 1]], axis=1)
            part = jnp.dot(data, rays, preferred_element_type=F32)
            for half in range(2):
                spot = target_ref[pair * slot_count + slot + half]
                total_ref[spot] += part[:, half * BS : (half + 1) * BS]
        return carry

    lax.fori_loop(0, pair_count, one_pair, 0)

    def pack(peer, carry):
        for rank in range(BCAP):
            message_ref[peer, rank * cols : (rank + 1) * cols, :] = total_ref[
                peer * BCAP + rank
            ].astype(BF16)
        return carry

    lax.fori_loop(0, peers, pack, 0, unroll=2)


def start_kernel(
    cells_ref, counts_ref, times_ref, rays_ref, message_ref, target_ref, total_ref, table_ref, used_ref
):
    pair_count, slot_count = rays_ref.shape[:2]
    peers = message_ref.shape[0]
    cols = times_ref.shape[0]
    owned = CELL_DEV // BS

    def clear(peer, carry):
        used_ref[peer] = 0
        for rank in range(BCAP):
            table_ref[peer * BCAP + rank] = 0
        return carry

    lax.fori_loop(0, peers, clear, 0)

    def one_pair(pair, carry):
        count = counts_ref[pair]
        for slot in range(slot_count):
            cell = cells_ref[pair, slot]
            owner = cell // owned
            local = cell % owned
            used = used_ref[owner]
            rank = used
            for other in range(BCAP - 1, -1, -1):
                same = (table_ref[owner * BCAP + other] == local) & (other < used)
                rank = jnp.where(same, other, rank)
            spot = owner * BCAP + rank
            table_ref[spot] = local
            used_ref[owner] = jnp.maximum(used, rank + 1)
            target_ref[pair * slot_count + slot] = jnp.where(slot < count, spot, peers * BCAP)
        return carry

    lax.fori_loop(0, pair_count, one_pair, 0)
    transposed(times_ref, rays_ref, target_ref, total_ref, message_ref)
    squares = jnp.zeros((cols, BS), F32)
    for pair in range(pair_count):
        part = times_ref[:, pair * BS : (pair + 1) * BS]
        squares += part * part
    tail = squares_tail(squares)
    place = lax.broadcasted_iota(jnp.int32, (TAIL, BS), 0)
    lane = lax.broadcasted_iota(jnp.int32, (TAIL, BS), 1)

    def ask(peer, carry):
        rows = tail
        for rank in range(BCAP):
            asked = table_ref[peer * BCAP + rank].astype(F32)
            rows = jnp.where((place == 3) & (lane == rank), asked, rows)
        message_ref[peer, BCAP * cols :, :] = rows.astype(BF16)
        return carry

    lax.fori_loop(0, peers, ask, 0)


def pair_kernel(
    target_ref, fetched_ref, data_ref, beta_ref, rays_ref,
    message_ref, raw_ref, alpha_ref, total_ref,
):
    pair_count, slot_count = rays_ref.shape[:2]
    peers = message_ref.shape[0]
    cols = data_ref.shape[0]
    spots = peers * BCAP
    alpha = norm_of_tails(fetched_ref, cols)
    alpha_ref[...] = alpha
    model_scale = 1.0 / alpha
    data_scale = alpha / beta_ref[...]

    def one_pair(pair, squares):
        chosen = []
        for slot in range(slot_count):
            spot = target_ref[pair * slot_count + slot]
            live = spot < spots
            spot = jnp.where(live, spot, 0)
            rows = pl.ds(pl.multiple_of((spot % BCAP) * cols, cols), cols)
            block = fetched_ref[spot // BCAP, rows, :]
            chosen.append(jnp.where(live, block, jnp.zeros_like(block)))
        rays = jnp.concatenate([rays_ref[pair, slot] for slot in range(slot_count)], axis=1)
        product = lax.dot_general(
            jnp.concatenate(chosen, axis=1), rays, (((1,), (1,)), ((), ())),
            preferred_element_type=F32,
        )
        raw = product * model_scale - data_ref[:, lanes(pair)] * data_scale
        raw_ref[:, lanes(pair)] = raw
        return squares + raw * raw

    squares = lax.fori_loop(0, pair_count, one_pair, jnp.zeros((cols, BS), F32))
    transposed(raw_ref, rays_ref, target_ref, total_ref, message_ref)
    tail = squares_tail(squares).astype(BF16)
    message_ref[:, BCAP * cols :, :] = jnp.broadcast_to(tail[None], (peers, TAIL, BS))


def cell_kernel(first, last, *refs):
    if first:
        arrived_ref, raw_ref, beta_ref, out_ref, asked_ref, table_ref, sem = refs
    else:
        asked_ref, arrived_ref, model_ref, alpha_ref, raw_ref, beta_ref, out_ref = refs
    peers = arrived_ref.shape[0]
    cols, cells = raw_ref.shape
    if first:
        table_ref[...] = arrived_ref[:, BCAP * cols :, :].astype(F32)[:, 3, :].astype(jnp.int32)
        copy = pltpu.make_async_copy(table_ref, asked_ref, sem)
        copy.start()
    beta = norm_of_tails(arrived_ref, cols)
    beta_ref[...] = beta
    raw_ref[...] = jnp.zeros((cols, cells), F32)
    if first:
        copy.wait()

    def add(peer, carry):
        for rank in range(BCAP):
            where = lanes(asked_ref[peer, rank])
            raw_ref[:, where] += arrived_ref[peer, rank * cols : (rank + 1) * cols, :].astype(F32)
        return carry

    lax.fori_loop(0, peers, add, 0, unroll=2)
    scale = 1.0 / beta
    if not first:
        model_scale = beta / alpha_ref[...]

    def settle(block, squares):
        raw = raw_ref[:, lanes(block)] * scale
        if not first:
            raw = raw - model_ref[:, lanes(block)] * model_scale
        raw_ref[:, lanes(block)] = raw
        return squares + raw * raw

    squares = lax.fori_loop(0, cells // BS, settle, jnp.zeros((cols, BS), F32), unroll=4)
    tail = squares_tail(squares)
    if last:
        out_ref[...] = jnp.broadcast_to(tail[None], out_ref.shape).astype(out_ref.dtype)
        return
    out_ref[:, BCAP * cols :, :] = jnp.broadcast_to(tail[None], (peers, TAIL, BS)).astype(BF16)

    def reply(peer, carry):
        for rank in range(BCAP):
            block = raw_ref[:, lanes(asked_ref[peer, rank])]
            out_ref[peer, rank * cols : (rank + 1) * cols, :] = block.astype(BF16)
        return carry

    lax.fori_loop(0, peers, reply, 0, unroll=2)


def estimate_kernel(*refs):
    betas = refs[0 : ITERS + 1]
    alphas = refs[ITERS + 1 : 2 * ITERS + 1]
    models = refs[2 * ITERS + 1 : 3 * ITERS + 1]
    estimate_ref = refs[-1]
    cols, cells = estimate_ref.shape
    phi_bar = betas[0][...]
    rho_bar = alphas[0][...]
    trace = [1.0 / alphas[0][...]]
    weight = [jnp.zeros((cols, BS), F32)] * ITERS
    for step in range(ITERS):
        beta = betas[step + 1][...]
        rho = jnp.sqrt(rho_bar * rho_bar + beta * beta)
        cosine = rho_bar / rho
        sine = beta / rho
        gain = cosine * phi_bar / rho
        weight = [
            weight[i] + gain * trace[i] if i < len(trace) else weight[i] for i in range(ITERS)
        ]
        if step + 1 < ITERS:
            alpha = alphas[step + 1][...]
            theta = sine * alpha
            rho_bar = -cosine * alpha
            phi_bar = sine * phi_bar
            trace = [-(theta / rho) * value for value in trace] + [1.0 / alpha]

    def one_block(block, carry):
        where = lanes(block)
        total = weight[0] * models[0][:, where]
        for i in range(1, ITERS):
            total += weight[i] * models[i][:, where]
        estimate_ref[:, where] = total
        return carry

    lax.fori_loop(0, cells // BS, one_block, 0, unroll=4)


def model_kernel(tails_ref, raw_ref, model_ref):
    cols, cells = raw_ref.shape
    summed = jnp.sum(tails_ref[...], axis=0)
    row = summed[0:1] + summed[1:2] + summed[2:3]
    column = jnp.sum(jnp.where(diagonal(cols), row, 0.0), axis=1, keepdims=True)
    scale = jnp.broadcast_to(1.0 / jnp.sqrt(column + EPS), (cols, BS))

    def one_block(block, carry):
        model_ref[:, lanes(block)] = raw_ref[:, lanes(block)] * scale
        return carry

    lax.fori_loop(0, cells // BS, one_block, 0, unroll=4)


def call(kernel, name, in_spaces, outs, scratch=(), flops=0, moved=0):
    return pl.pallas_call(
        kernel,
        name=name,
        in_specs=[pl.BlockSpec(memory_space=space) for space in in_spaces],
        out_specs=[pl.BlockSpec(memory_space=space) for _, _, space in outs],
        out_shape=[jax.ShapeDtypeStruct(shape, dtype) for shape, dtype, _ in outs],
        scratch_shapes=list(scratch),
        compiler_params=pltpu.CompilerParams(vmem_limit_bytes=24 * 1024 * 1024),
        cost_estimate=pl.CostEstimate(flops=flops, bytes_accessed=moved, transcendentals=0),
    )


def on_device(ray_blocks, block_cells, block_counts, travel_times):
    pair_count, slot_count = ray_blocks.shape[:2]
    slots = pair_count * slot_count
    peers = lax.axis_size("pair")
    spots = peers * BCAP
    times = travel_times.T
    cols, pairs = times.shape
    message = ((peers, BCAP * cols + TAIL, BS), BF16, VMEM)
    tile = ((cols, BS), F32, VMEM)
    data = ((cols, pairs), F32, VMEM)
    model = ((cols, CELL_DEV), F32, VMEM)
    totals = VMEM((spots + 1, cols, BS), F32)
    flops = 2 * slots * BS * BS * cols

    def exchange(values):
        return lax.all_to_all(values, "pair", split_axis=0, concat_axis=0, tiled=True)

    outgoing, target = call(
        start_kernel, "start", [SMEM, SMEM, VMEM, VMEM],
        [message, ((slots,), jnp.int32, SMEM)],
        [totals, SMEM((spots,), jnp.int32), SMEM((peers,), jnp.int32)],
        flops, 6 << 20,
    )(block_cells, block_counts, times, ray_blocks)
    arrived = exchange(outgoing)
    raw, beta, reply, asked = call(
        functools.partial(cell_kernel, True, False), "cells_first", [VMEM],
        [model, tile, message, ((peers, BS), jnp.int32, SMEM)],
        [VMEM((peers, BS), jnp.int32), pltpu.SemaphoreType.DMA],
        0, 6 << 20,
    )(arrived)
    models, betas, alphas = [raw], [beta], []
    current = times
    for step in range(ITERS):
        fetched = exchange(reply)
        outgoing, current, alpha = call(
            pair_kernel, "pairs", [SMEM, VMEM, VMEM, VMEM, VMEM],
            [message, data, tile], [totals], 2 * flops, 8 << 20,
        )(target, fetched, current, betas[-1], ray_blocks)
        alphas.append(alpha)
        arrived = exchange(outgoing)
        last = step + 1 == ITERS
        out = ((peers, TAIL, BS), F32, VMEM) if last else message
        raw, beta, reply = call(
            functools.partial(cell_kernel, False, last), "cells_last" if last else "cells",
            [SMEM, VMEM, VMEM, VMEM], [model, tile, out], (), 0, 8 << 20,
        )(asked, arrived, models[-1], alpha)
        betas.append(beta)
        models.append(raw)
    tails = exchange(reply)
    (estimate,) = call(
        estimate_kernel, "estimate", [VMEM] * (3 * ITERS + 1), [model], (), 0, 6 << 20
    )(*betas, *alphas, *models[:ITERS])
    (model_vec,) = call(model_kernel, "model", [VMEM, VMEM], [model], (), 0, 4 << 20)(
        tails, models[-1]
    )
    return (estimate.T, model_vec.T)


def solution(mesh):
    return jax.shard_map(
        on_device,
        mesh=mesh,
        in_specs=(
            P(("groups", "pair"), None, None, None),
            P(("groups", "pair"), None),
            P(("groups", "pair")),
            P(("groups", "pair"), None),
        ),
        out_specs=(P(("groups", "pair"), None), P(("groups", "pair"), None)),
        check_vma=False,
    )
```

```python
import functools

import jax
import jax.numpy as jnp
from jax import lax
from jax.experimental import pallas as pl
from jax.experimental.pallas import tpu as pltpu
from jax.sharding import PartitionSpec as P

CELL_DEV = 8192
BCAP = 4
BS = 128
TAIL = 16
ITERS = 2
PARTS = 2
EPS = 1e-12
F32 = jnp.float32
BF16 = jnp.bfloat16
VMEM = pltpu.VMEM
SMEM = pltpu.SMEM


def diagonal(cols):
    shape = (cols, BS)
    return lax.broadcasted_iota(jnp.int32, shape, 0) == lax.broadcasted_iota(jnp.int32, shape, 1)


def squares_tail(squares):
    cols = squares.shape[0]
    total = jnp.sum(squares, axis=1, keepdims=True)
    row = jnp.sum(jnp.where(diagonal(cols), total, 0.0), axis=0, keepdims=True)
    high = row.astype(BF16).astype(F32)
    middle = (row - high).astype(BF16).astype(F32)
    low = row - high - middle
    place = lax.broadcasted_iota(jnp.int32, (TAIL, BS), 0)
    return jnp.where(
        place == 0, high, jnp.where(place == 1, middle, jnp.where(place == 2, low, 0.0))
    )


def norm_of_tails(message_ref, cols):
    tails = message_ref[:, BCAP * cols :, :].astype(F32)
    summed = jnp.sum(tails, axis=0)
    row = summed[0:1] + summed[1:2] + summed[2:3]
    column = jnp.sum(jnp.where(diagonal(cols), row, 0.0), axis=1, keepdims=True)
    return jnp.broadcast_to(jnp.sqrt(column + EPS), (cols, BS))


def lanes(block):
    return pl.ds(pl.multiple_of(block * BS, BS), BS)


def transposed(data_ref, rows, rays_ref, target_ref, total_ref, message_ref):
    pair_count, slot_count = rays_ref.shape[:2]
    cols = total_ref.shape[1]
    peers = message_ref.shape[0]
    spots = peers * BCAP

    def clear(index, carry):
        total_ref[index] = jnp.zeros((cols, BS), F32)
        return carry

    lax.fori_loop(0, spots, clear, 0, unroll=8)

    def one_pair(pair, carry):
        data = data_ref[rows, lanes(pair)]
        high = data.astype(BF16)
        low = (data - high.astype(F32)).astype(BF16)
        pieces = jnp.concatenate([high, low], axis=0)
        for slot in range(0, slot_count, 2):
            rays = jnp.concatenate([rays_ref[pair, slot], rays_ref[pair, slot + 1]], axis=1)
            part = jnp.dot(pieces, rays, preferred_element_type=F32)
            part = part[:cols] + part[cols:]
            for half in range(2):
                spot = target_ref[pair * slot_count + slot + half]
                total_ref[spot] += part[:, half * BS : (half + 1) * BS]
        return carry

    lax.fori_loop(0, pair_count, one_pair, 0)

    def pack(peer, carry):
        for rank in range(BCAP):
            message_ref[peer, rank * cols : (rank + 1) * cols, :] = total_ref[
                peer * BCAP + rank
            ].astype(BF16)
        return carry

    lax.fori_loop(0, peers, pack, 0, unroll=2)


def start_kernel(part, *refs):
    if part == 0:
        cells_ref, counts_ref, times_ref, rays_ref, message_ref, target_ref = refs[:6]
        total_ref, table_ref, used_ref = refs[6:]
    else:
        target_ref, times_ref, rays_ref, message_ref, total_ref = refs
    pair_count, slot_count = rays_ref.shape[:2]
    peers = message_ref.shape[0]
    cols = total_ref.shape[1]
    columns = slice(part * cols, (part + 1) * cols)
    if part == 0:
        find_places(cells_ref, counts_ref, target_ref, table_ref, used_ref)
    transposed(times_ref, columns, rays_ref, target_ref, total_ref, message_ref)
    squares = jnp.zeros((cols, BS), F32)
    for pair in range(pair_count):
        values = times_ref[columns, pair * BS : (pair + 1) * BS]
        squares += values * values
    tail = squares_tail(squares)
    if part != 0:
        message_ref[:, BCAP * cols :, :] = jnp.broadcast_to(
            tail.astype(BF16)[None], (peers, TAIL, BS)
        )
        return
    place = lax.broadcasted_iota(jnp.int32, (TAIL, BS), 0)
    lane = lax.broadcasted_iota(jnp.int32, (TAIL, BS), 1)

    def ask(peer, carry):
        rows = tail
        for rank in range(BCAP):
            asked = table_ref[peer * BCAP + rank].astype(F32)
            rows = jnp.where((place == 3) & (lane == rank), asked, rows)
        message_ref[peer, BCAP * cols :, :] = rows.astype(BF16)
        return carry

    lax.fori_loop(0, peers, ask, 0)


def find_places(cells_ref, counts_ref, target_ref, table_ref, used_ref):
    pair_count, slot_count = cells_ref.shape
    peers = used_ref.shape[0]
    owned = CELL_DEV // BS

    def clear(peer, carry):
        used_ref[peer] = 0
        for rank in range(BCAP):
            table_ref[peer * BCAP + rank] = 0
        return carry

    lax.fori_loop(0, peers, clear, 0)

    def one_pair(pair, carry):
        count = counts_ref[pair]
        for slot in range(slot_count):
            cell = cells_ref[pair, slot]
            owner = cell // owned
            local = cell % owned
            used = used_ref[owner]
            rank = used
            for other in range(BCAP - 1, -1, -1):
                same = (table_ref[owner * BCAP + other] == local) & (other < used)
                rank = jnp.where(same, other, rank)
            spot = owner * BCAP + rank
            table_ref[spot] = local
            used_ref[owner] = jnp.maximum(used, rank + 1)
            target_ref[pair * slot_count + slot] = jnp.where(slot < count, spot, peers * BCAP)
        return carry

    lax.fori_loop(0, pair_count, one_pair, 0)


def pair_kernel(
    rows, target_ref, fetched_ref, data_ref, beta_ref, rays_ref,
    message_ref, raw_ref, alpha_ref, total_ref,
):
    pair_count, slot_count = rays_ref.shape[:2]
    peers = message_ref.shape[0]
    cols = raw_ref.shape[0]
    spots = peers * BCAP
    alpha = norm_of_tails(fetched_ref, cols)
    alpha_ref[...] = alpha
    model_scale = 1.0 / alpha
    data_scale = alpha / beta_ref[...]

    def one_pair(pair, squares):
        chosen = []
        for slot in range(slot_count):
            spot = target_ref[pair * slot_count + slot]
            live = spot < spots
            spot = jnp.where(live, spot, 0)
            inside = pl.ds(pl.multiple_of((spot % BCAP) * cols, cols), cols)
            block = fetched_ref[spot // BCAP, inside, :]
            chosen.append(jnp.where(live, block, jnp.zeros_like(block)))
        rays = jnp.concatenate([rays_ref[pair, slot] for slot in range(slot_count)], axis=1)
        product = lax.dot_general(
            jnp.concatenate(chosen, axis=1), rays, (((1,), (1,)), ((), ())),
            preferred_element_type=F32,
        )
        raw = product * model_scale - data_ref[rows, lanes(pair)] * data_scale
        raw_ref[:, lanes(pair)] = raw
        return squares + raw * raw

    squares = lax.fori_loop(0, pair_count, one_pair, jnp.zeros((cols, BS), F32))
    transposed(raw_ref, slice(0, cols), rays_ref, target_ref, total_ref, message_ref)
    tail = squares_tail(squares).astype(BF16)
    message_ref[:, BCAP * cols :, :] = jnp.broadcast_to(tail[None], (peers, TAIL, BS))


def cell_kernel(first, last, *refs):
    finds = first and len(refs) == 7
    if finds:
        arrived_ref, raw_ref, beta_ref, out_ref, asked_ref, table_ref, sem = refs
    elif first:
        asked_ref, arrived_ref, raw_ref, beta_ref, out_ref = refs
    else:
        asked_ref, arrived_ref, model_ref, alpha_ref, *others, raw_ref, beta_ref, out_ref = refs
    peers = arrived_ref.shape[0]
    cols, cells = raw_ref.shape
    if finds:
        table_ref[...] = arrived_ref[:, BCAP * cols :, :].astype(F32)[:, 3, :].astype(jnp.int32)
        copy = pltpu.make_async_copy(table_ref, asked_ref, sem)
        copy.start()
    beta = norm_of_tails(arrived_ref, cols)
    beta_ref[...] = beta
    raw_ref[...] = jnp.zeros((cols, cells), F32)
    if finds:
        copy.wait()

    def add(peer, carry):
        for rank in range(BCAP):
            where = lanes(asked_ref[peer, rank])
            raw_ref[:, where] += arrived_ref[peer, rank * cols : (rank + 1) * cols, :].astype(F32)
        return carry

    lax.fori_loop(0, peers, add, 0, unroll=2)
    scale = 1.0 / beta
    if not first:
        model_scale = beta / alpha_ref[...]

    def settle(block, squares):
        raw = raw_ref[:, lanes(block)] * scale
        if not first:
            raw = raw - model_ref[:, lanes(block)] * model_scale
        raw_ref[:, lanes(block)] = raw
        return squares + raw * raw

    squares = lax.fori_loop(0, cells // BS, settle, jnp.zeros((cols, BS), F32), unroll=4)
    tail = squares_tail(squares)
    if last:
        tails = jnp.concatenate([other[...] for other in others] + [tail], axis=0)
        out_ref[...] = jnp.broadcast_to(tails, out_ref.shape)
        return
    out_ref[:, BCAP * cols :, :] = jnp.broadcast_to(tail[None], (peers, TAIL, BS)).astype(BF16)

    def reply(peer, carry):
        for rank in range(BCAP):
            block = raw_ref[:, lanes(asked_ref[peer, rank])]
            out_ref[peer, rank * cols : (rank + 1) * cols, :] = block.astype(BF16)
        return carry

    lax.fori_loop(0, peers, reply, 0, unroll=2)


def estimate_kernel(*refs):
    estimate_ref = refs[-1]
    each = 3 * ITERS + 1
    for part in range(len(refs) // each):
        some = refs[part * each : (part + 1) * each]
        estimate_part(
            some[: ITERS + 1], some[ITERS + 1 : 2 * ITERS + 1], some[2 * ITERS + 1 :],
            estimate_ref, part,
        )


def estimate_part(betas, alphas, models, estimate_ref, part):
    cols, cells = models[0].shape
    rows = slice(part * cols, (part + 1) * cols)
    phi_bar = betas[0][...]
    rho_bar = alphas[0][...]
    trace = [1.0 / alphas[0][...]]
    weight = [jnp.zeros((cols, BS), F32)] * ITERS
    for step in range(ITERS):
        beta = betas[step + 1][...]
        rho = jnp.sqrt(rho_bar * rho_bar + beta * beta)
        cosine = rho_bar / rho
        sine = beta / rho
        gain = cosine * phi_bar / rho
        weight = [
            weight[i] + gain * trace[i] if i < len(trace) else weight[i] for i in range(ITERS)
        ]
        if step + 1 < ITERS:
            alpha = alphas[step + 1][...]
            theta = sine * alpha
            rho_bar = -cosine * alpha
            phi_bar = sine * phi_bar
            trace = [-(theta / rho) * value for value in trace] + [1.0 / alpha]

    def one_block(block, carry):
        where = lanes(block)
        total = weight[0] * models[0][:, where]
        for i in range(1, ITERS):
            total += weight[i] * models[i][:, where]
        estimate_ref[rows, where] = total
        return carry

    lax.fori_loop(0, cells // BS, one_block, 0, unroll=4)


def model_kernel(tails_ref, *refs):
    model_ref = refs[-1]
    summed = jnp.sum(tails_ref[...], axis=0)
    for part, raw_ref in enumerate(refs[:-1]):
        cols, cells = raw_ref.shape
        rows = slice(part * cols, (part + 1) * cols)
        some = summed[part * TAIL : (part + 1) * TAIL]
        row = some[0:1] + some[1:2] + some[2:3]
        column = jnp.sum(jnp.where(diagonal(cols), row, 0.0), axis=1, keepdims=True)
        scale = jnp.broadcast_to(1.0 / jnp.sqrt(column + EPS), (cols, BS))

        def one_block(block, carry):
            model_ref[rows, lanes(block)] = raw_ref[:, lanes(block)] * scale
            return carry

        lax.fori_loop(0, cells // BS, one_block, 0, unroll=4)


def call(kernel, name, in_spaces, outs, scratch=(), flops=0, moved=0):
    return pl.pallas_call(
        kernel,
        name=name,
        in_specs=[pl.BlockSpec(memory_space=space) for space in in_spaces],
        out_specs=[pl.BlockSpec(memory_space=space) for _, _, space in outs],
        out_shape=[jax.ShapeDtypeStruct(shape, dtype) for shape, dtype, _ in outs],
        scratch_shapes=list(scratch),
        compiler_params=pltpu.CompilerParams(vmem_limit_bytes=24 * 1024 * 1024),
        cost_estimate=pl.CostEstimate(flops=flops, bytes_accessed=moved, transcendentals=0),
    )


def on_device(ray_blocks, block_cells, block_counts, travel_times):
    pair_count, slot_count = ray_blocks.shape[:2]
    slots = pair_count * slot_count
    peers = lax.axis_size("pair")
    spots = peers * BCAP
    times = travel_times.T
    pairs = times.shape[1]
    cols = times.shape[0] // PARTS
    parts = range(PARTS)
    message = ((peers, BCAP * cols + TAIL, BS), BF16, VMEM)
    tile = ((cols, BS), F32, VMEM)
    data = ((cols, pairs), F32, VMEM)
    model = ((cols, CELL_DEV), F32, VMEM)
    whole = ((times.shape[0], CELL_DEV), F32, VMEM)
    totals = VMEM((spots + 1, cols, BS), F32)
    flops = 4 * slots * BS * BS * cols

    def exchange(values):
        return lax.all_to_all(values, "pair", split_axis=0, concat_axis=0, tiled=True)

    arrived, fetched = [None] * PARTS, [None] * PARTS
    models, betas, alphas = ([[] for _ in parts] for _ in range(3))
    for part in parts:
        if part == 0:
            outgoing, target = call(
                functools.partial(start_kernel, part), "start", [SMEM, SMEM, VMEM, VMEM],
                [message, ((slots,), jnp.int32, SMEM)],
                [totals, SMEM((spots,), jnp.int32), SMEM((peers,), jnp.int32)], flops, 6 << 20,
            )(block_cells, block_counts, times, ray_blocks)
        else:
            (outgoing,) = call(
                functools.partial(start_kernel, part), "start_more", [SMEM, VMEM, VMEM],
                [message], [totals], flops, 6 << 20,
            )(target, times, ray_blocks)
        arrived[part] = exchange(outgoing)
    for part in parts:
        if part == 0:
            raw, beta, reply, asked = call(
                functools.partial(cell_kernel, True, False), "cells_first", [VMEM],
                [model, tile, message, ((peers, BS), jnp.int32, SMEM)],
                [VMEM((peers, BS), jnp.int32), pltpu.SemaphoreType.DMA], 0, 6 << 20,
            )(arrived[part])
        else:
            raw, beta, reply = call(
                functools.partial(cell_kernel, True, False), "cells_more", [SMEM, VMEM],
                [model, tile, message], (), 0, 6 << 20,
            )(asked, arrived[part])
        models[part].append(raw)
        betas[part].append(beta)
        fetched[part] = exchange(reply)
    current = [times] * PARTS
    tails = []
    for step in range(ITERS):
        for part in parts:
            rows = slice(part * cols, (part + 1) * cols) if step == 0 else slice(0, cols)
            outgoing, current[part], alpha = call(
                functools.partial(pair_kernel, rows), "pairs", [SMEM, VMEM, VMEM, VMEM, VMEM],
                [message, data, tile], [totals], 2 * flops, 8 << 20,
            )(target, fetched[part], current[part], betas[part][-1], ray_blocks)
            alphas[part].append(alpha)
            arrived[part] = exchange(outgoing)
        last = step + 1 == ITERS
        for part in parts:
            out, others = message, []
            if last and part + 1 < PARTS:
                out = ((TAIL, BS), F32, VMEM)
            elif last:
                out, others = ((peers, PARTS * TAIL, BS), F32, VMEM), tails
            raw, beta, reply = call(
                functools.partial(cell_kernel, False, last), "cells_last" if last else "cells",
                [SMEM] + [VMEM] * (3 + len(others)), [model, tile, out], (), 0, 8 << 20,
            )(asked, arrived[part], models[part][-1], alphas[part][-1], *others)
            betas[part].append(beta)
            models[part].append(raw)
            if not last:
                fetched[part] = exchange(reply)
            elif part + 1 < PARTS:
                tails.append(reply)
    summed = exchange(reply)
    given = [
        ref for part in parts for ref in betas[part] + alphas[part] + models[part][:ITERS]
    ]
    (estimate,) = call(estimate_kernel, "estimate", [VMEM] * len(given), [whole], (), 0, 6 << 20)(
        *given
    )
    (model_vec,) = call(
        model_kernel, "model", [VMEM] * (PARTS + 1), [whole], (), 0, 4 << 20
    )(summed, *[models[part][-1] for part in parts])
    return (estimate.T, model_vec.T)


def solution(mesh):
    return jax.shard_map(
        on_device,
        mesh=mesh,
        in_specs=(
            P(("groups", "pair"), None, None, None),
            P(("groups", "pair"), None),
            P(("groups", "pair")),
            P(("groups", "pair"), None),
        ),
        out_specs=(P(("groups", "pair"), None), P(("groups", "pair"), None)),
        check_vma=False,
    )
```

```python
import functools

import jax
import jax.numpy as jnp
from jax import lax
from jax.experimental import pallas as pl
from jax.experimental.pallas import tpu as pltpu
from jax.sharding import PartitionSpec as P

CELL_DEV = 8192
BCAP = 4
BS = 128
TAIL = 16
ITERS = 2
PARTS = 1
EPS = 1e-12
F32 = jnp.float32
BF16 = jnp.bfloat16
VMEM = pltpu.VMEM
SMEM = pltpu.SMEM


def diagonal(cols):
    shape = (cols, BS)
    return lax.broadcasted_iota(jnp.int32, shape, 0) == lax.broadcasted_iota(jnp.int32, shape, 1)


def squares_tail(squares):
    cols = squares.shape[0]
    total = jnp.sum(squares, axis=1, keepdims=True)
    row = jnp.sum(jnp.where(diagonal(cols), total, 0.0), axis=0, keepdims=True)
    high = row.astype(BF16).astype(F32)
    middle = (row - high).astype(BF16).astype(F32)
    low = row - high - middle
    place = lax.broadcasted_iota(jnp.int32, (TAIL, BS), 0)
    return jnp.where(
        place == 0, high, jnp.where(place == 1, middle, jnp.where(place == 2, low, 0.0))
    )


def norm_of_tails(message_refs, cols):
    summed = sum(message_ref[BCAP * cols :, :].astype(F32) for message_ref in message_refs)
    row = summed[0:1] + summed[1:2] + summed[2:3]
    column = jnp.sum(jnp.where(diagonal(cols), row, 0.0), axis=1, keepdims=True)
    return jnp.broadcast_to(jnp.sqrt(column + EPS), (cols, BS))


def lanes(block):
    return pl.ds(pl.multiple_of(block * BS, BS), BS)


def transposed(data_ref, rows, rays_ref, target_ref, total_ref, message_refs):
    pair_count, slot_count = rays_ref.shape[:2]
    cols = total_ref.shape[1]
    spots = len(message_refs) * BCAP

    def clear(index, carry):
        total_ref[index] = jnp.zeros((cols, BS), F32)
        return carry

    lax.fori_loop(0, spots, clear, 0, unroll=8)

    def one_pair(pair, carry):
        data = data_ref[rows, lanes(pair)]
        high = data.astype(BF16)
        low = (data - high.astype(F32)).astype(BF16)
        pieces = jnp.concatenate([high, low], axis=0)
        for slot in range(0, slot_count, 2):
            rays = jnp.concatenate([rays_ref[pair, slot], rays_ref[pair, slot + 1]], axis=1)
            part = jnp.dot(pieces, rays, preferred_element_type=F32)
            part = part[:cols] + part[cols:]
            for half in range(2):
                spot = target_ref[pair * slot_count + slot + half]
                total_ref[spot] += part[:, half * BS : (half + 1) * BS]
        return carry

    lax.fori_loop(0, pair_count, one_pair, 0)

    for peer, message_ref in enumerate(message_refs):
        for rank in range(BCAP):
            message_ref[rank * cols : (rank + 1) * cols, :] = total_ref[
                peer * BCAP + rank
            ].astype(BF16)


def start_kernel(part, peers, *refs):
    if part == 0:
        me_ref, cells_ref, counts_ref, times_ref, rays_ref = refs[:5]
        message_refs = refs[5 : 5 + peers]
        target_ref, total_ref, table_ref, used_ref = refs[5 + peers :]
    else:
        target_ref, times_ref, rays_ref = refs[:3]
        message_refs = refs[3 : 3 + peers]
        total_ref = refs[-1]
    pair_count, slot_count = rays_ref.shape[:2]
    cols = total_ref.shape[1]
    columns = slice(part * cols, (part + 1) * cols)
    if part == 0:
        find_places(me_ref, cells_ref, counts_ref, target_ref, table_ref, used_ref)
    transposed(times_ref, columns, rays_ref, target_ref, total_ref, message_refs)
    squares = jnp.zeros((cols, BS), F32)
    for pair in range(pair_count):
        values = times_ref[columns, pair * BS : (pair + 1) * BS]
        squares += values * values
    tail = squares_tail(squares)
    place = lax.broadcasted_iota(jnp.int32, (TAIL, BS), 0)
    lane = lax.broadcasted_iota(jnp.int32, (TAIL, BS), 1)
    for peer, message_ref in enumerate(message_refs):
        rows = tail
        if part == 0:
            for rank in range(BCAP):
                asked = table_ref[peer * BCAP + rank].astype(F32)
                rows = jnp.where((place == 3) & (lane == rank), asked, rows)
        message_ref[BCAP * cols :, :] = rows.astype(BF16)


def find_places(me_ref, cells_ref, counts_ref, target_ref, table_ref, used_ref):
    pair_count, slot_count = cells_ref.shape
    peers = used_ref.shape[0]
    owned = CELL_DEV // BS

    def clear(peer, carry):
        used_ref[peer] = 0
        for rank in range(BCAP):
            table_ref[peer * BCAP + rank] = 0
        return carry

    lax.fori_loop(0, peers, clear, 0)

    def one_pair(pair, carry):
        count = counts_ref[pair]
        for slot in range(slot_count):
            cell = cells_ref[pair, slot]
            owner = (cell // owned) ^ me_ref[0]
            local = cell % owned
            used = used_ref[owner]
            rank = used
            for other in range(BCAP - 1, -1, -1):
                same = (table_ref[owner * BCAP + other] == local) & (other < used)
                rank = jnp.where(same, other, rank)
            spot = owner * BCAP + rank
            table_ref[spot] = local
            used_ref[owner] = jnp.maximum(used, rank + 1)
            target_ref[pair * slot_count + slot] = jnp.where(slot < count, spot, peers * BCAP)
        return carry

    lax.fori_loop(0, pair_count, one_pair, 0)


def pair_kernel(rows, peers, target_ref, *refs):
    fetched_refs = refs[:peers]
    data_ref, beta_ref, rays_ref = refs[peers : peers + 3]
    message_refs = refs[peers + 3 : 2 * peers + 3]
    raw_ref, alpha_ref, total_ref, fetched_ref = refs[2 * peers + 3 :]
    pair_count, slot_count = rays_ref.shape[:2]
    cols = raw_ref.shape[0]
    spots = peers * BCAP
    for peer in range(peers):
        fetched_ref[peer] = fetched_refs[peer][: BCAP * cols, :]
    alpha = norm_of_tails(fetched_refs, cols)
    alpha_ref[...] = alpha
    model_scale = 1.0 / alpha
    data_scale = alpha / beta_ref[...]

    def one_pair(pair, squares):
        chosen = []
        for slot in range(slot_count):
            spot = target_ref[pair * slot_count + slot]
            live = spot < spots
            spot = jnp.where(live, spot, 0)
            inside = pl.ds(pl.multiple_of((spot % BCAP) * cols, cols), cols)
            block = fetched_ref[spot // BCAP, inside, :]
            chosen.append(jnp.where(live, block, jnp.zeros_like(block)))
        rays = jnp.concatenate([rays_ref[pair, slot] for slot in range(slot_count)], axis=1)
        product = lax.dot_general(
            jnp.concatenate(chosen, axis=1), rays, (((1,), (1,)), ((), ())),
            preferred_element_type=F32,
        )
        raw = product * model_scale - data_ref[rows, lanes(pair)] * data_scale
        raw_ref[:, lanes(pair)] = raw
        return squares + raw * raw

    squares = lax.fori_loop(0, pair_count, one_pair, jnp.zeros((cols, BS), F32))
    transposed(raw_ref, slice(0, cols), rays_ref, target_ref, total_ref, message_refs)
    tail = squares_tail(squares).astype(BF16)
    for message_ref in message_refs:
        message_ref[BCAP * cols :, :] = tail


def cell_kernel(first, last, peers, *refs):
    finds = first and refs[0].dtype == BF16
    if not finds:
        asked_ref, *refs = refs
    arrived_refs, refs = refs[:peers], refs[peers:]
    if not first:
        model_ref, alpha_ref, *refs = refs
    if last:
        *others, raw_ref, beta_ref, out_ref = refs
    else:
        raw_ref, beta_ref, *refs = refs
        out_refs = refs[:peers]
    cols, cells = raw_ref.shape
    if finds:
        asked_ref, table_ref, sem = refs[peers:]
        for peer in range(peers):
            table_ref[peer : peer + 1, :] = (
                arrived_refs[peer][BCAP * cols :, :].astype(F32)[3:4].astype(jnp.int32)
            )
        copy = pltpu.make_async_copy(table_ref, asked_ref, sem)
        copy.start()
    beta = norm_of_tails(arrived_refs, cols)
    beta_ref[...] = beta
    raw_ref[...] = jnp.zeros((cols, cells), F32)
    if finds:
        copy.wait()
    for peer in range(peers):
        for rank in range(BCAP):
            where = lanes(asked_ref[peer, rank])
            block = arrived_refs[peer][rank * cols : (rank + 1) * cols, :]
            raw_ref[:, where] += block.astype(F32)
    scale = 1.0 / beta
    if not first:
        model_scale = beta / alpha_ref[...]

    def settle(block, squares):
        raw = raw_ref[:, lanes(block)] * scale
        if not first:
            raw = raw - model_ref[:, lanes(block)] * model_scale
        raw_ref[:, lanes(block)] = raw
        return squares + raw * raw

    squares = lax.fori_loop(0, cells // BS, settle, jnp.zeros((cols, BS), F32), unroll=4)
    tail = squares_tail(squares)
    if last:
        tails = jnp.concatenate([other[...] for other in others] + [tail], axis=0)
        out_ref[...] = jnp.broadcast_to(tails, out_ref.shape)
        return
    for peer, out_ref in enumerate(out_refs):
        out_ref[BCAP * cols :, :] = tail.astype(BF16)
        for rank in range(BCAP):
            block = raw_ref[:, lanes(asked_ref[peer, rank])]
            out_ref[rank * cols : (rank + 1) * cols, :] = block.astype(BF16)


def estimate_kernel(*refs):
    estimate_ref = refs[-1]
    each = 3 * ITERS + 1
    for part in range(len(refs) // each):
        some = refs[part * each : (part + 1) * each]
        estimate_part(
            some[: ITERS + 1], some[ITERS + 1 : 2 * ITERS + 1], some[2 * ITERS + 1 :],
            estimate_ref, part,
        )


def estimate_part(betas, alphas, models, estimate_ref, part):
    cols, cells = models[0].shape
    rows = slice(part * cols, (part + 1) * cols)
    phi_bar = betas[0][...]
    rho_bar = alphas[0][...]
    trace = [1.0 / alphas[0][...]]
    weight = [jnp.zeros((cols, BS), F32)] * ITERS
    for step in range(ITERS):
        beta = betas[step + 1][...]
        rho = jnp.sqrt(rho_bar * rho_bar + beta * beta)
        cosine = rho_bar / rho
        sine = beta / rho
        gain = cosine * phi_bar / rho
        weight = [
            weight[i] + gain * trace[i] if i < len(trace) else weight[i] for i in range(ITERS)
        ]
        if step + 1 < ITERS:
            alpha = alphas[step + 1][...]
            theta = sine * alpha
            rho_bar = -cosine * alpha
            phi_bar = sine * phi_bar
            trace = [-(theta / rho) * value for value in trace] + [1.0 / alpha]

    def one_block(block, carry):
        where = lanes(block)
        total = weight[0] * models[0][:, where]
        for i in range(1, ITERS):
            total += weight[i] * models[i][:, where]
        estimate_ref[rows, where] = total
        return carry

    lax.fori_loop(0, cells // BS, one_block, 0, unroll=4)


def model_kernel(tails_ref, *refs):
    model_ref = refs[-1]
    summed = jnp.sum(tails_ref[...], axis=0)
    for part, raw_ref in enumerate(refs[:-1]):
        cols, cells = raw_ref.shape
        rows = slice(part * cols, (part + 1) * cols)
        some = summed[part * TAIL : (part + 1) * TAIL]
        row = some[0:1] + some[1:2] + some[2:3]
        column = jnp.sum(jnp.where(diagonal(cols), row, 0.0), axis=1, keepdims=True)
        scale = jnp.broadcast_to(1.0 / jnp.sqrt(column + EPS), (cols, BS))

        def one_block(block, carry):
            model_ref[rows, lanes(block)] = raw_ref[:, lanes(block)] * scale
            return carry

        lax.fori_loop(0, cells // BS, one_block, 0, unroll=4)


def call(kernel, name, in_spaces, outs, scratch=(), flops=0, moved=0):
    return pl.pallas_call(
        kernel,
        name=name,
        in_specs=[pl.BlockSpec(memory_space=space) for space in in_spaces],
        out_specs=[pl.BlockSpec(memory_space=space) for _, _, space in outs],
        out_shape=[jax.ShapeDtypeStruct(shape, dtype) for shape, dtype, _ in outs],
        scratch_shapes=list(scratch),
        compiler_params=pltpu.CompilerParams(vmem_limit_bytes=24 * 1024 * 1024),
        cost_estimate=pl.CostEstimate(flops=flops, bytes_accessed=moved, transcendentals=0),
    )


def exchange(values):
    peers = len(values)
    return [values[0]] + [
        lax.ppermute(values[step], "pair", [(i, i ^ step) for i in range(peers)])
        for step in range(1, peers)
    ]


def on_device(ray_blocks, block_cells, block_counts, travel_times):
    pair_count, slot_count = ray_blocks.shape[:2]
    slots = pair_count * slot_count
    peers = lax.axis_size("pair")
    spots = peers * BCAP
    times = travel_times.T
    pairs = times.shape[1]
    cols = times.shape[0] // PARTS
    parts = range(PARTS)
    messages = [((BCAP * cols + TAIL, BS), BF16, VMEM)] * peers
    ins = [VMEM] * peers
    tile = ((cols, BS), F32, VMEM)
    data = ((cols, pairs), F32, VMEM)
    model = ((cols, CELL_DEV), F32, VMEM)
    whole = ((times.shape[0], CELL_DEV), F32, VMEM)
    totals = VMEM((spots + 1, cols, BS), F32)
    gathered = VMEM((peers, BCAP * cols, BS), BF16)
    flops = 4 * slots * BS * BS * cols
    me = lax.axis_index("pair").astype(jnp.int32).reshape(1)

    arrived, fetched = [None] * PARTS, [None] * PARTS
    models, betas, alphas = ([[] for _ in parts] for _ in range(3))
    for part in parts:
        kernel = functools.partial(start_kernel, part, peers)
        if part == 0:
            *outgoing, target = call(
                kernel, "start", [SMEM, SMEM, SMEM, VMEM, VMEM],
                messages + [((slots,), jnp.int32, SMEM)],
                [totals, SMEM((spots,), jnp.int32), SMEM((peers,), jnp.int32)], flops, 6 << 20,
            )(me, block_cells, block_counts, times, ray_blocks)
        else:
            outgoing = call(
                kernel, "start_more", [SMEM, VMEM, VMEM], messages, [totals], flops, 6 << 20,
            )(target, times, ray_blocks)
        arrived[part] = exchange(outgoing)
    for part in parts:
        kernel = functools.partial(cell_kernel, True, False, peers)
        if part == 0:
            raw, beta, *reply, asked = call(
                kernel, "cells_first", ins,
                [model, tile] + messages + [((peers, BS), jnp.int32, SMEM)],
                [VMEM((peers, BS), jnp.int32), pltpu.SemaphoreType.DMA], 0, 6 << 20,
            )(*arrived[part])
        else:
            raw, beta, *reply = call(
                kernel, "cells_more", [SMEM] + ins, [model, tile] + messages, (), 0, 6 << 20,
            )(asked, *arrived[part])
        models[part].append(raw)
        betas[part].append(beta)
        fetched[part] = exchange(reply)
    current = [times] * PARTS
    tails = []
    for step in range(ITERS):
        for part in parts:
            rows = slice(part * cols, (part + 1) * cols) if step == 0 else slice(0, cols)
            *outgoing, current[part], alpha = call(
                functools.partial(pair_kernel, rows, peers), "pairs",
                [SMEM] + ins + [VMEM, VMEM, VMEM],
                messages + [data, tile], [totals, gathered], 2 * flops, 8 << 20,
            )(target, *fetched[part], current[part], betas[part][-1], ray_blocks)
            alphas[part].append(alpha)
            arrived[part] = exchange(outgoing)
        last = step + 1 == ITERS
        for part in parts:
            out, others = messages, []
            if last and part + 1 < PARTS:
                out = [((TAIL, BS), F32, VMEM)]
            elif last:
                out, others = [((peers, PARTS * TAIL, BS), F32, VMEM)], tails
            raw, beta, *reply = call(
                functools.partial(cell_kernel, False, last, peers),
                "cells_last" if last else "cells",
                [SMEM] + ins + [VMEM] * (2 + len(others)), [model, tile] + out, (), 0, 8 << 20,
            )(asked, *arrived[part], models[part][-1], alphas[part][-1], *others)
            betas[part].append(beta)
            models[part].append(raw)
            if not last:
                fetched[part] = exchange(reply)
            elif part + 1 < PARTS:
                tails.append(reply[0])
    summed = lax.all_to_all(reply[0], "pair", split_axis=0, concat_axis=0, tiled=True)
    given = [
        ref for part in parts for ref in betas[part] + alphas[part] + models[part][:ITERS]
    ]
    (estimate,) = call(estimate_kernel, "estimate", [VMEM] * len(given), [whole], (), 0, 6 << 20)(
        *given
    )
    (model_vec,) = call(
        model_kernel, "model", [VMEM] * (PARTS + 1), [whole], (), 0, 4 << 20
    )(summed, *[models[part][-1] for part in parts])
    return (estimate.T, model_vec.T)


def solution(mesh):
    return jax.shard_map(
        on_device,
        mesh=mesh,
        in_specs=(
            P(("groups", "pair"), None, None, None),
            P(("groups", "pair"), None),
            P(("groups", "pair")),
            P(("groups", "pair"), None),
        ),
        out_specs=(P(("groups", "pair"), None), P(("groups", "pair"), None)),
        check_vma=False,
    )
```

```python
import functools

import jax
import jax.numpy as jnp
from jax import lax
from jax.experimental import pallas as pl
from jax.experimental.pallas import tpu as pltpu
from jax.sharding import PartitionSpec as P

CELL_DEV = 8192
BCAP = 4
BS = 128
TAIL = 16
ITERS = 2
PARTS = 1
EPS = 1e-12
F32 = jnp.float32
BF16 = jnp.bfloat16
VMEM = pltpu.VMEM
SMEM = pltpu.SMEM


def diagonal(cols):
    shape = (cols, BS)
    return lax.broadcasted_iota(jnp.int32, shape, 0) == lax.broadcasted_iota(jnp.int32, shape, 1)


def squares_tail(squares):
    cols = squares.shape[0]
    total = jnp.sum(squares, axis=1, keepdims=True)
    row = jnp.sum(jnp.where(diagonal(cols), total, 0.0), axis=0, keepdims=True)
    high = row.astype(BF16).astype(F32)
    middle = (row - high).astype(BF16).astype(F32)
    low = row - high - middle
    place = lax.broadcasted_iota(jnp.int32, (TAIL, BS), 0)
    return jnp.where(
        place == 0, high, jnp.where(place == 1, middle, jnp.where(place == 2, low, 0.0))
    )


def norm_of_tails(message_refs, cols):
    summed = sum(message_ref[BCAP * cols :, :].astype(F32) for message_ref in message_refs)
    row = summed[0:1] + summed[1:2] + summed[2:3]
    column = jnp.sum(jnp.where(diagonal(cols), row, 0.0), axis=1, keepdims=True)
    return jnp.broadcast_to(jnp.sqrt(column + EPS), (cols, BS))


def lanes(block):
    return pl.ds(pl.multiple_of(block * BS, BS), BS)


def transposed(data_ref, rows, rays_ref, target_ref, total_ref, message_refs):
    pair_count, slot_count = rays_ref.shape[:2]
    cols = total_ref.shape[1]
    spots = len(message_refs) * BCAP

    def clear(index, carry):
        total_ref[index] = jnp.zeros((cols, BS), F32)
        return carry

    lax.fori_loop(0, spots, clear, 0, unroll=8)

    def one_pair(pair, carry):
        data = data_ref[rows, lanes(pair)]
        high = data.astype(BF16)
        low = (data - high.astype(F32)).astype(BF16)
        pieces = jnp.concatenate([high, low], axis=0)
        for slot in range(0, slot_count, 2):
            rays = jnp.concatenate([rays_ref[pair, slot], rays_ref[pair, slot + 1]], axis=1)
            part = jnp.dot(pieces, rays, preferred_element_type=F32)
            part = part[:cols] + part[cols:]
            for half in range(2):
                spot = target_ref[pair * slot_count + slot + half]
                total_ref[spot] += part[:, half * BS : (half + 1) * BS]
        return carry

    lax.fori_loop(0, pair_count, one_pair, 0)

    for peer, message_ref in enumerate(message_refs):
        for rank in range(BCAP):
            message_ref[rank * cols : (rank + 1) * cols, :] = total_ref[
                peer * BCAP + rank
            ].astype(BF16)


def start_kernel(part, peers, *refs):
    if part == 0:
        me_ref, cells_ref, counts_ref, times_ref, rays_ref = refs[:5]
        message_refs = refs[5 : 5 + peers]
        target_ref, total_ref, table_ref, used_ref = refs[5 + peers :]
    else:
        target_ref, times_ref, rays_ref = refs[:3]
        message_refs = refs[3 : 3 + peers]
        total_ref = refs[-1]
    pair_count, slot_count = rays_ref.shape[:2]
    cols = total_ref.shape[1]
    columns = slice(part * cols, (part + 1) * cols)
    if part == 0:
        find_places(me_ref, cells_ref, counts_ref, target_ref, table_ref, used_ref)
    transposed(times_ref, columns, rays_ref, target_ref, total_ref, message_refs)
    squares = jnp.zeros((cols, BS), F32)
    for pair in range(pair_count):
        values = times_ref[columns, pair * BS : (pair + 1) * BS]
        squares += values * values
    tail = squares_tail(squares)
    place = lax.broadcasted_iota(jnp.int32, (TAIL, BS), 0)
    lane = lax.broadcasted_iota(jnp.int32, (TAIL, BS), 1)
    for peer, message_ref in enumerate(message_refs):
        rows = tail
        if part == 0:
            for rank in range(BCAP):
                asked = table_ref[peer * BCAP + rank].astype(F32)
                rows = jnp.where((place == 3) & (lane == rank), asked, rows)
        message_ref[BCAP * cols :, :] = rows.astype(BF16)


def find_places(me_ref, cells_ref, counts_ref, target_ref, table_ref, used_ref):
    pair_count, slot_count = cells_ref.shape
    peers = used_ref.shape[0]
    owned = CELL_DEV // BS

    def clear(peer, carry):
        used_ref[peer] = 0
        for rank in range(BCAP):
            table_ref[peer * BCAP + rank] = 0
        return carry

    lax.fori_loop(0, peers, clear, 0)

    def one_pair(pair, carry):
        count = counts_ref[pair]
        for slot in range(slot_count):
            cell = cells_ref[pair, slot]
            owner = (peers - ((cell // owned) ^ me_ref[0])) % peers
            local = cell % owned
            used = used_ref[owner]
            rank = used
            for other in range(BCAP - 1, -1, -1):
                same = (table_ref[owner * BCAP + other] == local) & (other < used)
                rank = jnp.where(same, other, rank)
            spot = owner * BCAP + rank
            table_ref[spot] = local
            used_ref[owner] = jnp.maximum(used, rank + 1)
            target_ref[pair * slot_count + slot] = jnp.where(slot < count, spot, peers * BCAP)
        return carry

    lax.fori_loop(0, pair_count, one_pair, 0)


def pair_kernel(rows, peers, target_ref, *refs):
    fetched_refs = refs[:peers]
    data_ref, beta_ref, rays_ref = refs[peers : peers + 3]
    message_refs = refs[peers + 3 : 2 * peers + 3]
    raw_ref, alpha_ref, total_ref, fetched_ref = refs[2 * peers + 3 :]
    pair_count, slot_count = rays_ref.shape[:2]
    cols = raw_ref.shape[0]
    spots = peers * BCAP
    for peer in range(peers):
        fetched_ref[peer] = fetched_refs[peer][: BCAP * cols, :]
    alpha = norm_of_tails(fetched_refs, cols)
    alpha_ref[...] = alpha
    model_scale = 1.0 / alpha
    data_scale = alpha / beta_ref[...]

    def one_pair(pair, squares):
        chosen = []
        for slot in range(slot_count):
            spot = target_ref[pair * slot_count + slot]
            live = spot < spots
            spot = jnp.where(live, spot, 0)
            inside = pl.ds(pl.multiple_of((spot % BCAP) * cols, cols), cols)
            block = fetched_ref[spot // BCAP, inside, :]
            chosen.append(jnp.where(live, block, jnp.zeros_like(block)))
        rays = jnp.concatenate([rays_ref[pair, slot] for slot in range(slot_count)], axis=1)
        product = lax.dot_general(
            jnp.concatenate(chosen, axis=1), rays, (((1,), (1,)), ((), ())),
            preferred_element_type=F32,
        )
        raw = product * model_scale - data_ref[rows, lanes(pair)] * data_scale
        raw_ref[:, lanes(pair)] = raw
        return squares + raw * raw

    squares = lax.fori_loop(0, pair_count, one_pair, jnp.zeros((cols, BS), F32))
    transposed(raw_ref, slice(0, cols), rays_ref, target_ref, total_ref, message_refs)
    tail = squares_tail(squares).astype(BF16)
    for message_ref in message_refs:
        message_ref[BCAP * cols :, :] = tail


def cell_kernel(first, last, peers, *refs):
    finds = first and refs[0].dtype == BF16
    if not finds:
        asked_ref, *refs = refs
    arrived_refs, refs = refs[:peers], refs[peers:]
    if not first:
        model_ref, alpha_ref, *refs = refs
    if last:
        *others, raw_ref, beta_ref, out_ref = refs
    else:
        raw_ref, beta_ref, *refs = refs
        out_refs = refs[:peers]
    cols, cells = raw_ref.shape
    if finds:
        asked_ref, table_ref, sem = refs[peers:]
        for peer in range(peers):
            table_ref[peer : peer + 1, :] = (
                arrived_refs[peer][BCAP * cols :, :].astype(F32)[3:4].astype(jnp.int32)
            )
        copy = pltpu.make_async_copy(table_ref, asked_ref, sem)
        copy.start()
    beta = norm_of_tails(arrived_refs, cols)
    beta_ref[...] = beta
    raw_ref[...] = jnp.zeros((cols, cells), F32)
    if finds:
        copy.wait()
    for peer in range(peers):
        for rank in range(BCAP):
            where = lanes(asked_ref[peer, rank])
            block = arrived_refs[peer][rank * cols : (rank + 1) * cols, :]
            raw_ref[:, where] += block.astype(F32)
    scale = 1.0 / beta
    if not first:
        model_scale = beta / alpha_ref[...]

    def settle(block, squares):
        raw = raw_ref[:, lanes(block)] * scale
        if not first:
            raw = raw - model_ref[:, lanes(block)] * model_scale
        raw_ref[:, lanes(block)] = raw
        return squares + raw * raw

    squares = lax.fori_loop(0, cells // BS, settle, jnp.zeros((cols, BS), F32), unroll=4)
    tail = squares_tail(squares)
    if last:
        tails = jnp.concatenate([other[...] for other in others] + [tail], axis=0)
        out_ref[...] = jnp.broadcast_to(tails, out_ref.shape)
        return
    for peer, out_ref in enumerate(out_refs):
        out_ref[BCAP * cols :, :] = tail.astype(BF16)
        for rank in range(BCAP):
            block = raw_ref[:, lanes(asked_ref[peer, rank])]
            out_ref[rank * cols : (rank + 1) * cols, :] = block.astype(BF16)


def estimate_kernel(*refs):
    estimate_ref = refs[-1]
    each = 3 * ITERS + 1
    for part in range(len(refs) // each):
        some = refs[part * each : (part + 1) * each]
        estimate_part(
            some[: ITERS + 1], some[ITERS + 1 : 2 * ITERS + 1], some[2 * ITERS + 1 :],
            estimate_ref, part,
        )


def estimate_part(betas, alphas, models, estimate_ref, part):
    cols, cells = models[0].shape
    rows = slice(part * cols, (part + 1) * cols)
    phi_bar = betas[0][...]
    rho_bar = alphas[0][...]
    trace = [1.0 / alphas[0][...]]
    weight = [jnp.zeros((cols, BS), F32)] * ITERS
    for step in range(ITERS):
        beta = betas[step + 1][...]
        rho = jnp.sqrt(rho_bar * rho_bar + beta * beta)
        cosine = rho_bar / rho
        sine = beta / rho
        gain = cosine * phi_bar / rho
        weight = [
            weight[i] + gain * trace[i] if i < len(trace) else weight[i] for i in range(ITERS)
        ]
        if step + 1 < ITERS:
            alpha = alphas[step + 1][...]
            theta = sine * alpha
            rho_bar = -cosine * alpha
            phi_bar = sine * phi_bar
            trace = [-(theta / rho) * value for value in trace] + [1.0 / alpha]

    def one_block(block, carry):
        where = lanes(block)
        total = weight[0] * models[0][:, where]
        for i in range(1, ITERS):
            total += weight[i] * models[i][:, where]
        estimate_ref[rows, where] = total
        return carry

    lax.fori_loop(0, cells // BS, one_block, 0, unroll=4)


def model_kernel(tails_ref, *refs):
    model_ref = refs[-1]
    summed = jnp.sum(tails_ref[...], axis=0)
    for part, raw_ref in enumerate(refs[:-1]):
        cols, cells = raw_ref.shape
        rows = slice(part * cols, (part + 1) * cols)
        some = summed[part * TAIL : (part + 1) * TAIL]
        row = some[0:1] + some[1:2] + some[2:3]
        column = jnp.sum(jnp.where(diagonal(cols), row, 0.0), axis=1, keepdims=True)
        scale = jnp.broadcast_to(1.0 / jnp.sqrt(column + EPS), (cols, BS))

        def one_block(block, carry):
            model_ref[rows, lanes(block)] = raw_ref[:, lanes(block)] * scale
            return carry

        lax.fori_loop(0, cells // BS, one_block, 0, unroll=4)


def call(kernel, name, in_spaces, outs, scratch=(), flops=0, moved=0):
    return pl.pallas_call(
        kernel,
        name=name,
        in_specs=[pl.BlockSpec(memory_space=space) for space in in_spaces],
        out_specs=[pl.BlockSpec(memory_space=space) for _, _, space in outs],
        out_shape=[jax.ShapeDtypeStruct(shape, dtype) for shape, dtype, _ in outs],
        scratch_shapes=list(scratch),
        compiler_params=pltpu.CompilerParams(vmem_limit_bytes=24 * 1024 * 1024),
        cost_estimate=pl.CostEstimate(flops=flops, bytes_accessed=moved, transcendentals=0),
    )


def exchange(values):
    peers = len(values)
    return [values[0]] + [
        lax.ppermute(values[i], "pair", [(one, one ^ (peers - i)) for one in range(peers)])
        for i in range(1, peers)
    ]


def on_device(ray_blocks, block_cells, block_counts, travel_times):
    pair_count, slot_count = ray_blocks.shape[:2]
    slots = pair_count * slot_count
    peers = lax.axis_size("pair")
    spots = peers * BCAP
    times = travel_times.T
    pairs = times.shape[1]
    cols = times.shape[0] // PARTS
    parts = range(PARTS)
    messages = [((BCAP * cols + TAIL, BS), BF16, VMEM)] * peers
    ins = [VMEM] * peers
    tile = ((cols, BS), F32, VMEM)
    data = ((cols, pairs), F32, VMEM)
    model = ((cols, CELL_DEV), F32, VMEM)
    whole = ((times.shape[0], CELL_DEV), F32, VMEM)
    totals = VMEM((spots + 1, cols, BS), F32)
    gathered = VMEM((peers, BCAP * cols, BS), BF16)
    flops = 4 * slots * BS * BS * cols
    me = lax.axis_index("pair").astype(jnp.int32).reshape(1)

    arrived, fetched = [None] * PARTS, [None] * PARTS
    models, betas, alphas = ([[] for _ in parts] for _ in range(3))
    for part in parts:
        kernel = functools.partial(start_kernel, part, peers)
        if part == 0:
            *outgoing, target = call(
                kernel, "start", [SMEM, SMEM, SMEM, VMEM, VMEM],
                messages + [((slots,), jnp.int32, SMEM)],
                [totals, SMEM((spots,), jnp.int32), SMEM((peers,), jnp.int32)], flops, 6 << 20,
            )(me, block_cells, block_counts, times, ray_blocks)
        else:
            outgoing = call(
                kernel, "start_more", [SMEM, VMEM, VMEM], messages, [totals], flops, 6 << 20,
            )(target, times, ray_blocks)
        arrived[part] = exchange(outgoing)
    for part in parts:
        kernel = functools.partial(cell_kernel, True, False, peers)
        if part == 0:
            raw, beta, *reply, asked = call(
                kernel, "cells_first", ins,
                [model, tile] + messages + [((peers, BS), jnp.int32, SMEM)],
                [VMEM((peers, BS), jnp.int32), pltpu.SemaphoreType.DMA], 0, 6 << 20,
            )(*arrived[part])
        else:
            raw, beta, *reply = call(
                kernel, "cells_more", [SMEM] + ins, [model, tile] + messages, (), 0, 6 << 20,
            )(asked, *arrived[part])
        models[part].append(raw)
        betas[part].append(beta)
        fetched[part] = exchange(reply)
    current = [times] * PARTS
    tails = []
    for step in range(ITERS):
        for part in parts:
            rows = slice(part * cols, (part + 1) * cols) if step == 0 else slice(0, cols)
            *outgoing, current[part], alpha = call(
                functools.partial(pair_kernel, rows, peers), "pairs",
                [SMEM] + ins + [VMEM, VMEM, VMEM],
                messages + [data, tile], [totals, gathered], 2 * flops, 8 << 20,
            )(target, *fetched[part], current[part], betas[part][-1], ray_blocks)
            alphas[part].append(alpha)
            arrived[part] = exchange(outgoing)
        last = step + 1 == ITERS
        for part in parts:
            out, others = messages, []
            if last and part + 1 < PARTS:
                out = [((TAIL, BS), F32, VMEM)]
            elif last:
                out, others = [((peers, PARTS * TAIL, BS), F32, VMEM)], tails
            raw, beta, *reply = call(
                functools.partial(cell_kernel, False, last, peers),
                "cells_last" if last else "cells",
                [SMEM] + ins + [VMEM] * (2 + len(others)), [model, tile] + out, (), 0, 8 << 20,
            )(asked, *arrived[part], models[part][-1], alphas[part][-1], *others)
            betas[part].append(beta)
            models[part].append(raw)
            if not last:
                fetched[part] = exchange(reply)
            elif part + 1 < PARTS:
                tails.append(reply[0])
    summed = lax.all_to_all(reply[0], "pair", split_axis=0, concat_axis=0, tiled=True)
    given = [
        ref for part in parts for ref in betas[part] + alphas[part] + models[part][:ITERS]
    ]
    (estimate,) = call(estimate_kernel, "estimate", [VMEM] * len(given), [whole], (), 0, 6 << 20)(
        *given
    )
    (model_vec,) = call(
        model_kernel, "model", [VMEM] * (PARTS + 1), [whole], (), 0, 4 << 20
    )(summed, *[models[part][-1] for part in parts])
    return (estimate.T, model_vec.T)


def solution(mesh):
    return jax.shard_map(
        on_device,
        mesh=mesh,
        in_specs=(
            P(("groups", "pair"), None, None, None),
            P(("groups", "pair"), None),
            P(("groups", "pair")),
            P(("groups", "pair"), None),
        ),
        out_specs=(P(("groups", "pair"), None), P(("groups", "pair"), None)),
        check_vma=False,
    )
```

```python
import functools

import jax
import jax.numpy as jnp
from jax import lax
from jax.experimental import pallas as pl
from jax.experimental.pallas import tpu as pltpu
from jax.sharding import PartitionSpec as P

CELL_DEV = 8192
BCAP = 4
BS = 128
TAIL = 16
ITERS = 2
EPS = 1e-12
F32 = jnp.float32
BF16 = jnp.bfloat16
VMEM = pltpu.VMEM
SMEM = pltpu.SMEM
HBM = pltpu.HBM
CHUNKS = 8


def diagonal(cols):
    shape = (cols, BS)
    return lax.broadcasted_iota(jnp.int32, shape, 0) == lax.broadcasted_iota(jnp.int32, shape, 1)


def squares_tail(squares, rows=TAIL):
    cols = squares.shape[0]
    total = jnp.sum(squares, axis=1, keepdims=True)
    row = jnp.sum(jnp.where(diagonal(cols), total, 0.0), axis=0, keepdims=True)
    high = row.astype(BF16).astype(F32)
    middle = (row - high).astype(BF16).astype(F32)
    low = row - high - middle
    place = lax.broadcasted_iota(jnp.int32, (rows, BS), 0)
    return jnp.where(
        place == 0, high, jnp.where(place == 1, middle, jnp.where(place == 2, low, 0.0))
    )


def norm_of_tails(message_ref, cols):
    tails = message_ref[:, BCAP * cols :, :].astype(F32)
    summed = jnp.sum(tails, axis=0)
    row = summed[0:1] + summed[1:2] + summed[2:3]
    column = jnp.sum(jnp.where(diagonal(cols), row, 0.0), axis=1, keepdims=True)
    return jnp.broadcast_to(jnp.sqrt(column + EPS), (cols, BS))


def lanes(block):
    return pl.ds(pl.multiple_of(block * BS, BS), BS)


def transposed(data_ref, rays_ref, ready, target_ref, total_ref, message_ref):
    pair_count, slot_count = rays_ref.shape[:2]
    cols = data_ref.shape[0]
    peers = message_ref.shape[0]
    spots = peers * BCAP

    def clear(index, carry):
        total_ref[index] = jnp.zeros((cols, BS), F32)
        return carry

    lax.fori_loop(0, spots, clear, 0, unroll=8)

    def one_pair(pair, carry):
        ready(pair)
        data = data_ref[:, lanes(pair)]
        high = data.astype(BF16)
        low = (data - high.astype(F32)).astype(BF16)
        pieces = jnp.concatenate([high, low], axis=0)
        for slot in range(0, slot_count, 2):
            rays = jnp.concatenate([rays_ref[pair, slot], rays_ref[pair, slot + 1]], axis=1)
            part = jnp.dot(pieces, rays, preferred_element_type=F32)
            part = part[:cols] + part[cols:]
            for half in range(2):
                spot = target_ref[pair * slot_count + slot + half]
                total_ref[spot] += part[:, half * BS : (half + 1) * BS]
        return carry

    lax.fori_loop(0, pair_count, one_pair, 0, unroll=2)

    def pack(peer, carry):
        for rank in range(BCAP):
            message_ref[peer, rank * cols : (rank + 1) * cols, :] = total_ref[
                peer * BCAP + rank
            ].astype(BF16)
        return carry

    lax.fori_loop(0, peers, pack, 0, unroll=2)


def start_kernel(
    cells_hbm, counts_hbm, times_hbm, rays_hbm, message_ref, target_ref,
    total_ref, table_ref, used_ref, cells_ref, counts_ref, times_ref, rays_ref, sems, ray_sems,
):
    pair_count, slot_count = rays_ref.shape[:2]
    peers = message_ref.shape[0]
    cols = times_ref.shape[0]
    owned = CELL_DEV // BS
    copies = [
        pltpu.make_async_copy(source, dest, sems.at[index])
        for index, (source, dest) in enumerate(
            [(cells_hbm, cells_ref), (counts_hbm, counts_ref), (times_hbm, times_ref)]
        )
    ]
    for copy in copies:
        copy.start()

    def ray_copy(pair):
        return pltpu.make_async_copy(rays_hbm.at[pair], rays_ref.at[pair], ray_sems.at[pair])

    def fetch(pair, carry):
        ray_copy(pair).start()
        return carry

    lax.fori_loop(0, pair_count, fetch, 0)

    def clear(peer, carry):
        used_ref[peer] = 0
        for rank in range(BCAP):
            table_ref[peer * BCAP + rank] = 0
        return carry

    lax.fori_loop(0, peers, clear, 0)
    copies[0].wait()
    copies[1].wait()

    def one_pair(pair, carry):
        count = counts_ref[pair]
        for slot in range(slot_count):
            cell = cells_ref[pair, slot]
            owner = cell // owned
            local = cell % owned
            used = used_ref[owner]
            rank = used
            for other in range(BCAP - 1, -1, -1):
                same = (table_ref[owner * BCAP + other] == local) & (other < used)
                rank = jnp.where(same, other, rank)
            spot = owner * BCAP + rank
            table_ref[spot] = local
            used_ref[owner] = jnp.maximum(used, rank + 1)
            target_ref[pair * slot_count + slot] = jnp.where(slot < count, spot, peers * BCAP)
        return carry

    lax.fori_loop(0, pair_count, one_pair, 0)
    copies[2].wait()
    transposed(
        times_ref, rays_ref, lambda pair: ray_copy(pair).wait(), target_ref, total_ref, message_ref
    )
    squares = jnp.zeros((cols, BS), F32)
    for pair in range(pair_count):
        part = times_ref[:, pair * BS : (pair + 1) * BS]
        squares += part * part
    tail = squares_tail(squares)
    place = lax.broadcasted_iota(jnp.int32, (TAIL, BS), 0)
    lane = lax.broadcasted_iota(jnp.int32, (TAIL, BS), 1)

    def ask(peer, carry):
        rows = tail
        for rank in range(BCAP):
            asked = table_ref[peer * BCAP + rank].astype(F32)
            rows = jnp.where((place == 3) & (lane == rank), asked, rows)
        message_ref[peer, BCAP * cols :, :] = rows.astype(BF16)
        return carry

    lax.fori_loop(0, peers, ask, 0)


def pair_kernel(
    target_ref, source_ref, fetched_ref, data_ref, rays_ref,
    message_ref, raw_ref, alpha_ref, total_ref,
):
    pair_count, slot_count = rays_ref.shape[:2]
    peers = message_ref.shape[0]
    cols = data_ref.shape[0]
    alpha = norm_of_tails(fetched_ref, cols)
    alpha_ref[...] = alpha
    model_scale = 1.0 / alpha

    def one_pair(pair, squares):
        chosen = []
        for slot in range(slot_count):
            index = pair * slot_count + slot
            rows = pl.ds(pl.multiple_of(source_ref[1, index], cols), cols)
            block = fetched_ref[source_ref[0, index], rows, :]
            chosen.append(jnp.where(source_ref[2, index] != 0, block, jnp.zeros_like(block)))
        rays = jnp.concatenate([rays_ref[pair, slot] for slot in range(slot_count)], axis=1)
        product = lax.dot_general(
            rays, jnp.concatenate(chosen, axis=1), (((1,), (1,)), ((), ())),
            preferred_element_type=F32,
        )
        raw = product.T * model_scale - data_ref[:, lanes(pair)] * alpha
        raw_ref[:, lanes(pair)] = raw
        return squares + raw * raw

    squares = lax.fori_loop(0, pair_count, one_pair, jnp.zeros((cols, BS), F32), unroll=2)
    transposed(raw_ref, rays_ref, lambda pair: None, target_ref, total_ref, message_ref)
    tail = squares_tail(squares).astype(BF16)
    message_ref[:, BCAP * cols :, :] = jnp.broadcast_to(tail[None], (peers, TAIL, BS))


def cell_kernel(first, last, *refs):
    if first:
        arrived_ref, raw_ref, beta_ref, out_ref, asked_ref, table_ref, sem = refs
    elif last:
        asked_ref, arrived_ref, model_ref, raw_hbm, beta_ref, out_ref, raw_ref, sems = refs
    else:
        asked_ref, arrived_ref, model_ref, raw_ref, beta_ref, out_ref = refs
    peers = arrived_ref.shape[0]
    cols, cells = raw_ref.shape
    if first:
        table_ref[...] = arrived_ref[:, BCAP * cols :, :].astype(F32)[:, 3, :].astype(jnp.int32)
        copy = pltpu.make_async_copy(table_ref, asked_ref, sem)
        copy.start()
    beta = norm_of_tails(arrived_ref, cols)
    beta_ref[...] = beta
    raw_ref[...] = jnp.zeros((cols, cells), F32)
    if first:
        copy.wait()

    def add(peer, carry):
        for rank in range(BCAP):
            where = lanes(asked_ref[peer, rank])
            raw_ref[:, where] += arrived_ref[peer, rank * cols : (rank + 1) * cols, :].astype(F32)
        return carry

    lax.fori_loop(0, peers, add, 0, unroll=2)
    scale = 1.0 / beta

    def settle(block, squares):
        raw = raw_ref[:, lanes(block)] * scale
        if not first:
            raw = raw - model_ref[:, lanes(block)] * beta
        raw_ref[:, lanes(block)] = raw
        return squares + raw * raw

    squares = jnp.zeros((cols, BS), F32)
    blocks = cells // BS
    if not last:
        squares = lax.fori_loop(0, blocks, settle, squares, unroll=4)
        tail = squares_tail(squares)
        out_ref[:, BCAP * cols :, :] = jnp.broadcast_to(tail[None], (peers, TAIL, BS)).astype(BF16)

        def reply(peer, carry):
            for rank in range(BCAP):
                block = raw_ref[:, lanes(asked_ref[peer, rank])]
                out_ref[peer, rank * cols : (rank + 1) * cols, :] = block.astype(BF16)
            return carry

        lax.fori_loop(0, peers, reply, 0, unroll=2)
        return
    copies = []
    for chunk in range(CHUNKS):
        each = blocks // CHUNKS
        squares = lax.fori_loop(chunk * each, (chunk + 1) * each, settle, squares, unroll=4)
        where = slice(chunk * each * BS, (chunk + 1) * each * BS)
        copies.append(
            pltpu.make_async_copy(raw_ref.at[:, where], raw_hbm.at[:, where], sems.at[chunk])
        )
        copies[-1].start()
    out_ref[...] = jnp.broadcast_to(squares_tail(squares, out_ref.shape[1])[None], out_ref.shape)
    for copy in copies:
        copy.wait()


def estimate_kernel(*refs):
    betas = refs[0 : ITERS + 1]
    alphas = refs[ITERS + 1 : 2 * ITERS + 1]
    models = refs[2 * ITERS + 1 : 3 * ITERS + 1]
    estimate_ref = refs[-1]
    cols, cells = estimate_ref.shape
    phi_bar = betas[0][...]
    rho_bar = alphas[0][...]
    trace = [jnp.ones((cols, BS), F32)]
    weight = [jnp.zeros((cols, BS), F32)] * ITERS
    for step in range(ITERS):
        beta = betas[step + 1][...]
        rho = jnp.sqrt(rho_bar * rho_bar + beta * beta)
        cosine = rho_bar / rho
        sine = beta / rho
        gain = cosine * phi_bar / rho
        weight = [
            weight[i] + gain * trace[i] if i < len(trace) else weight[i] for i in range(ITERS)
        ]
        if step + 1 < ITERS:
            alpha = alphas[step + 1][...]
            theta = sine * alpha
            rho_bar = -cosine * alpha
            phi_bar = sine * phi_bar
            trace = [-(theta / rho) * value for value in trace] + [jnp.ones((cols, BS), F32)]

    def one_block(block, carry):
        where = lanes(block)
        total = weight[0] * models[0][:, where]
        for i in range(1, ITERS):
            total += weight[i] * models[i][:, where]
        estimate_ref[:, where] = total
        return carry

    lax.fori_loop(0, cells // BS, one_block, 0, unroll=4)


def model_kernel(tails_ref, raw_hbm, model_hbm, raw_ref, in_sems, out_sems):
    cols, cells = raw_ref.shape
    blocks = cells // BS // CHUNKS
    ins, outs = [], []
    for chunk in range(CHUNKS):
        where = slice(chunk * blocks * BS, (chunk + 1) * blocks * BS)
        ins.append(
            pltpu.make_async_copy(raw_hbm.at[:, where], raw_ref.at[:, where], in_sems.at[chunk])
        )
        outs.append(
            pltpu.make_async_copy(raw_ref.at[:, where], model_hbm.at[:, where], out_sems.at[chunk])
        )
        ins[-1].start()
    summed = jnp.sum(tails_ref[...], axis=0)
    row = summed[0:1] + summed[1:2] + summed[2:3]
    column = jnp.sum(jnp.where(diagonal(cols), row, 0.0), axis=1, keepdims=True)
    scale = jnp.broadcast_to(1.0 / jnp.sqrt(column + EPS), (cols, BS))

    def one_block(block, carry):
        raw_ref[:, lanes(block)] *= scale
        return carry

    for chunk in range(CHUNKS):
        ins[chunk].wait()
        lax.fori_loop(chunk * blocks, (chunk + 1) * blocks, one_block, 0, unroll=4)
        outs[chunk].start()
    for copy in outs:
        copy.wait()


def call(kernel, name, in_spaces, outs, scratch=(), flops=0, moved=0, limit=16 << 20):
    return pl.pallas_call(
        kernel,
        name=name,
        in_specs=[pl.BlockSpec(memory_space=space) for space in in_spaces],
        out_specs=[pl.BlockSpec(memory_space=space) for _, _, space in outs],
        out_shape=[jax.ShapeDtypeStruct(shape, dtype) for shape, dtype, _ in outs],
        scratch_shapes=list(scratch),
        compiler_params=pltpu.CompilerParams(vmem_limit_bytes=limit),
        cost_estimate=pl.CostEstimate(flops=flops, bytes_accessed=moved, transcendentals=0),
    )


def on_device(ray_blocks, block_cells, block_counts, travel_times):
    pair_count, slot_count = ray_blocks.shape[:2]
    slots = pair_count * slot_count
    peers = lax.axis_size("pair")
    spots = peers * BCAP
    times = travel_times.T
    cols, pairs = times.shape
    message = ((peers, BCAP * cols + TAIL, BS), BF16, VMEM)
    tile = ((cols, BS), F32, VMEM)
    data = ((cols, pairs), F32, VMEM)
    model = ((cols, CELL_DEV), F32, VMEM)
    totals = VMEM((spots + 1, cols, BS), F32)
    flops = 2 * slots * BS * BS * cols

    def exchange(values):
        return lax.all_to_all(values, "pair", split_axis=0, concat_axis=0, tiled=True)

    outgoing, target = call(
        start_kernel, "start", [HBM, HBM, HBM, HBM],
        [message, ((slots,), jnp.int32, SMEM)],
        [
            totals, SMEM((spots,), jnp.int32), SMEM((peers,), jnp.int32),
            SMEM(block_cells.shape, jnp.int32), SMEM(block_counts.shape, jnp.int32),
            VMEM(times.shape, F32), VMEM(ray_blocks.shape, BF16),
            pltpu.SemaphoreType.DMA((3,)), pltpu.SemaphoreType.DMA((pair_count,)),
        ],
        flops, 6 << 20, 60 << 20,
    )(block_cells, block_counts, times, ray_blocks)
    arrived = exchange(outgoing)
    within = jnp.minimum(target, spots - 1)
    source = jnp.stack(
        [within // BCAP, within % BCAP * cols, (target < spots).astype(jnp.int32)]
    )
    raw, beta, reply, asked = call(
        functools.partial(cell_kernel, True, False), "cells_first", [VMEM],
        [model, tile, message, ((peers, BS), jnp.int32, SMEM)],
        [VMEM((peers, BS), jnp.int32), pltpu.SemaphoreType.DMA],
        0, 6 << 20,
    )(arrived)
    models, betas, alphas = [], [beta], []
    current = times
    for step in range(ITERS):
        fetched = exchange(reply)
        current = current / betas[-1][:, :1]
        outgoing, data_raw, alpha = call(
            pair_kernel, "pairs", [SMEM, SMEM, VMEM, VMEM, VMEM],
            [message, data, tile], [totals], 2 * flops, 8 << 20,
        )(target, source, fetched, current, ray_blocks)
        current = data_raw
        alphas.append(alpha)
        arrived = exchange(outgoing)
        models.append(raw / alpha[:, :1])
        last = step + 1 == ITERS
        raw, beta, reply = call(
            functools.partial(cell_kernel, False, last), "cells_last" if last else "cells",
            [SMEM, VMEM, VMEM],
            [((cols, CELL_DEV), F32, HBM), tile, ((peers, 8, BS), F32, VMEM)]
            if last else [model, tile, message],
            [VMEM((cols, CELL_DEV), F32), pltpu.SemaphoreType.DMA((CHUNKS,))] if last else (),
            0, 8 << 20,
        )(asked, arrived, models[-1])
        betas.append(beta)
    tails = exchange(reply)
    (estimate,) = call(
        estimate_kernel, "estimate", [VMEM] * (3 * ITERS + 1), [model], (), 0, 6 << 20
    )(*betas, *alphas, *models)
    (model_vec,) = call(
        model_kernel, "model", [VMEM, HBM], [((cols, CELL_DEV), F32, HBM)],
        [VMEM((cols, CELL_DEV), F32)] + [pltpu.SemaphoreType.DMA((CHUNKS,))] * 2, 0, 4 << 20,
    )(tails, raw)
    return (estimate.T, model_vec.T)


def solution(mesh):
    return jax.shard_map(
        on_device,
        mesh=mesh,
        in_specs=(
            P(("groups", "pair"), None, None, None),
            P(("groups", "pair"), None),
            P(("groups", "pair")),
            P(("groups", "pair"), None),
        ),
        out_specs=(P(("groups", "pair"), None), P(("groups", "pair"), None)),
        check_vma=False,
    )
```

```python
import functools

import jax
import jax.numpy as jnp
from jax import lax
from jax.experimental import pallas as pl
from jax.experimental.pallas import tpu as pltpu
from jax.sharding import PartitionSpec as P

CELL_DEV = 8192
BCAP = 4
BS = 128
TAIL = 8
ITERS = 2
EPS = 1e-12
F32 = jnp.float32
BF16 = jnp.bfloat16
VMEM = pltpu.VMEM
SMEM = pltpu.SMEM
HBM = pltpu.HBM
CHUNKS = 8


def diagonal(cols):
    shape = (cols, BS)
    return lax.broadcasted_iota(jnp.int32, shape, 0) == lax.broadcasted_iota(jnp.int32, shape, 1)


def squares_tail(squares):
    cols = squares.shape[0]
    total = jnp.sum(squares, axis=1, keepdims=True)
    row = jnp.sum(jnp.where(diagonal(cols), total, 0.0), axis=0, keepdims=True)
    high = row.astype(BF16).astype(F32)
    middle = (row - high).astype(BF16).astype(F32)
    low = row - high - middle
    place = lax.broadcasted_iota(jnp.int32, (TAIL, BS), 0)
    return jnp.where(
        place == 0, high, jnp.where(place == 1, middle, jnp.where(place == 2, low, 0.0))
    )


def norm_of_tails(message_ref, cols):
    tails = message_ref[:, BCAP * cols :, :].astype(F32)
    summed = jnp.sum(tails, axis=0)
    row = summed[0:1] + summed[1:2] + summed[2:3]
    column = jnp.sum(jnp.where(diagonal(cols), row, 0.0), axis=1, keepdims=True)
    return jnp.broadcast_to(jnp.sqrt(column + EPS), (cols, BS))


def lanes(block):
    return pl.ds(pl.multiple_of(block * BS, BS), BS)


def transposed(data_ref, rays_ref, before, target_ref, total_ref, message_ref):
    pair_count, slot_count = rays_ref.shape[:2]
    cols = data_ref.shape[0]
    peers = message_ref.shape[0]
    spots = peers * BCAP

    def clear(index, carry):
        total_ref[index] = jnp.zeros((cols, BS), F32)
        return carry

    lax.fori_loop(0, spots, clear, 0, unroll=8)

    def one_pair(pair, carry):
        before(pair)
        data = data_ref[:, lanes(pair)]
        high = data.astype(BF16)
        low = (data - high.astype(F32)).astype(BF16)
        pieces = jnp.concatenate([high, low], axis=0)
        for slot in range(0, slot_count, 2):
            rays = jnp.concatenate([rays_ref[pair, slot], rays_ref[pair, slot + 1]], axis=1)
            part = jnp.dot(pieces, rays, preferred_element_type=F32)
            part = part[:cols] + part[cols:]
            for half in range(2):
                spot = target_ref[pair * slot_count + slot + half]
                total_ref[spot] += part[:, half * BS : (half + 1) * BS]
        return carry

    lax.fori_loop(0, pair_count, one_pair, 0, unroll=2)

    def pack(peer, carry):
        for rank in range(BCAP):
            message_ref[peer, rank * cols : (rank + 1) * cols, :] = total_ref[
                peer * BCAP + rank
            ].astype(BF16)
        return carry

    lax.fori_loop(0, peers, pack, 0, unroll=2)


def start_kernel(
    cells_hbm, counts_hbm, times_hbm, rays_hbm, message_ref, target_ref,
    total_ref, table_ref, used_ref, cells_ref, counts_ref, times_ref, rays_ref, sems, ray_sems,
):
    pair_count, slot_count = rays_ref.shape[:2]
    peers = message_ref.shape[0]
    cols = times_ref.shape[0]
    owned = CELL_DEV // BS
    copies = [
        pltpu.make_async_copy(source, dest, sems.at[index])
        for index, (source, dest) in enumerate(
            [(cells_hbm, cells_ref), (counts_hbm, counts_ref), (times_hbm, times_ref)]
        )
    ]
    for copy in copies:
        copy.start()

    def ray_copy(pair):
        return pltpu.make_async_copy(rays_hbm.at[pair], rays_ref.at[pair], ray_sems.at[pair])

    def fetch(pair, carry):
        ray_copy(pair).start()
        return carry

    lax.fori_loop(0, pair_count, fetch, 0)

    def clear(peer, carry):
        used_ref[peer] = 0
        for rank in range(BCAP):
            table_ref[peer * BCAP + rank] = 0
        return carry

    lax.fori_loop(0, peers, clear, 0)
    for copy in copies:
        copy.wait()

    def find_places(pair):
        count = counts_ref[pair]
        for slot in range(slot_count):
            cell = cells_ref[pair, slot]
            owner = cell // owned
            local = cell % owned
            used = used_ref[owner]
            rank = used
            for other in range(BCAP - 1, -1, -1):
                same = (table_ref[owner * BCAP + other] == local) & (other < used)
                rank = jnp.where(same, other, rank)
            spot = owner * BCAP + rank
            table_ref[spot] = local
            used_ref[owner] = jnp.maximum(used, rank + 1)
            target_ref[pair * slot_count + slot] = jnp.where(slot < count, spot, peers * BCAP)

    def before(pair):
        find_places(pair)
        ray_copy(pair).wait()

    transposed(times_ref, rays_ref, before, target_ref, total_ref, message_ref)
    squares = jnp.zeros((cols, BS), F32)
    for pair in range(pair_count):
        part = times_ref[:, pair * BS : (pair + 1) * BS]
        squares += part * part
    tail = squares_tail(squares)
    place = lax.broadcasted_iota(jnp.int32, (TAIL, BS), 0)
    lane = lax.broadcasted_iota(jnp.int32, (TAIL, BS), 1)

    def ask(peer, carry):
        rows = tail
        for rank in range(BCAP):
            asked = table_ref[peer * BCAP + rank].astype(F32)
            rows = jnp.where((place == 3) & (lane == rank), asked, rows)
        message_ref[peer, BCAP * cols :, :] = rows.astype(BF16)
        return carry

    lax.fori_loop(0, peers, ask, 0)


def pair_kernel(
    target_ref, fetched_ref, data_ref, beta_ref, rays_ref,
    message_ref, raw_ref, alpha_ref, total_ref,
):
    pair_count, slot_count = rays_ref.shape[:2]
    peers = message_ref.shape[0]
    cols = data_ref.shape[0]
    spots = peers * BCAP
    alpha = norm_of_tails(fetched_ref, cols)
    alpha_ref[...] = alpha
    beta = beta_ref[...]
    model_scale = 1.0 / (alpha * beta)
    data_scale = alpha / beta

    def one_pair(pair, squares):
        chosen = []
        for slot in range(slot_count):
            spot = target_ref[pair * slot_count + slot]
            live = spot < spots
            spot = jnp.where(live, spot, 0)
            rows = pl.ds(pl.multiple_of((spot % BCAP) * cols, cols), cols)
            block = fetched_ref[spot // BCAP, rows, :]
            chosen.append(jnp.where(live, block, jnp.zeros_like(block)))
        rays = jnp.concatenate([rays_ref[pair, slot] for slot in range(slot_count)], axis=1)
        product = lax.dot_general(
            rays, jnp.concatenate(chosen, axis=1), (((1,), (1,)), ((), ())),
            preferred_element_type=F32,
        )
        raw = product.T * model_scale - data_ref[:, lanes(pair)] * data_scale
        raw_ref[:, lanes(pair)] = raw
        return squares + raw * raw

    squares = lax.fori_loop(0, pair_count, one_pair, jnp.zeros((cols, BS), F32), unroll=2)
    transposed(raw_ref, rays_ref, lambda pair: None, target_ref, total_ref, message_ref)
    tail = squares_tail(squares).astype(BF16)
    message_ref[:, BCAP * cols :, :] = jnp.broadcast_to(tail[None], (peers, TAIL, BS))


def gathered(arrived_ref, asked_ref, model_ref):
    peers = arrived_ref.shape[0]
    cols = model_ref.shape[0]

    def add(peer, carry):
        for rank in range(BCAP):
            where = lanes(asked_ref[peer, rank])
            block = arrived_ref[peer, rank * cols : (rank + 1) * cols, :]
            model_ref[:, where] += block.astype(F32)
        return carry

    lax.fori_loop(0, peers, add, 0, unroll=2)


def reply(squares, scale, asked_ref, model_ref, out_ref):
    peers = out_ref.shape[0]
    cols = model_ref.shape[0]
    tail = squares_tail(squares * scale * scale).astype(BF16)
    out_ref[:, BCAP * cols :, :] = jnp.broadcast_to(tail[None], (peers, TAIL, BS))

    def one_peer(peer, carry):
        for rank in range(BCAP):
            block = model_ref[:, lanes(asked_ref[peer, rank])]
            out_ref[peer, rank * cols : (rank + 1) * cols, :] = block.astype(BF16)
        return carry

    lax.fori_loop(0, peers, one_peer, 0, unroll=2)


def squares_of(model_ref):
    cols, cells = model_ref.shape

    def one_block(block, squares):
        values = model_ref[:, lanes(block)]
        return squares + values * values

    return lax.fori_loop(0, cells // BS, one_block, jnp.zeros((cols, BS), F32), unroll=8)


def first_cell_kernel(arrived_ref, model_ref, beta_ref, out_ref, asked_ref, table_ref, sem):
    cols, cells = model_ref.shape
    table_ref[...] = arrived_ref[:, BCAP * cols :, :].astype(F32)[:, 3, :].astype(jnp.int32)
    copy = pltpu.make_async_copy(table_ref, asked_ref, sem)
    copy.start()
    beta = norm_of_tails(arrived_ref, cols)
    beta_ref[...] = beta
    model_ref[...] = jnp.zeros((cols, cells), F32)
    copy.wait()
    gathered(arrived_ref, asked_ref, model_ref)
    reply(squares_of(model_ref), 1.0 / beta, asked_ref, model_ref, out_ref)


def start_from(before_ref, scale, model_ref):
    def one_block(block, carry):
        model_ref[:, lanes(block)] = before_ref[:, lanes(block)] * -scale
        return carry

    lax.fori_loop(0, model_ref.shape[1] // BS, one_block, 0, unroll=8)


def cell_kernel(
    asked_ref, arrived_ref, before_ref, alpha_ref, beta_before_ref, model_ref, beta_ref, out_ref
):
    beta = norm_of_tails(arrived_ref, model_ref.shape[0])
    beta_ref[...] = beta
    start_from(before_ref, beta * beta / (alpha_ref[...] * beta_before_ref[...]), model_ref)
    gathered(arrived_ref, asked_ref, model_ref)
    reply(squares_of(model_ref), 1.0 / beta, asked_ref, model_ref, out_ref)


def last_cell_kernel(asked_ref, arrived_ref, *refs):
    models = refs[:ITERS]
    alphas = [ref[...] for ref in refs[ITERS : 2 * ITERS]]
    betas = [ref[...] for ref in refs[2 * ITERS : 3 * ITERS]]
    model_ref, beta_ref, out_ref, estimate_hbm, estimate_ref, sems = refs[3 * ITERS :]
    cols, cells = model_ref.shape
    beta = norm_of_tails(arrived_ref, cols)
    beta_ref[...] = beta
    weights = estimate_weights(betas + [beta], alphas)
    scale = beta * beta / (alphas[-1] * betas[-1])
    blocks = cells // BS // CHUNKS

    def one_block(block, carry):
        where = lanes(block)
        values = models[-1][:, where]
        model_ref[:, where] = values * -scale
        total = values * weights[-1]
        for i in range(ITERS - 1):
            total += weights[i] * models[i][:, where]
        estimate_ref[:, where] = total
        return carry

    copies = []
    for chunk in range(CHUNKS):
        lax.fori_loop(chunk * blocks, (chunk + 1) * blocks, one_block, 0, unroll=4)
        where = slice(chunk * blocks * BS, (chunk + 1) * blocks * BS)
        copies.append(
            pltpu.make_async_copy(
                estimate_ref.at[:, where], estimate_hbm.at[:, where], sems.at[chunk]
            )
        )
        copies[-1].start()
    gathered(arrived_ref, asked_ref, model_ref)
    scale = 1.0 / beta
    tail = squares_tail(squares_of(model_ref) * scale * scale)
    out_ref[...] = jnp.broadcast_to(tail[None], out_ref.shape)
    for copy in copies:
        copy.wait()


def estimate_weights(betas, alphas):
    phi_bar = betas[0]
    rho_bar = alphas[0]
    trace = [1.0 / (alphas[0] * betas[0])]
    weight = [jnp.zeros_like(phi_bar)] * ITERS
    for step in range(ITERS):
        beta = betas[step + 1]
        rho = jnp.sqrt(rho_bar * rho_bar + beta * beta)
        cosine = rho_bar / rho
        sine = beta / rho
        gain = cosine * phi_bar / rho
        weight = [
            weight[i] + gain * trace[i] if i < len(trace) else weight[i] for i in range(ITERS)
        ]
        if step + 1 < ITERS:
            alpha = alphas[step + 1]
            theta = sine * alpha
            rho_bar = -cosine * alpha
            phi_bar = sine * phi_bar
            trace = [-(theta / rho) * value for value in trace] + [1.0 / (alpha * beta)]
    return weight


def model_kernel(tails_ref, beta_ref, model_ref, out_hbm, out_ref, sems):
    cols, cells = model_ref.shape
    blocks = cells // BS // CHUNKS
    summed = jnp.sum(tails_ref[...], axis=0)
    row = summed[0:1] + summed[1:2] + summed[2:3]
    column = jnp.sum(jnp.where(diagonal(cols), row, 0.0), axis=1, keepdims=True)
    alpha = jnp.broadcast_to(jnp.sqrt(column + EPS), (cols, BS))
    scale = 1.0 / (alpha * beta_ref[...])

    def one_block(block, carry):
        out_ref[:, lanes(block)] = model_ref[:, lanes(block)] * scale
        return carry

    copies = []
    for chunk in range(CHUNKS):
        lax.fori_loop(chunk * blocks, (chunk + 1) * blocks, one_block, 0, unroll=4)
        where = slice(chunk * blocks * BS, (chunk + 1) * blocks * BS)
        copies.append(
            pltpu.make_async_copy(out_ref.at[:, where], out_hbm.at[:, where], sems.at[chunk])
        )
        copies[-1].start()
    for copy in copies:
        copy.wait()


def call(kernel, name, in_spaces, outs, scratch=(), flops=0, moved=0, limit=16 << 20):
    return pl.pallas_call(
        kernel,
        name=name,
        in_specs=[pl.BlockSpec(memory_space=space) for space in in_spaces],
        out_specs=[pl.BlockSpec(memory_space=space) for _, _, space in outs],
        out_shape=[jax.ShapeDtypeStruct(shape, dtype) for shape, dtype, _ in outs],
        scratch_shapes=list(scratch),
        compiler_params=pltpu.CompilerParams(vmem_limit_bytes=limit),
        cost_estimate=pl.CostEstimate(flops=flops, bytes_accessed=moved, transcendentals=0),
    )


def on_device(ray_blocks, block_cells, block_counts, travel_times):
    pair_count, slot_count = ray_blocks.shape[:2]
    slots = pair_count * slot_count
    peers = lax.axis_size("pair")
    spots = peers * BCAP
    times = travel_times.T
    cols, pairs = times.shape
    message = ((peers, BCAP * cols + TAIL, BS), BF16, VMEM)
    tile = ((cols, BS), F32, VMEM)
    data = ((cols, pairs), F32, VMEM)
    whole = ((cols, CELL_DEV), F32, VMEM)
    totals = VMEM((spots + 1, cols, BS), F32)
    flops = 2 * slots * BS * BS * cols

    def exchange(values):
        return lax.all_to_all(values, "pair", split_axis=0, concat_axis=0, tiled=True)

    outgoing, target = call(
        start_kernel, "start", [HBM, HBM, HBM, HBM],
        [message, ((slots,), jnp.int32, SMEM)],
        [
            totals, SMEM((spots,), jnp.int32), SMEM((peers,), jnp.int32),
            SMEM(block_cells.shape, jnp.int32), SMEM(block_counts.shape, jnp.int32),
            VMEM(times.shape, F32), VMEM(ray_blocks.shape, BF16),
            pltpu.SemaphoreType.DMA((3,)), pltpu.SemaphoreType.DMA((pair_count,)),
        ],
        flops, 6 << 20, 60 << 20,
    )(block_cells, block_counts, times, ray_blocks)
    arrived = exchange(outgoing)
    model, beta, reply_, asked = call(
        first_cell_kernel, "cells_first", [VMEM],
        [whole, tile, message, ((peers, BS), jnp.int32, SMEM)],
        [VMEM((peers, BS), jnp.int32), pltpu.SemaphoreType.DMA],
        0, 6 << 20,
    )(arrived)
    models, betas, alphas = [model], [beta], []
    current = times
    for step in range(ITERS):
        fetched = exchange(reply_)
        outgoing, current, alpha = call(
            pair_kernel, "pairs", [SMEM, VMEM, VMEM, VMEM, VMEM],
            [message, data, tile], [totals], 2 * flops, 8 << 20,
        )(target, fetched, current, betas[-1], ray_blocks)
        alphas.append(alpha)
        arrived = exchange(outgoing)
        if step + 1 < ITERS:
            model, beta, reply_ = call(
                cell_kernel, "cells", [SMEM] + [VMEM] * 4, [whole, tile, message], (), 0, 8 << 20
            )(asked, arrived, models[-1], alpha, betas[-1])
            models.append(model)
            betas.append(beta)
    scratch = [VMEM(whole[0], F32), pltpu.SemaphoreType.DMA((CHUNKS,))]
    model, beta, tails, estimate = call(
        last_cell_kernel, "cells_last", [SMEM] + [VMEM] * (3 * ITERS + 1),
        [whole, tile, ((peers, TAIL, BS), F32, VMEM), (whole[0], F32, HBM)], scratch, 0, 10 << 20,
    )(asked, arrived, *models, *alphas, *betas)
    (model_vec,) = call(
        model_kernel, "model", [VMEM, VMEM, VMEM], [(whole[0], F32, HBM)], scratch, 0, 4 << 20
    )(exchange(tails), beta, model)
    return (estimate.T, model_vec.T)


def solution(mesh):
    return jax.shard_map(
        on_device,
        mesh=mesh,
        in_specs=(
            P(("groups", "pair"), None, None, None),
            P(("groups", "pair"), None),
            P(("groups", "pair")),
            P(("groups", "pair"), None),
        ),
        out_specs=(P(("groups", "pair"), None), P(("groups", "pair"), None)),
        check_vma=False,
    )
```

```python
import functools

import jax
import jax.numpy as jnp
from jax import lax
from jax.experimental import pallas as pl
from jax.experimental.pallas import tpu as pltpu
from jax.sharding import PartitionSpec as P

CELL_DEV = 8192
BCAP = 4
BS = 128
TAIL = 8
ITERS = 2
EPS = 1e-12
F32 = jnp.float32
BF16 = jnp.bfloat16
VMEM = pltpu.VMEM
SMEM = pltpu.SMEM
HBM = pltpu.HBM
CHUNKS = 8


def diagonal(cols):
    shape = (cols, BS)
    return lax.broadcasted_iota(jnp.int32, shape, 0) == lax.broadcasted_iota(jnp.int32, shape, 1)


def squares_tail(squares):
    cols = squares.shape[0]
    total = jnp.sum(squares, axis=1, keepdims=True)
    row = jnp.sum(jnp.where(diagonal(cols), total, 0.0), axis=0, keepdims=True)
    high = row.astype(BF16).astype(F32)
    middle = (row - high).astype(BF16).astype(F32)
    low = row - high - middle
    place = lax.broadcasted_iota(jnp.int32, (TAIL, BS), 0)
    return jnp.where(
        place == 0, high, jnp.where(place == 1, middle, jnp.where(place == 2, low, 0.0))
    )


def norm_of_tails(message_ref, cols):
    tails = message_ref[:, BCAP * cols :, :].astype(F32)
    summed = jnp.sum(tails, axis=0)
    row = summed[0:1] + summed[1:2] + summed[2:3]
    column = jnp.sum(jnp.where(diagonal(cols), row, 0.0), axis=1, keepdims=True)
    return jnp.broadcast_to(jnp.sqrt(column + EPS), (cols, BS))


def lanes(block):
    return pl.ds(pl.multiple_of(block * BS, BS), BS)


def transposed(data_ref, rays_ref, before, target_ref, total_ref, message_ref):
    pair_count, slot_count = rays_ref.shape[:2]
    cols = data_ref.shape[0]
    peers = message_ref.shape[0]
    spots = peers * BCAP

    def clear(index, carry):
        total_ref[index] = jnp.zeros((cols, BS), F32)
        return carry

    lax.fori_loop(0, spots, clear, 0, unroll=8)

    def one_pair(pair, carry):
        before(pair)
        data = data_ref[:, lanes(pair)]
        high = data.astype(BF16)
        low = (data - high.astype(F32)).astype(BF16)
        pieces = jnp.concatenate([high, low], axis=0)
        for slot in range(0, slot_count, 2):
            rays = jnp.concatenate([rays_ref[pair, slot], rays_ref[pair, slot + 1]], axis=1)
            part = jnp.dot(pieces, rays, preferred_element_type=F32)
            part = part[:cols] + part[cols:]
            for half in range(2):
                spot = target_ref[pair * slot_count + slot + half]
                total_ref[spot] += part[:, half * BS : (half + 1) * BS]
        return carry

    lax.fori_loop(0, pair_count, one_pair, 0, unroll=2)

    def pack(peer, carry):
        for rank in range(BCAP):
            message_ref[peer, rank * cols : (rank + 1) * cols, :] = total_ref[
                peer * BCAP + rank
            ].astype(BF16)
        return carry

    lax.fori_loop(0, peers, pack, 0, unroll=2)


def start_kernel(
    cells_hbm, counts_hbm, times_hbm, rays_hbm, message_ref, target_ref,
    total_ref, table_ref, used_ref, cells_ref, counts_ref, times_ref, rays_ref, sems, ray_sems,
):
    pair_count, slot_count = rays_ref.shape[:2]
    peers = message_ref.shape[0]
    cols = times_ref.shape[0]
    owned = CELL_DEV // BS
    copies = [
        pltpu.make_async_copy(source, dest, sems.at[index])
        for index, (source, dest) in enumerate(
            [(cells_hbm, cells_ref), (counts_hbm, counts_ref), (times_hbm, times_ref)]
        )
    ]
    for copy in copies:
        copy.start()

    def ray_copy(pair):
        return pltpu.make_async_copy(rays_hbm.at[pair], rays_ref.at[pair], ray_sems.at[pair])

    def fetch(pair, carry):
        ray_copy(pair).start()
        return carry

    lax.fori_loop(0, pair_count, fetch, 0)

    def clear(peer, carry):
        used_ref[peer] = 0
        for rank in range(BCAP):
            table_ref[peer * BCAP + rank] = 0
        return carry

    lax.fori_loop(0, peers, clear, 0)
    for copy in copies:
        copy.wait()

    def find_places(pair):
        count = counts_ref[pair]
        for slot in range(slot_count):
            cell = cells_ref[pair, slot]
            owner = cell // owned
            owner = owner * 2 - jnp.where(owner < peers // 2, 0, peers - 1)
            local = cell % owned
            used = used_ref[owner]
            rank = used
            for other in range(BCAP - 1, -1, -1):
                same = (table_ref[owner * BCAP + other] == local) & (other < used)
                rank = jnp.where(same, other, rank)
            spot = owner * BCAP + rank
            table_ref[spot] = local
            used_ref[owner] = jnp.maximum(used, rank + 1)
            target_ref[pair * slot_count + slot] = jnp.where(slot < count, spot, peers * BCAP)

    def before(pair):
        find_places(pair)
        ray_copy(pair).wait()

    transposed(times_ref, rays_ref, before, target_ref, total_ref, message_ref)
    squares = jnp.zeros((cols, BS), F32)
    for pair in range(pair_count):
        part = times_ref[:, pair * BS : (pair + 1) * BS]
        squares += part * part
    tail = squares_tail(squares)
    place = lax.broadcasted_iota(jnp.int32, (TAIL, BS), 0)
    lane = lax.broadcasted_iota(jnp.int32, (TAIL, BS), 1)

    def ask(peer, carry):
        rows = tail
        for rank in range(BCAP):
            asked = table_ref[peer * BCAP + rank].astype(F32)
            rows = jnp.where((place == 3) & (lane == rank), asked, rows)
        message_ref[peer, BCAP * cols :, :] = rows.astype(BF16)
        return carry

    lax.fori_loop(0, peers, ask, 0)


def pair_kernel(
    target_ref, fetched_ref, data_ref, beta_ref, rays_ref,
    message_ref, raw_ref, alpha_ref, total_ref,
):
    pair_count, slot_count = rays_ref.shape[:2]
    peers = message_ref.shape[0]
    cols = data_ref.shape[0]
    spots = peers * BCAP
    alpha = norm_of_tails(fetched_ref, cols)
    alpha_ref[...] = alpha
    beta = beta_ref[...]
    model_scale = 1.0 / (alpha * beta)
    data_scale = alpha / beta

    def one_pair(pair, squares):
        chosen = []
        for slot in range(slot_count):
            spot = target_ref[pair * slot_count + slot]
            live = spot < spots
            spot = jnp.where(live, spot, 0)
            rows = pl.ds(pl.multiple_of((spot % BCAP) * cols, cols), cols)
            block = fetched_ref[spot // BCAP, rows, :]
            chosen.append(jnp.where(live, block, jnp.zeros_like(block)))
        rays = jnp.concatenate([rays_ref[pair, slot] for slot in range(slot_count)], axis=1)
        product = lax.dot_general(
            rays, jnp.concatenate(chosen, axis=1), (((1,), (1,)), ((), ())),
            preferred_element_type=F32,
        )
        raw = product.T * model_scale - data_ref[:, lanes(pair)] * data_scale
        raw_ref[:, lanes(pair)] = raw
        return squares + raw * raw

    squares = lax.fori_loop(0, pair_count, one_pair, jnp.zeros((cols, BS), F32), unroll=2)
    transposed(raw_ref, rays_ref, lambda pair: None, target_ref, total_ref, message_ref)
    tail = squares_tail(squares).astype(BF16)
    message_ref[:, BCAP * cols :, :] = jnp.broadcast_to(tail[None], (peers, TAIL, BS))


def gathered(arrived_ref, asked_ref, model_ref):
    peers = arrived_ref.shape[0]
    cols = model_ref.shape[0]

    def add(peer, carry):
        for rank in range(BCAP):
            where = lanes(asked_ref[peer, rank])
            block = arrived_ref[peer, rank * cols : (rank + 1) * cols, :]
            model_ref[:, where] += block.astype(F32)
        return carry

    lax.fori_loop(0, peers, add, 0, unroll=2)


def reply(squares, scale, asked_ref, model_ref, out_ref):
    peers = out_ref.shape[0]
    cols = model_ref.shape[0]
    tail = squares_tail(squares * scale * scale).astype(BF16)
    out_ref[:, BCAP * cols :, :] = jnp.broadcast_to(tail[None], (peers, TAIL, BS))

    def one_peer(peer, carry):
        for rank in range(BCAP):
            block = model_ref[:, lanes(asked_ref[peer, rank])]
            out_ref[peer, rank * cols : (rank + 1) * cols, :] = block.astype(BF16)
        return carry

    lax.fori_loop(0, peers, one_peer, 0, unroll=2)


def squares_of(model_ref):
    cols, cells = model_ref.shape

    def one_block(block, squares):
        values = model_ref[:, lanes(block)]
        return squares + values * values

    return lax.fori_loop(0, cells // BS, one_block, jnp.zeros((cols, BS), F32), unroll=8)


def first_cell_kernel(arrived_ref, model_ref, beta_ref, out_ref, asked_ref, table_ref, sem):
    cols, cells = model_ref.shape
    table_ref[...] = arrived_ref[:, BCAP * cols :, :].astype(F32)[:, 3, :].astype(jnp.int32)
    copy = pltpu.make_async_copy(table_ref, asked_ref, sem)
    copy.start()
    beta = norm_of_tails(arrived_ref, cols)
    beta_ref[...] = beta
    model_ref[...] = jnp.zeros((cols, cells), F32)
    copy.wait()
    gathered(arrived_ref, asked_ref, model_ref)
    reply(squares_of(model_ref), 1.0 / beta, asked_ref, model_ref, out_ref)


def start_from(before_ref, scale, model_ref):
    def one_block(block, carry):
        model_ref[:, lanes(block)] = before_ref[:, lanes(block)] * -scale
        return carry

    lax.fori_loop(0, model_ref.shape[1] // BS, one_block, 0, unroll=8)


def cell_kernel(
    asked_ref, arrived_ref, before_ref, alpha_ref, beta_before_ref, model_ref, beta_ref, out_ref
):
    beta = norm_of_tails(arrived_ref, model_ref.shape[0])
    beta_ref[...] = beta
    start_from(before_ref, beta * beta / (alpha_ref[...] * beta_before_ref[...]), model_ref)
    gathered(arrived_ref, asked_ref, model_ref)
    reply(squares_of(model_ref), 1.0 / beta, asked_ref, model_ref, out_ref)


def last_cell_kernel(asked_ref, arrived_ref, *refs):
    models = refs[:ITERS]
    alphas = [ref[...] for ref in refs[ITERS : 2 * ITERS]]
    betas = [ref[...] for ref in refs[2 * ITERS : 3 * ITERS]]
    model_ref, beta_ref, out_ref, estimate_hbm, estimate_ref, sems = refs[3 * ITERS :]
    cols, cells = model_ref.shape
    beta = norm_of_tails(arrived_ref, cols)
    beta_ref[...] = beta
    weights = estimate_weights(betas + [beta], alphas)
    scale = beta * beta / (alphas[-1] * betas[-1])
    blocks = cells // BS // CHUNKS

    def one_block(block, carry):
        where = lanes(block)
        values = models[-1][:, where]
        model_ref[:, where] = values * -scale
        total = values * weights[-1]
        for i in range(ITERS - 1):
            total += weights[i] * models[i][:, where]
        estimate_ref[:, where] = total
        return carry

    copies = []
    for chunk in range(CHUNKS):
        lax.fori_loop(chunk * blocks, (chunk + 1) * blocks, one_block, 0, unroll=4)
        where = slice(chunk * blocks * BS, (chunk + 1) * blocks * BS)
        copies.append(
            pltpu.make_async_copy(
                estimate_ref.at[:, where], estimate_hbm.at[:, where], sems.at[chunk]
            )
        )
        copies[-1].start()
    gathered(arrived_ref, asked_ref, model_ref)
    scale = 1.0 / beta
    tail = squares_tail(squares_of(model_ref) * scale * scale)
    out_ref[...] = jnp.broadcast_to(tail[None], out_ref.shape)
    for copy in copies:
        copy.wait()


def estimate_weights(betas, alphas):
    phi_bar = betas[0]
    rho_bar = alphas[0]
    trace = [1.0 / (alphas[0] * betas[0])]
    weight = [jnp.zeros_like(phi_bar)] * ITERS
    for step in range(ITERS):
        beta = betas[step + 1]
        rho = jnp.sqrt(rho_bar * rho_bar + beta * beta)
        cosine = rho_bar / rho
        sine = beta / rho
        gain = cosine * phi_bar / rho
        weight = [
            weight[i] + gain * trace[i] if i < len(trace) else weight[i] for i in range(ITERS)
        ]
        if step + 1 < ITERS:
            alpha = alphas[step + 1]
            theta = sine * alpha
            rho_bar = -cosine * alpha
            phi_bar = sine * phi_bar
            trace = [-(theta / rho) * value for value in trace] + [1.0 / (alpha * beta)]
    return weight


def model_kernel(tails_ref, beta_ref, model_ref, out_hbm, out_ref, sems):
    cols, cells = model_ref.shape
    blocks = cells // BS // CHUNKS
    summed = jnp.sum(tails_ref[...], axis=0)
    row = summed[0:1] + summed[1:2] + summed[2:3]
    column = jnp.sum(jnp.where(diagonal(cols), row, 0.0), axis=1, keepdims=True)
    alpha = jnp.broadcast_to(jnp.sqrt(column + EPS), (cols, BS))
    scale = 1.0 / (alpha * beta_ref[...])

    def one_block(block, carry):
        out_ref[:, lanes(block)] = model_ref[:, lanes(block)] * scale
        return carry

    copies = []
    for chunk in range(CHUNKS):
        lax.fori_loop(chunk * blocks, (chunk + 1) * blocks, one_block, 0, unroll=4)
        where = slice(chunk * blocks * BS, (chunk + 1) * blocks * BS)
        copies.append(
            pltpu.make_async_copy(out_ref.at[:, where], out_hbm.at[:, where], sems.at[chunk])
        )
        copies[-1].start()
    for copy in copies:
        copy.wait()


def call(kernel, name, in_spaces, outs, scratch=(), flops=0, moved=0, limit=16 << 20):
    return pl.pallas_call(
        kernel,
        name=name,
        in_specs=[pl.BlockSpec(memory_space=space) for space in in_spaces],
        out_specs=[pl.BlockSpec(memory_space=space) for _, _, space in outs],
        out_shape=[jax.ShapeDtypeStruct(shape, dtype) for shape, dtype, _ in outs],
        scratch_shapes=list(scratch),
        compiler_params=pltpu.CompilerParams(vmem_limit_bytes=limit),
        cost_estimate=pl.CostEstimate(flops=flops, bytes_accessed=moved, transcendentals=0),
    )


def on_device(ray_blocks, block_cells, block_counts, travel_times):
    pair_count, slot_count = ray_blocks.shape[:2]
    slots = pair_count * slot_count
    peers = lax.axis_size("pair")
    spots = peers * BCAP
    times = travel_times.T
    cols, pairs = times.shape
    message = ((peers, BCAP * cols + TAIL, BS), BF16, VMEM)
    tile = ((cols, BS), F32, VMEM)
    data = ((cols, pairs), F32, VMEM)
    whole = ((cols, CELL_DEV), F32, VMEM)
    totals = VMEM((spots + 1, cols, BS), F32)
    flops = 2 * slots * BS * BS * cols

    order = [peer // 2 + peer % 2 * (peers // 2) for peer in range(peers)]

    def exchange(values):
        return lax.all_to_all(
            values, "pair", split_axis=0, concat_axis=0, axis_index_groups=[order], tiled=True
        )

    outgoing, target = call(
        start_kernel, "start", [HBM, HBM, HBM, HBM],
        [message, ((slots,), jnp.int32, SMEM)],
        [
            totals, SMEM((spots,), jnp.int32), SMEM((peers,), jnp.int32),
            SMEM(block_cells.shape, jnp.int32), SMEM(block_counts.shape, jnp.int32),
            VMEM(times.shape, F32), VMEM(ray_blocks.shape, BF16),
            pltpu.SemaphoreType.DMA((3,)), pltpu.SemaphoreType.DMA((pair_count,)),
        ],
        flops, 6 << 20, 60 << 20,
    )(block_cells, block_counts, times, ray_blocks)
    arrived = exchange(outgoing)
    model, beta, reply_, asked = call(
        first_cell_kernel, "cells_first", [VMEM],
        [whole, tile, message, ((peers, BS), jnp.int32, SMEM)],
        [VMEM((peers, BS), jnp.int32), pltpu.SemaphoreType.DMA],
        0, 6 << 20,
    )(arrived)
    models, betas, alphas = [model], [beta], []
    current = times
    for step in range(ITERS):
        fetched = exchange(reply_)
        outgoing, current, alpha = call(
            pair_kernel, "pairs", [SMEM, VMEM, VMEM, VMEM, VMEM],
            [message, data, tile], [totals], 2 * flops, 8 << 20,
        )(target, fetched, current, betas[-1], ray_blocks)
        alphas.append(alpha)
        arrived = exchange(outgoing)
        if step + 1 < ITERS:
            model, beta, reply_ = call(
                cell_kernel, "cells", [SMEM] + [VMEM] * 4, [whole, tile, message], (), 0, 8 << 20
            )(asked, arrived, models[-1], alpha, betas[-1])
            models.append(model)
            betas.append(beta)
    scratch = [VMEM(whole[0], F32), pltpu.SemaphoreType.DMA((CHUNKS,))]
    model, beta, tails, estimate = call(
        last_cell_kernel, "cells_last", [SMEM] + [VMEM] * (3 * ITERS + 1),
        [whole, tile, ((peers, TAIL, BS), F32, VMEM), (whole[0], F32, HBM)], scratch, 0, 10 << 20,
    )(asked, arrived, *models, *alphas, *betas)
    (model_vec,) = call(
        model_kernel, "model", [VMEM, VMEM, VMEM], [(whole[0], F32, HBM)], scratch, 0, 4 << 20
    )(exchange(tails), beta, model)
    return (estimate.T, model_vec.T)


def solution(mesh):
    return jax.shard_map(
        on_device,
        mesh=mesh,
        in_specs=(
            P(("groups", "pair"), None, None, None),
            P(("groups", "pair"), None),
            P(("groups", "pair")),
            P(("groups", "pair"), None),
        ),
        out_specs=(P(("groups", "pair"), None), P(("groups", "pair"), None)),
        check_vma=False,
    )
```

```python
import functools

import jax
import jax.numpy as jnp
from jax import lax
from jax.experimental import pallas as pl
from jax.experimental.pallas import tpu as pltpu
from jax.sharding import PartitionSpec as P

CELL_DEV = 8192
BCAP = 4
BS = 128
TAIL = 8
ITERS = 2
EPS = 1e-12
F32 = jnp.float32
BF16 = jnp.bfloat16
VMEM = pltpu.VMEM
SMEM = pltpu.SMEM
HBM = pltpu.HBM
CHUNKS = 8


def diagonal(cols):
    shape = (cols, BS)
    return lax.broadcasted_iota(jnp.int32, shape, 0) == lax.broadcasted_iota(jnp.int32, shape, 1)


def squares_tail(squares):
    cols = squares.shape[0]
    total = jnp.sum(squares, axis=1, keepdims=True)
    row = jnp.sum(jnp.where(diagonal(cols), total, 0.0), axis=0, keepdims=True)
    high = row.astype(BF16).astype(F32)
    middle = (row - high).astype(BF16).astype(F32)
    low = row - high - middle
    place = lax.broadcasted_iota(jnp.int32, (TAIL, BS), 0)
    return jnp.where(
        place == 0, high, jnp.where(place == 1, middle, jnp.where(place == 2, low, 0.0))
    )


def norm_of_tails(message_ref, cols):
    tails = message_ref[:, BCAP * cols :, :].astype(F32)
    summed = jnp.sum(tails, axis=0)
    row = summed[0:1] + summed[1:2] + summed[2:3]
    column = jnp.sum(jnp.where(diagonal(cols), row, 0.0), axis=1, keepdims=True)
    return jnp.broadcast_to(jnp.sqrt(column + EPS), (cols, BS))


def lanes(block):
    return pl.ds(pl.multiple_of(block * BS, BS), BS)


def transposed(data_ref, rays_ref, before, target_ref, total_ref, message_ref):
    pair_count, slot_count = rays_ref.shape[:2]
    cols = data_ref.shape[0]
    peers = message_ref.shape[0]
    spots = peers * BCAP

    def clear(index, carry):
        total_ref[index] = jnp.zeros((cols, BS), F32)
        return carry

    lax.fori_loop(0, spots, clear, 0, unroll=8)

    def one_pair(pair, carry):
        before(pair)
        data = data_ref[:, lanes(pair)]
        high = data.astype(BF16)
        low = (data - high.astype(F32)).astype(BF16)
        pieces = jnp.concatenate([high, low], axis=0)
        for slot in range(0, slot_count, 2):
            rays = jnp.concatenate([rays_ref[pair, slot], rays_ref[pair, slot + 1]], axis=1)
            part = jnp.dot(pieces, rays, preferred_element_type=F32)
            part = part[:cols] + part[cols:]
            for half in range(2):
                spot = target_ref[pair * slot_count + slot + half]
                total_ref[spot] += part[:, half * BS : (half + 1) * BS]
        return carry

    lax.fori_loop(0, pair_count, one_pair, 0, unroll=4)

    def pack(peer, carry):
        for rank in range(BCAP):
            message_ref[peer, rank * cols : (rank + 1) * cols, :] = total_ref[
                peer * BCAP + rank
            ].astype(BF16)
        return carry

    lax.fori_loop(0, peers, pack, 0, unroll=2)


def start_kernel(
    cells_hbm, counts_hbm, times_hbm, rays_hbm, message_ref, target_ref,
    total_ref, table_ref, used_ref, cells_ref, counts_ref, times_ref, rays_ref, sems, ray_sems,
):
    pair_count, slot_count = rays_ref.shape[:2]
    peers = message_ref.shape[0]
    cols = times_ref.shape[0]
    owned = CELL_DEV // BS
    copies = [
        pltpu.make_async_copy(source, dest, sems.at[index])
        for index, (source, dest) in enumerate(
            [(cells_hbm, cells_ref), (counts_hbm, counts_ref), (times_hbm, times_ref)]
        )
    ]
    for copy in copies:
        copy.start()

    def ray_copy(pair):
        return pltpu.make_async_copy(rays_hbm.at[pair], rays_ref.at[pair], ray_sems.at[pair])

    def fetch(pair, carry):
        ray_copy(pair).start()
        return carry

    lax.fori_loop(0, pair_count, fetch, 0)

    def clear(peer, carry):
        used_ref[peer] = 0
        for rank in range(BCAP):
            table_ref[peer * BCAP + rank] = 0
        return carry

    lax.fori_loop(0, peers, clear, 0)
    for copy in copies:
        copy.wait()

    def find_places(pair):
        count = counts_ref[pair]
        for slot in range(slot_count):
            cell = cells_ref[pair, slot]
            owner = cell // owned
            local = cell % owned
            used = used_ref[owner]
            rank = used
            for other in range(BCAP - 1, -1, -1):
                same = (table_ref[owner * BCAP + other] == local) & (other < used)
                rank = jnp.where(same, other, rank)
            spot = owner * BCAP + rank
            table_ref[spot] = local
            used_ref[owner] = jnp.maximum(used, rank + 1)
            target_ref[pair * slot_count + slot] = jnp.where(slot < count, spot, peers * BCAP)

    def before(pair):
        find_places(pair)
        ray_copy(pair).wait()

    transposed(times_ref, rays_ref, before, target_ref, total_ref, message_ref)
    squares = jnp.zeros((cols, BS), F32)
    for pair in range(pair_count):
        part = times_ref[:, pair * BS : (pair + 1) * BS]
        squares += part * part
    tail = squares_tail(squares)
    place = lax.broadcasted_iota(jnp.int32, (TAIL, BS), 0)
    lane = lax.broadcasted_iota(jnp.int32, (TAIL, BS), 1)

    def ask(peer, carry):
        rows = tail
        for rank in range(BCAP):
            asked = table_ref[peer * BCAP + rank].astype(F32)
            rows = jnp.where((place == 3) & (lane == rank), asked, rows)
        message_ref[peer, BCAP * cols :, :] = rows.astype(BF16)
        return carry

    lax.fori_loop(0, peers, ask, 0)


def pair_kernel(
    target_ref, fetched_ref, data_ref, beta_ref, rays_ref,
    message_ref, alpha_ref, raw_ref, total_ref,
):
    pair_count, slot_count = rays_ref.shape[:2]
    peers = message_ref.shape[0]
    cols = data_ref.shape[0]
    spots = peers * BCAP
    alpha = norm_of_tails(fetched_ref, cols)
    alpha_ref[...] = alpha
    beta = beta_ref[...]
    model_scale = 1.0 / (alpha * beta)
    data_scale = alpha / beta

    def one_pair(pair, squares):
        chosen = []
        for slot in range(slot_count):
            spot = target_ref[pair * slot_count + slot]
            live = spot < spots
            spot = jnp.where(live, spot, 0)
            rows = pl.ds(pl.multiple_of((spot % BCAP) * cols, cols), cols)
            block = fetched_ref[spot // BCAP, rows, :]
            chosen.append(jnp.where(live, block, jnp.zeros_like(block)))
        rays = jnp.concatenate([rays_ref[pair, slot] for slot in range(slot_count)], axis=1)
        product = lax.dot_general(
            rays, jnp.concatenate(chosen, axis=1), (((1,), (1,)), ((), ())),
            preferred_element_type=F32,
        )
        raw = product.T * model_scale - data_ref[:, lanes(pair)] * data_scale
        raw_ref[:, lanes(pair)] = raw
        return squares + raw * raw

    squares = lax.fori_loop(0, pair_count, one_pair, jnp.zeros((cols, BS), F32), unroll=4)
    transposed(raw_ref, rays_ref, lambda pair: None, target_ref, total_ref, message_ref)
    tail = squares_tail(squares).astype(BF16)
    message_ref[:, BCAP * cols :, :] = jnp.broadcast_to(tail[None], (peers, TAIL, BS))


def gathered(arrived_ref, asked_ref, model_ref):
    peers = arrived_ref.shape[0]
    cols = model_ref.shape[0]

    def add(peer, carry):
        for rank in range(BCAP):
            where = lanes(asked_ref[peer, rank])
            block = arrived_ref[peer, rank * cols : (rank + 1) * cols, :]
            model_ref[:, where] += block.astype(F32)
        return carry

    lax.fori_loop(0, peers, add, 0, unroll=2)


def reply(squares, scale, asked_ref, model_ref, out_ref):
    peers = out_ref.shape[0]
    cols = model_ref.shape[0]
    tail = squares_tail(squares * scale * scale).astype(BF16)
    out_ref[:, BCAP * cols :, :] = jnp.broadcast_to(tail[None], (peers, TAIL, BS))

    def one_peer(peer, carry):
        for rank in range(BCAP):
            block = model_ref[:, lanes(asked_ref[peer, rank])]
            out_ref[peer, rank * cols : (rank + 1) * cols, :] = block.astype(BF16)
        return carry

    lax.fori_loop(0, peers, one_peer, 0, unroll=2)


def squares_of(model_ref):
    cols, cells = model_ref.shape

    def one_block(block, squares):
        values = model_ref[:, lanes(block)]
        return squares + values * values

    return lax.fori_loop(0, cells // BS, one_block, jnp.zeros((cols, BS), F32), unroll=8)


def first_cell_kernel(arrived_ref, model_ref, beta_ref, out_ref, asked_ref, table_ref, sem):
    cols, cells = model_ref.shape
    table_ref[...] = arrived_ref[:, BCAP * cols :, :].astype(F32)[:, 3, :].astype(jnp.int32)
    copy = pltpu.make_async_copy(table_ref, asked_ref, sem)
    copy.start()
    beta = norm_of_tails(arrived_ref, cols)
    beta_ref[...] = beta
    model_ref[...] = jnp.zeros((cols, cells), F32)
    copy.wait()
    gathered(arrived_ref, asked_ref, model_ref)
    reply(squares_of(model_ref), 1.0 / beta, asked_ref, model_ref, out_ref)


def start_from(before_ref, scale, model_ref):
    def one_block(block, carry):
        model_ref[:, lanes(block)] = before_ref[:, lanes(block)] * -scale
        return carry

    lax.fori_loop(0, model_ref.shape[1] // BS, one_block, 0, unroll=8)


def cell_kernel(
    asked_ref, arrived_ref, before_ref, alpha_ref, beta_before_ref, model_ref, beta_ref, out_ref
):
    beta = norm_of_tails(arrived_ref, model_ref.shape[0])
    beta_ref[...] = beta
    start_from(before_ref, beta * beta / (alpha_ref[...] * beta_before_ref[...]), model_ref)
    gathered(arrived_ref, asked_ref, model_ref)
    reply(squares_of(model_ref), 1.0 / beta, asked_ref, model_ref, out_ref)


def last_cell_kernel(asked_ref, arrived_ref, *refs):
    models = refs[:ITERS]
    alphas = [ref[...] for ref in refs[ITERS : 2 * ITERS]]
    betas = [ref[...] for ref in refs[2 * ITERS : 3 * ITERS]]
    model_ref, beta_ref, out_ref, estimate_hbm, estimate_ref, sems = refs[3 * ITERS :]
    cols, cells = model_ref.shape
    beta = norm_of_tails(arrived_ref, cols)
    beta_ref[...] = beta
    weights = estimate_weights(betas + [beta], alphas)
    scale = beta * beta / (alphas[-1] * betas[-1])
    blocks = cells // BS // CHUNKS

    def one_block(block, carry):
        where = lanes(block)
        values = models[-1][:, where]
        model_ref[:, where] = values * -scale
        total = values * weights[-1]
        for i in range(ITERS - 1):
            total += weights[i] * models[i][:, where]
        estimate_ref[:, where] = total
        return carry

    copies = []
    for chunk in range(CHUNKS):
        lax.fori_loop(chunk * blocks, (chunk + 1) * blocks, one_block, 0, unroll=4)
        where = slice(chunk * blocks * BS, (chunk + 1) * blocks * BS)
        copies.append(
            pltpu.make_async_copy(
                estimate_ref.at[:, where], estimate_hbm.at[:, where], sems.at[chunk]
            )
        )
        copies[-1].start()
    gathered(arrived_ref, asked_ref, model_ref)
    scale = 1.0 / beta
    tail = squares_tail(squares_of(model_ref) * scale * scale)
    out_ref[...] = jnp.broadcast_to(tail[None], out_ref.shape)
    for copy in copies:
        copy.wait()


def estimate_weights(betas, alphas):
    phi_bar = betas[0]
    rho_bar = alphas[0]
    trace = [1.0 / (alphas[0] * betas[0])]
    weight = [jnp.zeros_like(phi_bar)] * ITERS
    for step in range(ITERS):
        beta = betas[step + 1]
        rho = jnp.sqrt(rho_bar * rho_bar + beta * beta)
        cosine = rho_bar / rho
        sine = beta / rho
        gain = cosine * phi_bar / rho
        weight = [
            weight[i] + gain * trace[i] if i < len(trace) else weight[i] for i in range(ITERS)
        ]
        if step + 1 < ITERS:
            alpha = alphas[step + 1]
            theta = sine * alpha
            rho_bar = -cosine * alpha
            phi_bar = sine * phi_bar
            trace = [-(theta / rho) * value for value in trace] + [1.0 / (alpha * beta)]
    return weight


def model_kernel(tails_ref, beta_ref, model_ref, out_hbm, out_ref, sems):
    cols, cells = model_ref.shape
    blocks = cells // BS // CHUNKS
    summed = jnp.sum(tails_ref[...], axis=0)
    row = summed[0:1] + summed[1:2] + summed[2:3]
    column = jnp.sum(jnp.where(diagonal(cols), row, 0.0), axis=1, keepdims=True)
    alpha = jnp.broadcast_to(jnp.sqrt(column + EPS), (cols, BS))
    scale = 1.0 / (alpha * beta_ref[...])

    def one_block(block, carry):
        out_ref[:, lanes(block)] = model_ref[:, lanes(block)] * scale
        return carry

    copies = []
    for chunk in range(CHUNKS):
        lax.fori_loop(chunk * blocks, (chunk + 1) * blocks, one_block, 0, unroll=4)
        where = slice(chunk * blocks * BS, (chunk + 1) * blocks * BS)
        copies.append(
            pltpu.make_async_copy(out_ref.at[:, where], out_hbm.at[:, where], sems.at[chunk])
        )
        copies[-1].start()
    for copy in copies:
        copy.wait()


def call(kernel, name, in_spaces, outs, scratch=(), flops=0, moved=0, limit=16 << 20):
    return pl.pallas_call(
        kernel,
        name=name,
        in_specs=[pl.BlockSpec(memory_space=space) for space in in_spaces],
        out_specs=[pl.BlockSpec(memory_space=space) for _, _, space in outs],
        out_shape=[jax.ShapeDtypeStruct(shape, dtype) for shape, dtype, _ in outs],
        scratch_shapes=list(scratch),
        compiler_params=pltpu.CompilerParams(vmem_limit_bytes=limit),
        cost_estimate=pl.CostEstimate(flops=flops, bytes_accessed=moved, transcendentals=0),
    )


def on_device(ray_blocks, block_cells, block_counts, travel_times):
    pair_count, slot_count = ray_blocks.shape[:2]
    slots = pair_count * slot_count
    peers = lax.axis_size("pair")
    spots = peers * BCAP
    times = travel_times.T
    cols, pairs = times.shape
    message = ((peers, BCAP * cols + TAIL, BS), BF16, VMEM)
    tile = ((cols, BS), F32, VMEM)
    data = ((cols, pairs), F32, VMEM)
    whole = ((cols, CELL_DEV), F32, VMEM)
    totals = VMEM((spots + 1, cols, BS), F32)
    flops = 2 * slots * BS * BS * cols

    def exchange(values):
        return lax.all_to_all(values, "pair", split_axis=0, concat_axis=0, tiled=True)

    outgoing, target = call(
        start_kernel, "start", [HBM, HBM, HBM, HBM],
        [message, ((slots,), jnp.int32, SMEM)],
        [
            totals, SMEM((spots,), jnp.int32), SMEM((peers,), jnp.int32),
            SMEM(block_cells.shape, jnp.int32), SMEM(block_counts.shape, jnp.int32),
            VMEM(times.shape, F32), VMEM(ray_blocks.shape, BF16),
            pltpu.SemaphoreType.DMA((3,)), pltpu.SemaphoreType.DMA((pair_count,)),
        ],
        flops, 6 << 20, 60 << 20,
    )(block_cells, block_counts, times, ray_blocks)
    arrived = exchange(outgoing)
    model, beta, reply_, asked = call(
        first_cell_kernel, "cells_first", [VMEM],
        [whole, tile, message, ((peers, BS), jnp.int32, SMEM)],
        [VMEM((peers, BS), jnp.int32), pltpu.SemaphoreType.DMA],
        0, 6 << 20,
    )(arrived)
    models, betas, alphas = [model], [beta], []
    current = times
    for step in range(ITERS):
        fetched = exchange(reply_)
        last = step + 1 == ITERS
        outgoing, alpha, *raw = call(
            pair_kernel, "pairs_last" if last else "pairs", [SMEM, VMEM, VMEM, VMEM, VMEM],
            [message, tile] + [data] * (not last), [VMEM(data[0], F32)] * last + [totals],
            2 * flops, 8 << 20,
        )(target, fetched, current, betas[-1], ray_blocks)
        current = raw[0] if raw else None
        alphas.append(alpha)
        arrived = exchange(outgoing)
        if not last:
            model, beta, reply_ = call(
                cell_kernel, "cells", [SMEM] + [VMEM] * 4, [whole, tile, message], (), 0, 8 << 20
            )(asked, arrived, models[-1], alpha, betas[-1])
            models.append(model)
            betas.append(beta)
    scratch = [VMEM(whole[0], F32), pltpu.SemaphoreType.DMA((CHUNKS,))]
    model, beta, tails, estimate = call(
        last_cell_kernel, "cells_last", [SMEM] + [VMEM] * (3 * ITERS + 1),
        [whole, tile, ((peers, TAIL, BS), F32, VMEM), (whole[0], F32, HBM)], scratch, 0, 10 << 20,
    )(asked, arrived, *models, *alphas, *betas)
    (model_vec,) = call(
        model_kernel, "model", [VMEM, VMEM, VMEM], [(whole[0], F32, HBM)], scratch, 0, 4 << 20
    )(exchange(tails), beta, model)
    return (estimate.T, model_vec.T)


def solution(mesh):
    return jax.shard_map(
        on_device,
        mesh=mesh,
        in_specs=(
            P(("groups", "pair"), None, None, None),
            P(("groups", "pair"), None),
            P(("groups", "pair")),
            P(("groups", "pair"), None),
        ),
        out_specs=(P(("groups", "pair"), None), P(("groups", "pair"), None)),
        check_vma=False,
    )
```

```python
import functools

import jax
import jax.numpy as jnp
from jax import lax
from jax.experimental import pallas as pl
from jax.experimental.pallas import tpu as pltpu
from jax.sharding import PartitionSpec as P

CELL_DEV = 8192
BCAP = 4
BS = 128
TAIL = 8
ITERS = 2
EPS = 1e-12
F32 = jnp.float32
BF16 = jnp.bfloat16
VMEM = pltpu.VMEM
SMEM = pltpu.SMEM
HBM = pltpu.HBM
CHUNKS = 8


def diagonal(cols):
    shape = (cols, BS)
    return lax.broadcasted_iota(jnp.int32, shape, 0) == lax.broadcasted_iota(jnp.int32, shape, 1)


def squares_tail(squares):
    cols = squares.shape[0]
    total = jnp.sum(squares, axis=1, keepdims=True)
    row = jnp.sum(jnp.where(diagonal(cols), total, 0.0), axis=0, keepdims=True)
    high = row.astype(BF16).astype(F32)
    middle = (row - high).astype(BF16).astype(F32)
    low = row - high - middle
    place = lax.broadcasted_iota(jnp.int32, (TAIL, BS), 0)
    return jnp.where(
        place == 0, high, jnp.where(place == 1, middle, jnp.where(place == 2, low, 0.0))
    )


def norm_of_tails(message_ref, cols):
    tails = message_ref[:, BCAP * cols :, :].astype(F32)
    summed = jnp.sum(tails, axis=0)
    row = summed[0:1] + summed[1:2] + summed[2:3]
    column = jnp.sum(jnp.where(diagonal(cols), row, 0.0), axis=1, keepdims=True)
    return jnp.broadcast_to(jnp.sqrt(column + EPS), (cols, BS))


def lanes(block):
    return pl.ds(pl.multiple_of(block * BS, BS), BS)


def transposed(data_ref, rays_ref, before, target_ref, total_ref, message_ref):
    pair_count, slot_count = rays_ref.shape[:2]
    cols = data_ref.shape[0]
    peers = message_ref.shape[0]
    spots = peers * BCAP

    def clear(index, carry):
        total_ref[index] = jnp.zeros((cols, BS), F32)
        return carry

    lax.fori_loop(0, spots, clear, 0, unroll=8)

    def one_pair(pair, carry):
        before(pair)
        data = data_ref[:, lanes(pair)]
        high = data.astype(BF16)
        low = (data - high.astype(F32)).astype(BF16)
        pieces = jnp.concatenate([high, low], axis=0)
        for slot in range(0, slot_count, 2):
            rays = jnp.concatenate([rays_ref[pair, slot], rays_ref[pair, slot + 1]], axis=1)
            part = jnp.dot(pieces, rays, preferred_element_type=F32)
            part = part[:cols] + part[cols:]
            for half in range(2):
                spot = target_ref[pair * slot_count + slot + half]
                total_ref[spot] += part[:, half * BS : (half + 1) * BS]
        return carry

    lax.fori_loop(0, pair_count, one_pair, 0, unroll=True)

    def pack(peer, carry):
        for rank in range(BCAP):
            message_ref[peer, rank * cols : (rank + 1) * cols, :] = total_ref[
                peer * BCAP + rank
            ].astype(BF16)
        return carry

    lax.fori_loop(0, peers, pack, 0, unroll=True)


def start_kernel(
    cells_hbm, counts_hbm, times_hbm, rays_hbm, message_ref, target_ref,
    total_ref, table_ref, used_ref, cells_ref, counts_ref, times_ref, rays_ref, sems, ray_sems,
):
    pair_count, slot_count = rays_ref.shape[:2]
    peers = message_ref.shape[0]
    cols = times_ref.shape[0]
    owned = CELL_DEV // BS
    copies = [
        pltpu.make_async_copy(source, dest, sems.at[index])
        for index, (source, dest) in enumerate(
            [(cells_hbm, cells_ref), (counts_hbm, counts_ref), (times_hbm, times_ref)]
        )
    ]
    for copy in copies:
        copy.start()

    def ray_copy(pair):
        return pltpu.make_async_copy(rays_hbm.at[pair], rays_ref.at[pair], ray_sems.at[pair])

    def fetch(pair, carry):
        ray_copy(pair).start()
        return carry

    lax.fori_loop(0, pair_count, fetch, 0)

    def clear(peer, carry):
        used_ref[peer] = 0
        for rank in range(BCAP):
            table_ref[peer * BCAP + rank] = 0
        return carry

    lax.fori_loop(0, peers, clear, 0)
    for copy in copies:
        copy.wait()

    def find_places(pair):
        count = counts_ref[pair]
        for slot in range(slot_count):
            cell = cells_ref[pair, slot]
            owner = cell // owned
            local = cell % owned
            used = used_ref[owner]
            rank = used
            for other in range(BCAP - 1, -1, -1):
                same = (table_ref[owner * BCAP + other] == local) & (other < used)
                rank = jnp.where(same, other, rank)
            spot = owner * BCAP + rank
            table_ref[spot] = local
            used_ref[owner] = jnp.maximum(used, rank + 1)
            target_ref[pair * slot_count + slot] = jnp.where(slot < count, spot, peers * BCAP)

    def before(pair):
        find_places(pair)
        ray_copy(pair).wait()

    transposed(times_ref, rays_ref, before, target_ref, total_ref, message_ref)
    squares = jnp.zeros((cols, BS), F32)
    for pair in range(pair_count):
        part = times_ref[:, pair * BS : (pair + 1) * BS]
        squares += part * part
    tail = squares_tail(squares)
    place = lax.broadcasted_iota(jnp.int32, (TAIL, BS), 0)
    lane = lax.broadcasted_iota(jnp.int32, (TAIL, BS), 1)

    def ask(peer, carry):
        rows = tail
        for rank in range(BCAP):
            asked = table_ref[peer * BCAP + rank].astype(F32)
            rows = jnp.where((place == 3) & (lane == rank), asked, rows)
        message_ref[peer, BCAP * cols :, :] = rows.astype(BF16)
        return carry

    lax.fori_loop(0, peers, ask, 0)


def pair_kernel(
    target_ref, fetched_ref, data_ref, beta_ref, rays_ref,
    message_ref, alpha_ref, raw_ref, total_ref,
):
    pair_count, slot_count = rays_ref.shape[:2]
    peers = message_ref.shape[0]
    cols = data_ref.shape[0]
    spots = peers * BCAP
    alpha = norm_of_tails(fetched_ref, cols)
    alpha_ref[...] = alpha
    beta = beta_ref[...]
    model_scale = 1.0 / (alpha * beta)
    data_scale = alpha / beta

    def one_pair(pair, squares):
        chosen = []
        for slot in range(slot_count):
            spot = target_ref[pair * slot_count + slot]
            live = spot < spots
            spot = jnp.where(live, spot, 0)
            rows = pl.ds(pl.multiple_of((spot % BCAP) * cols, cols), cols)
            block = fetched_ref[spot // BCAP, rows, :]
            chosen.append(jnp.where(live, block, jnp.zeros_like(block)))
        rays = jnp.concatenate([rays_ref[pair, slot] for slot in range(slot_count)], axis=1)
        product = lax.dot_general(
            rays, jnp.concatenate(chosen, axis=1), (((1,), (1,)), ((), ())),
            preferred_element_type=F32,
        )
        raw = product.T * model_scale - data_ref[:, lanes(pair)] * data_scale
        raw_ref[:, lanes(pair)] = raw
        return squares + raw * raw

    squares = lax.fori_loop(0, pair_count, one_pair, jnp.zeros((cols, BS), F32), unroll=True)
    transposed(raw_ref, rays_ref, lambda pair: None, target_ref, total_ref, message_ref)
    tail = squares_tail(squares).astype(BF16)
    message_ref[:, BCAP * cols :, :] = jnp.broadcast_to(tail[None], (peers, TAIL, BS))


def gathered(arrived_ref, asked_ref, model_ref):
    peers = arrived_ref.shape[0]
    cols = model_ref.shape[0]

    def add(peer, carry):
        for rank in range(BCAP):
            where = lanes(asked_ref[peer, rank])
            block = arrived_ref[peer, rank * cols : (rank + 1) * cols, :]
            model_ref[:, where] += block.astype(F32)
        return carry

    lax.fori_loop(0, peers, add, 0, unroll=True)


def reply(squares, scale, asked_ref, model_ref, out_ref):
    peers = out_ref.shape[0]
    cols = model_ref.shape[0]
    tail = squares_tail(squares * scale * scale).astype(BF16)
    out_ref[:, BCAP * cols :, :] = jnp.broadcast_to(tail[None], (peers, TAIL, BS))

    def one_peer(peer, carry):
        for rank in range(BCAP):
            block = model_ref[:, lanes(asked_ref[peer, rank])]
            out_ref[peer, rank * cols : (rank + 1) * cols, :] = block.astype(BF16)
        return carry

    lax.fori_loop(0, peers, one_peer, 0, unroll=True)


def squares_of(model_ref):
    cols, cells = model_ref.shape

    def one_block(block, squares):
        values = model_ref[:, lanes(block)]
        return squares + values * values

    return lax.fori_loop(0, cells // BS, one_block, jnp.zeros((cols, BS), F32), unroll=8)


def first_cell_kernel(arrived_ref, model_ref, beta_ref, out_ref, asked_ref, table_ref, sem):
    cols, cells = model_ref.shape
    table_ref[...] = arrived_ref[:, BCAP * cols :, :].astype(F32)[:, 3, :].astype(jnp.int32)
    copy = pltpu.make_async_copy(table_ref, asked_ref, sem)
    copy.start()
    beta = norm_of_tails(arrived_ref, cols)
    beta_ref[...] = beta
    model_ref[...] = jnp.zeros((cols, cells), F32)
    copy.wait()
    gathered(arrived_ref, asked_ref, model_ref)
    reply(squares_of(model_ref), 1.0 / beta, asked_ref, model_ref, out_ref)


def start_from(before_ref, scale, model_ref):
    def one_block(block, carry):
        model_ref[:, lanes(block)] = before_ref[:, lanes(block)] * -scale
        return carry

    lax.fori_loop(0, model_ref.shape[1] // BS, one_block, 0, unroll=8)


def cell_kernel(
    asked_ref, arrived_ref, before_ref, alpha_ref, beta_before_ref, model_ref, beta_ref, out_ref
):
    beta = norm_of_tails(arrived_ref, model_ref.shape[0])
    beta_ref[...] = beta
    start_from(before_ref, beta * beta / (alpha_ref[...] * beta_before_ref[...]), model_ref)
    gathered(arrived_ref, asked_ref, model_ref)
    reply(squares_of(model_ref), 1.0 / beta, asked_ref, model_ref, out_ref)


def last_cell_kernel(asked_ref, arrived_ref, *refs):
    models = refs[:ITERS]
    alphas = [ref[...] for ref in refs[ITERS : 2 * ITERS]]
    betas = [ref[...] for ref in refs[2 * ITERS : 3 * ITERS]]
    model_ref, beta_ref, out_ref, estimate_hbm, estimate_ref, sems = refs[3 * ITERS :]
    cols, cells = model_ref.shape
    beta = norm_of_tails(arrived_ref, cols)
    beta_ref[...] = beta
    weights = estimate_weights(betas + [beta], alphas)
    scale = beta * beta / (alphas[-1] * betas[-1])
    blocks = cells // BS // CHUNKS

    def one_block(block, carry):
        where = lanes(block)
        values = models[-1][:, where]
        model_ref[:, where] = values * -scale
        total = values * weights[-1]
        for i in range(ITERS - 1):
            total += weights[i] * models[i][:, where]
        estimate_ref[:, where] = total
        return carry

    copies = []
    for chunk in range(CHUNKS):
        lax.fori_loop(chunk * blocks, (chunk + 1) * blocks, one_block, 0, unroll=4)
        where = slice(chunk * blocks * BS, (chunk + 1) * blocks * BS)
        copies.append(
            pltpu.make_async_copy(
                estimate_ref.at[:, where], estimate_hbm.at[:, where], sems.at[chunk]
            )
        )
        copies[-1].start()
    gathered(arrived_ref, asked_ref, model_ref)
    scale = 1.0 / beta
    tail = squares_tail(squares_of(model_ref) * scale * scale)
    out_ref[...] = jnp.broadcast_to(tail[None], out_ref.shape)
    for copy in copies:
        copy.wait()


def estimate_weights(betas, alphas):
    phi_bar = betas[0]
    rho_bar = alphas[0]
    trace = [1.0 / (alphas[0] * betas[0])]
    weight = [jnp.zeros_like(phi_bar)] * ITERS
    for step in range(ITERS):
        beta = betas[step + 1]
        rho = jnp.sqrt(rho_bar * rho_bar + beta * beta)
        cosine = rho_bar / rho
        sine = beta / rho
        gain = cosine * phi_bar / rho
        weight = [
            weight[i] + gain * trace[i] if i < len(trace) else weight[i] for i in range(ITERS)
        ]
        if step + 1 < ITERS:
            alpha = alphas[step + 1]
            theta = sine * alpha
            rho_bar = -cosine * alpha
            phi_bar = sine * phi_bar
            trace = [-(theta / rho) * value for value in trace] + [1.0 / (alpha * beta)]
    return weight


def model_kernel(tails_ref, beta_ref, model_ref, out_hbm, out_ref, sems):
    cols, cells = model_ref.shape
    blocks = cells // BS // CHUNKS
    summed = jnp.sum(tails_ref[...], axis=0)
    row = summed[0:1] + summed[1:2] + summed[2:3]
    column = jnp.sum(jnp.where(diagonal(cols), row, 0.0), axis=1, keepdims=True)
    alpha = jnp.broadcast_to(jnp.sqrt(column + EPS), (cols, BS))
    scale = 1.0 / (alpha * beta_ref[...])

    def one_block(block, carry):
        out_ref[:, lanes(block)] = model_ref[:, lanes(block)] * scale
        return carry

    copies = []
    for chunk in range(CHUNKS):
        lax.fori_loop(chunk * blocks, (chunk + 1) * blocks, one_block, 0, unroll=4)
        where = slice(chunk * blocks * BS, (chunk + 1) * blocks * BS)
        copies.append(
            pltpu.make_async_copy(out_ref.at[:, where], out_hbm.at[:, where], sems.at[chunk])
        )
        copies[-1].start()
    for copy in copies:
        copy.wait()


def call(kernel, name, in_spaces, outs, scratch=(), flops=0, moved=0, limit=16 << 20):
    return pl.pallas_call(
        kernel,
        name=name,
        in_specs=[pl.BlockSpec(memory_space=space) for space in in_spaces],
        out_specs=[pl.BlockSpec(memory_space=space) for _, _, space in outs],
        out_shape=[jax.ShapeDtypeStruct(shape, dtype) for shape, dtype, _ in outs],
        scratch_shapes=list(scratch),
        compiler_params=pltpu.CompilerParams(vmem_limit_bytes=limit),
        cost_estimate=pl.CostEstimate(flops=flops, bytes_accessed=moved, transcendentals=0),
    )


def on_device(ray_blocks, block_cells, block_counts, travel_times):
    pair_count, slot_count = ray_blocks.shape[:2]
    slots = pair_count * slot_count
    peers = lax.axis_size("pair")
    spots = peers * BCAP
    times = travel_times.T
    cols, pairs = times.shape
    message = ((peers, BCAP * cols + TAIL, BS), BF16, VMEM)
    tile = ((cols, BS), F32, VMEM)
    data = ((cols, pairs), F32, VMEM)
    whole = ((cols, CELL_DEV), F32, VMEM)
    totals = VMEM((spots + 1, cols, BS), F32)
    flops = 2 * slots * BS * BS * cols

    def exchange(values):
        return lax.all_to_all(values, "pair", split_axis=0, concat_axis=0, tiled=True)

    outgoing, target = call(
        start_kernel, "start", [HBM, HBM, HBM, HBM],
        [message, ((slots,), jnp.int32, SMEM)],
        [
            totals, SMEM((spots,), jnp.int32), SMEM((peers,), jnp.int32),
            SMEM(block_cells.shape, jnp.int32), SMEM(block_counts.shape, jnp.int32),
            VMEM(times.shape, F32), VMEM(ray_blocks.shape, BF16),
            pltpu.SemaphoreType.DMA((3,)), pltpu.SemaphoreType.DMA((pair_count,)),
        ],
        flops, 6 << 20, 60 << 20,
    )(block_cells, block_counts, times, ray_blocks)
    arrived = exchange(outgoing)
    model, beta, reply_, asked = call(
        first_cell_kernel, "cells_first", [VMEM],
        [whole, tile, message, ((peers, BS), jnp.int32, SMEM)],
        [VMEM((peers, BS), jnp.int32), pltpu.SemaphoreType.DMA],
        0, 6 << 20,
    )(arrived)
    models, betas, alphas = [model], [beta], []
    current = times
    for step in range(ITERS):
        fetched = exchange(reply_)
        last = step + 1 == ITERS
        outgoing, alpha, *raw = call(
            pair_kernel, "pairs_last" if last else "pairs", [SMEM, VMEM, VMEM, VMEM, VMEM],
            [message, tile] + [data] * (not last), [VMEM(data[0], F32)] * last + [totals],
            2 * flops, 8 << 20,
        )(target, fetched, current, betas[-1], ray_blocks)
        current = raw[0] if raw else None
        alphas.append(alpha)
        arrived = exchange(outgoing)
        if not last:
            model, beta, reply_ = call(
                cell_kernel, "cells", [SMEM] + [VMEM] * 4, [whole, tile, message], (), 0, 8 << 20
            )(asked, arrived, models[-1], alpha, betas[-1])
            models.append(model)
            betas.append(beta)
    scratch = [VMEM(whole[0], F32), pltpu.SemaphoreType.DMA((CHUNKS,))]
    model, beta, tails, estimate = call(
        last_cell_kernel, "cells_last", [SMEM] + [VMEM] * (3 * ITERS + 1),
        [whole, tile, ((peers, TAIL, BS), F32, VMEM), (whole[0], F32, HBM)], scratch, 0, 10 << 20,
    )(asked, arrived, *models, *alphas, *betas)
    (model_vec,) = call(
        model_kernel, "model", [VMEM, VMEM, VMEM], [(whole[0], F32, HBM)], scratch, 0, 4 << 20
    )(exchange(tails), beta, model)
    return (estimate.T, model_vec.T)


def solution(mesh):
    return jax.shard_map(
        on_device,
        mesh=mesh,
        in_specs=(
            P(("groups", "pair"), None, None, None),
            P(("groups", "pair"), None),
            P(("groups", "pair")),
            P(("groups", "pair"), None),
        ),
        out_specs=(P(("groups", "pair"), None), P(("groups", "pair"), None)),
        check_vma=False,
    )
```

```python
import functools

import jax
import jax.numpy as jnp
from jax import lax
from jax.experimental import pallas as pl
from jax.experimental.pallas import tpu as pltpu
from jax.sharding import PartitionSpec as P

CELL_DEV = 8192
BCAP = 4
BS = 128
TAIL = 8
ITERS = 2
EPS = 1e-12
F32 = jnp.float32
BF16 = jnp.bfloat16
VMEM = pltpu.VMEM
SMEM = pltpu.SMEM
HBM = pltpu.HBM
CHUNKS = 8


def diagonal(cols):
    shape = (cols, BS)
    return lax.broadcasted_iota(jnp.int32, shape, 0) == lax.broadcasted_iota(jnp.int32, shape, 1)


def squares_tail(squares):
    cols = squares.shape[0]
    total = jnp.sum(squares, axis=1, keepdims=True)
    row = jnp.sum(jnp.where(diagonal(cols), total, 0.0), axis=0, keepdims=True)
    high = row.astype(BF16).astype(F32)
    middle = (row - high).astype(BF16).astype(F32)
    low = row - high - middle
    place = lax.broadcasted_iota(jnp.int32, (TAIL, BS), 0)
    return jnp.where(
        place == 0, high, jnp.where(place == 1, middle, jnp.where(place == 2, low, 0.0))
    )


def norm_of_tails(message_refs, cols):
    summed = sum(message_ref[BCAP * cols :, :].astype(F32) for message_ref in message_refs)
    row = summed[0:1] + summed[1:2] + summed[2:3]
    column = jnp.sum(jnp.where(diagonal(cols), row, 0.0), axis=1, keepdims=True)
    return jnp.broadcast_to(jnp.sqrt(column + EPS), (cols, BS))


def lanes(block):
    return pl.ds(pl.multiple_of(block * BS, BS), BS)


def transposed(data_ref, rays_ref, before, target_ref, total_ref, message_refs):
    pair_count, slot_count = rays_ref.shape[:2]
    cols = data_ref.shape[0]
    spots = len(message_refs) * BCAP

    def clear(index, carry):
        total_ref[index] = jnp.zeros((cols, BS), F32)
        return carry

    lax.fori_loop(0, spots, clear, 0, unroll=8)

    def one_pair(pair, carry):
        before(pair)
        data = data_ref[:, lanes(pair)]
        high = data.astype(BF16)
        low = (data - high.astype(F32)).astype(BF16)
        pieces = jnp.concatenate([high, low], axis=0)
        for slot in range(0, slot_count, 2):
            rays = jnp.concatenate([rays_ref[pair, slot], rays_ref[pair, slot + 1]], axis=1)
            part = jnp.dot(pieces, rays, preferred_element_type=F32)
            part = part[:cols] + part[cols:]
            for half in range(2):
                spot = target_ref[pair * slot_count + slot + half]
                total_ref[spot] += part[:, half * BS : (half + 1) * BS]
        return carry

    lax.fori_loop(0, pair_count, one_pair, 0, unroll=True)

    for peer, message_ref in enumerate(message_refs):
        for rank in range(BCAP):
            message_ref[rank * cols : (rank + 1) * cols, :] = total_ref[
                peer * BCAP + rank
            ].astype(BF16)


def start_kernel(peers, me_ref, cells_hbm, counts_hbm, times_hbm, rays_hbm, *refs):
    message_refs = refs[:peers]
    target_ref, total_ref, table_ref, used_ref, cells_ref, counts_ref = refs[peers : peers + 6]
    times_ref, rays_ref, sems, ray_sems = refs[peers + 6 :]
    pair_count, slot_count = rays_ref.shape[:2]
    cols = times_ref.shape[0]
    owned = CELL_DEV // BS
    copies = [
        pltpu.make_async_copy(source, dest, sems.at[index])
        for index, (source, dest) in enumerate(
            [(cells_hbm, cells_ref), (counts_hbm, counts_ref), (times_hbm, times_ref)]
        )
    ]
    for copy in copies:
        copy.start()

    def ray_copy(pair):
        return pltpu.make_async_copy(rays_hbm.at[pair], rays_ref.at[pair], ray_sems.at[pair])

    def fetch(pair, carry):
        ray_copy(pair).start()
        return carry

    lax.fori_loop(0, pair_count, fetch, 0)

    def clear(peer, carry):
        used_ref[peer] = 0
        for rank in range(BCAP):
            table_ref[peer * BCAP + rank] = 0
        return carry

    lax.fori_loop(0, peers, clear, 0)
    for copy in copies:
        copy.wait()

    def find_places(pair):
        count = counts_ref[pair]
        for slot in range(slot_count):
            cell = cells_ref[pair, slot]
            apart = (cell // owned) ^ me_ref[0]
            owner = apart * 2 - jnp.where(apart < peers // 2, 0, peers - 1)
            local = cell % owned
            used = used_ref[owner]
            rank = used
            for other in range(BCAP - 1, -1, -1):
                same = (table_ref[owner * BCAP + other] == local) & (other < used)
                rank = jnp.where(same, other, rank)
            spot = owner * BCAP + rank
            table_ref[spot] = local
            used_ref[owner] = jnp.maximum(used, rank + 1)
            target_ref[pair * slot_count + slot] = jnp.where(slot < count, spot, peers * BCAP)

    def before(pair):
        find_places(pair)
        ray_copy(pair).wait()

    transposed(times_ref, rays_ref, before, target_ref, total_ref, message_refs)
    squares = jnp.zeros((cols, BS), F32)
    for pair in range(pair_count):
        part = times_ref[:, pair * BS : (pair + 1) * BS]
        squares += part * part
    tail = squares_tail(squares)
    place = lax.broadcasted_iota(jnp.int32, (TAIL, BS), 0)
    lane = lax.broadcasted_iota(jnp.int32, (TAIL, BS), 1)

    for peer, message_ref in enumerate(message_refs):
        rows = tail
        for rank in range(BCAP):
            asked = table_ref[peer * BCAP + rank].astype(F32)
            rows = jnp.where((place == 3) & (lane == rank), asked, rows)
        message_ref[BCAP * cols :, :] = rows.astype(BF16)


def pair_kernel(peers, target_ref, *refs):
    fetched_refs = refs[:peers]
    data_ref, beta_ref, rays_ref = refs[peers : peers + 3]
    message_refs = refs[peers + 3 : 2 * peers + 3]
    alpha_ref, raw_ref, total_ref, fetched_ref = refs[2 * peers + 3 :]
    pair_count, slot_count = rays_ref.shape[:2]
    cols = data_ref.shape[0]
    spots = peers * BCAP
    for peer in range(peers):
        fetched_ref[peer] = fetched_refs[peer][: BCAP * cols, :]
    alpha = norm_of_tails(fetched_refs, cols)
    alpha_ref[...] = alpha
    beta = beta_ref[...]
    model_scale = 1.0 / (alpha * beta)
    data_scale = alpha / beta

    def one_pair(pair, squares):
        chosen = []
        for slot in range(slot_count):
            spot = target_ref[pair * slot_count + slot]
            live = spot < spots
            spot = jnp.where(live, spot, 0)
            rows = pl.ds(pl.multiple_of((spot % BCAP) * cols, cols), cols)
            block = fetched_ref[spot // BCAP, rows, :]
            chosen.append(jnp.where(live, block, jnp.zeros_like(block)))
        rays = jnp.concatenate([rays_ref[pair, slot] for slot in range(slot_count)], axis=1)
        product = lax.dot_general(
            rays, jnp.concatenate(chosen, axis=1), (((1,), (1,)), ((), ())),
            preferred_element_type=F32,
        )
        raw = product.T * model_scale - data_ref[:, lanes(pair)] * data_scale
        raw_ref[:, lanes(pair)] = raw
        return squares + raw * raw

    squares = lax.fori_loop(0, pair_count, one_pair, jnp.zeros((cols, BS), F32), unroll=True)
    transposed(raw_ref, rays_ref, lambda pair: None, target_ref, total_ref, message_refs)
    tail = squares_tail(squares).astype(BF16)
    for message_ref in message_refs:
        message_ref[BCAP * cols :, :] = tail


def gathered(arrived_refs, asked_ref, model_ref):
    cols = model_ref.shape[0]
    for peer, arrived_ref in enumerate(arrived_refs):
        for rank in range(BCAP):
            where = lanes(asked_ref[peer, rank])
            model_ref[:, where] += arrived_ref[rank * cols : (rank + 1) * cols, :].astype(F32)


def reply(squares, scale, asked_ref, model_ref, out_refs):
    cols = model_ref.shape[0]
    tail = squares_tail(squares * scale * scale).astype(BF16)
    for peer, out_ref in enumerate(out_refs):
        out_ref[BCAP * cols :, :] = tail
        for rank in range(BCAP):
            block = model_ref[:, lanes(asked_ref[peer, rank])]
            out_ref[rank * cols : (rank + 1) * cols, :] = block.astype(BF16)


def squares_of(model_ref):
    cols, cells = model_ref.shape

    def one_block(block, squares):
        values = model_ref[:, lanes(block)]
        return squares + values * values

    return lax.fori_loop(0, cells // BS, one_block, jnp.zeros((cols, BS), F32), unroll=8)


def first_cell_kernel(peers, *refs):
    arrived_refs, out_refs = refs[:peers], refs[peers + 2 : 2 * peers + 2]
    model_ref, beta_ref = refs[peers : peers + 2]
    asked_ref, table_ref, sem = refs[2 * peers + 2 :]
    cols, cells = model_ref.shape
    for peer in range(peers):
        tail = arrived_refs[peer][BCAP * cols :, :].astype(F32)
        table_ref[peer : peer + 1, :] = tail[3:4].astype(jnp.int32)
    copy = pltpu.make_async_copy(table_ref, asked_ref, sem)
    copy.start()
    beta = norm_of_tails(arrived_refs, cols)
    beta_ref[...] = beta
    model_ref[...] = jnp.zeros((cols, cells), F32)
    copy.wait()
    gathered(arrived_refs, asked_ref, model_ref)
    reply(squares_of(model_ref), 1.0 / beta, asked_ref, model_ref, out_refs)


def start_from(before_ref, scale, model_ref):
    def one_block(block, carry):
        model_ref[:, lanes(block)] = before_ref[:, lanes(block)] * -scale
        return carry

    lax.fori_loop(0, model_ref.shape[1] // BS, one_block, 0, unroll=8)


def cell_kernel(peers, asked_ref, *refs):
    arrived_refs, out_refs = refs[:peers], refs[peers + 5 :]
    before_ref, alpha_ref, beta_before_ref, model_ref, beta_ref = refs[peers : peers + 5]
    beta = norm_of_tails(arrived_refs, model_ref.shape[0])
    beta_ref[...] = beta
    start_from(before_ref, beta * beta / (alpha_ref[...] * beta_before_ref[...]), model_ref)
    gathered(arrived_refs, asked_ref, model_ref)
    reply(squares_of(model_ref), 1.0 / beta, asked_ref, model_ref, out_refs)


def last_cell_kernel(peers, asked_ref, *refs):
    arrived_refs, refs = refs[:peers], refs[peers:]
    models = refs[:ITERS]
    alphas = [ref[...] for ref in refs[ITERS : 2 * ITERS]]
    betas = [ref[...] for ref in refs[2 * ITERS : 3 * ITERS]]
    model_ref, beta_ref, out_ref, estimate_hbm, estimate_ref, sems = refs[3 * ITERS :]
    cols, cells = model_ref.shape
    beta = norm_of_tails(arrived_refs, cols)
    beta_ref[...] = beta
    weights = estimate_weights(betas + [beta], alphas)
    scale = beta * beta / (alphas[-1] * betas[-1])
    blocks = cells // BS // CHUNKS

    def one_block(block, carry):
        where = lanes(block)
        values = models[-1][:, where]
        model_ref[:, where] = values * -scale
        total = values * weights[-1]
        for i in range(ITERS - 1):
            total += weights[i] * models[i][:, where]
        estimate_ref[:, where] = total
        return carry

    copies = []
    for chunk in range(CHUNKS):
        lax.fori_loop(chunk * blocks, (chunk + 1) * blocks, one_block, 0, unroll=4)
        where = slice(chunk * blocks * BS, (chunk + 1) * blocks * BS)
        copies.append(
            pltpu.make_async_copy(
                estimate_ref.at[:, where], estimate_hbm.at[:, where], sems.at[chunk]
            )
        )
        copies[-1].start()
    gathered(arrived_refs, asked_ref, model_ref)
    scale = 1.0 / beta
    tail = squares_tail(squares_of(model_ref) * scale * scale)
    out_ref[...] = jnp.broadcast_to(tail[None], out_ref.shape)
    for copy in copies:
        copy.wait()


def estimate_weights(betas, alphas):
    phi_bar = betas[0]
    rho_bar = alphas[0]
    trace = [1.0 / (alphas[0] * betas[0])]
    weight = [jnp.zeros_like(phi_bar)] * ITERS
    for step in range(ITERS):
        beta = betas[step + 1]
        rho = jnp.sqrt(rho_bar * rho_bar + beta * beta)
        cosine = rho_bar / rho
        sine = beta / rho
        gain = cosine * phi_bar / rho
        weight = [
            weight[i] + gain * trace[i] if i < len(trace) else weight[i] for i in range(ITERS)
        ]
        if step + 1 < ITERS:
            alpha = alphas[step + 1]
            theta = sine * alpha
            rho_bar = -cosine * alpha
            phi_bar = sine * phi_bar
            trace = [-(theta / rho) * value for value in trace] + [1.0 / (alpha * beta)]
    return weight


def model_kernel(tails_ref, beta_ref, model_ref, out_hbm, out_ref, sems):
    cols, cells = model_ref.shape
    blocks = cells // BS // CHUNKS
    summed = jnp.sum(tails_ref[...], axis=0)
    row = summed[0:1] + summed[1:2] + summed[2:3]
    column = jnp.sum(jnp.where(diagonal(cols), row, 0.0), axis=1, keepdims=True)
    alpha = jnp.broadcast_to(jnp.sqrt(column + EPS), (cols, BS))
    scale = 1.0 / (alpha * beta_ref[...])

    def one_block(block, carry):
        out_ref[:, lanes(block)] = model_ref[:, lanes(block)] * scale
        return carry

    copies = []
    for chunk in range(CHUNKS):
        lax.fori_loop(chunk * blocks, (chunk + 1) * blocks, one_block, 0, unroll=4)
        where = slice(chunk * blocks * BS, (chunk + 1) * blocks * BS)
        copies.append(
            pltpu.make_async_copy(out_ref.at[:, where], out_hbm.at[:, where], sems.at[chunk])
        )
        copies[-1].start()
    for copy in copies:
        copy.wait()


def call(kernel, name, in_spaces, outs, scratch=(), flops=0, moved=0, limit=16 << 20):
    return pl.pallas_call(
        kernel,
        name=name,
        in_specs=[pl.BlockSpec(memory_space=space) for space in in_spaces],
        out_specs=[pl.BlockSpec(memory_space=space) for _, _, space in outs],
        out_shape=[jax.ShapeDtypeStruct(shape, dtype) for shape, dtype, _ in outs],
        scratch_shapes=list(scratch),
        compiler_params=pltpu.CompilerParams(vmem_limit_bytes=limit),
        cost_estimate=pl.CostEstimate(flops=flops, bytes_accessed=moved, transcendentals=0),
    )


def on_device(ray_blocks, block_cells, block_counts, travel_times):
    pair_count, slot_count = ray_blocks.shape[:2]
    slots = pair_count * slot_count
    peers = lax.axis_size("pair")
    spots = peers * BCAP
    times = travel_times.T
    cols, pairs = times.shape
    messages = [((BCAP * cols + TAIL, BS), BF16, VMEM)] * peers
    ins = [VMEM] * peers
    gathered_blocks = VMEM((peers, BCAP * cols, BS), BF16)
    tile = ((cols, BS), F32, VMEM)
    data = ((cols, pairs), F32, VMEM)
    whole = ((cols, CELL_DEV), F32, VMEM)
    totals = VMEM((spots + 1, cols, BS), F32)
    flops = 2 * slots * BS * BS * cols

    def exchange(values):
        half = peers // 2
        steps = [i // 2 + i % 2 * half for i in range(peers)]
        return [values[0]] + [
            lax.ppermute(value, "pair", [(one, one ^ step) for one in range(peers)])
            for value, step in zip(values[1:], steps[1:])
        ]

    me = lax.axis_index("pair").astype(jnp.int32).reshape(1)
    *outgoing, target = call(
        functools.partial(start_kernel, peers), "start", [SMEM, HBM, HBM, HBM, HBM],
        messages + [((slots,), jnp.int32, SMEM)],
        [
            totals, SMEM((spots,), jnp.int32), SMEM((peers,), jnp.int32),
            SMEM(block_cells.shape, jnp.int32), SMEM(block_counts.shape, jnp.int32),
            VMEM(times.shape, F32), VMEM(ray_blocks.shape, BF16),
            pltpu.SemaphoreType.DMA((3,)), pltpu.SemaphoreType.DMA((pair_count,)),
        ],
        flops, 6 << 20, 60 << 20,
    )(me, block_cells, block_counts, times, ray_blocks)
    arrived = exchange(outgoing)
    model, beta, *replies, asked = call(
        functools.partial(first_cell_kernel, peers), "cells_first", ins,
        [whole, tile] + messages + [((peers, BS), jnp.int32, SMEM)],
        [VMEM((peers, BS), jnp.int32), pltpu.SemaphoreType.DMA],
        0, 6 << 20,
    )(*arrived)
    models, betas, alphas = [model], [beta], []
    current = times
    for step in range(ITERS):
        fetched = exchange(replies)
        last = step + 1 == ITERS
        made = call(
            functools.partial(pair_kernel, peers), "pairs_last" if last else "pairs",
            [SMEM] + ins + [VMEM, VMEM, VMEM], messages + [tile] + [data] * (not last),
            [VMEM(data[0], F32)] * last + [totals, gathered_blocks], 2 * flops, 8 << 20,
        )(target, *fetched, current, betas[-1], ray_blocks)
        alphas.append(made[peers])
        current = made[-1]
        arrived = exchange(made[:peers])
        if not last:
            model, beta, *replies = call(
                functools.partial(cell_kernel, peers), "cells", [SMEM] + ins + [VMEM] * 3,
                [whole, tile] + messages, (), 0, 8 << 20,
            )(asked, *arrived, models[-1], alphas[-1], betas[-1])
            models.append(model)
            betas.append(beta)
    scratch = [VMEM(whole[0], F32), pltpu.SemaphoreType.DMA((CHUNKS,))]
    model, beta, tails, estimate = call(
        functools.partial(last_cell_kernel, peers), "cells_last",
        [SMEM] + ins + [VMEM] * (3 * ITERS),
        [whole, tile, ((peers, TAIL, BS), F32, VMEM), (whole[0], F32, HBM)], scratch, 0, 10 << 20,
    )(asked, *arrived, *models, *alphas, *betas)
    tails = lax.all_to_all(tails, "pair", split_axis=0, concat_axis=0, tiled=True)
    (model_vec,) = call(
        model_kernel, "model", [VMEM, VMEM, VMEM], [(whole[0], F32, HBM)], scratch, 0, 4 << 20
    )(tails, beta, model)
    return (estimate.T, model_vec.T)


def solution(mesh):
    return jax.shard_map(
        on_device,
        mesh=mesh,
        in_specs=(
            P(("groups", "pair"), None, None, None),
            P(("groups", "pair"), None),
            P(("groups", "pair")),
            P(("groups", "pair"), None),
        ),
        out_specs=(P(("groups", "pair"), None), P(("groups", "pair"), None)),
        check_vma=False,
    )
```

```python
import functools

import jax
import jax.numpy as jnp
from jax import lax
from jax.experimental import pallas as pl
from jax.experimental.pallas import tpu as pltpu
from jax.sharding import PartitionSpec as P

CELL_DEV = 8192
BCAP = 4
BS = 128
TAIL = 8
ITERS = 2
EPS = 1e-12
F32 = jnp.float32
BF16 = jnp.bfloat16
VMEM = pltpu.VMEM
SMEM = pltpu.SMEM
HBM = pltpu.HBM
CHUNKS = 8


def diagonal(cols):
    shape = (cols, BS)
    return lax.broadcasted_iota(jnp.int32, shape, 0) == lax.broadcasted_iota(jnp.int32, shape, 1)


def squares_tail(squares):
    cols = squares.shape[0]
    total = jnp.sum(squares, axis=1, keepdims=True)
    row = jnp.sum(jnp.where(diagonal(cols), total, 0.0), axis=0, keepdims=True)
    high = row.astype(BF16).astype(F32)
    middle = (row - high).astype(BF16).astype(F32)
    low = row - high - middle
    place = lax.broadcasted_iota(jnp.int32, (TAIL, BS), 0)
    return jnp.where(
        place == 0, high, jnp.where(place == 1, middle, jnp.where(place == 2, low, 0.0))
    )


def norm_of_tails(message_refs, cols):
    summed = sum(message_ref[BCAP * cols :, :].astype(F32) for message_ref in message_refs)
    row = summed[0:1] + summed[1:2] + summed[2:3]
    column = jnp.sum(jnp.where(diagonal(cols), row, 0.0), axis=1, keepdims=True)
    return jnp.broadcast_to(jnp.sqrt(column + EPS), (cols, BS))


def lanes(block):
    return pl.ds(pl.multiple_of(block * BS, BS), BS)


def transposed(data_ref, rays_ref, before, target_ref, total_ref, message_refs):
    pair_count, slot_count = rays_ref.shape[:2]
    cols = data_ref.shape[0]
    spots = len(message_refs) * BCAP

    def clear(index, carry):
        total_ref[index] = jnp.zeros((cols, BS), F32)
        return carry

    lax.fori_loop(0, spots, clear, 0, unroll=8)

    def one_pair(pair, carry):
        before(pair)
        data = data_ref[:, lanes(pair)]
        high = data.astype(BF16)
        low = (data - high.astype(F32)).astype(BF16)
        pieces = jnp.concatenate([high, low], axis=0)
        for slot in range(0, slot_count, 2):
            rays = jnp.concatenate([rays_ref[pair, slot], rays_ref[pair, slot + 1]], axis=1)
            part = jnp.dot(pieces, rays, preferred_element_type=F32)
            part = part[:cols] + part[cols:]
            for half in range(2):
                spot = target_ref[pair * slot_count + slot + half]
                total_ref[spot] += part[:, half * BS : (half + 1) * BS]
        return carry

    lax.fori_loop(0, pair_count, one_pair, 0, unroll=True)

    for peer, message_ref in enumerate(message_refs):
        for rank in range(BCAP):
            message_ref[rank * cols : (rank + 1) * cols, :] = total_ref[
                peer * BCAP + rank
            ].astype(BF16)


def start_kernel(peers, me_ref, cells_hbm, counts_hbm, times_hbm, rays_hbm, *refs):
    message_refs = refs[:peers]
    target_ref, total_ref, table_ref, used_ref, cells_ref, counts_ref = refs[peers : peers + 6]
    times_ref, rays_ref, sems, ray_sems = refs[peers + 6 :]
    pair_count, slot_count = rays_ref.shape[:2]
    cols = times_ref.shape[0]
    owned = CELL_DEV // BS
    copies = [
        pltpu.make_async_copy(source, dest, sems.at[index])
        for index, (source, dest) in enumerate(
            [(cells_hbm, cells_ref), (counts_hbm, counts_ref), (times_hbm, times_ref)]
        )
    ]
    for copy in copies:
        copy.start()

    def ray_copy(pair):
        return pltpu.make_async_copy(rays_hbm.at[pair], rays_ref.at[pair], ray_sems.at[pair])

    def fetch(pair, carry):
        ray_copy(pair).start()
        return carry

    lax.fori_loop(0, pair_count, fetch, 0)

    def clear(peer, carry):
        used_ref[peer] = 0
        for rank in range(BCAP):
            table_ref[peer * BCAP + rank] = 0
        return carry

    lax.fori_loop(0, peers, clear, 0)
    for copy in copies:
        copy.wait()

    def find_places(pair):
        count = counts_ref[pair]
        for slot in range(slot_count):
            cell = cells_ref[pair, slot]
            apart = (cell // owned) ^ me_ref[0]
            owner = apart * 2 - jnp.where(apart < peers // 2, 0, peers - 1)
            local = cell % owned
            used = used_ref[owner]
            rank = used
            for other in range(BCAP - 1, -1, -1):
                same = (table_ref[owner * BCAP + other] == local) & (other < used)
                rank = jnp.where(same, other, rank)
            spot = owner * BCAP + rank
            table_ref[spot] = local
            used_ref[owner] = jnp.maximum(used, rank + 1)
            target_ref[pair * slot_count + slot] = jnp.where(slot < count, spot, peers * BCAP)

    def before(pair):
        find_places(pair)
        ray_copy(pair).wait()

    transposed(times_ref, rays_ref, before, target_ref, total_ref, message_refs)
    squares = jnp.zeros((cols, BS), F32)
    for pair in range(pair_count):
        part = times_ref[:, pair * BS : (pair + 1) * BS]
        squares += part * part
    tail = squares_tail(squares)
    place = lax.broadcasted_iota(jnp.int32, (TAIL, BS), 0)
    lane = lax.broadcasted_iota(jnp.int32, (TAIL, BS), 1)

    for peer, message_ref in enumerate(message_refs):
        rows = tail
        for rank in range(BCAP):
            asked = table_ref[peer * BCAP + rank].astype(F32)
            rows = jnp.where((place == 3) & (lane == rank), asked, rows)
        message_ref[BCAP * cols :, :] = rows.astype(BF16)


def keep_kernel(after_ref, target_hbm, rays_hbm, target_ref, rays_ref, sems):
    del after_ref
    copies = [
        pltpu.make_async_copy(target_hbm, target_ref, sems.at[0]),
        pltpu.make_async_copy(rays_hbm, rays_ref, sems.at[1]),
    ]
    for copy in copies:
        copy.start()
    for copy in copies:
        copy.wait()


def pair_kernel(peers, target_ref, *refs):
    fetched_refs = refs[:peers]
    data_ref, beta_ref, rays_ref = refs[peers : peers + 3]
    message_refs = refs[peers + 3 : 2 * peers + 3]
    alpha_ref, raw_ref, total_ref, fetched_ref = refs[2 * peers + 3 :]
    pair_count, slot_count = rays_ref.shape[:2]
    cols = data_ref.shape[0]
    spots = peers * BCAP
    for peer in range(peers):
        fetched_ref[peer] = fetched_refs[peer][: BCAP * cols, :]
    alpha = norm_of_tails(fetched_refs, cols)
    alpha_ref[...] = alpha
    beta = beta_ref[...]
    model_scale = 1.0 / (alpha * beta)
    data_scale = alpha / beta

    def one_pair(pair, squares):
        chosen = []
        for slot in range(slot_count):
            spot = target_ref[pair * slot_count + slot]
            live = spot < spots
            spot = jnp.where(live, spot, 0)
            rows = pl.ds(pl.multiple_of((spot % BCAP) * cols, cols), cols)
            block = fetched_ref[spot // BCAP, rows, :]
            chosen.append(jnp.where(live, block, jnp.zeros_like(block)))
        rays = jnp.concatenate([rays_ref[pair, slot] for slot in range(slot_count)], axis=1)
        product = lax.dot_general(
            rays, jnp.concatenate(chosen, axis=1), (((1,), (1,)), ((), ())),
            preferred_element_type=F32,
        )
        raw = product.T * model_scale - data_ref[:, lanes(pair)] * data_scale
        raw_ref[:, lanes(pair)] = raw
        return squares + raw * raw

    squares = lax.fori_loop(0, pair_count, one_pair, jnp.zeros((cols, BS), F32), unroll=True)
    transposed(raw_ref, rays_ref, lambda pair: None, target_ref, total_ref, message_refs)
    tail = squares_tail(squares).astype(BF16)
    for message_ref in message_refs:
        message_ref[BCAP * cols :, :] = tail


def gathered(arrived_refs, asked_ref, model_ref):
    cols = model_ref.shape[0]
    for peer, arrived_ref in enumerate(arrived_refs):
        for rank in range(BCAP):
            where = lanes(asked_ref[peer, rank])
            model_ref[:, where] += arrived_ref[rank * cols : (rank + 1) * cols, :].astype(F32)


def reply(squares, scale, asked_ref, model_ref, out_refs):
    cols = model_ref.shape[0]
    tail = squares_tail(squares * scale * scale).astype(BF16)
    for peer, out_ref in enumerate(out_refs):
        out_ref[BCAP * cols :, :] = tail
        for rank in range(BCAP):
            block = model_ref[:, lanes(asked_ref[peer, rank])]
            out_ref[rank * cols : (rank + 1) * cols, :] = block.astype(BF16)


def squares_of(model_ref):
    cols, cells = model_ref.shape

    def one_block(block, squares):
        values = model_ref[:, lanes(block)]
        return squares + values * values

    return lax.fori_loop(0, cells // BS, one_block, jnp.zeros((cols, BS), F32), unroll=8)


def first_cell_kernel(peers, *refs):
    arrived_refs, out_refs = refs[:peers], refs[peers + 2 : 2 * peers + 2]
    model_ref, beta_ref = refs[peers : peers + 2]
    asked_ref, table_ref, sem = refs[2 * peers + 2 :]
    cols, cells = model_ref.shape
    for peer in range(peers):
        tail = arrived_refs[peer][BCAP * cols :, :].astype(F32)
        table_ref[peer : peer + 1, :] = tail[3:4].astype(jnp.int32)
    copy = pltpu.make_async_copy(table_ref, asked_ref, sem)
    copy.start()
    beta = norm_of_tails(arrived_refs, cols)
    beta_ref[...] = beta
    model_ref[...] = jnp.zeros((cols, cells), F32)
    copy.wait()
    gathered(arrived_refs, asked_ref, model_ref)
    reply(squares_of(model_ref), 1.0 / beta, asked_ref, model_ref, out_refs)


def start_from(before_ref, scale, model_ref):
    def one_block(block, carry):
        model_ref[:, lanes(block)] = before_ref[:, lanes(block)] * -scale
        return carry

    lax.fori_loop(0, model_ref.shape[1] // BS, one_block, 0, unroll=8)


def cell_kernel(peers, asked_ref, *refs):
    arrived_refs, out_refs = refs[:peers], refs[peers + 5 :]
    before_ref, alpha_ref, beta_before_ref, model_ref, beta_ref = refs[peers : peers + 5]
    beta = norm_of_tails(arrived_refs, model_ref.shape[0])
    beta_ref[...] = beta
    start_from(before_ref, beta * beta / (alpha_ref[...] * beta_before_ref[...]), model_ref)
    gathered(arrived_refs, asked_ref, model_ref)
    reply(squares_of(model_ref), 1.0 / beta, asked_ref, model_ref, out_refs)


def last_cell_kernel(peers, asked_ref, *refs):
    arrived_refs, refs = refs[:peers], refs[peers:]
    models = refs[:ITERS]
    alphas = [ref[...] for ref in refs[ITERS : 2 * ITERS]]
    betas = [ref[...] for ref in refs[2 * ITERS : 3 * ITERS]]
    model_ref, beta_ref, out_ref, estimate_hbm, estimate_ref, sems = refs[3 * ITERS :]
    cols, cells = model_ref.shape
    beta = norm_of_tails(arrived_refs, cols)
    beta_ref[...] = beta
    weights = estimate_weights(betas + [beta], alphas)
    scale = beta * beta / (alphas[-1] * betas[-1])
    blocks = cells // BS // CHUNKS

    def one_block(block, carry):
        where = lanes(block)
        values = models[-1][:, where]
        model_ref[:, where] = values * -scale
        total = values * weights[-1]
        for i in range(ITERS - 1):
            total += weights[i] * models[i][:, where]
        estimate_ref[:, where] = total
        return carry

    copies = []
    for chunk in range(CHUNKS):
        lax.fori_loop(chunk * blocks, (chunk + 1) * blocks, one_block, 0, unroll=4)
        where = slice(chunk * blocks * BS, (chunk + 1) * blocks * BS)
        copies.append(
            pltpu.make_async_copy(
                estimate_ref.at[:, where], estimate_hbm.at[:, where], sems.at[chunk]
            )
        )
        copies[-1].start()
    gathered(arrived_refs, asked_ref, model_ref)
    scale = 1.0 / beta
    tail = squares_tail(squares_of(model_ref) * scale * scale)
    out_ref[...] = jnp.broadcast_to(tail[None], out_ref.shape)
    for copy in copies:
        copy.wait()


def estimate_weights(betas, alphas):
    phi_bar = betas[0]
    rho_bar = alphas[0]
    trace = [1.0 / (alphas[0] * betas[0])]
    weight = [jnp.zeros_like(phi_bar)] * ITERS
    for step in range(ITERS):
        beta = betas[step + 1]
        rho = jnp.sqrt(rho_bar * rho_bar + beta * beta)
        cosine = rho_bar / rho
        sine = beta / rho
        gain = cosine * phi_bar / rho
        weight = [
            weight[i] + gain * trace[i] if i < len(trace) else weight[i] for i in range(ITERS)
        ]
        if step + 1 < ITERS:
            alpha = alphas[step + 1]
            theta = sine * alpha
            rho_bar = -cosine * alpha
            phi_bar = sine * phi_bar
            trace = [-(theta / rho) * value for value in trace] + [1.0 / (alpha * beta)]
    return weight


def model_kernel(tails_ref, beta_ref, model_ref, out_hbm, out_ref, sems):
    cols, cells = model_ref.shape
    blocks = cells // BS // CHUNKS
    summed = jnp.sum(tails_ref[...], axis=0)
    row = summed[0:1] + summed[1:2] + summed[2:3]
    column = jnp.sum(jnp.where(diagonal(cols), row, 0.0), axis=1, keepdims=True)
    alpha = jnp.broadcast_to(jnp.sqrt(column + EPS), (cols, BS))
    scale = 1.0 / (alpha * beta_ref[...])

    def one_block(block, carry):
        out_ref[:, lanes(block)] = model_ref[:, lanes(block)] * scale
        return carry

    copies = []
    for chunk in range(CHUNKS):
        lax.fori_loop(chunk * blocks, (chunk + 1) * blocks, one_block, 0, unroll=4)
        where = slice(chunk * blocks * BS, (chunk + 1) * blocks * BS)
        copies.append(
            pltpu.make_async_copy(out_ref.at[:, where], out_hbm.at[:, where], sems.at[chunk])
        )
        copies[-1].start()
    for copy in copies:
        copy.wait()


def call(kernel, name, in_spaces, outs, scratch=(), flops=0, moved=0, limit=16 << 20):
    return pl.pallas_call(
        kernel,
        name=name,
        in_specs=[pl.BlockSpec(memory_space=space) for space in in_spaces],
        out_specs=[pl.BlockSpec(memory_space=space) for _, _, space in outs],
        out_shape=[jax.ShapeDtypeStruct(shape, dtype) for shape, dtype, _ in outs],
        scratch_shapes=list(scratch),
        compiler_params=pltpu.CompilerParams(vmem_limit_bytes=limit),
        cost_estimate=pl.CostEstimate(flops=flops, bytes_accessed=moved, transcendentals=0),
    )


def on_device(ray_blocks, block_cells, block_counts, travel_times):
    pair_count, slot_count = ray_blocks.shape[:2]
    slots = pair_count * slot_count
    peers = lax.axis_size("pair")
    spots = peers * BCAP
    times = travel_times.T
    cols, pairs = times.shape
    messages = [((BCAP * cols + TAIL, BS), BF16, VMEM)] * peers
    ins = [VMEM] * peers
    gathered_blocks = VMEM((peers, BCAP * cols, BS), BF16)
    tile = ((cols, BS), F32, VMEM)
    data = ((cols, pairs), F32, VMEM)
    whole = ((cols, CELL_DEV), F32, VMEM)
    totals = VMEM((spots + 1, cols, BS), F32)
    flops = 2 * slots * BS * BS * cols

    def exchange(values):
        half = peers // 2
        steps = [i // 2 + i % 2 * half for i in range(peers)]
        return [values[0]] + [
            lax.ppermute(value, "pair", [(one, one ^ step) for one in range(peers)])
            for value, step in zip(values[1:], steps[1:])
        ]

    me = lax.axis_index("pair").astype(jnp.int32).reshape(1)
    *outgoing, target = call(
        functools.partial(start_kernel, peers), "start", [SMEM, HBM, HBM, HBM, HBM],
        messages + [((slots,), jnp.int32, SMEM)],
        [
            totals, SMEM((spots,), jnp.int32), SMEM((peers,), jnp.int32),
            SMEM(block_cells.shape, jnp.int32), SMEM(block_counts.shape, jnp.int32),
            VMEM(times.shape, F32), VMEM(ray_blocks.shape, BF16),
            pltpu.SemaphoreType.DMA((3,)), pltpu.SemaphoreType.DMA((pair_count,)),
        ],
        flops, 6 << 20, 60 << 20,
    )(me, block_cells, block_counts, times, ray_blocks)
    arrived = exchange(outgoing)
    model, beta, *replies, asked = call(
        functools.partial(first_cell_kernel, peers), "cells_first", ins,
        [whole, tile] + messages + [((peers, BS), jnp.int32, SMEM)],
        [VMEM((peers, BS), jnp.int32), pltpu.SemaphoreType.DMA],
        0, 6 << 20,
    )(*arrived)
    models, betas, alphas = [model], [beta], []
    current = times
    for step in range(ITERS):
        fetched = exchange(replies)
        if step == 0:
            target, ray_blocks = call(
                keep_kernel, "keep", [VMEM, HBM, HBM],
                [((slots,), jnp.int32, SMEM), (ray_blocks.shape, BF16, VMEM)],
                [pltpu.SemaphoreType.DMA((2,))], 0, 8 << 20, 48 << 20,
            )(beta, target, ray_blocks)
        last = step + 1 == ITERS
        made = call(
            functools.partial(pair_kernel, peers), "pairs_last" if last else "pairs",
            [SMEM] + ins + [VMEM, VMEM, VMEM], messages + [tile] + [data] * (not last),
            [VMEM(data[0], F32)] * last + [totals, gathered_blocks], 2 * flops, 8 << 20,
        )(target, *fetched, current, betas[-1], ray_blocks)
        alphas.append(made[peers])
        current = made[-1]
        arrived = exchange(made[:peers])
        if not last:
            model, beta, *replies = call(
                functools.partial(cell_kernel, peers), "cells", [SMEM] + ins + [VMEM] * 3,
                [whole, tile] + messages, (), 0, 8 << 20,
            )(asked, *arrived, models[-1], alphas[-1], betas[-1])
            models.append(model)
            betas.append(beta)
    scratch = [VMEM(whole[0], F32), pltpu.SemaphoreType.DMA((CHUNKS,))]
    model, beta, tails, estimate = call(
        functools.partial(last_cell_kernel, peers), "cells_last",
        [SMEM] + ins + [VMEM] * (3 * ITERS),
        [whole, tile, ((peers, TAIL, BS), F32, VMEM), (whole[0], F32, HBM)], scratch, 0, 10 << 20,
    )(asked, *arrived, *models, *alphas, *betas)
    tails = lax.all_to_all(tails, "pair", split_axis=0, concat_axis=0, tiled=True)
    (model_vec,) = call(
        model_kernel, "model", [VMEM, VMEM, VMEM], [(whole[0], F32, HBM)], scratch, 0, 4 << 20
    )(tails, beta, model)
    return (estimate.T, model_vec.T)


def solution(mesh):
    return jax.shard_map(
        on_device,
        mesh=mesh,
        in_specs=(
            P(("groups", "pair"), None, None, None),
            P(("groups", "pair"), None),
            P(("groups", "pair")),
            P(("groups", "pair"), None),
        ),
        out_specs=(P(("groups", "pair"), None), P(("groups", "pair"), None)),
        check_vma=False,
    )
```

```python
import functools

import jax
import jax.numpy as jnp
from jax import lax
from jax.experimental import pallas as pl
from jax.experimental.pallas import tpu as pltpu
from jax.sharding import PartitionSpec as P

CELL_DEV = 8192
BCAP = 4
BS = 128
TAIL = 8
ITERS = 2
EPS = 1e-12
F32 = jnp.float32
BF16 = jnp.bfloat16
VMEM = pltpu.VMEM
SMEM = pltpu.SMEM
HBM = pltpu.HBM
CHUNKS = 8


def diagonal(cols):
    shape = (cols, BS)
    return lax.broadcasted_iota(jnp.int32, shape, 0) == lax.broadcasted_iota(jnp.int32, shape, 1)


def squares_tail(squares):
    cols = squares.shape[0]
    total = jnp.sum(squares, axis=1, keepdims=True)
    row = jnp.sum(jnp.where(diagonal(cols), total, 0.0), axis=0, keepdims=True)
    high = row.astype(BF16).astype(F32)
    middle = (row - high).astype(BF16).astype(F32)
    low = row - high - middle
    place = lax.broadcasted_iota(jnp.int32, (TAIL, BS), 0)
    return jnp.where(
        place == 0, high, jnp.where(place == 1, middle, jnp.where(place == 2, low, 0.0))
    )


def norm_of_tails(message_refs, cols):
    summed = sum(message_ref[BCAP * cols :, :].astype(F32) for message_ref in message_refs)
    row = summed[0:1] + summed[1:2] + summed[2:3]
    column = jnp.sum(jnp.where(diagonal(cols), row, 0.0), axis=1, keepdims=True)
    return jnp.broadcast_to(jnp.sqrt(column + EPS), (cols, BS))


def lanes(block):
    return pl.ds(pl.multiple_of(block * BS, BS), BS)


def transposed(data_ref, rays_ref, before, target_ref, total_ref, message_refs):
    pair_count, slot_count = rays_ref.shape[:2]
    cols = data_ref.shape[0]
    spots = len(message_refs) * BCAP

    def clear(index, carry):
        total_ref[index] = jnp.zeros((cols, BS), F32)
        return carry

    lax.fori_loop(0, spots, clear, 0, unroll=8)

    def one_pair(pair, carry):
        before(pair)
        data = data_ref[:, lanes(pair)]
        high = data.astype(BF16)
        low = (data - high.astype(F32)).astype(BF16)
        pieces = jnp.concatenate([high, low], axis=0)
        for slot in range(0, slot_count, 2):
            rays = jnp.concatenate([rays_ref[pair, slot], rays_ref[pair, slot + 1]], axis=1)
            part = jnp.dot(pieces, rays, preferred_element_type=F32)
            part = part[:cols] + part[cols:]
            for half in range(2):
                spot = target_ref[pair * slot_count + slot + half]
                total_ref[spot] += part[:, half * BS : (half + 1) * BS]
        return carry

    lax.fori_loop(0, pair_count, one_pair, 0, unroll=True)

    for peer, message_ref in enumerate(message_refs):
        for rank in range(BCAP):
            message_ref[rank * cols : (rank + 1) * cols, :] = total_ref[
                peer * BCAP + rank
            ].astype(BF16)


def start_kernel(peers, me_ref, cells_hbm, counts_hbm, times_hbm, rays_hbm, *refs):
    message_refs = refs[:peers]
    target_ref, total_ref, table_ref, used_ref, cells_ref, counts_ref = refs[peers : peers + 6]
    times_ref, rays_ref, sems, ray_sems = refs[peers + 6 :]
    pair_count, slot_count = rays_ref.shape[:2]
    cols = times_ref.shape[0]
    owned = CELL_DEV // BS
    copies = [
        pltpu.make_async_copy(source, dest, sems.at[index])
        for index, (source, dest) in enumerate(
            [(cells_hbm, cells_ref), (counts_hbm, counts_ref), (times_hbm, times_ref)]
        )
    ]
    for copy in copies:
        copy.start()

    def ray_copy(pair):
        return pltpu.make_async_copy(rays_hbm.at[pair], rays_ref.at[pair], ray_sems.at[pair])

    def fetch(pair, carry):
        ray_copy(pair).start()
        return carry

    lax.fori_loop(0, pair_count, fetch, 0)

    def clear(peer, carry):
        used_ref[peer] = 0
        for rank in range(BCAP):
            table_ref[peer * BCAP + rank] = 0
        return carry

    lax.fori_loop(0, peers, clear, 0)
    for copy in copies:
        copy.wait()

    def find_places(pair):
        count = counts_ref[pair]
        for slot in range(slot_count):
            cell = cells_ref[pair, slot]
            apart = (cell // owned) ^ me_ref[0]
            owner = apart * 2 - jnp.where(apart < peers // 2, 0, peers - 1)
            local = cell % owned
            used = used_ref[owner]
            rank = used
            for other in range(BCAP - 1, -1, -1):
                same = (table_ref[owner * BCAP + other] == local) & (other < used)
                rank = jnp.where(same, other, rank)
            spot = owner * BCAP + rank
            table_ref[spot] = local
            used_ref[owner] = jnp.maximum(used, rank + 1)
            target_ref[pair * slot_count + slot] = jnp.where(slot < count, spot, peers * BCAP)

    def before(pair):
        find_places(pair)
        ray_copy(pair).wait()

    transposed(times_ref, rays_ref, before, target_ref, total_ref, message_refs)
    squares = jnp.zeros((cols, BS), F32)
    for pair in range(pair_count):
        part = times_ref[:, pair * BS : (pair + 1) * BS]
        squares += part * part
    tail = squares_tail(squares)
    place = lax.broadcasted_iota(jnp.int32, (TAIL, BS), 0)
    lane = lax.broadcasted_iota(jnp.int32, (TAIL, BS), 1)

    for peer, message_ref in enumerate(message_refs):
        rows = tail
        for rank in range(BCAP):
            asked = table_ref[peer * BCAP + rank].astype(F32)
            rows = jnp.where((place == 3) & (lane == rank), asked, rows)
        message_ref[BCAP * cols :, :] = rows.astype(BF16)


def keep_kernel(target_hbm, own_hbm, rays_hbm, target_ref, own_ref, rays_ref, sems):
    copies = [
        pltpu.make_async_copy(source, dest, sems.at[index])
        for index, (source, dest) in enumerate(
            [(target_hbm, target_ref), (own_hbm, own_ref), (rays_hbm, rays_ref)]
        )
    ]
    for copy in copies:
        copy.start()
    for copy in copies:
        copy.wait()


def pair_kernel(peers, target_ref, *refs):
    fetched_refs = refs[:peers]
    data_ref, beta_ref, rays_ref = refs[peers : peers + 3]
    message_refs = refs[peers + 3 : 2 * peers + 3]
    alpha_ref, raw_ref, total_ref, fetched_ref = refs[2 * peers + 3 :]
    pair_count, slot_count = rays_ref.shape[:2]
    cols = data_ref.shape[0]
    spots = peers * BCAP
    for peer in range(peers):
        fetched_ref[peer] = fetched_refs[peer][: BCAP * cols, :]
    alpha = norm_of_tails(fetched_refs, cols)
    alpha_ref[...] = alpha
    beta = beta_ref[...]
    model_scale = 1.0 / (alpha * beta)
    data_scale = alpha / beta

    def one_pair(pair, squares):
        chosen = []
        for slot in range(slot_count):
            spot = target_ref[pair * slot_count + slot]
            live = spot < spots
            spot = jnp.where(live, spot, 0)
            rows = pl.ds(pl.multiple_of((spot % BCAP) * cols, cols), cols)
            block = fetched_ref[spot // BCAP, rows, :]
            chosen.append(jnp.where(live, block, jnp.zeros_like(block)))
        rays = jnp.concatenate([rays_ref[pair, slot] for slot in range(slot_count)], axis=1)
        product = lax.dot_general(
            rays, jnp.concatenate(chosen, axis=1), (((1,), (1,)), ((), ())),
            preferred_element_type=F32,
        )
        raw = product.T * model_scale - data_ref[:, lanes(pair)] * data_scale
        raw_ref[:, lanes(pair)] = raw
        return squares + raw * raw

    squares = lax.fori_loop(0, pair_count, one_pair, jnp.zeros((cols, BS), F32), unroll=True)
    transposed(raw_ref, rays_ref, lambda pair: None, target_ref, total_ref, message_refs)
    tail = squares_tail(squares).astype(BF16)
    for message_ref in message_refs:
        message_ref[BCAP * cols :, :] = tail


def gathered(arrived_refs, asked_ref, model_ref):
    cols = model_ref.shape[0]
    for peer, arrived_ref in enumerate(arrived_refs):
        for rank in range(BCAP):
            where = lanes(asked_ref[peer, rank])
            model_ref[:, where] += arrived_ref[rank * cols : (rank + 1) * cols, :].astype(F32)


def reply(squares, scale, asked_ref, model_ref, out_refs):
    cols = model_ref.shape[0]
    tail = squares_tail(squares * scale * scale).astype(BF16)
    for peer, out_ref in enumerate(out_refs):
        out_ref[BCAP * cols :, :] = tail
        for rank in range(BCAP):
            block = model_ref[:, lanes(asked_ref[peer, rank])]
            out_ref[rank * cols : (rank + 1) * cols, :] = block.astype(BF16)


def squares_of(model_ref):
    cols, cells = model_ref.shape

    def one_block(block, squares):
        values = model_ref[:, lanes(block)]
        return squares + values * values

    return lax.fori_loop(0, cells // BS, one_block, jnp.zeros((cols, BS), F32), unroll=8)


def first_cell_kernel(peers, *refs):
    arrived_refs, out_refs = refs[:peers], refs[peers + 2 : 2 * peers + 2]
    model_ref, beta_ref = refs[peers : peers + 2]
    asked_ref, table_ref, sem = refs[2 * peers + 2 :]
    cols, cells = model_ref.shape
    for peer in range(peers):
        tail = arrived_refs[peer][BCAP * cols :, :].astype(F32)
        table_ref[peer : peer + 1, :] = tail[3:4].astype(jnp.int32)
    copy = pltpu.make_async_copy(table_ref, asked_ref, sem)
    copy.start()
    beta = norm_of_tails(arrived_refs, cols)
    beta_ref[...] = beta
    model_ref[...] = jnp.zeros((cols, cells), F32)
    copy.wait()
    gathered(arrived_refs, asked_ref, model_ref)
    reply(squares_of(model_ref), 1.0 / beta, asked_ref, model_ref, out_refs)


def start_from(before_ref, scale, model_ref):
    def one_block(block, carry):
        model_ref[:, lanes(block)] = before_ref[:, lanes(block)] * -scale
        return carry

    lax.fori_loop(0, model_ref.shape[1] // BS, one_block, 0, unroll=8)


def cell_kernel(peers, asked_ref, *refs):
    arrived_refs, out_refs = refs[:peers], refs[peers + 5 :]
    before_ref, alpha_ref, beta_before_ref, model_ref, beta_ref = refs[peers : peers + 5]
    beta = norm_of_tails(arrived_refs, model_ref.shape[0])
    beta_ref[...] = beta
    start_from(before_ref, beta * beta / (alpha_ref[...] * beta_before_ref[...]), model_ref)
    gathered(arrived_refs, asked_ref, model_ref)
    reply(squares_of(model_ref), 1.0 / beta, asked_ref, model_ref, out_refs)


def last_cell_kernel(peers, asked_ref, *refs):
    arrived_refs = refs[:peers]
    before_ref, alpha_ref, beta_before_ref, model_ref, beta_ref, out_ref = refs[peers:]
    beta = norm_of_tails(arrived_refs, model_ref.shape[0])
    beta_ref[...] = beta
    start_from(before_ref, beta * beta / (alpha_ref[...] * beta_before_ref[...]), model_ref)
    gathered(arrived_refs, asked_ref, model_ref)
    squares = squares_of(model_ref) / (beta * beta)
    total = jnp.sum(squares, axis=1, keepdims=True)
    row = jnp.sum(jnp.where(diagonal(total.shape[0]), total, 0.0), axis=0, keepdims=True)
    out_ref[...] = jnp.broadcast_to(row, out_ref.shape)


def estimate_kernel(*refs):
    models = refs[:ITERS]
    alphas = [ref[...] for ref in refs[ITERS : 2 * ITERS]]
    betas = [ref[...] for ref in refs[2 * ITERS : 3 * ITERS + 1]]
    estimate_hbm, estimate_ref, sems = refs[3 * ITERS + 1 :]
    cells = estimate_ref.shape[1]
    weights = estimate_weights(betas, alphas)
    blocks = cells // BS // CHUNKS

    def one_block(block, carry):
        where = lanes(block)
        total = weights[0] * models[0][:, where]
        for i in range(1, ITERS):
            total += weights[i] * models[i][:, where]
        estimate_ref[:, where] = total
        return carry

    copies = []
    for chunk in range(CHUNKS):
        lax.fori_loop(chunk * blocks, (chunk + 1) * blocks, one_block, 0, unroll=4)
        where = slice(chunk * blocks * BS, (chunk + 1) * blocks * BS)
        copies.append(
            pltpu.make_async_copy(
                estimate_ref.at[:, where], estimate_hbm.at[:, where], sems.at[chunk]
            )
        )
        copies[-1].start()
    for copy in copies:
        copy.wait()


def estimate_weights(betas, alphas):
    phi_bar = betas[0]
    rho_bar = alphas[0]
    trace = [1.0 / (alphas[0] * betas[0])]
    weight = [jnp.zeros_like(phi_bar)] * ITERS
    for step in range(ITERS):
        beta = betas[step + 1]
        rho = jnp.sqrt(rho_bar * rho_bar + beta * beta)
        cosine = rho_bar / rho
        sine = beta / rho
        gain = cosine * phi_bar / rho
        weight = [
            weight[i] + gain * trace[i] if i < len(trace) else weight[i] for i in range(ITERS)
        ]
        if step + 1 < ITERS:
            alpha = alphas[step + 1]
            theta = sine * alpha
            rho_bar = -cosine * alpha
            phi_bar = sine * phi_bar
            trace = [-(theta / rho) * value for value in trace] + [1.0 / (alpha * beta)]
    return weight


def model_kernel(*refs):
    *share_refs, beta_ref, model_ref, out_hbm, out_ref, sems = refs
    cols, cells = model_ref.shape
    blocks = cells // BS // CHUNKS
    row = sum(ref[...] for ref in share_refs)[0:1]
    column = jnp.sum(jnp.where(diagonal(cols), row, 0.0), axis=1, keepdims=True)
    alpha = jnp.broadcast_to(jnp.sqrt(column + EPS), (cols, BS))
    scale = 1.0 / (alpha * beta_ref[...])

    def one_block(block, carry):
        out_ref[:, lanes(block)] = model_ref[:, lanes(block)] * scale
        return carry

    copies = []
    for chunk in range(CHUNKS):
        lax.fori_loop(chunk * blocks, (chunk + 1) * blocks, one_block, 0, unroll=4)
        where = slice(chunk * blocks * BS, (chunk + 1) * blocks * BS)
        copies.append(
            pltpu.make_async_copy(out_ref.at[:, where], out_hbm.at[:, where], sems.at[chunk])
        )
        copies[-1].start()
    for copy in copies:
        copy.wait()


def call(kernel, name, in_spaces, outs, scratch=(), flops=0, moved=0, limit=16 << 20):
    return pl.pallas_call(
        kernel,
        name=name,
        in_specs=[pl.BlockSpec(memory_space=space) for space in in_spaces],
        out_specs=[pl.BlockSpec(memory_space=space) for _, _, space in outs],
        out_shape=[jax.ShapeDtypeStruct(shape, dtype) for shape, dtype, _ in outs],
        scratch_shapes=list(scratch),
        compiler_params=pltpu.CompilerParams(vmem_limit_bytes=limit),
        cost_estimate=pl.CostEstimate(flops=flops, bytes_accessed=moved, transcendentals=0),
    )


def on_device(ray_blocks, block_cells, block_counts, travel_times):
    pair_count, slot_count = ray_blocks.shape[:2]
    slots = pair_count * slot_count
    peers = lax.axis_size("pair")
    spots = peers * BCAP
    times = travel_times.T
    cols, pairs = times.shape
    messages = [((BCAP * cols + TAIL, BS), BF16, VMEM)] * peers
    ins = [VMEM] * peers
    gathered_blocks = VMEM((peers, BCAP * cols, BS), BF16)
    tile = ((cols, BS), F32, VMEM)
    data = ((cols, pairs), F32, VMEM)
    whole = ((cols, CELL_DEV), F32, VMEM)
    totals = VMEM((spots + 1, cols, BS), F32)
    flops = 2 * slots * BS * BS * cols

    def exchange(values):
        half = peers // 2
        steps = [i // 2 + i % 2 * half for i in range(peers)]
        return [values[0]] + [
            lax.ppermute(value, "pair", [(one, one ^ step) for one in range(peers)])
            for value, step in zip(values[1:], steps[1:])
        ]

    me = lax.axis_index("pair").astype(jnp.int32).reshape(1)
    *outgoing, target = call(
        functools.partial(start_kernel, peers), "start", [SMEM, HBM, HBM, HBM, HBM],
        messages + [((slots,), jnp.int32, SMEM)],
        [
            totals, SMEM((spots,), jnp.int32), SMEM((peers,), jnp.int32),
            SMEM(block_cells.shape, jnp.int32), SMEM(block_counts.shape, jnp.int32),
            VMEM(times.shape, F32), VMEM(ray_blocks.shape, BF16),
            pltpu.SemaphoreType.DMA((3,)), pltpu.SemaphoreType.DMA((pair_count,)),
        ],
        flops, 6 << 20, 60 << 20,
    )(me, block_cells, block_counts, times, ray_blocks)
    arrived = exchange(outgoing)
    target, arrived[0], ray_blocks = call(
        keep_kernel, "keep", [HBM, HBM, HBM],
        [((slots,), jnp.int32, SMEM), messages[0], (ray_blocks.shape, BF16, VMEM)],
        [pltpu.SemaphoreType.DMA((3,))], 0, 8 << 20, 48 << 20,
    )(target, arrived[0], ray_blocks)
    model, beta, *replies, asked = call(
        functools.partial(first_cell_kernel, peers), "cells_first", ins,
        [whole, tile] + messages + [((peers, BS), jnp.int32, SMEM)],
        [VMEM((peers, BS), jnp.int32), pltpu.SemaphoreType.DMA],
        0, 6 << 20,
    )(*arrived)
    models, betas, alphas = [model], [beta], []
    current = times
    for step in range(ITERS):
        fetched = exchange(replies)
        last = step + 1 == ITERS
        made = call(
            functools.partial(pair_kernel, peers), "pairs_last" if last else "pairs",
            [SMEM] + ins + [VMEM, VMEM, VMEM], messages + [tile] + [data] * (not last),
            [VMEM(data[0], F32)] * last + [totals, gathered_blocks], 2 * flops, 8 << 20,
        )(target, *fetched, current, betas[-1], ray_blocks)
        alphas.append(made[peers])
        current = made[-1]
        arrived = exchange(made[:peers])
        if not last:
            model, beta, *replies = call(
                functools.partial(cell_kernel, peers), "cells", [SMEM] + ins + [VMEM] * 3,
                [whole, tile] + messages, (), 0, 8 << 20,
            )(asked, *arrived, models[-1], alphas[-1], betas[-1])
            models.append(model)
            betas.append(beta)
    model, beta, share = call(
        functools.partial(last_cell_kernel, peers), "cells_last", [SMEM] + ins + [VMEM] * 3,
        [whole, tile, ((8, BS), F32, VMEM)], (), 0, 8 << 20,
    )(asked, *arrived, models[-1], alphas[-1], betas[-1])
    betas.append(beta)
    reach, shares = peers, [share]
    while reach > 1:
        share = sum(shares[1:], shares[0])
        low = max(reach // 4, 1)
        shares = [share] + [
            lax.ppermute(share, "pair", [(one, one ^ step) for one in range(peers)])
            for step in range(low, reach, low)
        ]
        reach = low
    scratch = [VMEM(whole[0], F32), pltpu.SemaphoreType.DMA((CHUNKS,))]
    (estimate,) = call(
        estimate_kernel, "estimate", [VMEM] * (3 * ITERS + 1), [(whole[0], F32, HBM)], scratch,
        0, 6 << 20,
    )(*models, *alphas, *betas)
    (model_vec,) = call(
        model_kernel, "model", [VMEM] * (len(shares) + 2), [(whole[0], F32, HBM)], scratch,
        0, 4 << 20,
    )(*shares, beta, model)
    return (estimate.T, model_vec.T)


def solution(mesh):
    return jax.shard_map(
        on_device,
        mesh=mesh,
        in_specs=(
            P(("groups", "pair"), None, None, None),
            P(("groups", "pair"), None),
            P(("groups", "pair")),
            P(("groups", "pair"), None),
        ),
        out_specs=(P(("groups", "pair"), None), P(("groups", "pair"), None)),
        check_vma=False,
    )
```

```python
import functools

import jax
import jax.numpy as jnp
from jax import lax
from jax.experimental import pallas as pl
from jax.experimental.pallas import tpu as pltpu
from jax.sharding import PartitionSpec as P

CELL_DEV = 8192
BCAP = 4
BS = 128
TAIL = 8
ITERS = 2
EPS = 1e-12
F32 = jnp.float32
BF16 = jnp.bfloat16
VMEM = pltpu.VMEM
SMEM = pltpu.SMEM
HBM = pltpu.HBM
CHUNKS = 8


def steps_of(peers):
    tailed = tailed_of(peers)
    rest = [step for step in range(1, peers) if step not in tailed]
    near = [step for step in rest if step < peers // 2]
    far = [step for step in rest if step >= peers // 2]
    turns = [step for both in zip(far, near) for step in both]
    return [0] + tailed + turns + far[len(near) :] + near[len(far) :]


def tailed_of(peers):
    return [peers // 2, peers // 4, peers // 2 + peers // 4]


def later(values, rows):
    cut = len(values) * 2 // 3
    return [*values[:cut], *rows, *values[cut:]]


def parted(refs, peers):
    cut = peers * 2 // 3
    rest = peers - cut
    return [*refs[:cut], *refs[len(refs) - rest :]], refs[cut : len(refs) - rest]


def diagonal(cols):
    shape = (cols, BS)
    return lax.broadcasted_iota(jnp.int32, shape, 0) == lax.broadcasted_iota(jnp.int32, shape, 1)


def squares_tail(squares):
    cols = squares.shape[0]
    total = jnp.sum(squares, axis=1, keepdims=True)
    row = jnp.sum(jnp.where(diagonal(cols), total, 0.0), axis=0, keepdims=True)
    high = row.astype(BF16).astype(F32)
    middle = (row - high).astype(BF16).astype(F32)
    low = row - high - middle
    place = lax.broadcasted_iota(jnp.int32, (TAIL, BS), 0)
    return jnp.where(
        place == 0, high, jnp.where(place == 1, middle, jnp.where(place == 2, low, 0.0))
    )


def norm_of(tails, cols):
    summed = sum(tails)
    row = summed[0:1] + summed[1:2] + summed[2:3]
    column = jnp.sum(jnp.where(diagonal(cols), row, 0.0), axis=1, keepdims=True)
    return jnp.broadcast_to(jnp.sqrt(column + EPS), (cols, BS))


def lanes(block):
    return pl.ds(pl.multiple_of(block * BS, BS), BS)


def transposed(data_ref, rays_ref, before, target_ref, total_ref, message_refs):
    pair_count, slot_count = rays_ref.shape[:2]
    cols = data_ref.shape[0]
    spots = len(message_refs) * BCAP

    def clear(index, carry):
        total_ref[index] = jnp.zeros((cols, BS), F32)
        return carry

    lax.fori_loop(0, spots, clear, 0, unroll=8)

    def one_pair(pair, carry):
        before(pair)
        data = data_ref[:, lanes(pair)]
        high = data.astype(BF16)
        low = (data - high.astype(F32)).astype(BF16)
        pieces = jnp.concatenate([high, low], axis=0)
        for slot in range(0, slot_count, 2):
            rays = jnp.concatenate([rays_ref[pair, slot], rays_ref[pair, slot + 1]], axis=1)
            part = jnp.dot(pieces, rays, preferred_element_type=F32)
            part = part[:cols] + part[cols:]
            for half in range(2):
                spot = target_ref[pair * slot_count + slot + half]
                total_ref[spot] += part[:, half * BS : (half + 1) * BS]
        return carry

    lax.fori_loop(0, pair_count, one_pair, 0, unroll=True)

    for peer, message_ref in enumerate(message_refs):
        for rank in range(BCAP):
            message_ref[rank * cols : (rank + 1) * cols, :] = total_ref[
                peer * BCAP + rank
            ].astype(BF16)


def start_kernel(peers, me_ref, cells_hbm, counts_hbm, times_hbm, rays_hbm, *refs):
    message_refs = refs[:peers]
    target_ref, total_ref, table_ref, used_ref, cells_ref, counts_ref = refs[peers : peers + 6]
    times_ref, rays_ref, place_ref, sems, ray_sems = refs[peers + 6 :]
    for index, step in enumerate(steps_of(peers)):
        place_ref[me_ref[0] ^ step] = index
    pair_count, slot_count = rays_ref.shape[:2]
    cols = times_ref.shape[0]
    owned = CELL_DEV // BS
    copies = [
        pltpu.make_async_copy(source, dest, sems.at[index])
        for index, (source, dest) in enumerate(
            [(cells_hbm, cells_ref), (counts_hbm, counts_ref), (times_hbm, times_ref)]
        )
    ]
    for copy in copies:
        copy.start()

    def ray_copy(pair):
        return pltpu.make_async_copy(rays_hbm.at[pair], rays_ref.at[pair], ray_sems.at[pair])

    def fetch(pair, carry):
        ray_copy(pair).start()
        return carry

    lax.fori_loop(0, pair_count, fetch, 0)

    def clear(peer, carry):
        used_ref[peer] = 0
        for rank in range(BCAP):
            table_ref[peer * BCAP + rank] = 0
        return carry

    lax.fori_loop(0, peers, clear, 0)
    for copy in copies:
        copy.wait()

    def find_places(pair):
        count = counts_ref[pair]
        for slot in range(slot_count):
            cell = cells_ref[pair, slot]
            owner = place_ref[cell // owned]
            local = cell % owned
            used = used_ref[owner]
            rank = used
            for other in range(BCAP - 1, -1, -1):
                same = (table_ref[owner * BCAP + other] == local) & (other < used)
                rank = jnp.where(same, other, rank)
            spot = owner * BCAP + rank
            table_ref[spot] = local
            used_ref[owner] = jnp.maximum(used, rank + 1)
            target_ref[pair * slot_count + slot] = jnp.where(slot < count, spot, peers * BCAP)

    def before(pair):
        find_places(pair)
        ray_copy(pair).wait()

    transposed(times_ref, rays_ref, before, target_ref, total_ref, message_refs)
    squares = jnp.zeros((cols, BS), F32)
    for pair in range(pair_count):
        part = times_ref[:, pair * BS : (pair + 1) * BS]
        squares += part * part
    tail = squares_tail(squares)
    place = lax.broadcasted_iota(jnp.int32, (TAIL, BS), 0)
    lane = lax.broadcasted_iota(jnp.int32, (TAIL, BS), 1)

    for peer, message_ref in enumerate(message_refs):
        rows = tail
        for rank in range(BCAP):
            asked = table_ref[peer * BCAP + rank].astype(F32)
            rows = jnp.where((place == 3) & (lane == rank), asked, rows)
        message_ref[BCAP * cols :, :] = rows.astype(BF16)


def keep_kernel(target_hbm, own_hbm, rays_hbm, target_ref, own_ref, rays_ref, sems):
    copies = [
        pltpu.make_async_copy(source, dest, sems.at[index])
        for index, (source, dest) in enumerate(
            [(target_hbm, target_ref), (own_hbm, own_ref), (rays_hbm, rays_ref)]
        )
    ]
    for copy in copies:
        copy.start()
    for copy in copies:
        copy.wait()


def pair_kernel(peers, rows, target_ref, *refs):
    fetched_refs, row_refs = parted(refs[: peers + rows], peers)
    refs = refs[peers + rows :]
    data_ref, beta_ref, rays_ref = refs[:3]
    message_refs = refs[3 : peers + 3]
    alpha_ref, share_ref, raw_ref, total_ref, fetched_ref = refs[peers + 3 :]
    pair_count, slot_count = rays_ref.shape[:2]
    cols = data_ref.shape[0]
    spots = peers * BCAP
    for peer in range(peers):
        fetched_ref[peer] = fetched_refs[peer][: BCAP * cols, :]
    alpha = norm_of([ref[...] for ref in row_refs], cols)
    alpha_ref[...] = alpha
    beta = beta_ref[...]
    model_scale = 1.0 / (alpha * beta)
    data_scale = alpha / beta

    def one_pair(pair, squares):
        chosen = []
        for slot in range(slot_count):
            spot = target_ref[pair * slot_count + slot]
            live = spot < spots
            spot = jnp.where(live, spot, 0)
            rows = pl.ds(pl.multiple_of((spot % BCAP) * cols, cols), cols)
            block = fetched_ref[spot // BCAP, rows, :]
            chosen.append(jnp.where(live, block, jnp.zeros_like(block)))
        rays = jnp.concatenate([rays_ref[pair, slot] for slot in range(slot_count)], axis=1)
        product = lax.dot_general(
            rays, jnp.concatenate(chosen, axis=1), (((1,), (1,)), ((), ())),
            preferred_element_type=F32,
        )
        raw = product.T * model_scale - data_ref[:, lanes(pair)] * data_scale
        raw_ref[:, lanes(pair)] = raw
        return squares + raw * raw

    squares = lax.fori_loop(0, pair_count, one_pair, jnp.zeros((cols, BS), F32), unroll=True)
    transposed(raw_ref, rays_ref, lambda pair: None, target_ref, total_ref, message_refs)
    write_tails(squares_tail(squares), message_refs, share_ref, cols)


def write_tails(tail, message_refs, share_ref, cols):
    share_ref[...] = tail
    for message_ref in message_refs:
        if message_ref.shape[0] > BCAP * cols:
            message_ref[BCAP * cols :, :] = tail.astype(BF16)


def gathered(arrived_refs, asked_ref, model_ref):
    cols = model_ref.shape[0]
    for peer, arrived_ref in enumerate(arrived_refs):
        for rank in range(BCAP):
            where = lanes(asked_ref[peer, rank])
            model_ref[:, where] += arrived_ref[rank * cols : (rank + 1) * cols, :].astype(F32)


def reply(squares, scale, asked_ref, model_ref, out_refs, share_ref):
    cols = model_ref.shape[0]
    write_tails(squares_tail(squares * scale * scale), out_refs, share_ref, cols)
    for peer, out_ref in enumerate(out_refs):
        for rank in range(BCAP):
            block = model_ref[:, lanes(asked_ref[peer, rank])]
            out_ref[rank * cols : (rank + 1) * cols, :] = block.astype(BF16)


def squares_of(model_ref):
    cols, cells = model_ref.shape

    def one_block(block, squares):
        values = model_ref[:, lanes(block)]
        return squares + values * values

    return lax.fori_loop(0, cells // BS, one_block, jnp.zeros((cols, BS), F32), unroll=8)


def first_cell_kernel(peers, *refs):
    arrived_refs, out_refs = refs[:peers], refs[peers + 3 : 2 * peers + 3]
    model_ref, beta_ref, share_ref = refs[peers : peers + 3]
    asked_ref, table_ref, sem = refs[2 * peers + 3 :]
    cols, cells = model_ref.shape
    for peer in range(peers):
        tail = arrived_refs[peer][BCAP * cols :, :].astype(F32)
        table_ref[peer : peer + 1, :] = tail[3:4].astype(jnp.int32)
    copy = pltpu.make_async_copy(table_ref, asked_ref, sem)
    copy.start()
    beta = norm_of([ref[BCAP * cols :, :].astype(F32) for ref in arrived_refs], cols)
    beta_ref[...] = beta
    model_ref[...] = jnp.zeros((cols, cells), F32)
    copy.wait()
    gathered(arrived_refs, asked_ref, model_ref)
    reply(squares_of(model_ref), 1.0 / beta, asked_ref, model_ref, out_refs, share_ref)


def start_from(before_ref, scale, model_ref):
    def one_block(block, carry):
        model_ref[:, lanes(block)] = before_ref[:, lanes(block)] * -scale
        return carry

    lax.fori_loop(0, model_ref.shape[1] // BS, one_block, 0, unroll=8)


def cell_kernel(peers, rows, asked_ref, *refs):
    arrived_refs, row_refs = parted(refs[: peers + rows], peers)
    before_ref, alpha_ref, beta_before_ref, model_ref, beta_ref, share_ref, *out_refs = refs[
        peers + rows :
    ]
    beta = norm_of([ref[...] for ref in row_refs], model_ref.shape[0])
    beta_ref[...] = beta
    start_from(before_ref, beta * beta / (alpha_ref[...] * beta_before_ref[...]), model_ref)
    gathered(arrived_refs, asked_ref, model_ref)
    reply(squares_of(model_ref), 1.0 / beta, asked_ref, model_ref, out_refs, share_ref)


def estimate_kernel(*refs):
    models = refs[:ITERS]
    alphas = [ref[...] for ref in refs[ITERS : 2 * ITERS]]
    betas = [ref[...] for ref in refs[2 * ITERS : 3 * ITERS + 1]]
    estimate_hbm, estimate_ref, sems = refs[3 * ITERS + 1 :]
    cells = estimate_ref.shape[1]
    weights = estimate_weights(betas, alphas)
    blocks = cells // BS // CHUNKS

    def one_block(block, carry):
        where = lanes(block)
        total = weights[0] * models[0][:, where]
        for i in range(1, ITERS):
            total += weights[i] * models[i][:, where]
        estimate_ref[:, where] = total
        return carry

    copies = []
    for chunk in range(CHUNKS):
        lax.fori_loop(chunk * blocks, (chunk + 1) * blocks, one_block, 0, unroll=4)
        where = slice(chunk * blocks * BS, (chunk + 1) * blocks * BS)
        copies.append(
            pltpu.make_async_copy(
                estimate_ref.at[:, where], estimate_hbm.at[:, where], sems.at[chunk]
            )
        )
        copies[-1].start()
    for copy in copies:
        copy.wait()


def estimate_weights(betas, alphas):
    phi_bar = betas[0]
    rho_bar = alphas[0]
    trace = [1.0 / (alphas[0] * betas[0])]
    weight = [jnp.zeros_like(phi_bar)] * ITERS
    for step in range(ITERS):
        beta = betas[step + 1]
        rho = jnp.sqrt(rho_bar * rho_bar + beta * beta)
        cosine = rho_bar / rho
        sine = beta / rho
        gain = cosine * phi_bar / rho
        weight = [
            weight[i] + gain * trace[i] if i < len(trace) else weight[i] for i in range(ITERS)
        ]
        if step + 1 < ITERS:
            alpha = alphas[step + 1]
            theta = sine * alpha
            rho_bar = -cosine * alpha
            phi_bar = sine * phi_bar
            trace = [-(theta / rho) * value for value in trace] + [1.0 / (alpha * beta)]
    return weight


def model_kernel(*refs):
    *share_refs, beta_ref, model_ref, out_hbm, out_ref, sems = refs
    cols, cells = model_ref.shape
    blocks = cells // BS // CHUNKS
    scale = 1.0 / (norm_of([ref[...] for ref in share_refs], cols) * beta_ref[...])

    def one_block(block, carry):
        out_ref[:, lanes(block)] = model_ref[:, lanes(block)] * scale
        return carry

    copies = []
    for chunk in range(CHUNKS):
        lax.fori_loop(chunk * blocks, (chunk + 1) * blocks, one_block, 0, unroll=4)
        where = slice(chunk * blocks * BS, (chunk + 1) * blocks * BS)
        copies.append(
            pltpu.make_async_copy(out_ref.at[:, where], out_hbm.at[:, where], sems.at[chunk])
        )
        copies[-1].start()
    for copy in copies:
        copy.wait()


def call(kernel, name, in_spaces, outs, scratch=(), flops=0, moved=0, limit=16 << 20):
    return pl.pallas_call(
        kernel,
        name=name,
        in_specs=[pl.BlockSpec(memory_space=space) for space in in_spaces],
        out_specs=[pl.BlockSpec(memory_space=space) for _, _, space in outs],
        out_shape=[jax.ShapeDtypeStruct(shape, dtype) for shape, dtype, _ in outs],
        scratch_shapes=list(scratch),
        compiler_params=pltpu.CompilerParams(vmem_limit_bytes=limit),
        cost_estimate=pl.CostEstimate(flops=flops, bytes_accessed=moved, transcendentals=0),
    )


def on_device(ray_blocks, block_cells, block_counts, travel_times):
    pair_count, slot_count = ray_blocks.shape[:2]
    slots = pair_count * slot_count
    peers = lax.axis_size("pair")
    spots = peers * BCAP
    times = travel_times.T
    cols, pairs = times.shape
    steps = steps_of(peers)
    messages = [
        ((BCAP * cols + TAIL * (step in tailed_of(peers)), BS), BF16, VMEM) for step in steps
    ]
    first_messages = [((BCAP * cols + TAIL, BS), BF16, VMEM)] * peers
    row = ((TAIL, BS), F32, VMEM)
    gathered_blocks = VMEM((peers, BCAP * cols, BS), BF16)
    tile = ((cols, BS), F32, VMEM)
    data = ((cols, pairs), F32, VMEM)
    whole = ((cols, CELL_DEV), F32, VMEM)
    totals = VMEM((spots + 1, cols, BS), F32)
    flops = 2 * slots * BS * BS * cols

    def send(value, step):
        return lax.ppermute(value, "pair", [(one, one ^ step) for one in range(peers)])

    def exchange(values):
        return [values[0]] + [send(value, step) for value, step in zip(values[1:], steps[1:])]

    def completed(share, arrived):
        share = sum((arrived[i][BCAP * cols :, :].astype(F32) for i in range(1, 4)), share)
        return [share] + [send(share, step) for step in range(1, peers // 4)]

    me = lax.axis_index("pair").astype(jnp.int32).reshape(1)
    *outgoing, target = call(
        functools.partial(start_kernel, peers), "start", [SMEM, HBM, HBM, HBM, HBM],
        first_messages + [((slots,), jnp.int32, SMEM)],
        [
            totals, SMEM((spots,), jnp.int32), SMEM((peers,), jnp.int32),
            SMEM(block_cells.shape, jnp.int32), SMEM(block_counts.shape, jnp.int32),
            VMEM(times.shape, F32), VMEM(ray_blocks.shape, BF16), SMEM((peers,), jnp.int32),
            pltpu.SemaphoreType.DMA((3,)), pltpu.SemaphoreType.DMA((pair_count,)),
        ],
        flops, 6 << 20, 60 << 20,
    )(me, block_cells, block_counts, times, ray_blocks)
    arrived = exchange(outgoing)
    target, arrived[0], ray_blocks = call(
        keep_kernel, "keep", [HBM, HBM, HBM],
        [((slots,), jnp.int32, SMEM), first_messages[0], (ray_blocks.shape, BF16, VMEM)],
        [pltpu.SemaphoreType.DMA((3,))], 0, 8 << 20, 48 << 20,
    )(target, arrived[0], ray_blocks)
    model, beta, share, *replies, asked = call(
        functools.partial(first_cell_kernel, peers), "cells_first", [VMEM] * peers,
        [whole, tile, row] + messages + [((peers, BS), jnp.int32, SMEM)],
        [VMEM((peers, BS), jnp.int32), pltpu.SemaphoreType.DMA],
        0, 6 << 20,
    )(*arrived)
    models, betas, alphas = [model], [beta], []
    current = times
    for step in range(ITERS):
        fetched = exchange(replies)
        rows = completed(share, fetched)
        ins = [VMEM] * (peers + len(rows))
        last = step + 1 == ITERS
        made = call(
            functools.partial(pair_kernel, peers, len(rows)), "pairs_last" if last else "pairs",
            [SMEM] + ins + [VMEM, VMEM, VMEM], messages + [tile, row] + [data] * (not last),
            [VMEM(data[0], F32)] * last + [totals, gathered_blocks], 2 * flops, 8 << 20,
        )(target, *later(fetched, rows), current, betas[-1], ray_blocks)
        alphas.append(made[peers])
        current = made[-1]
        arrived = exchange(made[:peers])
        rows = completed(made[peers + 1], arrived)
        model, beta, share, *replies = call(
            functools.partial(cell_kernel, peers, len(rows)), "cells_last" if last else "cells",
            [SMEM] + ins + [VMEM] * 3, [whole, tile, row] + messages * (not last), (), 0, 8 << 20,
        )(asked, *later(arrived, rows), models[-1], alphas[-1], betas[-1])
        models.append(model)
        betas.append(beta)
    for low, reach in ((peers // 4, peers), (1, peers // 4)):
        rows = [share] + [send(share, step) for step in range(low, reach, low)]
        share = sum(rows[1:], rows[0])
    scratch = [VMEM(whole[0], F32), pltpu.SemaphoreType.DMA((CHUNKS,))]
    (estimate,) = call(
        estimate_kernel, "estimate", [VMEM] * (3 * ITERS + 1), [(whole[0], F32, HBM)], scratch,
        0, 6 << 20,
    )(*models[:ITERS], *alphas, *betas)
    (model_vec,) = call(
        model_kernel, "model", [VMEM] * (len(rows) + 2), [(whole[0], F32, HBM)], scratch,
        0, 4 << 20,
    )(*rows, beta, model)
    return (estimate.T, model_vec.T)


def solution(mesh):
    return jax.shard_map(
        on_device,
        mesh=mesh,
        in_specs=(
            P(("groups", "pair"), None, None, None),
            P(("groups", "pair"), None),
            P(("groups", "pair")),
            P(("groups", "pair"), None),
        ),
        out_specs=(P(("groups", "pair"), None), P(("groups", "pair"), None)),
        check_vma=False,
    )
```

```python
import functools

import jax
import jax.numpy as jnp
from jax import lax
from jax.experimental import pallas as pl
from jax.experimental.pallas import tpu as pltpu
from jax.sharding import PartitionSpec as P

CELL_DEV = 8192
BCAP = 4
BS = 128
TAIL = 8
ITERS = 2
EPS = 1e-12
F32 = jnp.float32
BF16 = jnp.bfloat16
VMEM = pltpu.VMEM
SMEM = pltpu.SMEM
HBM = pltpu.HBM
CHUNKS = 8


def steps_of(peers):
    near, far = list(range(1, peers // 2)), list(range(peers // 2, peers))
    steps = [0]
    while far:
        steps += far[:2] + near[:1]
        far, near = far[2:], near[1:]
    return steps + near


def diagonal(cols):
    shape = (cols, BS)
    return lax.broadcasted_iota(jnp.int32, shape, 0) == lax.broadcasted_iota(jnp.int32, shape, 1)


def squares_tail(squares):
    cols = squares.shape[0]
    total = jnp.sum(squares, axis=1, keepdims=True)
    row = jnp.sum(jnp.where(diagonal(cols), total, 0.0), axis=0, keepdims=True)
    high = row.astype(BF16).astype(F32)
    middle = (row - high).astype(BF16).astype(F32)
    low = row - high - middle
    place = lax.broadcasted_iota(jnp.int32, (TAIL, BS), 0)
    return jnp.where(
        place == 0, high, jnp.where(place == 1, middle, jnp.where(place == 2, low, 0.0))
    )


def norm_of_tails(message_refs, cols):
    summed = sum(message_ref[BCAP * cols :, :].astype(F32) for message_ref in message_refs)
    row = summed[0:1] + summed[1:2] + summed[2:3]
    column = jnp.sum(jnp.where(diagonal(cols), row, 0.0), axis=1, keepdims=True)
    return jnp.broadcast_to(jnp.sqrt(column + EPS), (cols, BS))


def lanes(block):
    return pl.ds(pl.multiple_of(block * BS, BS), BS)


def transposed(data_ref, rays_ref, before, target_ref, total_ref, message_refs):
    pair_count, slot_count = rays_ref.shape[:2]
    cols = data_ref.shape[0]
    spots = len(message_refs) * BCAP

    def clear(index, carry):
        total_ref[index] = jnp.zeros((cols, BS), F32)
        return carry

    lax.fori_loop(0, spots, clear, 0, unroll=8)

    def one_pair(pair, carry):
        before(pair)
        data = data_ref[:, lanes(pair)]
        high = data.astype(BF16)
        low = (data - high.astype(F32)).astype(BF16)
        pieces = jnp.concatenate([high, low], axis=0)
        for slot in range(0, slot_count, 2):
            rays = jnp.concatenate([rays_ref[pair, slot], rays_ref[pair, slot + 1]], axis=1)
            part = jnp.dot(pieces, rays, preferred_element_type=F32)
            part = part[:cols] + part[cols:]
            for half in range(2):
                spot = target_ref[pair * slot_count + slot + half]
                total_ref[spot] += part[:, half * BS : (half + 1) * BS]
        return carry

    lax.fori_loop(0, pair_count, one_pair, 0, unroll=True)

    for peer, message_ref in enumerate(message_refs):
        for rank in range(BCAP):
            message_ref[rank * cols : (rank + 1) * cols, :] = total_ref[
                peer * BCAP + rank
            ].astype(BF16)


def start_kernel(peers, me_ref, cells_hbm, counts_hbm, times_hbm, rays_hbm, *refs):
    message_refs = refs[:peers]
    target_ref, total_ref, table_ref, used_ref, cells_ref, counts_ref = refs[peers : peers + 6]
    times_ref, rays_ref, place_ref, sems, ray_sems = refs[peers + 6 :]
    for index, step in enumerate(steps_of(peers)):
        place_ref[me_ref[0] ^ step] = index
    pair_count, slot_count = rays_ref.shape[:2]
    cols = times_ref.shape[0]
    owned = CELL_DEV // BS
    copies = [
        pltpu.make_async_copy(source, dest, sems.at[index])
        for index, (source, dest) in enumerate(
            [(cells_hbm, cells_ref), (counts_hbm, counts_ref), (times_hbm, times_ref)]
        )
    ]
    for copy in copies:
        copy.start()

    def ray_copy(pair):
        return pltpu.make_async_copy(rays_hbm.at[pair], rays_ref.at[pair], ray_sems.at[pair])

    def fetch(pair, carry):
        ray_copy(pair).start()
        return carry

    lax.fori_loop(0, pair_count, fetch, 0)

    def clear(peer, carry):
        used_ref[peer] = 0
        for rank in range(BCAP):
            table_ref[peer * BCAP + rank] = 0
        return carry

    lax.fori_loop(0, peers, clear, 0)
    for copy in copies:
        copy.wait()

    def find_places(pair):
        count = counts_ref[pair]
        for slot in range(slot_count):
            cell = cells_ref[pair, slot]
            owner = place_ref[cell // owned]
            local = cell % owned
            used = used_ref[owner]
            rank = used
            for other in range(BCAP - 1, -1, -1):
                same = (table_ref[owner * BCAP + other] == local) & (other < used)
                rank = jnp.where(same, other, rank)
            spot = owner * BCAP + rank
            table_ref[spot] = local
            used_ref[owner] = jnp.maximum(used, rank + 1)
            target_ref[pair * slot_count + slot] = jnp.where(slot < count, spot, peers * BCAP)

    def before(pair):
        find_places(pair)
        ray_copy(pair).wait()

    transposed(times_ref, rays_ref, before, target_ref, total_ref, message_refs)
    squares = jnp.zeros((cols, BS), F32)
    for pair in range(pair_count):
        part = times_ref[:, pair * BS : (pair + 1) * BS]
        squares += part * part
    tail = squares_tail(squares)
    place = lax.broadcasted_iota(jnp.int32, (TAIL, BS), 0)
    lane = lax.broadcasted_iota(jnp.int32, (TAIL, BS), 1)

    for peer, message_ref in enumerate(message_refs):
        rows = tail
        for rank in range(BCAP):
            asked = table_ref[peer * BCAP + rank].astype(F32)
            rows = jnp.where((place == 3) & (lane == rank), asked, rows)
        message_ref[BCAP * cols :, :] = rows.astype(BF16)


def keep_kernel(target_hbm, own_hbm, rays_hbm, target_ref, own_ref, rays_ref, sems):
    copies = [
        pltpu.make_async_copy(source, dest, sems.at[index])
        for index, (source, dest) in enumerate(
            [(target_hbm, target_ref), (own_hbm, own_ref), (rays_hbm, rays_ref)]
        )
    ]
    for copy in copies:
        copy.start()
    for copy in copies:
        copy.wait()


def pair_kernel(peers, target_ref, *refs):
    fetched_refs = refs[:peers]
    data_ref, beta_ref, rays_ref = refs[peers : peers + 3]
    message_refs = refs[peers + 3 : 2 * peers + 3]
    alpha_ref, raw_ref, total_ref, fetched_ref = refs[2 * peers + 3 :]
    pair_count, slot_count = rays_ref.shape[:2]
    cols = data_ref.shape[0]
    spots = peers * BCAP
    for peer in range(peers):
        fetched_ref[peer] = fetched_refs[peer][: BCAP * cols, :]
    alpha = norm_of_tails(fetched_refs, cols)
    alpha_ref[...] = alpha
    beta = beta_ref[...]
    model_scale = 1.0 / (alpha * beta)
    data_scale = alpha / beta

    def one_pair(pair, squares):
        chosen = []
        for slot in range(slot_count):
            spot = target_ref[pair * slot_count + slot]
            live = spot < spots
            spot = jnp.where(live, spot, 0)
            rows = pl.ds(pl.multiple_of((spot % BCAP) * cols, cols), cols)
            block = fetched_ref[spot // BCAP, rows, :]
            chosen.append(jnp.where(live, block, jnp.zeros_like(block)))
        rays = jnp.concatenate([rays_ref[pair, slot] for slot in range(slot_count)], axis=1)
        product = lax.dot_general(
            rays, jnp.concatenate(chosen, axis=1), (((1,), (1,)), ((), ())),
            preferred_element_type=F32,
        )
        raw = product.T * model_scale - data_ref[:, lanes(pair)] * data_scale
        raw_ref[:, lanes(pair)] = raw
        return squares + raw * raw

    squares = lax.fori_loop(0, pair_count, one_pair, jnp.zeros((cols, BS), F32), unroll=True)
    transposed(raw_ref, rays_ref, lambda pair: None, target_ref, total_ref, message_refs)
    tail = squares_tail(squares).astype(BF16)
    for message_ref in message_refs:
        message_ref[BCAP * cols :, :] = tail


def gathered(arrived_refs, asked_ref, model_ref):
    cols = model_ref.shape[0]
    for peer, arrived_ref in enumerate(arrived_refs):
        for rank in range(BCAP):
            where = lanes(asked_ref[peer, rank])
            model_ref[:, where] += arrived_ref[rank * cols : (rank + 1) * cols, :].astype(F32)


def reply(squares, scale, asked_ref, model_ref, out_refs):
    cols = model_ref.shape[0]
    tail = squares_tail(squares * scale * scale).astype(BF16)
    for peer, out_ref in enumerate(out_refs):
        out_ref[BCAP * cols :, :] = tail
        for rank in range(BCAP):
            block = model_ref[:, lanes(asked_ref[peer, rank])]
            out_ref[rank * cols : (rank + 1) * cols, :] = block.astype(BF16)


def squares_of(model_ref):
    cols, cells = model_ref.shape

    def one_block(block, squares):
        values = model_ref[:, lanes(block)]
        return squares + values * values

    return lax.fori_loop(0, cells // BS, one_block, jnp.zeros((cols, BS), F32), unroll=8)


def first_cell_kernel(peers, *refs):
    arrived_refs, out_refs = refs[:peers], refs[peers + 2 : 2 * peers + 2]
    model_ref, beta_ref = refs[peers : peers + 2]
    asked_ref, table_ref, sem = refs[2 * peers + 2 :]
    cols, cells = model_ref.shape
    for peer in range(peers):
        tail = arrived_refs[peer][BCAP * cols :, :].astype(F32)
        table_ref[peer : peer + 1, :] = tail[3:4].astype(jnp.int32)
    copy = pltpu.make_async_copy(table_ref, asked_ref, sem)
    copy.start()
    beta = norm_of_tails(arrived_refs, cols)
    beta_ref[...] = beta
    model_ref[...] = jnp.zeros((cols, cells), F32)
    copy.wait()
    gathered(arrived_refs, asked_ref, model_ref)
    reply(squares_of(model_ref), 1.0 / beta, asked_ref, model_ref, out_refs)


def start_from(before_ref, scale, model_ref):
    def one_block(block, carry):
        model_ref[:, lanes(block)] = before_ref[:, lanes(block)] * -scale
        return carry

    lax.fori_loop(0, model_ref.shape[1] // BS, one_block, 0, unroll=8)


def cell_kernel(peers, asked_ref, *refs):
    arrived_refs, out_refs = refs[:peers], refs[peers + 5 :]
    before_ref, alpha_ref, beta_before_ref, model_ref, beta_ref = refs[peers : peers + 5]
    beta = norm_of_tails(arrived_refs, model_ref.shape[0])
    beta_ref[...] = beta
    start_from(before_ref, beta * beta / (alpha_ref[...] * beta_before_ref[...]), model_ref)
    gathered(arrived_refs, asked_ref, model_ref)
    reply(squares_of(model_ref), 1.0 / beta, asked_ref, model_ref, out_refs)


def last_cell_kernel(peers, asked_ref, *refs):
    arrived_refs = refs[:peers]
    before_ref, alpha_ref, beta_before_ref, model_ref, beta_ref, out_ref = refs[peers:]
    beta = norm_of_tails(arrived_refs, model_ref.shape[0])
    beta_ref[...] = beta
    start_from(before_ref, beta * beta / (alpha_ref[...] * beta_before_ref[...]), model_ref)
    gathered(arrived_refs, asked_ref, model_ref)
    squares = squares_of(model_ref) / (beta * beta)
    total = jnp.sum(squares, axis=1, keepdims=True)
    row = jnp.sum(jnp.where(diagonal(total.shape[0]), total, 0.0), axis=0, keepdims=True)
    out_ref[...] = jnp.broadcast_to(row, out_ref.shape)


def estimate_kernel(*refs):
    models = refs[:ITERS]
    alphas = [ref[...] for ref in refs[ITERS : 2 * ITERS]]
    betas = [ref[...] for ref in refs[2 * ITERS : 3 * ITERS + 1]]
    estimate_hbm, estimate_ref, sems = refs[3 * ITERS + 1 :]
    cells = estimate_ref.shape[1]
    weights = estimate_weights(betas, alphas)
    blocks = cells // BS // CHUNKS

    def one_block(block, carry):
        where = lanes(block)
        total = weights[0] * models[0][:, where]
        for i in range(1, ITERS):
            total += weights[i] * models[i][:, where]
        estimate_ref[:, where] = total
        return carry

    copies = []
    for chunk in range(CHUNKS):
        lax.fori_loop(chunk * blocks, (chunk + 1) * blocks, one_block, 0, unroll=4)
        where = slice(chunk * blocks * BS, (chunk + 1) * blocks * BS)
        copies.append(
            pltpu.make_async_copy(
                estimate_ref.at[:, where], estimate_hbm.at[:, where], sems.at[chunk]
            )
        )
        copies[-1].start()
    for copy in copies:
        copy.wait()


def estimate_weights(betas, alphas):
    phi_bar = betas[0]
    rho_bar = alphas[0]
    trace = [1.0 / (alphas[0] * betas[0])]
    weight = [jnp.zeros_like(phi_bar)] * ITERS
    for step in range(ITERS):
        beta = betas[step + 1]
        rho = jnp.sqrt(rho_bar * rho_bar + beta * beta)
        cosine = rho_bar / rho
        sine = beta / rho
        gain = cosine * phi_bar / rho
        weight = [
            weight[i] + gain * trace[i] if i < len(trace) else weight[i] for i in range(ITERS)
        ]
        if step + 1 < ITERS:
            alpha = alphas[step + 1]
            theta = sine * alpha
            rho_bar = -cosine * alpha
            phi_bar = sine * phi_bar
            trace = [-(theta / rho) * value for value in trace] + [1.0 / (alpha * beta)]
    return weight


def model_kernel(*refs):
    *share_refs, beta_ref, model_ref, out_hbm, out_ref, sems = refs
    cols, cells = model_ref.shape
    blocks = cells // BS // CHUNKS
    row = sum(ref[...] for ref in share_refs)[0:1]
    column = jnp.sum(jnp.where(diagonal(cols), row, 0.0), axis=1, keepdims=True)
    alpha = jnp.broadcast_to(jnp.sqrt(column + EPS), (cols, BS))
    scale = 1.0 / (alpha * beta_ref[...])

    def one_block(block, carry):
        out_ref[:, lanes(block)] = model_ref[:, lanes(block)] * scale
        return carry

    copies = []
    for chunk in range(CHUNKS):
        lax.fori_loop(chunk * blocks, (chunk + 1) * blocks, one_block, 0, unroll=4)
        where = slice(chunk * blocks * BS, (chunk + 1) * blocks * BS)
        copies.append(
            pltpu.make_async_copy(out_ref.at[:, where], out_hbm.at[:, where], sems.at[chunk])
        )
        copies[-1].start()
    for copy in copies:
        copy.wait()


def call(kernel, name, in_spaces, outs, scratch=(), flops=0, moved=0, limit=16 << 20):
    return pl.pallas_call(
        kernel,
        name=name,
        in_specs=[pl.BlockSpec(memory_space=space) for space in in_spaces],
        out_specs=[pl.BlockSpec(memory_space=space) for _, _, space in outs],
        out_shape=[jax.ShapeDtypeStruct(shape, dtype) for shape, dtype, _ in outs],
        scratch_shapes=list(scratch),
        compiler_params=pltpu.CompilerParams(vmem_limit_bytes=limit),
        cost_estimate=pl.CostEstimate(flops=flops, bytes_accessed=moved, transcendentals=0),
    )


def on_device(ray_blocks, block_cells, block_counts, travel_times):
    pair_count, slot_count = ray_blocks.shape[:2]
    slots = pair_count * slot_count
    peers = lax.axis_size("pair")
    spots = peers * BCAP
    times = travel_times.T
    cols, pairs = times.shape
    messages = [((BCAP * cols + TAIL, BS), BF16, VMEM)] * peers
    ins = [VMEM] * peers
    gathered_blocks = VMEM((peers, BCAP * cols, BS), BF16)
    tile = ((cols, BS), F32, VMEM)
    data = ((cols, pairs), F32, VMEM)
    whole = ((cols, CELL_DEV), F32, VMEM)
    totals = VMEM((spots + 1, cols, BS), F32)
    flops = 2 * slots * BS * BS * cols

    steps = steps_of(peers)

    def exchange(values):
        return [values[0]] + [
            lax.ppermute(value, "pair", [(one, one ^ step) for one in range(peers)])
            for value, step in zip(values[1:], steps[1:])
        ]

    me = lax.axis_index("pair").astype(jnp.int32).reshape(1)
    *outgoing, target = call(
        functools.partial(start_kernel, peers), "start", [SMEM, HBM, HBM, HBM, HBM],
        messages + [((slots,), jnp.int32, SMEM)],
        [
            totals, SMEM((spots,), jnp.int32), SMEM((peers,), jnp.int32),
            SMEM(block_cells.shape, jnp.int32), SMEM(block_counts.shape, jnp.int32),
            VMEM(times.shape, F32), VMEM(ray_blocks.shape, BF16), SMEM((peers,), jnp.int32),
            pltpu.SemaphoreType.DMA((3,)), pltpu.SemaphoreType.DMA((pair_count,)),
        ],
        flops, 6 << 20, 60 << 20,
    )(me, block_cells, block_counts, times, ray_blocks)
    arrived = exchange(outgoing)
    target, arrived[0], ray_blocks = call(
        keep_kernel, "keep", [HBM, HBM, HBM],
        [((slots,), jnp.int32, SMEM), messages[0], (ray_blocks.shape, BF16, VMEM)],
        [pltpu.SemaphoreType.DMA((3,))], 0, 8 << 20, 48 << 20,
    )(target, arrived[0], ray_blocks)
    model, beta, *replies, asked = call(
        functools.partial(first_cell_kernel, peers), "cells_first", ins,
        [whole, tile] + messages + [((peers, BS), jnp.int32, SMEM)],
        [VMEM((peers, BS), jnp.int32), pltpu.SemaphoreType.DMA],
        0, 6 << 20,
    )(*arrived)
    models, betas, alphas = [model], [beta], []
    current = times
    for step in range(ITERS):
        fetched = exchange(replies)
        last = step + 1 == ITERS
        made = call(
            functools.partial(pair_kernel, peers), "pairs_last" if last else "pairs",
            [SMEM] + ins + [VMEM, VMEM, VMEM], messages + [tile] + [data] * (not last),
            [VMEM(data[0], F32)] * last + [totals, gathered_blocks], 2 * flops, 8 << 20,
        )(target, *fetched, current, betas[-1], ray_blocks)
        alphas.append(made[peers])
        current = made[-1]
        arrived = exchange(made[:peers])
        if not last:
            model, beta, *replies = call(
                functools.partial(cell_kernel, peers), "cells", [SMEM] + ins + [VMEM] * 3,
                [whole, tile] + messages, (), 0, 8 << 20,
            )(asked, *arrived, models[-1], alphas[-1], betas[-1])
            models.append(model)
            betas.append(beta)
    model, beta, share = call(
        functools.partial(last_cell_kernel, peers), "cells_last", [SMEM] + ins + [VMEM] * 3,
        [whole, tile, ((8, BS), F32, VMEM)], (), 0, 8 << 20,
    )(asked, *arrived, models[-1], alphas[-1], betas[-1])
    betas.append(beta)
    reach, shares = peers, [share]
    while reach > 1:
        share = sum(shares[1:], shares[0])
        low = max(reach // 4, 1)
        shares = [share] + [
            lax.ppermute(share, "pair", [(one, one ^ step) for one in range(peers)])
            for step in range(low, reach, low)
        ]
        reach = low
    scratch = [VMEM(whole[0], F32), pltpu.SemaphoreType.DMA((CHUNKS,))]
    (estimate,) = call(
        estimate_kernel, "estimate", [VMEM] * (3 * ITERS + 1), [(whole[0], F32, HBM)], scratch,
        0, 6 << 20,
    )(*models, *alphas, *betas)
    (model_vec,) = call(
        model_kernel, "model", [VMEM] * (len(shares) + 2), [(whole[0], F32, HBM)], scratch,
        0, 4 << 20,
    )(*shares, beta, model)
    return (estimate.T, model_vec.T)


def solution(mesh):
    return jax.shard_map(
        on_device,
        mesh=mesh,
        in_specs=(
            P(("groups", "pair"), None, None, None),
            P(("groups", "pair"), None),
            P(("groups", "pair")),
            P(("groups", "pair"), None),
        ),
        out_specs=(P(("groups", "pair"), None), P(("groups", "pair"), None)),
        check_vma=False,
    )
```

```python
import functools

import jax
import jax.numpy as jnp
from jax import lax
from jax.experimental import pallas as pl
from jax.experimental.pallas import tpu as pltpu
from jax.sharding import PartitionSpec as P

CELL_DEV = 8192
BCAP = 4
BS = 128
TAIL = 8
ITERS = 2
EPS = 1e-12
F32 = jnp.float32
BF16 = jnp.bfloat16
VMEM = pltpu.VMEM
SMEM = pltpu.SMEM
HBM = pltpu.HBM
CHUNKS = 8


def diagonal(cols):
    shape = (cols, BS)
    return lax.broadcasted_iota(jnp.int32, shape, 0) == lax.broadcasted_iota(jnp.int32, shape, 1)


def squares_tail(squares):
    cols = squares.shape[0]
    total = jnp.sum(squares, axis=1, keepdims=True)
    row = jnp.sum(jnp.where(diagonal(cols), total, 0.0), axis=0, keepdims=True)
    high = row.astype(BF16).astype(F32)
    middle = (row - high).astype(BF16).astype(F32)
    low = row - high - middle
    place = lax.broadcasted_iota(jnp.int32, (TAIL, BS), 0)
    return jnp.where(
        place == 0, high, jnp.where(place == 1, middle, jnp.where(place == 2, low, 0.0))
    )


def norm_of_tails(message_refs, cols):
    summed = sum(message_ref[BCAP * cols :, :].astype(F32) for message_ref in message_refs)
    row = summed[0:1] + summed[1:2] + summed[2:3]
    column = jnp.sum(jnp.where(diagonal(cols), row, 0.0), axis=1, keepdims=True)
    return jnp.broadcast_to(jnp.sqrt(column + EPS), (cols, BS))


def lanes(block):
    return pl.ds(pl.multiple_of(block * BS, BS), BS)


def transposed(data_ref, rays_ref, before, target_ref, total_ref, message_refs):
    pair_count, slot_count = rays_ref.shape[:2]
    cols = data_ref.shape[0]
    spots = len(message_refs) * BCAP

    def clear(index, carry):
        total_ref[index] = jnp.zeros((cols, BS), F32)
        return carry

    lax.fori_loop(0, spots, clear, 0, unroll=8)

    def one_pair(pair, carry):
        before(pair)
        data = data_ref[:, lanes(pair)]
        high = data.astype(BF16)
        low = (data - high.astype(F32)).astype(BF16)
        pieces = jnp.concatenate([high, low], axis=0)
        for slot in range(0, slot_count, 2):
            rays = jnp.concatenate([rays_ref[pair, slot], rays_ref[pair, slot + 1]], axis=1)
            part = jnp.dot(pieces, rays, preferred_element_type=F32)
            part = part[:cols] + part[cols:]
            for half in range(2):
                spot = target_ref[pair * slot_count + slot + half]
                total_ref[spot] += part[:, half * BS : (half + 1) * BS]
        return carry

    lax.fori_loop(0, pair_count, one_pair, 0, unroll=True)

    for peer, message_ref in enumerate(message_refs):
        for rank in range(BCAP):
            message_ref[rank * cols : (rank + 1) * cols, :] = total_ref[
                peer * BCAP + rank
            ].astype(BF16)


def start_kernel(peers, me_ref, cells_hbm, counts_hbm, times_hbm, rays_hbm, *refs):
    message_refs = refs[:peers]
    target_ref, total_ref, table_ref, used_ref, cells_ref, counts_ref = refs[peers : peers + 6]
    times_ref, rays_ref, sems, ray_sems = refs[peers + 6 :]
    pair_count, slot_count = rays_ref.shape[:2]
    cols = times_ref.shape[0]
    owned = CELL_DEV // BS
    copies = [
        pltpu.make_async_copy(source, dest, sems.at[index])
        for index, (source, dest) in enumerate(
            [(cells_hbm, cells_ref), (counts_hbm, counts_ref), (times_hbm, times_ref)]
        )
    ]
    for copy in copies:
        copy.start()

    def ray_copy(pair):
        return pltpu.make_async_copy(rays_hbm.at[pair], rays_ref.at[pair], ray_sems.at[pair])

    def fetch(pair, carry):
        ray_copy(pair).start()
        return carry

    lax.fori_loop(0, pair_count, fetch, 0)

    def clear(peer, carry):
        used_ref[peer] = 0
        for rank in range(BCAP):
            table_ref[peer * BCAP + rank] = 0
        return carry

    lax.fori_loop(0, peers, clear, 0)
    for copy in copies:
        copy.wait()

    def find_places(pair):
        count = counts_ref[pair]
        for slot in range(slot_count):
            cell = cells_ref[pair, slot]
            apart = (cell // owned) ^ me_ref[0]
            owner = apart * 2 - jnp.where(apart < peers // 2, 0, peers - 1)
            local = cell % owned
            used = used_ref[owner]
            rank = used
            for other in range(BCAP - 1, -1, -1):
                same = (table_ref[owner * BCAP + other] == local) & (other < used)
                rank = jnp.where(same, other, rank)
            spot = owner * BCAP + rank
            table_ref[spot] = local
            used_ref[owner] = jnp.maximum(used, rank + 1)
            target_ref[pair * slot_count + slot] = jnp.where(slot < count, spot, peers * BCAP)

    def before(pair):
        find_places(pair)
        ray_copy(pair).wait()

    transposed(times_ref, rays_ref, before, target_ref, total_ref, message_refs)
    squares = jnp.zeros((cols, BS), F32)
    for pair in range(pair_count):
        part = times_ref[:, pair * BS : (pair + 1) * BS]
        squares += part * part
    tail = squares_tail(squares)
    place = lax.broadcasted_iota(jnp.int32, (TAIL, BS), 0)
    lane = lax.broadcasted_iota(jnp.int32, (TAIL, BS), 1)

    for peer, message_ref in enumerate(message_refs):
        rows = tail
        for rank in range(BCAP):
            asked = table_ref[peer * BCAP + rank].astype(F32)
            rows = jnp.where((place == 3) & (lane == rank), asked, rows)
        message_ref[BCAP * cols :, :] = rows.astype(BF16)


def keep_kernel(target_hbm, own_hbm, rays_hbm, target_ref, own_ref, rays_ref, sems):
    copies = [
        pltpu.make_async_copy(source, dest, sems.at[index])
        for index, (source, dest) in enumerate(
            [(target_hbm, target_ref), (own_hbm, own_ref), (rays_hbm, rays_ref)]
        )
    ]
    for copy in copies:
        copy.start()
    for copy in copies:
        copy.wait()


def pair_kernel(peers, target_ref, *refs):
    fetched_refs = refs[:peers]
    data_ref, beta_ref, rays_ref = refs[peers : peers + 3]
    message_refs = refs[peers + 3 : 2 * peers + 3]
    alpha_ref, raw_ref, total_ref, fetched_ref = refs[2 * peers + 3 :]
    pair_count, slot_count = rays_ref.shape[:2]
    cols = data_ref.shape[0]
    spots = peers * BCAP
    for peer in range(peers):
        fetched_ref[peer] = fetched_refs[peer][: BCAP * cols, :]
    alpha = norm_of_tails(fetched_refs, cols)
    alpha_ref[...] = alpha
    beta = beta_ref[...]
    model_scale = 1.0 / (alpha * beta)
    data_scale = alpha / beta

    def one_pair(pair, squares):
        chosen = []
        for slot in range(slot_count):
            spot = target_ref[pair * slot_count + slot]
            live = spot < spots
            spot = jnp.where(live, spot, 0)
            rows = pl.ds(pl.multiple_of((spot % BCAP) * cols, cols), cols)
            block = fetched_ref[spot // BCAP, rows, :]
            chosen.append(jnp.where(live, block, jnp.zeros_like(block)))
        rays = jnp.concatenate([rays_ref[pair, slot] for slot in range(slot_count)], axis=1)
        product = lax.dot_general(
            rays, jnp.concatenate(chosen, axis=1), (((1,), (1,)), ((), ())),
            preferred_element_type=F32,
        )
        raw = product.T * model_scale - data_ref[:, lanes(pair)] * data_scale
        raw_ref[:, lanes(pair)] = raw
        return squares + raw * raw

    squares = lax.fori_loop(0, pair_count, one_pair, jnp.zeros((cols, BS), F32), unroll=True)
    transposed(raw_ref, rays_ref, lambda pair: None, target_ref, total_ref, message_refs)
    tail = squares_tail(squares).astype(BF16)
    for message_ref in message_refs:
        message_ref[BCAP * cols :, :] = tail


def gathered(arrived_refs, first, asked_ref, model_ref):
    cols = model_ref.shape[0]
    for peer, arrived_ref in enumerate(arrived_refs, first):
        for rank in range(BCAP):
            where = lanes(asked_ref[peer, rank])
            model_ref[:, where] += arrived_ref[rank * cols : (rank + 1) * cols, :].astype(F32)


def read_asked(arrived_refs, table_ref, asked_ref, sem):
    for peer, arrived_ref in enumerate(arrived_refs):
        tail = arrived_ref[arrived_ref.shape[0] - TAIL :, :].astype(F32)
        table_ref[peer : peer + 1, :] = tail[3:4].astype(jnp.int32)
    copy = pltpu.make_async_copy(table_ref, asked_ref, sem)
    copy.start()
    return copy


def early_kernel(early, *refs):
    model_ref = refs[-1]
    asked_ref, *arrived_refs = refs[: early + 1]
    model_ref[...] = jnp.zeros(model_ref.shape, F32)
    gathered(arrived_refs, 0, asked_ref, model_ref)


def first_early_kernel(early, *refs):
    arrived_refs = refs[:early]
    model_ref, asked_ref, table_ref, sem = refs[early:]
    copy = read_asked(arrived_refs, table_ref, asked_ref, sem)
    model_ref[...] = jnp.zeros(model_ref.shape, F32)
    copy.wait()
    gathered(arrived_refs, 0, asked_ref, model_ref)


def reply(squares, scale, asked_ref, model_ref, out_refs):
    cols = model_ref.shape[0]
    tail = squares_tail(squares * scale * scale).astype(BF16)
    for peer, out_ref in enumerate(out_refs):
        out_ref[BCAP * cols :, :] = tail
        for rank in range(BCAP):
            block = model_ref[:, lanes(asked_ref[peer, rank])]
            out_ref[rank * cols : (rank + 1) * cols, :] = block.astype(BF16)


def squares_of(model_ref):
    cols, cells = model_ref.shape

    def one_block(block, squares):
        values = model_ref[:, lanes(block)]
        return squares + values * values

    return lax.fori_loop(0, cells // BS, one_block, jnp.zeros((cols, BS), F32), unroll=8)


def first_cell_kernel(peers, early, *refs):
    arrived_refs, sum_ref, refs = refs[:peers], refs[peers], refs[peers + 1 :]
    model_ref, beta_ref, *out_refs = refs[: peers + 2]
    asked_ref, table_ref, sem = refs[peers + 2 :]
    copy = read_asked(arrived_refs, table_ref, asked_ref, sem)
    beta = norm_of_tails(arrived_refs, model_ref.shape[0])
    beta_ref[...] = beta
    model_ref[...] = sum_ref[...]
    copy.wait()
    gathered(arrived_refs[early:], early, asked_ref, model_ref)
    reply(squares_of(model_ref), 1.0 / beta, asked_ref, model_ref, out_refs)


def start_from(sum_ref, before_ref, scale, model_ref):
    def one_block(block, carry):
        where = lanes(block)
        model_ref[:, where] = sum_ref[:, where] - before_ref[:, where] * scale
        return carry

    lax.fori_loop(0, model_ref.shape[1] // BS, one_block, 0, unroll=8)


def cell_kernel(peers, early, asked_ref, *refs):
    arrived_refs, out_refs = refs[:peers], refs[peers + 6 :]
    sum_ref, before_ref, alpha_ref, beta_before_ref, model_ref, beta_ref = refs[
        peers : peers + 6
    ]
    beta = norm_of_tails(arrived_refs, model_ref.shape[0])
    beta_ref[...] = beta
    scale = beta * beta / (alpha_ref[...] * beta_before_ref[...])
    start_from(sum_ref, before_ref, scale, model_ref)
    gathered(arrived_refs[early:], early, asked_ref, model_ref)
    reply(squares_of(model_ref), 1.0 / beta, asked_ref, model_ref, out_refs)


def last_cell_kernel(peers, early, asked_ref, *refs):
    arrived_refs = refs[:peers]
    sum_ref, before_ref, alpha_ref, beta_before_ref, model_ref, beta_ref, out_ref = refs[peers:]
    beta = norm_of_tails(arrived_refs, model_ref.shape[0])
    beta_ref[...] = beta
    scale = beta * beta / (alpha_ref[...] * beta_before_ref[...])
    start_from(sum_ref, before_ref, scale, model_ref)
    gathered(arrived_refs[early:], early, asked_ref, model_ref)
    squares = squares_of(model_ref) / (beta * beta)
    total = jnp.sum(squares, axis=1, keepdims=True)
    row = jnp.sum(jnp.where(diagonal(total.shape[0]), total, 0.0), axis=0, keepdims=True)
    out_ref[...] = jnp.broadcast_to(row, out_ref.shape)


def estimate_kernel(*refs):
    models = refs[:ITERS]
    alphas = [ref[...] for ref in refs[ITERS : 2 * ITERS]]
    betas = [ref[...] for ref in refs[2 * ITERS : 3 * ITERS + 1]]
    estimate_hbm, estimate_ref, sems = refs[3 * ITERS + 1 :]
    cells = estimate_ref.shape[1]
    weights = estimate_weights(betas, alphas)
    blocks = cells // BS // CHUNKS

    def one_block(block, carry):
        where = lanes(block)
        total = weights[0] * models[0][:, where]
        for i in range(1, ITERS):
            total += weights[i] * models[i][:, where]
        estimate_ref[:, where] = total
        return carry

    copies = []
    for chunk in range(CHUNKS):
        lax.fori_loop(chunk * blocks, (chunk + 1) * blocks, one_block, 0, unroll=4)
        where = slice(chunk * blocks * BS, (chunk + 1) * blocks * BS)
        copies.append(
            pltpu.make_async_copy(
                estimate_ref.at[:, where], estimate_hbm.at[:, where], sems.at[chunk]
            )
        )
        copies[-1].start()
    for copy in copies:
        copy.wait()


def estimate_weights(betas, alphas):
    phi_bar = betas[0]
    rho_bar = alphas[0]
    trace = [1.0 / (alphas[0] * betas[0])]
    weight = [jnp.zeros_like(phi_bar)] * ITERS
    for step in range(ITERS):
        beta = betas[step + 1]
        rho = jnp.sqrt(rho_bar * rho_bar + beta * beta)
        cosine = rho_bar / rho
        sine = beta / rho
        gain = cosine * phi_bar / rho
        weight = [
            weight[i] + gain * trace[i] if i < len(trace) else weight[i] for i in range(ITERS)
        ]
        if step + 1 < ITERS:
            alpha = alphas[step + 1]
            theta = sine * alpha
            rho_bar = -cosine * alpha
            phi_bar = sine * phi_bar
            trace = [-(theta / rho) * value for value in trace] + [1.0 / (alpha * beta)]
    return weight


def model_kernel(*refs):
    *share_refs, beta_ref, model_ref, out_hbm, out_ref, sems = refs
    cols, cells = model_ref.shape
    blocks = cells // BS // CHUNKS
    row = sum(ref[...] for ref in share_refs)[0:1]
    column = jnp.sum(jnp.where(diagonal(cols), row, 0.0), axis=1, keepdims=True)
    alpha = jnp.broadcast_to(jnp.sqrt(column + EPS), (cols, BS))
    scale = 1.0 / (alpha * beta_ref[...])

    def one_block(block, carry):
        out_ref[:, lanes(block)] = model_ref[:, lanes(block)] * scale
        return carry

    copies = []
    for chunk in range(CHUNKS):
        lax.fori_loop(chunk * blocks, (chunk + 1) * blocks, one_block, 0, unroll=4)
        where = slice(chunk * blocks * BS, (chunk + 1) * blocks * BS)
        copies.append(
            pltpu.make_async_copy(out_ref.at[:, where], out_hbm.at[:, where], sems.at[chunk])
        )
        copies[-1].start()
    for copy in copies:
        copy.wait()


def call(kernel, name, in_spaces, outs, scratch=(), flops=0, moved=0, limit=16 << 20):
    return pl.pallas_call(
        kernel,
        name=name,
        in_specs=[pl.BlockSpec(memory_space=space) for space in in_spaces],
        out_specs=[pl.BlockSpec(memory_space=space) for _, _, space in outs],
        out_shape=[jax.ShapeDtypeStruct(shape, dtype) for shape, dtype, _ in outs],
        scratch_shapes=list(scratch),
        compiler_params=pltpu.CompilerParams(vmem_limit_bytes=limit),
        cost_estimate=pl.CostEstimate(flops=flops, bytes_accessed=moved, transcendentals=0),
    )


def on_device(ray_blocks, block_cells, block_counts, travel_times):
    pair_count, slot_count = ray_blocks.shape[:2]
    slots = pair_count * slot_count
    peers = lax.axis_size("pair")
    spots = peers * BCAP
    times = travel_times.T
    cols, pairs = times.shape
    messages = [((BCAP * cols + TAIL, BS), BF16, VMEM)] * peers
    ins = [VMEM] * peers
    gathered_blocks = VMEM((peers, BCAP * cols, BS), BF16)
    tile = ((cols, BS), F32, VMEM)
    data = ((cols, pairs), F32, VMEM)
    whole = ((cols, CELL_DEV), F32, VMEM)
    totals = VMEM((spots + 1, cols, BS), F32)
    flops = 2 * slots * BS * BS * cols

    def exchange(values):
        half = peers // 2
        steps = [i // 2 + i % 2 * half for i in range(peers)]
        return [values[0]] + [
            lax.ppermute(value, "pair", [(one, one ^ step) for one in range(peers)])
            for value, step in zip(values[1:], steps[1:])
        ]

    me = lax.axis_index("pair").astype(jnp.int32).reshape(1)
    *outgoing, target = call(
        functools.partial(start_kernel, peers), "start", [SMEM, HBM, HBM, HBM, HBM],
        messages + [((slots,), jnp.int32, SMEM)],
        [
            totals, SMEM((spots,), jnp.int32), SMEM((peers,), jnp.int32),
            SMEM(block_cells.shape, jnp.int32), SMEM(block_counts.shape, jnp.int32),
            VMEM(times.shape, F32), VMEM(ray_blocks.shape, BF16),
            pltpu.SemaphoreType.DMA((3,)), pltpu.SemaphoreType.DMA((pair_count,)),
        ],
        flops, 6 << 20, 60 << 20,
    )(me, block_cells, block_counts, times, ray_blocks)
    arrived = exchange(outgoing)
    target, arrived[0], ray_blocks = call(
        keep_kernel, "keep", [HBM, HBM, HBM],
        [((slots,), jnp.int32, SMEM), messages[0], (ray_blocks.shape, BF16, VMEM)],
        [pltpu.SemaphoreType.DMA((3,))], 0, 8 << 20, 48 << 20,
    )(target, arrived[0], ray_blocks)
    early = max(peers - 5, 1)
    (summed,) = call(
        functools.partial(first_early_kernel, early), "early_first", [VMEM] * early, [whole],
        [SMEM((early, BS), jnp.int32), VMEM((early, BS), jnp.int32), pltpu.SemaphoreType.DMA],
        0, 4 << 20,
    )(*arrived[:early])
    model, beta, *replies, asked = call(
        functools.partial(first_cell_kernel, peers, early), "cells_first", ins + [VMEM],
        [whole, tile] + messages + [((peers, BS), jnp.int32, SMEM)],
        [VMEM((peers, BS), jnp.int32), pltpu.SemaphoreType.DMA],
        0, 6 << 20,
    )(*arrived, summed)
    models, betas, alphas = [model], [beta], []
    current = times
    for step in range(ITERS):
        fetched = exchange(replies)
        last = step + 1 == ITERS
        made = call(
            functools.partial(pair_kernel, peers), "pairs_last" if last else "pairs",
            [SMEM] + ins + [VMEM, VMEM, VMEM], messages + [tile] + [data] * (not last),
            [VMEM(data[0], F32)] * last + [totals, gathered_blocks], 2 * flops, 8 << 20,
        )(target, *fetched, current, betas[-1], ray_blocks)
        alphas.append(made[peers])
        current = made[-1]
        arrived = exchange(made[:peers])
        (summed,) = call(
            functools.partial(early_kernel, early), "early", [SMEM] + [VMEM] * early, [whole],
            (), 0, 4 << 20,
        )(asked, *arrived[:early])
        if not last:
            model, beta, *replies = call(
                functools.partial(cell_kernel, peers, early), "cells", [SMEM] + ins + [VMEM] * 4,
                [whole, tile] + messages, (), 0, 8 << 20,
            )(asked, *arrived, summed, models[-1], alphas[-1], betas[-1])
            models.append(model)
            betas.append(beta)
    model, beta, share = call(
        functools.partial(last_cell_kernel, peers, early), "cells_last",
        [SMEM] + ins + [VMEM] * 4, [whole, tile, ((8, BS), F32, VMEM)], (), 0, 8 << 20,
    )(asked, *arrived, summed, models[-1], alphas[-1], betas[-1])
    betas.append(beta)
    scratch = [VMEM(whole[0], F32), pltpu.SemaphoreType.DMA((CHUNKS,))]
    (estimate,) = call(
        estimate_kernel, "estimate", [VMEM] * (3 * ITERS + 1), [(whole[0], F32, HBM)], scratch,
        0, 6 << 20,
    )(*models, *alphas, *betas)
    reach, shares = peers, [share]
    while reach > 1:
        share = sum(shares[1:], shares[0])
        if reach < peers:
            share, estimate = lax.optimization_barrier((share, estimate))
        low = max(reach // 4, 1)
        shares = [share] + [
            lax.ppermute(share, "pair", [(one, one ^ step) for one in range(peers)])
            for step in range(low, reach, low)
        ]
        reach = low
    (model_vec,) = call(
        model_kernel, "model", [VMEM] * (len(shares) + 2), [(whole[0], F32, HBM)], scratch,
        0, 4 << 20,
    )(*shares, beta, model)
    return (estimate.T, model_vec.T)


def solution(mesh):
    return jax.shard_map(
        on_device,
        mesh=mesh,
        in_specs=(
            P(("groups", "pair"), None, None, None),
            P(("groups", "pair"), None),
            P(("groups", "pair")),
            P(("groups", "pair"), None),
        ),
        out_specs=(P(("groups", "pair"), None), P(("groups", "pair"), None)),
        check_vma=False,
    )
```

```python
import functools

import jax
import jax.numpy as jnp
from jax import lax
from jax.experimental import pallas as pl
from jax.experimental.pallas import tpu as pltpu
from jax.sharding import PartitionSpec as P

CELL_DEV = 8192
BCAP = 4
BS = 128
TAIL = 8
ITERS = 2
EPS = 1e-12
F32 = jnp.float32
BF16 = jnp.bfloat16
VMEM = pltpu.VMEM
SMEM = pltpu.SMEM
HBM = pltpu.HBM
CHUNKS = 8


def pairs_of(peers):
    half = peers // 2
    return [(half + step, step) for step in range(1, half)]


def diagonal(cols):
    shape = (cols, BS)
    return lax.broadcasted_iota(jnp.int32, shape, 0) == lax.broadcasted_iota(jnp.int32, shape, 1)


def squares_tail(squares):
    cols = squares.shape[0]
    total = jnp.sum(squares, axis=1, keepdims=True)
    row = jnp.sum(jnp.where(diagonal(cols), total, 0.0), axis=0, keepdims=True)
    high = row.astype(BF16).astype(F32)
    middle = (row - high).astype(BF16).astype(F32)
    low = row - high - middle
    place = lax.broadcasted_iota(jnp.int32, (TAIL, BS), 0)
    return jnp.where(
        place == 0, high, jnp.where(place == 1, middle, jnp.where(place == 2, low, 0.0))
    )


def norm_of_tails(message_refs, cols):
    summed = sum(message_ref[BCAP * cols :, :].astype(F32) for message_ref in message_refs)
    row = summed[0:1] + summed[1:2] + summed[2:3]
    column = jnp.sum(jnp.where(diagonal(cols), row, 0.0), axis=1, keepdims=True)
    return jnp.broadcast_to(jnp.sqrt(column + EPS), (cols, BS))


def lanes(block):
    return pl.ds(pl.multiple_of(block * BS, BS), BS)


def transposed(data_ref, rays_ref, before, target_ref, total_ref, message_refs):
    pair_count, slot_count = rays_ref.shape[:2]
    cols = data_ref.shape[0]
    spots = len(message_refs) * BCAP

    def clear(index, carry):
        total_ref[index] = jnp.zeros((cols, BS), F32)
        return carry

    lax.fori_loop(0, spots, clear, 0, unroll=8)

    def one_pair(pair, carry):
        before(pair)
        data = data_ref[:, lanes(pair)]
        high = data.astype(BF16)
        low = (data - high.astype(F32)).astype(BF16)
        pieces = jnp.concatenate([high, low], axis=0)
        for slot in range(0, slot_count, 2):
            rays = jnp.concatenate([rays_ref[pair, slot], rays_ref[pair, slot + 1]], axis=1)
            part = jnp.dot(pieces, rays, preferred_element_type=F32)
            part = part[:cols] + part[cols:]
            for half in range(2):
                spot = target_ref[pair * slot_count + slot + half]
                total_ref[spot] += part[:, half * BS : (half + 1) * BS]
        return carry

    lax.fori_loop(0, pair_count, one_pair, 0, unroll=True)

    for peer, message_ref in enumerate(message_refs):
        for rank in range(BCAP):
            message_ref[rank * cols : (rank + 1) * cols, :] = total_ref[
                peer * BCAP + rank
            ].astype(BF16)


def start_kernel(peers, me_ref, cells_hbm, counts_hbm, times_hbm, rays_hbm, *refs):
    message_refs = refs[:peers]
    target_ref, total_ref, table_ref, used_ref, cells_ref, counts_ref = refs[peers : peers + 6]
    times_ref, rays_ref, place_ref, sems, ray_sems = refs[peers + 6 :]
    me = me_ref[0]
    core = me % 2
    place_ref[me] = 0
    place_ref[me ^ (peers // 2)] = 1
    for index, (far, near) in enumerate(pairs_of(peers), 1):
        place_ref[me ^ far] = 2 * index + core
        place_ref[me ^ near] = 2 * index + 1 - core
    pair_count, slot_count = rays_ref.shape[:2]
    cols = times_ref.shape[0]
    owned = CELL_DEV // BS
    copies = [
        pltpu.make_async_copy(source, dest, sems.at[index])
        for index, (source, dest) in enumerate(
            [(cells_hbm, cells_ref), (counts_hbm, counts_ref), (times_hbm, times_ref)]
        )
    ]
    for copy in copies:
        copy.start()

    def ray_copy(pair):
        return pltpu.make_async_copy(rays_hbm.at[pair], rays_ref.at[pair], ray_sems.at[pair])

    def fetch(pair, carry):
        ray_copy(pair).start()
        return carry

    lax.fori_loop(0, pair_count, fetch, 0)

    def clear(peer, carry):
        used_ref[peer] = 0
        for rank in range(BCAP):
            table_ref[peer * BCAP + rank] = 0
        return carry

    lax.fori_loop(0, peers, clear, 0)
    for copy in copies:
        copy.wait()

    def find_places(pair):
        count = counts_ref[pair]
        for slot in range(slot_count):
            cell = cells_ref[pair, slot]
            owner = place_ref[cell // owned]
            local = cell % owned
            used = used_ref[owner]
            rank = used
            for other in range(BCAP - 1, -1, -1):
                same = (table_ref[owner * BCAP + other] == local) & (other < used)
                rank = jnp.where(same, other, rank)
            spot = owner * BCAP + rank
            table_ref[spot] = local
            used_ref[owner] = jnp.maximum(used, rank + 1)
            target_ref[pair * slot_count + slot] = jnp.where(slot < count, spot, peers * BCAP)

    def before(pair):
        find_places(pair)
        ray_copy(pair).wait()

    transposed(times_ref, rays_ref, before, target_ref, total_ref, message_refs)
    squares = jnp.zeros((cols, BS), F32)
    for pair in range(pair_count):
        part = times_ref[:, pair * BS : (pair + 1) * BS]
        squares += part * part
    tail = squares_tail(squares)
    place = lax.broadcasted_iota(jnp.int32, (TAIL, BS), 0)
    lane = lax.broadcasted_iota(jnp.int32, (TAIL, BS), 1)

    for peer, message_ref in enumerate(message_refs):
        rows = tail
        for rank in range(BCAP):
            asked = table_ref[peer * BCAP + rank].astype(F32)
            rows = jnp.where((place == 3) & (lane == rank), asked, rows)
        message_ref[BCAP * cols :, :] = rows.astype(BF16)


def keep_kernel(target_hbm, own_hbm, rays_hbm, target_ref, own_ref, rays_ref, sems):
    copies = [
        pltpu.make_async_copy(source, dest, sems.at[index])
        for index, (source, dest) in enumerate(
            [(target_hbm, target_ref), (own_hbm, own_ref), (rays_hbm, rays_ref)]
        )
    ]
    for copy in copies:
        copy.start()
    for copy in copies:
        copy.wait()


def pair_kernel(peers, target_ref, *refs):
    fetched_refs = refs[:peers]
    data_ref, beta_ref, rays_ref = refs[peers : peers + 3]
    message_refs = refs[peers + 3 : 2 * peers + 3]
    alpha_ref, raw_ref, total_ref, fetched_ref = refs[2 * peers + 3 :]
    pair_count, slot_count = rays_ref.shape[:2]
    cols = data_ref.shape[0]
    spots = peers * BCAP
    for peer in range(peers):
        fetched_ref[peer] = fetched_refs[peer][: BCAP * cols, :]
    alpha = norm_of_tails(fetched_refs, cols)
    alpha_ref[...] = alpha
    beta = beta_ref[...]
    model_scale = 1.0 / (alpha * beta)
    data_scale = alpha / beta

    def one_pair(pair, squares):
        chosen = []
        for slot in range(slot_count):
            spot = target_ref[pair * slot_count + slot]
            live = spot < spots
            spot = jnp.where(live, spot, 0)
            rows = pl.ds(pl.multiple_of((spot % BCAP) * cols, cols), cols)
            block = fetched_ref[spot // BCAP, rows, :]
            chosen.append(jnp.where(live, block, jnp.zeros_like(block)))
        rays = jnp.concatenate([rays_ref[pair, slot] for slot in range(slot_count)], axis=1)
        product = lax.dot_general(
            rays, jnp.concatenate(chosen, axis=1), (((1,), (1,)), ((), ())),
            preferred_element_type=F32,
        )
        raw = product.T * model_scale - data_ref[:, lanes(pair)] * data_scale
        raw_ref[:, lanes(pair)] = raw
        return squares + raw * raw

    squares = lax.fori_loop(0, pair_count, one_pair, jnp.zeros((cols, BS), F32), unroll=True)
    transposed(raw_ref, rays_ref, lambda pair: None, target_ref, total_ref, message_refs)
    tail = squares_tail(squares).astype(BF16)
    for message_ref in message_refs:
        message_ref[BCAP * cols :, :] = tail


def gathered(arrived_refs, asked_ref, model_ref):
    cols = model_ref.shape[0]
    for peer, arrived_ref in enumerate(arrived_refs):
        for rank in range(BCAP):
            where = lanes(asked_ref[peer, rank])
            model_ref[:, where] += arrived_ref[rank * cols : (rank + 1) * cols, :].astype(F32)


def reply(squares, scale, asked_ref, model_ref, out_refs):
    cols = model_ref.shape[0]
    tail = squares_tail(squares * scale * scale).astype(BF16)
    for peer, out_ref in enumerate(out_refs):
        out_ref[BCAP * cols :, :] = tail
        for rank in range(BCAP):
            block = model_ref[:, lanes(asked_ref[peer, rank])]
            out_ref[rank * cols : (rank + 1) * cols, :] = block.astype(BF16)


def squares_of(model_ref):
    cols, cells = model_ref.shape

    def one_block(block, squares):
        values = model_ref[:, lanes(block)]
        return squares + values * values

    return lax.fori_loop(0, cells // BS, one_block, jnp.zeros((cols, BS), F32), unroll=8)


def first_cell_kernel(peers, *refs):
    arrived_refs, out_refs = refs[:peers], refs[peers + 2 : 2 * peers + 2]
    model_ref, beta_ref = refs[peers : peers + 2]
    asked_ref, table_ref, sem = refs[2 * peers + 2 :]
    cols, cells = model_ref.shape
    for peer in range(peers):
        tail = arrived_refs[peer][BCAP * cols :, :].astype(F32)
        table_ref[peer : peer + 1, :] = tail[3:4].astype(jnp.int32)
    copy = pltpu.make_async_copy(table_ref, asked_ref, sem)
    copy.start()
    beta = norm_of_tails(arrived_refs, cols)
    beta_ref[...] = beta
    model_ref[...] = jnp.zeros((cols, cells), F32)
    copy.wait()
    gathered(arrived_refs, asked_ref, model_ref)
    reply(squares_of(model_ref), 1.0 / beta, asked_ref, model_ref, out_refs)


def start_from(before_ref, scale, model_ref):
    def one_block(block, carry):
        model_ref[:, lanes(block)] = before_ref[:, lanes(block)] * -scale
        return carry

    lax.fori_loop(0, model_ref.shape[1] // BS, one_block, 0, unroll=8)


def cell_kernel(peers, asked_ref, *refs):
    arrived_refs, out_refs = refs[:peers], refs[peers + 5 :]
    before_ref, alpha_ref, beta_before_ref, model_ref, beta_ref = refs[peers : peers + 5]
    beta = norm_of_tails(arrived_refs, model_ref.shape[0])
    beta_ref[...] = beta
    start_from(before_ref, beta * beta / (alpha_ref[...] * beta_before_ref[...]), model_ref)
    gathered(arrived_refs, asked_ref, model_ref)
    reply(squares_of(model_ref), 1.0 / beta, asked_ref, model_ref, out_refs)


def last_cell_kernel(peers, asked_ref, *refs):
    arrived_refs = refs[:peers]
    before_ref, alpha_ref, beta_before_ref, model_ref, beta_ref, out_ref = refs[peers:]
    beta = norm_of_tails(arrived_refs, model_ref.shape[0])
    beta_ref[...] = beta
    start_from(before_ref, beta * beta / (alpha_ref[...] * beta_before_ref[...]), model_ref)
    gathered(arrived_refs, asked_ref, model_ref)
    squares = squares_of(model_ref) / (beta * beta)
    total = jnp.sum(squares, axis=1, keepdims=True)
    row = jnp.sum(jnp.where(diagonal(total.shape[0]), total, 0.0), axis=0, keepdims=True)
    out_ref[...] = jnp.broadcast_to(row, out_ref.shape)


def estimate_kernel(*refs):
    models = refs[:ITERS]
    alphas = [ref[...] for ref in refs[ITERS : 2 * ITERS]]
    betas = [ref[...] for ref in refs[2 * ITERS : 3 * ITERS + 1]]
    estimate_hbm, estimate_ref, sems = refs[3 * ITERS + 1 :]
    cells = estimate_ref.shape[1]
    weights = estimate_weights(betas, alphas)
    blocks = cells // BS // CHUNKS

    def one_block(block, carry):
        where = lanes(block)
        total = weights[0] * models[0][:, where]
        for i in range(1, ITERS):
            total += weights[i] * models[i][:, where]
        estimate_ref[:, where] = total
        return carry

    copies = []
    for chunk in range(CHUNKS):
        lax.fori_loop(chunk * blocks, (chunk + 1) * blocks, one_block, 0, unroll=4)
        where = slice(chunk * blocks * BS, (chunk + 1) * blocks * BS)
        copies.append(
            pltpu.make_async_copy(
                estimate_ref.at[:, where], estimate_hbm.at[:, where], sems.at[chunk]
            )
        )
        copies[-1].start()
    for copy in copies:
        copy.wait()


def estimate_weights(betas, alphas):
    phi_bar = betas[0]
    rho_bar = alphas[0]
    trace = [1.0 / (alphas[0] * betas[0])]
    weight = [jnp.zeros_like(phi_bar)] * ITERS
    for step in range(ITERS):
        beta = betas[step + 1]
        rho = jnp.sqrt(rho_bar * rho_bar + beta * beta)
        cosine = rho_bar / rho
        sine = beta / rho
        gain = cosine * phi_bar / rho
        weight = [
            weight[i] + gain * trace[i] if i < len(trace) else weight[i] for i in range(ITERS)
        ]
        if step + 1 < ITERS:
            alpha = alphas[step + 1]
            theta = sine * alpha
            rho_bar = -cosine * alpha
            phi_bar = sine * phi_bar
            trace = [-(theta / rho) * value for value in trace] + [1.0 / (alpha * beta)]
    return weight


def model_kernel(*refs):
    *share_refs, beta_ref, model_ref, out_hbm, out_ref, sems = refs
    cols, cells = model_ref.shape
    blocks = cells // BS // CHUNKS
    row = sum(ref[...] for ref in share_refs)[0:1]
    column = jnp.sum(jnp.where(diagonal(cols), row, 0.0), axis=1, keepdims=True)
    alpha = jnp.broadcast_to(jnp.sqrt(column + EPS), (cols, BS))
    scale = 1.0 / (alpha * beta_ref[...])

    def one_block(block, carry):
        out_ref[:, lanes(block)] = model_ref[:, lanes(block)] * scale
        return carry

    copies = []
    for chunk in range(CHUNKS):
        lax.fori_loop(chunk * blocks, (chunk + 1) * blocks, one_block, 0, unroll=4)
        where = slice(chunk * blocks * BS, (chunk + 1) * blocks * BS)
        copies.append(
            pltpu.make_async_copy(out_ref.at[:, where], out_hbm.at[:, where], sems.at[chunk])
        )
        copies[-1].start()
    for copy in copies:
        copy.wait()


def call(kernel, name, in_spaces, outs, scratch=(), flops=0, moved=0, limit=16 << 20):
    return pl.pallas_call(
        kernel,
        name=name,
        in_specs=[pl.BlockSpec(memory_space=space) for space in in_spaces],
        out_specs=[pl.BlockSpec(memory_space=space) for _, _, space in outs],
        out_shape=[jax.ShapeDtypeStruct(shape, dtype) for shape, dtype, _ in outs],
        scratch_shapes=list(scratch),
        compiler_params=pltpu.CompilerParams(vmem_limit_bytes=limit),
        cost_estimate=pl.CostEstimate(flops=flops, bytes_accessed=moved, transcendentals=0),
    )


def on_device(ray_blocks, block_cells, block_counts, travel_times):
    pair_count, slot_count = ray_blocks.shape[:2]
    slots = pair_count * slot_count
    peers = lax.axis_size("pair")
    spots = peers * BCAP
    times = travel_times.T
    cols, pairs = times.shape
    messages = [((BCAP * cols + TAIL, BS), BF16, VMEM)] * peers
    ins = [VMEM] * peers
    gathered_blocks = VMEM((peers, BCAP * cols, BS), BF16)
    tile = ((cols, BS), F32, VMEM)
    data = ((cols, pairs), F32, VMEM)
    whole = ((cols, CELL_DEV), F32, VMEM)
    totals = VMEM((spots + 1, cols, BS), F32)
    flops = 2 * slots * BS * BS * cols

    def send(value, steps):
        return lax.ppermute(value, "pair", [(i, i ^ steps[i % 2]) for i in range(peers)])

    def exchange(values):
        back = [values[0], send(values[1], (peers // 2, peers // 2))]
        for index, (far, near) in enumerate(pairs_of(peers), 1):
            two = [
                send(values[2 * index], (far, near)), send(values[2 * index + 1], (near, far))
            ]
            back += two[::-1] if far % 2 else two
        return back

    me = lax.axis_index("pair").astype(jnp.int32).reshape(1)
    *outgoing, target = call(
        functools.partial(start_kernel, peers), "start", [SMEM, HBM, HBM, HBM, HBM],
        messages + [((slots,), jnp.int32, SMEM)],
        [
            totals, SMEM((spots,), jnp.int32), SMEM((peers,), jnp.int32),
            SMEM(block_cells.shape, jnp.int32), SMEM(block_counts.shape, jnp.int32),
            VMEM(times.shape, F32), VMEM(ray_blocks.shape, BF16), SMEM((peers,), jnp.int32),
            pltpu.SemaphoreType.DMA((3,)), pltpu.SemaphoreType.DMA((pair_count,)),
        ],
        flops, 6 << 20, 60 << 20,
    )(me, block_cells, block_counts, times, ray_blocks)
    arrived = exchange(outgoing)
    target, arrived[0], ray_blocks = call(
        keep_kernel, "keep", [HBM, HBM, HBM],
        [((slots,), jnp.int32, SMEM), messages[0], (ray_blocks.shape, BF16, VMEM)],
        [pltpu.SemaphoreType.DMA((3,))], 0, 8 << 20, 48 << 20,
    )(target, arrived[0], ray_blocks)
    model, beta, *replies, asked = call(
        functools.partial(first_cell_kernel, peers), "cells_first", ins,
        [whole, tile] + messages + [((peers, BS), jnp.int32, SMEM)],
        [VMEM((peers, BS), jnp.int32), pltpu.SemaphoreType.DMA],
        0, 6 << 20,
    )(*arrived)
    models, betas, alphas = [model], [beta], []
    current = times
    for step in range(ITERS):
        fetched = exchange(replies)
        last = step + 1 == ITERS
        made = call(
            functools.partial(pair_kernel, peers), "pairs_last" if last else "pairs",
            [SMEM] + ins + [VMEM, VMEM, VMEM], messages + [tile] + [data] * (not last),
            [VMEM(data[0], F32)] * last + [totals, gathered_blocks], 2 * flops, 8 << 20,
        )(target, *fetched, current, betas[-1], ray_blocks)
        alphas.append(made[peers])
        current = made[-1]
        arrived = exchange(made[:peers])
        if not last:
            model, beta, *replies = call(
                functools.partial(cell_kernel, peers), "cells", [SMEM] + ins + [VMEM] * 3,
                [whole, tile] + messages, (), 0, 8 << 20,
            )(asked, *arrived, models[-1], alphas[-1], betas[-1])
            models.append(model)
            betas.append(beta)
    model, beta, share = call(
        functools.partial(last_cell_kernel, peers), "cells_last", [SMEM] + ins + [VMEM] * 3,
        [whole, tile, ((8, BS), F32, VMEM)], (), 0, 8 << 20,
    )(asked, *arrived, models[-1], alphas[-1], betas[-1])
    betas.append(beta)
    reach, shares = peers, [share]
    while reach > 1:
        share = sum(shares[1:], shares[0])
        low = max(reach // 4, 1)
        shares = [share] + [
            lax.ppermute(share, "pair", [(one, one ^ step) for one in range(peers)])
            for step in range(low, reach, low)
        ]
        reach = low
    scratch = [VMEM(whole[0], F32), pltpu.SemaphoreType.DMA((CHUNKS,))]
    (estimate,) = call(
        estimate_kernel, "estimate", [VMEM] * (3 * ITERS + 1), [(whole[0], F32, HBM)], scratch,
        0, 6 << 20,
    )(*models, *alphas, *betas)
    (model_vec,) = call(
        model_kernel, "model", [VMEM] * (len(shares) + 2), [(whole[0], F32, HBM)], scratch,
        0, 4 << 20,
    )(*shares, beta, model)
    return (estimate.T, model_vec.T)


def solution(mesh):
    return jax.shard_map(
        on_device,
        mesh=mesh,
        in_specs=(
            P(("groups", "pair"), None, None, None),
            P(("groups", "pair"), None),
            P(("groups", "pair")),
            P(("groups", "pair"), None),
        ),
        out_specs=(P(("groups", "pair"), None), P(("groups", "pair"), None)),
        check_vma=False,
    )
```

```python
import functools

import jax
import jax.numpy as jnp
from jax import lax
from jax.experimental import pallas as pl
from jax.experimental.pallas import tpu as pltpu
from jax.sharding import PartitionSpec as P

CELL_DEV = 8192
BCAP = 4
BS = 128
TAIL = 8
ITERS = 2
EPS = 1e-12
F32 = jnp.float32
BF16 = jnp.bfloat16
VMEM = pltpu.VMEM
SMEM = pltpu.SMEM
HBM = pltpu.HBM
CHUNKS = 8


def steps_of(peers):
    half, quarter = peers // 2, peers // 4
    near = [step for low in range(quarter) for step in (low, quarter + low)][1:]
    return [0, half] + [step for low in near for step in (low, half + low)]


def diagonal(cols):
    shape = (cols, BS)
    return lax.broadcasted_iota(jnp.int32, shape, 0) == lax.broadcasted_iota(jnp.int32, shape, 1)


def squares_tail(squares):
    cols = squares.shape[0]
    total = jnp.sum(squares, axis=1, keepdims=True)
    row = jnp.sum(jnp.where(diagonal(cols), total, 0.0), axis=0, keepdims=True)
    high = row.astype(BF16).astype(F32)
    middle = (row - high).astype(BF16).astype(F32)
    low = row - high - middle
    place = lax.broadcasted_iota(jnp.int32, (TAIL, BS), 0)
    return jnp.where(
        place == 0, high, jnp.where(place == 1, middle, jnp.where(place == 2, low, 0.0))
    )


def norm_of_tails(message_refs, cols):
    summed = sum(message_ref[BCAP * cols :, :].astype(F32) for message_ref in message_refs)
    row = summed[0:1] + summed[1:2] + summed[2:3]
    column = jnp.sum(jnp.where(diagonal(cols), row, 0.0), axis=1, keepdims=True)
    return jnp.broadcast_to(jnp.sqrt(column + EPS), (cols, BS))


def lanes(block):
    return pl.ds(pl.multiple_of(block * BS, BS), BS)


def transposed(data_ref, rays_ref, before, target_ref, total_ref, message_refs):
    pair_count, slot_count = rays_ref.shape[:2]
    cols = data_ref.shape[0]
    spots = len(message_refs) * BCAP

    def clear(index, carry):
        total_ref[index] = jnp.zeros((cols, BS), F32)
        return carry

    lax.fori_loop(0, spots, clear, 0, unroll=8)

    def one_pair(pair, carry):
        before(pair)
        data = data_ref[:, lanes(pair)]
        high = data.astype(BF16)
        low = (data - high.astype(F32)).astype(BF16)
        pieces = jnp.concatenate([high, low], axis=0)
        for slot in range(0, slot_count, 2):
            rays = jnp.concatenate([rays_ref[pair, slot], rays_ref[pair, slot + 1]], axis=1)
            part = jnp.dot(pieces, rays, preferred_element_type=F32)
            part = part[:cols] + part[cols:]
            for half in range(2):
                spot = target_ref[pair * slot_count + slot + half]
                total_ref[spot] += part[:, half * BS : (half + 1) * BS]
        return carry

    lax.fori_loop(0, pair_count, one_pair, 0, unroll=True)

    for peer, message_ref in enumerate(message_refs):
        for rank in range(BCAP):
            message_ref[rank * cols : (rank + 1) * cols, :] = total_ref[
                peer * BCAP + rank
            ].astype(BF16)


def start_kernel(peers, me_ref, cells_hbm, counts_hbm, times_hbm, rays_hbm, *refs):
    message_refs = refs[:peers]
    target_ref, total_ref, table_ref, used_ref, cells_ref, counts_ref = refs[peers : peers + 6]
    times_ref, rays_ref, place_ref, sems, ray_sems = refs[peers + 6 :]
    for index, step in enumerate(steps_of(peers)):
        place_ref[me_ref[0] ^ step] = index
    pair_count, slot_count = rays_ref.shape[:2]
    cols = times_ref.shape[0]
    owned = CELL_DEV // BS
    copies = [
        pltpu.make_async_copy(source, dest, sems.at[index])
        for index, (source, dest) in enumerate(
            [(cells_hbm, cells_ref), (counts_hbm, counts_ref), (times_hbm, times_ref)]
        )
    ]
    for copy in copies:
        copy.start()

    def ray_copy(pair):
        return pltpu.make_async_copy(rays_hbm.at[pair], rays_ref.at[pair], ray_sems.at[pair])

    def fetch(pair, carry):
        ray_copy(pair).start()
        return carry

    lax.fori_loop(0, pair_count, fetch, 0)

    def clear(peer, carry):
        used_ref[peer] = 0
        for rank in range(BCAP):
            table_ref[peer * BCAP + rank] = 0
        return carry

    lax.fori_loop(0, peers, clear, 0)
    for copy in copies:
        copy.wait()

    def find_places(pair):
        count = counts_ref[pair]
        for slot in range(slot_count):
            cell = cells_ref[pair, slot]
            owner = place_ref[cell // owned]
            local = cell % owned
            used = used_ref[owner]
            rank = used
            for other in range(BCAP - 1, -1, -1):
                same = (table_ref[owner * BCAP + other] == local) & (other < used)
                rank = jnp.where(same, other, rank)
            spot = owner * BCAP + rank
            table_ref[spot] = local
            used_ref[owner] = jnp.maximum(used, rank + 1)
            target_ref[pair * slot_count + slot] = jnp.where(slot < count, spot, peers * BCAP)

    def before(pair):
        find_places(pair)
        ray_copy(pair).wait()

    transposed(times_ref, rays_ref, before, target_ref, total_ref, message_refs)
    squares = jnp.zeros((cols, BS), F32)
    for pair in range(pair_count):
        part = times_ref[:, pair * BS : (pair + 1) * BS]
        squares += part * part
    tail = squares_tail(squares)
    place = lax.broadcasted_iota(jnp.int32, (TAIL, BS), 0)
    lane = lax.broadcasted_iota(jnp.int32, (TAIL, BS), 1)

    for peer, message_ref in enumerate(message_refs):
        rows = tail
        for rank in range(BCAP):
            asked = table_ref[peer * BCAP + rank].astype(F32)
            rows = jnp.where((place == 3) & (lane == rank), asked, rows)
        message_ref[BCAP * cols :, :] = rows.astype(BF16)


def keep_kernel(target_hbm, own_hbm, rays_hbm, target_ref, own_ref, rays_ref, sems):
    copies = [
        pltpu.make_async_copy(source, dest, sems.at[index])
        for index, (source, dest) in enumerate(
            [(target_hbm, target_ref), (own_hbm, own_ref), (rays_hbm, rays_ref)]
        )
    ]
    for copy in copies:
        copy.start()
    for copy in copies:
        copy.wait()


def pair_kernel(peers, target_ref, *refs):
    fetched_refs = refs[:peers]
    data_ref, beta_ref, rays_ref = refs[peers : peers + 3]
    message_refs = refs[peers + 3 : 2 * peers + 3]
    alpha_ref, raw_ref, total_ref, fetched_ref = refs[2 * peers + 3 :]
    pair_count, slot_count = rays_ref.shape[:2]
    cols = data_ref.shape[0]
    spots = peers * BCAP
    for peer in range(peers):
        fetched_ref[peer] = fetched_refs[peer][: BCAP * cols, :]
    alpha = norm_of_tails(fetched_refs, cols)
    alpha_ref[...] = alpha
    beta = beta_ref[...]
    model_scale = 1.0 / (alpha * beta)
    data_scale = alpha / beta

    def one_pair(pair, squares):
        chosen = []
        for slot in range(slot_count):
            spot = target_ref[pair * slot_count + slot]
            live = spot < spots
            spot = jnp.where(live, spot, 0)
            rows = pl.ds(pl.multiple_of((spot % BCAP) * cols, cols), cols)
            block = fetched_ref[spot // BCAP, rows, :]
            chosen.append(jnp.where(live, block, jnp.zeros_like(block)))
        rays = jnp.concatenate([rays_ref[pair, slot] for slot in range(slot_count)], axis=1)
        product = lax.dot_general(
            rays, jnp.concatenate(chosen, axis=1), (((1,), (1,)), ((), ())),
            preferred_element_type=F32,
        )
        raw = product.T * model_scale - data_ref[:, lanes(pair)] * data_scale
        raw_ref[:, lanes(pair)] = raw
        return squares + raw * raw

    squares = lax.fori_loop(0, pair_count, one_pair, jnp.zeros((cols, BS), F32), unroll=True)
    transposed(raw_ref, rays_ref, lambda pair: None, target_ref, total_ref, message_refs)
    tail = squares_tail(squares).astype(BF16)
    for message_ref in message_refs:
        message_ref[BCAP * cols :, :] = tail


def gathered(arrived_refs, asked_ref, model_ref):
    cols = model_ref.shape[0]
    for peer, arrived_ref in enumerate(arrived_refs):
        for rank in range(BCAP):
            where = lanes(asked_ref[peer, rank])
            model_ref[:, where] += arrived_ref[rank * cols : (rank + 1) * cols, :].astype(F32)


def reply(squares, scale, asked_ref, model_ref, out_refs):
    cols = model_ref.shape[0]
    tail = squares_tail(squares * scale * scale).astype(BF16)
    for peer, out_ref in enumerate(out_refs):
        out_ref[BCAP * cols :, :] = tail
        for rank in range(BCAP):
            block = model_ref[:, lanes(asked_ref[peer, rank])]
            out_ref[rank * cols : (rank + 1) * cols, :] = block.astype(BF16)


def squares_of(model_ref):
    cols, cells = model_ref.shape

    def one_block(block, squares):
        values = model_ref[:, lanes(block)]
        return squares + values * values

    return lax.fori_loop(0, cells // BS, one_block, jnp.zeros((cols, BS), F32), unroll=8)


def first_cell_kernel(peers, *refs):
    arrived_refs, out_refs = refs[:peers], refs[peers + 2 : 2 * peers + 2]
    model_ref, beta_ref = refs[peers : peers + 2]
    asked_ref, table_ref, sem = refs[2 * peers + 2 :]
    cols, cells = model_ref.shape
    for peer in range(peers):
        tail = arrived_refs[peer][BCAP * cols :, :].astype(F32)
        table_ref[peer : peer + 1, :] = tail[3:4].astype(jnp.int32)
    copy = pltpu.make_async_copy(table_ref, asked_ref, sem)
    copy.start()
    beta = norm_of_tails(arrived_refs, cols)
    beta_ref[...] = beta
    model_ref[...] = jnp.zeros((cols, cells), F32)
    copy.wait()
    gathered(arrived_refs, asked_ref, model_ref)
    reply(squares_of(model_ref), 1.0 / beta, asked_ref, model_ref, out_refs)


def start_from(before_ref, scale, model_ref):
    def one_block(block, carry):
        model_ref[:, lanes(block)] = before_ref[:, lanes(block)] * -scale
        return carry

    lax.fori_loop(0, model_ref.shape[1] // BS, one_block, 0, unroll=8)


def cell_kernel(peers, asked_ref, *refs):
    arrived_refs, out_refs = refs[:peers], refs[peers + 5 :]
    before_ref, alpha_ref, beta_before_ref, model_ref, beta_ref = refs[peers : peers + 5]
    beta = norm_of_tails(arrived_refs, model_ref.shape[0])
    beta_ref[...] = beta
    start_from(before_ref, beta * beta / (alpha_ref[...] * beta_before_ref[...]), model_ref)
    gathered(arrived_refs, asked_ref, model_ref)
    reply(squares_of(model_ref), 1.0 / beta, asked_ref, model_ref, out_refs)


def last_cell_kernel(peers, asked_ref, *refs):
    arrived_refs = refs[:peers]
    before_ref, alpha_ref, beta_before_ref, model_ref, beta_ref, out_ref = refs[peers:]
    beta = norm_of_tails(arrived_refs, model_ref.shape[0])
    beta_ref[...] = beta
    start_from(before_ref, beta * beta / (alpha_ref[...] * beta_before_ref[...]), model_ref)
    gathered(arrived_refs, asked_ref, model_ref)
    squares = squares_of(model_ref) / (beta * beta)
    total = jnp.sum(squares, axis=1, keepdims=True)
    row = jnp.sum(jnp.where(diagonal(total.shape[0]), total, 0.0), axis=0, keepdims=True)
    out_ref[...] = jnp.broadcast_to(row, out_ref.shape)


def estimate_kernel(*refs):
    models = refs[:ITERS]
    alphas = [ref[...] for ref in refs[ITERS : 2 * ITERS]]
    betas = [ref[...] for ref in refs[2 * ITERS : 3 * ITERS + 1]]
    estimate_hbm, estimate_ref, sems = refs[3 * ITERS + 1 :]
    cells = estimate_ref.shape[1]
    weights = estimate_weights(betas, alphas)
    blocks = cells // BS // CHUNKS

    def one_block(block, carry):
        where = lanes(block)
        total = weights[0] * models[0][:, where]
        for i in range(1, ITERS):
            total += weights[i] * models[i][:, where]
        estimate_ref[:, where] = total
        return carry

    copies = []
    for chunk in range(CHUNKS):
        lax.fori_loop(chunk * blocks, (chunk + 1) * blocks, one_block, 0, unroll=4)
        where = slice(chunk * blocks * BS, (chunk + 1) * blocks * BS)
        copies.append(
            pltpu.make_async_copy(
                estimate_ref.at[:, where], estimate_hbm.at[:, where], sems.at[chunk]
            )
        )
        copies[-1].start()
    for copy in copies:
        copy.wait()


def estimate_weights(betas, alphas):
    phi_bar = betas[0]
    rho_bar = alphas[0]
    trace = [1.0 / (alphas[0] * betas[0])]
    weight = [jnp.zeros_like(phi_bar)] * ITERS
    for step in range(ITERS):
        beta = betas[step + 1]
        rho = jnp.sqrt(rho_bar * rho_bar + beta * beta)
        cosine = rho_bar / rho
        sine = beta / rho
        gain = cosine * phi_bar / rho
        weight = [
            weight[i] + gain * trace[i] if i < len(trace) else weight[i] for i in range(ITERS)
        ]
        if step + 1 < ITERS:
            alpha = alphas[step + 1]
            theta = sine * alpha
            rho_bar = -cosine * alpha
            phi_bar = sine * phi_bar
            trace = [-(theta / rho) * value for value in trace] + [1.0 / (alpha * beta)]
    return weight


def model_kernel(*refs):
    *share_refs, beta_ref, model_ref, out_hbm, out_ref, sems = refs
    cols, cells = model_ref.shape
    blocks = cells // BS // CHUNKS
    row = sum(ref[...] for ref in share_refs)[0:1]
    column = jnp.sum(jnp.where(diagonal(cols), row, 0.0), axis=1, keepdims=True)
    alpha = jnp.broadcast_to(jnp.sqrt(column + EPS), (cols, BS))
    scale = 1.0 / (alpha * beta_ref[...])

    def one_block(block, carry):
        out_ref[:, lanes(block)] = model_ref[:, lanes(block)] * scale
        return carry

    copies = []
    for chunk in range(CHUNKS):
        lax.fori_loop(chunk * blocks, (chunk + 1) * blocks, one_block, 0, unroll=4)
        where = slice(chunk * blocks * BS, (chunk + 1) * blocks * BS)
        copies.append(
            pltpu.make_async_copy(out_ref.at[:, where], out_hbm.at[:, where], sems.at[chunk])
        )
        copies[-1].start()
    for copy in copies:
        copy.wait()


def call(kernel, name, in_spaces, outs, scratch=(), flops=0, moved=0, limit=16 << 20):
    return pl.pallas_call(
        kernel,
        name=name,
        in_specs=[pl.BlockSpec(memory_space=space) for space in in_spaces],
        out_specs=[pl.BlockSpec(memory_space=space) for _, _, space in outs],
        out_shape=[jax.ShapeDtypeStruct(shape, dtype) for shape, dtype, _ in outs],
        scratch_shapes=list(scratch),
        compiler_params=pltpu.CompilerParams(vmem_limit_bytes=limit),
        cost_estimate=pl.CostEstimate(flops=flops, bytes_accessed=moved, transcendentals=0),
    )


def on_device(ray_blocks, block_cells, block_counts, travel_times):
    pair_count, slot_count = ray_blocks.shape[:2]
    slots = pair_count * slot_count
    peers = lax.axis_size("pair")
    spots = peers * BCAP
    times = travel_times.T
    cols, pairs = times.shape
    messages = [((BCAP * cols + TAIL, BS), BF16, VMEM)] * peers
    ins = [VMEM] * peers
    gathered_blocks = VMEM((peers, BCAP * cols, BS), BF16)
    tile = ((cols, BS), F32, VMEM)
    data = ((cols, pairs), F32, VMEM)
    whole = ((cols, CELL_DEV), F32, VMEM)
    totals = VMEM((spots + 1, cols, BS), F32)
    flops = 2 * slots * BS * BS * cols

    steps = steps_of(peers)

    def exchange(values):
        return [values[0]] + [
            lax.ppermute(value, "pair", [(one, one ^ step) for one in range(peers)])
            for value, step in zip(values[1:], steps[1:])
        ]

    me = lax.axis_index("pair").astype(jnp.int32).reshape(1)
    *outgoing, target = call(
        functools.partial(start_kernel, peers), "start", [SMEM, HBM, HBM, HBM, HBM],
        messages + [((slots,), jnp.int32, SMEM)],
        [
            totals, SMEM((spots,), jnp.int32), SMEM((peers,), jnp.int32),
            SMEM(block_cells.shape, jnp.int32), SMEM(block_counts.shape, jnp.int32),
            VMEM(times.shape, F32), VMEM(ray_blocks.shape, BF16), SMEM((peers,), jnp.int32),
            pltpu.SemaphoreType.DMA((3,)), pltpu.SemaphoreType.DMA((pair_count,)),
        ],
        flops, 6 << 20, 60 << 20,
    )(me, block_cells, block_counts, times, ray_blocks)
    arrived = exchange(outgoing)
    target, arrived[0], ray_blocks = call(
        keep_kernel, "keep", [HBM, HBM, HBM],
        [((slots,), jnp.int32, SMEM), messages[0], (ray_blocks.shape, BF16, VMEM)],
        [pltpu.SemaphoreType.DMA((3,))], 0, 8 << 20, 48 << 20,
    )(target, arrived[0], ray_blocks)
    model, beta, *replies, asked = call(
        functools.partial(first_cell_kernel, peers), "cells_first", ins,
        [whole, tile] + messages + [((peers, BS), jnp.int32, SMEM)],
        [VMEM((peers, BS), jnp.int32), pltpu.SemaphoreType.DMA],
        0, 6 << 20,
    )(*arrived)
    models, betas, alphas = [model], [beta], []
    current = times
    for step in range(ITERS):
        fetched = exchange(replies)
        last = step + 1 == ITERS
        made = call(
            functools.partial(pair_kernel, peers), "pairs_last" if last else "pairs",
            [SMEM] + ins + [VMEM, VMEM, VMEM], messages + [tile] + [data] * (not last),
            [VMEM(data[0], F32)] * last + [totals, gathered_blocks], 2 * flops, 8 << 20,
        )(target, *fetched, current, betas[-1], ray_blocks)
        alphas.append(made[peers])
        current = made[-1]
        arrived = exchange(made[:peers])
        if not last:
            model, beta, *replies = call(
                functools.partial(cell_kernel, peers), "cells", [SMEM] + ins + [VMEM] * 3,
                [whole, tile] + messages, (), 0, 8 << 20,
            )(asked, *arrived, models[-1], alphas[-1], betas[-1])
            models.append(model)
            betas.append(beta)
    model, beta, share = call(
        functools.partial(last_cell_kernel, peers), "cells_last", [SMEM] + ins + [VMEM] * 3,
        [whole, tile, ((8, BS), F32, VMEM)], (), 0, 8 << 20,
    )(asked, *arrived, models[-1], alphas[-1], betas[-1])
    betas.append(beta)
    reach, shares = peers, [share]
    while reach > 1:
        share = sum(shares[1:], shares[0])
        low = max(reach // 4, 1)
        shares = [share] + [
            lax.ppermute(share, "pair", [(one, one ^ step) for one in range(peers)])
            for step in range(low, reach, low)
        ]
        reach = low
    scratch = [VMEM(whole[0], F32), pltpu.SemaphoreType.DMA((CHUNKS,))]
    (estimate,) = call(
        estimate_kernel, "estimate", [VMEM] * (3 * ITERS + 1), [(whole[0], F32, HBM)], scratch,
        0, 6 << 20,
    )(*models, *alphas, *betas)
    (model_vec,) = call(
        model_kernel, "model", [VMEM] * (len(shares) + 2), [(whole[0], F32, HBM)], scratch,
        0, 4 << 20,
    )(*shares, beta, model)
    return (estimate.T, model_vec.T)


def solution(mesh):
    return jax.shard_map(
        on_device,
        mesh=mesh,
        in_specs=(
            P(("groups", "pair"), None, None, None),
            P(("groups", "pair"), None),
            P(("groups", "pair")),
            P(("groups", "pair"), None),
        ),
        out_specs=(P(("groups", "pair"), None), P(("groups", "pair"), None)),
        check_vma=False,
    )
```

```python
import functools

import jax
import jax.numpy as jnp
from jax import lax
from jax.experimental import pallas as pl
from jax.experimental.pallas import tpu as pltpu
from jax.sharding import PartitionSpec as P

CELL_DEV = 8192
BCAP = 4
BS = 128
TAIL = 8
ITERS = 2
EPS = 1e-12
F32 = jnp.float32
BF16 = jnp.bfloat16
VMEM = pltpu.VMEM
SMEM = pltpu.SMEM
HBM = pltpu.HBM
CHUNKS = 8


def steps_of(peers):
    half, quarter = peers // 2, peers // 4
    near = [step for low in range(quarter) for step in (low, quarter + low)][1:]
    return [0, half] + [step for low in near for step in (low, half + low)]


def diagonal(cols):
    shape = (cols, BS)
    return lax.broadcasted_iota(jnp.int32, shape, 0) == lax.broadcasted_iota(jnp.int32, shape, 1)


def squares_tail(squares):
    cols = squares.shape[0]
    total = jnp.sum(squares, axis=1, keepdims=True)
    row = jnp.sum(jnp.where(diagonal(cols), total, 0.0), axis=0, keepdims=True)
    high = row.astype(BF16).astype(F32)
    middle = (row - high).astype(BF16).astype(F32)
    low = row - high - middle
    place = lax.broadcasted_iota(jnp.int32, (TAIL, BS), 0)
    return jnp.where(
        place == 0, high, jnp.where(place == 1, middle, jnp.where(place == 2, low, 0.0))
    )


def norm_of_tails(message_refs, cols):
    summed = sum(message_ref[BCAP * cols :, :].astype(F32) for message_ref in message_refs)
    row = summed[0:1] + summed[1:2] + summed[2:3]
    column = jnp.sum(jnp.where(diagonal(cols), row, 0.0), axis=1, keepdims=True)
    return jnp.broadcast_to(jnp.sqrt(column + EPS), (cols, BS))


def lanes(block):
    return pl.ds(pl.multiple_of(block * BS, BS), BS)


def transposed(data_ref, rays_ref, before, target_ref, total_ref, message_refs):
    pair_count, slot_count = rays_ref.shape[:2]
    cols = data_ref.shape[0]
    spots = len(message_refs) * BCAP

    def clear(index, carry):
        total_ref[index] = jnp.zeros((cols, BS), F32)
        return carry

    lax.fori_loop(0, spots, clear, 0, unroll=8)

    def one_pair(pair, carry):
        before(pair)
        data = data_ref[:, lanes(pair)]
        high = data.astype(BF16)
        low = (data - high.astype(F32)).astype(BF16)
        pieces = jnp.concatenate([high, low], axis=0)
        for slot in range(0, slot_count, 2):
            rays = jnp.concatenate([rays_ref[pair, slot], rays_ref[pair, slot + 1]], axis=1)
            part = jnp.dot(pieces, rays, preferred_element_type=F32)
            part = part[:cols] + part[cols:]
            for half in range(2):
                spot = target_ref[pair * slot_count + slot + half]
                total_ref[spot] += part[:, half * BS : (half + 1) * BS]
        return carry

    lax.fori_loop(0, pair_count, one_pair, 0, unroll=True)

    for peer, message_ref in enumerate(message_refs):
        for rank in range(BCAP):
            message_ref[rank * cols : (rank + 1) * cols, :] = total_ref[
                peer * BCAP + rank
            ].astype(BF16)


def start_kernel(peers, me_ref, cells_hbm, counts_hbm, times_hbm, rays_hbm, *refs):
    message_refs = refs[:peers]
    target_ref, total_ref, table_ref, used_ref, cells_ref, counts_ref = refs[peers : peers + 6]
    times_ref, rays_ref, place_ref, sems, ray_sems = refs[peers + 6 :]
    for index, step in enumerate(steps_of(peers)):
        place_ref[me_ref[0] ^ step] = index
    pair_count, slot_count = rays_ref.shape[:2]
    cols = times_ref.shape[0]
    owned = CELL_DEV // BS
    copies = [
        pltpu.make_async_copy(source, dest, sems.at[index])
        for index, (source, dest) in enumerate(
            [(cells_hbm, cells_ref), (counts_hbm, counts_ref), (times_hbm, times_ref)]
        )
    ]
    for copy in copies:
        copy.start()

    def ray_copy(pair):
        return pltpu.make_async_copy(rays_hbm.at[pair], rays_ref.at[pair], ray_sems.at[pair])

    def fetch(pair, carry):
        ray_copy(pair).start()
        return carry

    lax.fori_loop(0, pair_count, fetch, 0)

    def clear(peer, carry):
        used_ref[peer] = 0
        for rank in range(BCAP):
            table_ref[peer * BCAP + rank] = 0
        return carry

    lax.fori_loop(0, peers, clear, 0)
    for copy in copies:
        copy.wait()

    def find_places(pair):
        count = counts_ref[pair]
        for slot in range(slot_count):
            cell = cells_ref[pair, slot]
            owner = place_ref[cell // owned]
            local = cell % owned
            used = used_ref[owner]
            rank = used
            for other in range(BCAP - 1, -1, -1):
                same = (table_ref[owner * BCAP + other] == local) & (other < used)
                rank = jnp.where(same, other, rank)
            spot = owner * BCAP + rank
            table_ref[spot] = local
            used_ref[owner] = jnp.maximum(used, rank + 1)
            target_ref[pair * slot_count + slot] = jnp.where(slot < count, spot, peers * BCAP)

    def before(pair):
        find_places(pair)
        ray_copy(pair).wait()

    transposed(times_ref, rays_ref, before, target_ref, total_ref, message_refs)
    squares = jnp.zeros((cols, BS), F32)
    for pair in range(pair_count):
        part = times_ref[:, pair * BS : (pair + 1) * BS]
        squares += part * part
    tail = squares_tail(squares)
    place = lax.broadcasted_iota(jnp.int32, (TAIL, BS), 0)
    lane = lax.broadcasted_iota(jnp.int32, (TAIL, BS), 1)

    for peer, message_ref in enumerate(message_refs):
        rows = tail
        for rank in range(BCAP):
            asked = table_ref[peer * BCAP + rank].astype(F32)
            rows = jnp.where((place == 3) & (lane == rank), asked, rows)
        message_ref[BCAP * cols :, :] = rows.astype(BF16)


def keep_kernel(target_hbm, own_hbm, rays_hbm, target_ref, own_ref, rays_ref, sems):
    copies = [
        pltpu.make_async_copy(source, dest, sems.at[index])
        for index, (source, dest) in enumerate(
            [(target_hbm, target_ref), (own_hbm, own_ref), (rays_hbm, rays_ref)]
        )
    ]
    for copy in copies:
        copy.start()
    for copy in copies:
        copy.wait()


def pair_kernel(peers, target_ref, *refs):
    fetched_refs = refs[:peers]
    data_ref, beta_ref, rays_ref = refs[peers : peers + 3]
    message_refs = refs[peers + 3 : 2 * peers + 3]
    alpha_ref, raw_ref, total_ref, fetched_ref = refs[2 * peers + 3 :]
    pair_count, slot_count = rays_ref.shape[:2]
    cols = data_ref.shape[0]
    spots = peers * BCAP
    for peer in range(peers):
        fetched_ref[peer] = fetched_refs[peer][: BCAP * cols, :]
    alpha = norm_of_tails(fetched_refs, cols)
    alpha_ref[...] = alpha
    beta = beta_ref[...]
    model_scale = 1.0 / (alpha * beta)
    data_scale = alpha / beta

    def one_pair(pair, squares):
        chosen = []
        for slot in range(slot_count):
            spot = target_ref[pair * slot_count + slot]
            live = spot < spots
            spot = jnp.where(live, spot, 0)
            rows = pl.ds(pl.multiple_of((spot % BCAP) * cols, cols), cols)
            block = fetched_ref[spot // BCAP, rows, :]
            chosen.append(jnp.where(live, block, jnp.zeros_like(block)))
        rays = jnp.concatenate([rays_ref[pair, slot] for slot in range(slot_count)], axis=1)
        product = lax.dot_general(
            rays, jnp.concatenate(chosen, axis=1), (((1,), (1,)), ((), ())),
            preferred_element_type=F32,
        )
        raw = product.T * model_scale - data_ref[:, lanes(pair)] * data_scale
        raw_ref[:, lanes(pair)] = raw
        return squares + raw * raw

    squares = lax.fori_loop(0, pair_count, one_pair, jnp.zeros((cols, BS), F32), unroll=True)
    transposed(raw_ref, rays_ref, lambda pair: None, target_ref, total_ref, message_refs)
    tail = squares_tail(squares).astype(BF16)
    for message_ref in message_refs:
        message_ref[BCAP * cols :, :] = tail


def gathered(arrived_refs, asked_ref, model_ref):
    cols = model_ref.shape[0]
    for peer, arrived_ref in enumerate(arrived_refs):
        for rank in range(BCAP):
            where = lanes(asked_ref[peer, rank])
            model_ref[:, where] += arrived_ref[rank * cols : (rank + 1) * cols, :].astype(F32)


def reply(squares, scale, asked_ref, model_ref, out_refs):
    cols = model_ref.shape[0]
    tail = squares_tail(squares * scale * scale).astype(BF16)
    for peer, out_ref in enumerate(out_refs):
        out_ref[BCAP * cols :, :] = tail
        for rank in range(BCAP):
            block = model_ref[:, lanes(asked_ref[peer, rank])]
            out_ref[rank * cols : (rank + 1) * cols, :] = block.astype(BF16)


def squares_of(model_ref):
    cols, cells = model_ref.shape

    def one_block(block, squares):
        values = model_ref[:, lanes(block)]
        return squares + values * values

    return lax.fori_loop(0, cells // BS, one_block, jnp.zeros((cols, BS), F32), unroll=8)


def first_cell_kernel(peers, *refs):
    arrived_refs, out_refs = refs[:peers], refs[peers + 2 : 2 * peers + 2]
    model_ref, beta_ref = refs[peers : peers + 2]
    asked_ref, table_ref, sem = refs[2 * peers + 2 :]
    cols, cells = model_ref.shape
    for peer in range(peers):
        tail = arrived_refs[peer][BCAP * cols :, :].astype(F32)
        table_ref[peer : peer + 1, :] = tail[3:4].astype(jnp.int32)
    copy = pltpu.make_async_copy(table_ref, asked_ref, sem)
    copy.start()
    beta = norm_of_tails(arrived_refs, cols)
    beta_ref[...] = beta
    model_ref[...] = jnp.zeros((cols, cells), F32)
    copy.wait()
    gathered(arrived_refs, asked_ref, model_ref)
    reply(squares_of(model_ref), 1.0 / beta, asked_ref, model_ref, out_refs)


def start_from(before_ref, scale, model_ref):
    def one_block(block, carry):
        model_ref[:, lanes(block)] = before_ref[:, lanes(block)] * -scale
        return carry

    lax.fori_loop(0, model_ref.shape[1] // BS, one_block, 0, unroll=8)


def cell_kernel(peers, asked_ref, *refs):
    arrived_refs, out_refs = refs[:peers], refs[peers + 5 :]
    before_ref, alpha_ref, beta_before_ref, model_ref, beta_ref = refs[peers : peers + 5]
    beta = norm_of_tails(arrived_refs, model_ref.shape[0])
    beta_ref[...] = beta
    start_from(before_ref, beta * beta / (alpha_ref[...] * beta_before_ref[...]), model_ref)
    gathered(arrived_refs, asked_ref, model_ref)
    reply(squares_of(model_ref), 1.0 / beta, asked_ref, model_ref, out_refs)


def last_cell_kernel(peers, asked_ref, *refs):
    arrived_refs = refs[:peers]
    before_ref, alpha_ref, beta_before_ref, model_ref, beta_ref, out_ref = refs[peers:]
    beta = norm_of_tails(arrived_refs, model_ref.shape[0])
    beta_ref[...] = beta
    start_from(before_ref, beta * beta / (alpha_ref[...] * beta_before_ref[...]), model_ref)
    gathered(arrived_refs, asked_ref, model_ref)
    squares = squares_of(model_ref) / (beta * beta)
    total = jnp.sum(squares, axis=1, keepdims=True)
    row = jnp.sum(jnp.where(diagonal(total.shape[0]), total, 0.0), axis=0, keepdims=True)
    out_ref[...] = jnp.broadcast_to(row, out_ref.shape)


def estimate_kernel(*refs):
    models = refs[:ITERS]
    alphas = [ref[...] for ref in refs[ITERS : 2 * ITERS]]
    betas = [ref[...] for ref in refs[2 * ITERS : 3 * ITERS + 1]]
    estimate_hbm, estimate_ref, sems = refs[3 * ITERS + 1 :]
    cells = estimate_ref.shape[1]
    weights = estimate_weights(betas, alphas)
    blocks = cells // BS // CHUNKS

    def one_block(block, carry):
        where = lanes(block)
        total = weights[0] * models[0][:, where]
        for i in range(1, ITERS):
            total += weights[i] * models[i][:, where]
        estimate_ref[:, where] = total
        return carry

    copies = []
    for chunk in range(CHUNKS):
        lax.fori_loop(chunk * blocks, (chunk + 1) * blocks, one_block, 0, unroll=4)
        where = slice(chunk * blocks * BS, (chunk + 1) * blocks * BS)
        copies.append(
            pltpu.make_async_copy(
                estimate_ref.at[:, where], estimate_hbm.at[:, where], sems.at[chunk]
            )
        )
        copies[-1].start()
    for copy in copies:
        copy.wait()


def estimate_weights(betas, alphas):
    phi_bar = betas[0]
    rho_bar = alphas[0]
    trace = [1.0 / (alphas[0] * betas[0])]
    weight = [jnp.zeros_like(phi_bar)] * ITERS
    for step in range(ITERS):
        beta = betas[step + 1]
        rho = jnp.sqrt(rho_bar * rho_bar + beta * beta)
        cosine = rho_bar / rho
        sine = beta / rho
        gain = cosine * phi_bar / rho
        weight = [
            weight[i] + gain * trace[i] if i < len(trace) else weight[i] for i in range(ITERS)
        ]
        if step + 1 < ITERS:
            alpha = alphas[step + 1]
            theta = sine * alpha
            rho_bar = -cosine * alpha
            phi_bar = sine * phi_bar
            trace = [-(theta / rho) * value for value in trace] + [1.0 / (alpha * beta)]
    return weight


def model_kernel(*refs):
    *share_refs, beta_ref, model_ref, out_hbm, out_ref, sems = refs
    cols, cells = model_ref.shape
    blocks = cells // BS // CHUNKS
    row = sum(ref[...] for ref in share_refs)[0:1]
    column = jnp.sum(jnp.where(diagonal(cols), row, 0.0), axis=1, keepdims=True)
    alpha = jnp.broadcast_to(jnp.sqrt(column + EPS), (cols, BS))
    scale = 1.0 / (alpha * beta_ref[...])

    def one_block(block, carry):
        out_ref[:, lanes(block)] = model_ref[:, lanes(block)] * scale
        return carry

    copies = []
    for chunk in range(CHUNKS):
        lax.fori_loop(chunk * blocks, (chunk + 1) * blocks, one_block, 0, unroll=4)
        where = slice(chunk * blocks * BS, (chunk + 1) * blocks * BS)
        copies.append(
            pltpu.make_async_copy(out_ref.at[:, where], out_hbm.at[:, where], sems.at[chunk])
        )
        copies[-1].start()
    for copy in copies:
        copy.wait()


def call(kernel, name, in_spaces, outs, scratch=(), flops=0, moved=0, limit=16 << 20):
    return pl.pallas_call(
        kernel,
        name=name,
        in_specs=[pl.BlockSpec(memory_space=space) for space in in_spaces],
        out_specs=[pl.BlockSpec(memory_space=space) for _, _, space in outs],
        out_shape=[jax.ShapeDtypeStruct(shape, dtype) for shape, dtype, _ in outs],
        scratch_shapes=list(scratch),
        compiler_params=pltpu.CompilerParams(vmem_limit_bytes=limit),
        cost_estimate=pl.CostEstimate(flops=flops, bytes_accessed=moved, transcendentals=0),
    )


def on_device(ray_blocks, block_cells, block_counts, travel_times):
    pair_count, slot_count = ray_blocks.shape[:2]
    slots = pair_count * slot_count
    peers = lax.axis_size("pair")
    spots = peers * BCAP
    times = travel_times.T
    cols, pairs = times.shape
    messages = [((BCAP * cols + TAIL, BS), BF16, VMEM)] * peers
    ins = [VMEM] * peers
    gathered_blocks = VMEM((peers, BCAP * cols, BS), BF16)
    tile = ((cols, BS), F32, VMEM)
    data = ((cols, pairs), F32, VMEM)
    whole = ((cols, CELL_DEV), F32, VMEM)
    totals = VMEM((spots + 1, cols, BS), F32)
    flops = 2 * slots * BS * BS * cols

    steps = steps_of(peers)

    def exchange(values):
        return [values[0]] + [
            lax.ppermute(value, "pair", [(one, one ^ step) for one in range(peers)])
            for value, step in zip(values[1:], steps[1:])
        ]

    me = lax.axis_index("pair").astype(jnp.int32).reshape(1)
    *outgoing, target = call(
        functools.partial(start_kernel, peers), "start", [SMEM, HBM, HBM, HBM, HBM],
        messages + [((slots,), jnp.int32, SMEM)],
        [
            totals, SMEM((spots,), jnp.int32), SMEM((peers,), jnp.int32),
            SMEM(block_cells.shape, jnp.int32), SMEM(block_counts.shape, jnp.int32),
            VMEM(times.shape, F32), VMEM(ray_blocks.shape, BF16), SMEM((peers,), jnp.int32),
            pltpu.SemaphoreType.DMA((3,)), pltpu.SemaphoreType.DMA((pair_count,)),
        ],
        flops, 6 << 20, 60 << 20,
    )(me, block_cells, block_counts, times, ray_blocks)
    arrived = exchange(outgoing)
    target, arrived[0], ray_blocks = call(
        keep_kernel, "keep", [HBM, HBM, HBM],
        [((slots,), jnp.int32, SMEM), messages[0], (ray_blocks.shape, BF16, VMEM)],
        [pltpu.SemaphoreType.DMA((3,))], 0, 8 << 20, 48 << 20,
    )(target, arrived[0], ray_blocks)
    model, beta, *replies, asked = call(
        functools.partial(first_cell_kernel, peers), "cells_first", ins,
        [whole, tile] + messages + [((peers, BS), jnp.int32, SMEM)],
        [VMEM((peers, BS), jnp.int32), pltpu.SemaphoreType.DMA],
        0, 6 << 20,
    )(*arrived)
    models, betas, alphas = [model], [beta], []
    current = times
    for step in range(ITERS):
        fetched = exchange(replies)
        last = step + 1 == ITERS
        made = call(
            functools.partial(pair_kernel, peers), "pairs_last" if last else "pairs",
            [SMEM] + ins + [VMEM, VMEM, VMEM], messages + [tile] + [data] * (not last),
            [VMEM(data[0], F32)] * last + [totals, gathered_blocks], 2 * flops, 8 << 20,
        )(target, *fetched, current, betas[-1], ray_blocks)
        alphas.append(made[peers])
        current = made[-1]
        arrived = exchange(made[:peers])
        if not last:
            model, beta, *replies = call(
                functools.partial(cell_kernel, peers), "cells", [SMEM] + ins + [VMEM] * 3,
                [whole, tile] + messages, (), 0, 8 << 20,
            )(asked, *arrived, models[-1], alphas[-1], betas[-1])
            models.append(model)
            betas.append(beta)
    model, beta, share = call(
        functools.partial(last_cell_kernel, peers), "cells_last", [SMEM] + ins + [VMEM] * 3,
        [whole, tile, ((8, BS), F32, VMEM)], (), 0, 8 << 20,
    )(asked, *arrived, models[-1], alphas[-1], betas[-1])
    betas.append(beta)
    scratch = [VMEM(whole[0], F32), pltpu.SemaphoreType.DMA((CHUNKS,))]
    (estimate,) = call(
        estimate_kernel, "estimate", [VMEM] * (3 * ITERS + 1), [(whole[0], F32, HBM)], scratch,
        0, 6 << 20,
    )(*models, *alphas, *betas)
    reach, shares = peers, [share]
    while reach > 1:
        share = sum(shares[1:], shares[0])
        if reach < peers:
            share, estimate = lax.optimization_barrier((share, estimate))
        low = reach // 2 if reach > 4 else 1
        shares = [share] + [
            lax.ppermute(share, "pair", [(one, one ^ step) for one in range(peers)])
            for step in range(low, reach, low)
        ]
        reach = low
    (model_vec,) = call(
        model_kernel, "model", [VMEM] * (len(shares) + 2), [(whole[0], F32, HBM)], scratch,
        0, 4 << 20,
    )(*shares, beta, model)
    return (estimate.T, model_vec.T)


def solution(mesh):
    return jax.shard_map(
        on_device,
        mesh=mesh,
        in_specs=(
            P(("groups", "pair"), None, None, None),
            P(("groups", "pair"), None),
            P(("groups", "pair")),
            P(("groups", "pair"), None),
        ),
        out_specs=(P(("groups", "pair"), None), P(("groups", "pair"), None)),
        check_vma=False,
    )
```

```python
import functools

import jax
import jax.numpy as jnp
from jax import lax
from jax.experimental import pallas as pl
from jax.experimental.pallas import tpu as pltpu
from jax.sharding import PartitionSpec as P

CELL_DEV = 8192
BCAP = 4
BS = 128
TAIL = 8
ITERS = 2
EPS = 1e-12
F32 = jnp.float32
BF16 = jnp.bfloat16
VMEM = pltpu.VMEM
SMEM = pltpu.SMEM
HBM = pltpu.HBM
CHUNKS = 8


def steps_of(peers):
    half, quarter = peers // 2, peers // 4
    near = [step for low in range(quarter) for step in (low, quarter + low)][1:]
    return [0, half] + [step for low in near for step in (low, half + low)]


def diagonal(cols):
    shape = (cols, BS)
    return lax.broadcasted_iota(jnp.int32, shape, 0) == lax.broadcasted_iota(jnp.int32, shape, 1)


def squares_tail(squares):
    cols = squares.shape[0]
    total = jnp.sum(squares, axis=1, keepdims=True)
    row = jnp.sum(jnp.where(diagonal(cols), total, 0.0), axis=0, keepdims=True)
    high = row.astype(BF16).astype(F32)
    middle = (row - high).astype(BF16).astype(F32)
    low = row - high - middle
    place = lax.broadcasted_iota(jnp.int32, (TAIL, BS), 0)
    return jnp.where(
        place == 0, high, jnp.where(place == 1, middle, jnp.where(place == 2, low, 0.0))
    )


def norm_of_tails(message_refs, cols):
    summed = sum(message_ref[BCAP * cols :, :].astype(F32) for message_ref in message_refs)
    row = summed[0:1] + summed[1:2] + summed[2:3]
    column = jnp.sum(jnp.where(diagonal(cols), row, 0.0), axis=1, keepdims=True)
    return jnp.broadcast_to(jnp.sqrt(column + EPS), (cols, BS))


def lanes(block):
    return pl.ds(pl.multiple_of(block * BS, BS), BS)


def transposed(data_ref, rays_ref, begin, before, target_ref, total_ref, message_refs):
    pair_count, slot_count = rays_ref.shape[:2]
    cols = data_ref.shape[0]
    spots = len(message_refs) * BCAP

    def clear(index, carry):
        total_ref[index] = jnp.zeros((cols, BS), F32)
        return carry

    lax.fori_loop(0, spots, clear, 0, unroll=8)
    begin()

    def one_pair(pair, carry):
        before(pair)
        data = data_ref[:, lanes(pair)]
        high = data.astype(BF16)
        low = (data - high.astype(F32)).astype(BF16)
        pieces = jnp.concatenate([high, low], axis=0)
        for slot in range(0, slot_count, 2):
            rays = jnp.concatenate([rays_ref[pair, slot], rays_ref[pair, slot + 1]], axis=1)
            part = jnp.dot(pieces, rays, preferred_element_type=F32)
            part = part[:cols] + part[cols:]
            for half in range(2):
                spot = target_ref[pair * slot_count + slot + half]
                total_ref[spot] += part[:, half * BS : (half + 1) * BS]
        return carry

    lax.fori_loop(0, pair_count, one_pair, 0, unroll=True)

    for peer, message_ref in enumerate(message_refs):
        for rank in range(BCAP):
            message_ref[rank * cols : (rank + 1) * cols, :] = total_ref[
                peer * BCAP + rank
            ].astype(BF16)


def start_kernel(peers, me_ref, cells_hbm, counts_hbm, times_hbm, rays_hbm, *refs):
    message_refs = refs[:peers]
    target_ref, total_ref, table_ref, used_ref, cells_ref, counts_ref = refs[peers : peers + 6]
    times_ref, rays_ref, place_ref, sems, ray_sems = refs[peers + 6 :]
    for index, step in enumerate(steps_of(peers)):
        place_ref[me_ref[0] ^ step] = index
    pair_count, slot_count = rays_ref.shape[:2]
    cols = times_ref.shape[0]
    owned = CELL_DEV // BS
    copies = [
        pltpu.make_async_copy(source, dest, sems.at[index])
        for index, (source, dest) in enumerate(
            [(cells_hbm, cells_ref), (counts_hbm, counts_ref), (times_hbm, times_ref)]
        )
    ]
    for copy in copies:
        copy.start()

    def ray_copy(pair):
        return pltpu.make_async_copy(rays_hbm.at[pair], rays_ref.at[pair], ray_sems.at[pair])

    def fetch(pair, carry):
        ray_copy(pair).start()
        return carry

    lax.fori_loop(0, pair_count, fetch, 0)

    def clear(peer, carry):
        used_ref[peer] = 0
        for rank in range(BCAP):
            table_ref[peer * BCAP + rank] = 0
        return carry

    lax.fori_loop(0, peers, clear, 0)
    def find_places(pair):
        count = counts_ref[pair]
        for slot in range(slot_count):
            cell = cells_ref[pair, slot]
            owner = place_ref[cell // owned]
            local = cell % owned
            used = used_ref[owner]
            rank = used
            for other in range(BCAP - 1, -1, -1):
                same = (table_ref[owner * BCAP + other] == local) & (other < used)
                rank = jnp.where(same, other, rank)
            spot = owner * BCAP + rank
            table_ref[spot] = local
            used_ref[owner] = jnp.maximum(used, rank + 1)
            target_ref[pair * slot_count + slot] = jnp.where(slot < count, spot, peers * BCAP)

    def before(pair):
        find_places(pair)
        ray_copy(pair).wait()

    def begin():
        for copy in copies:
            copy.wait()
        squares = jnp.zeros((cols, BS), F32)
        for pair in range(pair_count):
            values = times_ref[:, pair * BS : (pair + 1) * BS]
            squares += values * values
        tail = squares_tail(squares).astype(BF16)
        for message_ref in message_refs:
            message_ref[BCAP * cols :, :] = tail

    transposed(times_ref, rays_ref, begin, before, target_ref, total_ref, message_refs)
    place = lax.broadcasted_iota(jnp.int32, (TAIL, BS), 0)
    lane = lax.broadcasted_iota(jnp.int32, (TAIL, BS), 1)
    for peer, message_ref in enumerate(message_refs):
        rows = message_ref[BCAP * cols :, :].astype(F32)
        for rank in range(BCAP):
            asked = table_ref[peer * BCAP + rank].astype(F32)
            rows = jnp.where((place == 3) & (lane == rank), asked, rows)
        message_ref[BCAP * cols :, :] = rows.astype(BF16)


def keep_kernel(target_hbm, own_hbm, rays_hbm, target_ref, own_ref, rays_ref, sems):
    copies = [
        pltpu.make_async_copy(source, dest, sems.at[index])
        for index, (source, dest) in enumerate(
            [(target_hbm, target_ref), (own_hbm, own_ref), (rays_hbm, rays_ref)]
        )
    ]
    for copy in copies:
        copy.start()
    for copy in copies:
        copy.wait()


def pair_kernel(peers, target_ref, *refs):
    fetched_refs = refs[:peers]
    data_ref, beta_ref, rays_ref = refs[peers : peers + 3]
    message_refs = refs[peers + 3 : 2 * peers + 3]
    alpha_ref, raw_ref, total_ref, fetched_ref = refs[2 * peers + 3 :]
    pair_count, slot_count = rays_ref.shape[:2]
    cols = data_ref.shape[0]
    spots = peers * BCAP
    for peer in range(peers):
        fetched_ref[peer] = fetched_refs[peer][: BCAP * cols, :]
    alpha = norm_of_tails(fetched_refs, cols)
    alpha_ref[...] = alpha
    beta = beta_ref[...]
    model_scale = 1.0 / (alpha * beta)
    data_scale = alpha / beta

    def one_pair(pair, squares):
        chosen = []
        for slot in range(slot_count):
            spot = target_ref[pair * slot_count + slot]
            live = spot < spots
            spot = jnp.where(live, spot, 0)
            rows = pl.ds(pl.multiple_of((spot % BCAP) * cols, cols), cols)
            block = fetched_ref[spot // BCAP, rows, :]
            chosen.append(jnp.where(live, block, jnp.zeros_like(block)))
        rays = jnp.concatenate([rays_ref[pair, slot] for slot in range(slot_count)], axis=1)
        product = lax.dot_general(
            rays, jnp.concatenate(chosen, axis=1), (((1,), (1,)), ((), ())),
            preferred_element_type=F32,
        )
        raw = product.T * model_scale - data_ref[:, lanes(pair)] * data_scale
        raw_ref[:, lanes(pair)] = raw
        return squares + raw * raw

    squares = lax.fori_loop(0, pair_count, one_pair, jnp.zeros((cols, BS), F32), unroll=True)
    tail = squares_tail(squares).astype(BF16)
    for message_ref in message_refs:
        message_ref[BCAP * cols :, :] = tail
    transposed(
        raw_ref, rays_ref, lambda: None, lambda pair: None, target_ref, total_ref, message_refs
    )


def gathered(arrived_refs, asked_ref, model_ref):
    cols = model_ref.shape[0]
    for peer, arrived_ref in enumerate(arrived_refs):
        for rank in range(BCAP):
            where = lanes(asked_ref[peer, rank])
            model_ref[:, where] += arrived_ref[rank * cols : (rank + 1) * cols, :].astype(F32)


def reply(squares, scale, asked_ref, model_ref, out_refs):
    cols = model_ref.shape[0]
    tail = squares_tail(squares * scale * scale).astype(BF16)
    for peer, out_ref in enumerate(out_refs):
        out_ref[BCAP * cols :, :] = tail
        for rank in range(BCAP):
            block = model_ref[:, lanes(asked_ref[peer, rank])]
            out_ref[rank * cols : (rank + 1) * cols, :] = block.astype(BF16)


def squares_of(model_ref):
    cols, cells = model_ref.shape

    def one_block(block, squares):
        values = model_ref[:, lanes(block)]
        return squares + values * values

    return lax.fori_loop(0, cells // BS, one_block, jnp.zeros((cols, BS), F32), unroll=8)


def first_cell_kernel(peers, *refs):
    arrived_refs, out_refs = refs[:peers], refs[peers + 2 : 2 * peers + 2]
    model_ref, beta_ref = refs[peers : peers + 2]
    asked_ref, table_ref, sem = refs[2 * peers + 2 :]
    cols, cells = model_ref.shape
    for peer in range(peers):
        tail = arrived_refs[peer][BCAP * cols :, :].astype(F32)
        table_ref[peer : peer + 1, :] = tail[3:4].astype(jnp.int32)
    copy = pltpu.make_async_copy(table_ref, asked_ref, sem)
    copy.start()
    beta = norm_of_tails(arrived_refs, cols)
    beta_ref[...] = beta
    model_ref[...] = jnp.zeros((cols, cells), F32)
    copy.wait()
    gathered(arrived_refs, asked_ref, model_ref)
    reply(squares_of(model_ref), 1.0 / beta, asked_ref, model_ref, out_refs)


def start_from(before_ref, scale, model_ref):
    def one_block(block, carry):
        model_ref[:, lanes(block)] = before_ref[:, lanes(block)] * -scale
        return carry

    lax.fori_loop(0, model_ref.shape[1] // BS, one_block, 0, unroll=8)


def cell_kernel(peers, asked_ref, *refs):
    arrived_refs, out_refs = refs[:peers], refs[peers + 5 :]
    before_ref, alpha_ref, beta_before_ref, model_ref, beta_ref = refs[peers : peers + 5]
    beta = norm_of_tails(arrived_refs, model_ref.shape[0])
    beta_ref[...] = beta
    start_from(before_ref, beta * beta / (alpha_ref[...] * beta_before_ref[...]), model_ref)
    gathered(arrived_refs, asked_ref, model_ref)
    reply(squares_of(model_ref), 1.0 / beta, asked_ref, model_ref, out_refs)


def last_cell_kernel(peers, asked_ref, *refs):
    arrived_refs = refs[:peers]
    before_ref, alpha_ref, beta_before_ref, model_ref, beta_ref, out_ref = refs[peers:]
    beta = norm_of_tails(arrived_refs, model_ref.shape[0])
    beta_ref[...] = beta
    start_from(before_ref, beta * beta / (alpha_ref[...] * beta_before_ref[...]), model_ref)
    gathered(arrived_refs, asked_ref, model_ref)
    squares = squares_of(model_ref) / (beta * beta)
    total = jnp.sum(squares, axis=1, keepdims=True)
    row = jnp.sum(jnp.where(diagonal(total.shape[0]), total, 0.0), axis=0, keepdims=True)
    out_ref[...] = jnp.broadcast_to(row, out_ref.shape)


def estimate_kernel(*refs):
    models = refs[:ITERS]
    alphas = [ref[...] for ref in refs[ITERS : 2 * ITERS]]
    betas = [ref[...] for ref in refs[2 * ITERS : 3 * ITERS + 1]]
    estimate_hbm, estimate_ref, sems = refs[3 * ITERS + 1 :]
    cells = estimate_ref.shape[1]
    weights = estimate_weights(betas, alphas)
    blocks = cells // BS // CHUNKS

    def one_block(block, carry):
        where = lanes(block)
        total = weights[0] * models[0][:, where]
        for i in range(1, ITERS):
            total += weights[i] * models[i][:, where]
        estimate_ref[:, where] = total
        return carry

    copies = []
    for chunk in range(CHUNKS):
        lax.fori_loop(chunk * blocks, (chunk + 1) * blocks, one_block, 0, unroll=4)
        where = slice(chunk * blocks * BS, (chunk + 1) * blocks * BS)
        copies.append(
            pltpu.make_async_copy(
                estimate_ref.at[:, where], estimate_hbm.at[:, where], sems.at[chunk]
            )
        )
        copies[-1].start()
    for copy in copies:
        copy.wait()


def estimate_weights(betas, alphas):
    phi_bar = betas[0]
    rho_bar = alphas[0]
    trace = [1.0 / (alphas[0] * betas[0])]
    weight = [jnp.zeros_like(phi_bar)] * ITERS
    for step in range(ITERS):
        beta = betas[step + 1]
        rho = jnp.sqrt(rho_bar * rho_bar + beta * beta)
        cosine = rho_bar / rho
        sine = beta / rho
        gain = cosine * phi_bar / rho
        weight = [
            weight[i] + gain * trace[i] if i < len(trace) else weight[i] for i in range(ITERS)
        ]
        if step + 1 < ITERS:
            alpha = alphas[step + 1]
            theta = sine * alpha
            rho_bar = -cosine * alpha
            phi_bar = sine * phi_bar
            trace = [-(theta / rho) * value for value in trace] + [1.0 / (alpha * beta)]
    return weight


def model_kernel(*refs):
    *share_refs, beta_ref, model_ref, out_hbm, out_ref, sems = refs
    cols, cells = model_ref.shape
    blocks = cells // BS // CHUNKS
    row = sum(ref[...] for ref in share_refs)[0:1]
    column = jnp.sum(jnp.where(diagonal(cols), row, 0.0), axis=1, keepdims=True)
    alpha = jnp.broadcast_to(jnp.sqrt(column + EPS), (cols, BS))
    scale = 1.0 / (alpha * beta_ref[...])

    def one_block(block, carry):
        out_ref[:, lanes(block)] = model_ref[:, lanes(block)] * scale
        return carry

    copies = []
    for chunk in range(CHUNKS):
        lax.fori_loop(chunk * blocks, (chunk + 1) * blocks, one_block, 0, unroll=4)
        where = slice(chunk * blocks * BS, (chunk + 1) * blocks * BS)
        copies.append(
            pltpu.make_async_copy(out_ref.at[:, where], out_hbm.at[:, where], sems.at[chunk])
        )
        copies[-1].start()
    for copy in copies:
        copy.wait()


def call(kernel, name, in_spaces, outs, scratch=(), flops=0, moved=0, limit=16 << 20):
    return pl.pallas_call(
        kernel,
        name=name,
        in_specs=[pl.BlockSpec(memory_space=space) for space in in_spaces],
        out_specs=[pl.BlockSpec(memory_space=space) for _, _, space in outs],
        out_shape=[jax.ShapeDtypeStruct(shape, dtype) for shape, dtype, _ in outs],
        scratch_shapes=list(scratch),
        compiler_params=pltpu.CompilerParams(vmem_limit_bytes=limit),
        cost_estimate=pl.CostEstimate(flops=flops, bytes_accessed=moved, transcendentals=0),
    )


def on_device(ray_blocks, block_cells, block_counts, travel_times):
    pair_count, slot_count = ray_blocks.shape[:2]
    slots = pair_count * slot_count
    peers = lax.axis_size("pair")
    spots = peers * BCAP
    times = travel_times.T
    cols, pairs = times.shape
    messages = [((BCAP * cols + TAIL, BS), BF16, VMEM)] * peers
    ins = [VMEM] * peers
    gathered_blocks = VMEM((peers, BCAP * cols, BS), BF16)
    tile = ((cols, BS), F32, VMEM)
    data = ((cols, pairs), F32, VMEM)
    whole = ((cols, CELL_DEV), F32, VMEM)
    totals = VMEM((spots + 1, cols, BS), F32)
    flops = 2 * slots * BS * BS * cols

    steps = steps_of(peers)

    def exchange(values):
        return [values[0]] + [
            lax.ppermute(value, "pair", [(one, one ^ step) for one in range(peers)])
            for value, step in zip(values[1:], steps[1:])
        ]

    me = lax.axis_index("pair").astype(jnp.int32).reshape(1)
    *outgoing, target = call(
        functools.partial(start_kernel, peers), "start", [SMEM, HBM, HBM, HBM, HBM],
        messages + [((slots,), jnp.int32, SMEM)],
        [
            totals, SMEM((spots,), jnp.int32), SMEM((peers,), jnp.int32),
            SMEM(block_cells.shape, jnp.int32), SMEM(block_counts.shape, jnp.int32),
            VMEM(times.shape, F32), VMEM(ray_blocks.shape, BF16), SMEM((peers,), jnp.int32),
            pltpu.SemaphoreType.DMA((3,)), pltpu.SemaphoreType.DMA((pair_count,)),
        ],
        flops, 6 << 20, 60 << 20,
    )(me, block_cells, block_counts, times, ray_blocks)
    arrived = exchange(outgoing)
    target, arrived[0], ray_blocks = call(
        keep_kernel, "keep", [HBM, HBM, HBM],
        [((slots,), jnp.int32, SMEM), messages[0], (ray_blocks.shape, BF16, VMEM)],
        [pltpu.SemaphoreType.DMA((3,))], 0, 8 << 20, 48 << 20,
    )(target, arrived[0], ray_blocks)
    model, beta, *replies, asked = call(
        functools.partial(first_cell_kernel, peers), "cells_first", ins,
        [whole, tile] + messages + [((peers, BS), jnp.int32, SMEM)],
        [VMEM((peers, BS), jnp.int32), pltpu.SemaphoreType.DMA],
        0, 6 << 20,
    )(*arrived)
    models, betas, alphas = [model], [beta], []
    current = times
    for step in range(ITERS):
        fetched = exchange(replies)
        last = step + 1 == ITERS
        made = call(
            functools.partial(pair_kernel, peers), "pairs_last" if last else "pairs",
            [SMEM] + ins + [VMEM, VMEM, VMEM], messages + [tile] + [data] * (not last),
            [VMEM(data[0], F32)] * last + [totals, gathered_blocks], 2 * flops, 8 << 20,
        )(target, *fetched, current, betas[-1], ray_blocks)
        alphas.append(made[peers])
        current = made[-1]
        arrived = exchange(made[:peers])
        if not last:
            model, beta, *replies = call(
                functools.partial(cell_kernel, peers), "cells", [SMEM] + ins + [VMEM] * 3,
                [whole, tile] + messages, (), 0, 8 << 20,
            )(asked, *arrived, models[-1], alphas[-1], betas[-1])
            models.append(model)
            betas.append(beta)
    model, beta, share = call(
        functools.partial(last_cell_kernel, peers), "cells_last", [SMEM] + ins + [VMEM] * 3,
        [whole, tile, ((8, BS), F32, VMEM)], (), 0, 8 << 20,
    )(asked, *arrived, models[-1], alphas[-1], betas[-1])
    betas.append(beta)
    reach, shares = peers, [share]
    while reach > 1:
        share = sum(shares[1:], shares[0])
        low = max(reach // 4, 1)
        shares = [share] + [
            lax.ppermute(share, "pair", [(one, one ^ step) for one in range(peers)])
            for step in range(low, reach, low)
        ]
        reach = low
    scratch = [VMEM(whole[0], F32), pltpu.SemaphoreType.DMA((CHUNKS,))]
    (estimate,) = call(
        estimate_kernel, "estimate", [VMEM] * (3 * ITERS + 1), [(whole[0], F32, HBM)], scratch,
        0, 6 << 20,
    )(*models, *alphas, *betas)
    (model_vec,) = call(
        model_kernel, "model", [VMEM] * (len(shares) + 2), [(whole[0], F32, HBM)], scratch,
        0, 4 << 20,
    )(*shares, beta, model)
    return (estimate.T, model_vec.T)


def solution(mesh):
    return jax.shard_map(
        on_device,
        mesh=mesh,
        in_specs=(
            P(("groups", "pair"), None, None, None),
            P(("groups", "pair"), None),
            P(("groups", "pair")),
            P(("groups", "pair"), None),
        ),
        out_specs=(P(("groups", "pair"), None), P(("groups", "pair"), None)),
        check_vma=False,
    )
```

```python
import functools

import jax
import jax.numpy as jnp
from jax import lax
from jax.experimental import pallas as pl
from jax.experimental.pallas import tpu as pltpu
from jax.sharding import PartitionSpec as P

CELL_DEV = 8192
BCAP = 4
BS = 128
TAIL = 8
ITERS = 2
EPS = 1e-12
F32 = jnp.float32
BF16 = jnp.bfloat16
VMEM = pltpu.VMEM
SMEM = pltpu.SMEM
HBM = pltpu.HBM
CHUNKS = 8


def steps_of(peers):
    half, quarter = peers // 2, peers // 4
    near = [step for low in range(quarter) for step in (low, quarter + low)][1:]
    far = half + quarter
    return [0, far] + [step for low in near for step in (low, far ^ low)]


def diagonal(cols):
    shape = (cols, BS)
    return lax.broadcasted_iota(jnp.int32, shape, 0) == lax.broadcasted_iota(jnp.int32, shape, 1)


def squares_tail(squares):
    cols = squares.shape[0]
    total = jnp.sum(squares, axis=1, keepdims=True)
    row = jnp.sum(jnp.where(diagonal(cols), total, 0.0), axis=0, keepdims=True)
    high = row.astype(BF16).astype(F32)
    middle = (row - high).astype(BF16).astype(F32)
    low = row - high - middle
    place = lax.broadcasted_iota(jnp.int32, (TAIL, BS), 0)
    return jnp.where(
        place == 0, high, jnp.where(place == 1, middle, jnp.where(place == 2, low, 0.0))
    )


def norm_of_tails(message_refs, cols):
    summed = sum(message_ref[BCAP * cols :, :].astype(F32) for message_ref in message_refs)
    row = summed[0:1] + summed[1:2] + summed[2:3]
    column = jnp.sum(jnp.where(diagonal(cols), row, 0.0), axis=1, keepdims=True)
    return jnp.broadcast_to(jnp.sqrt(column + EPS), (cols, BS))


def lanes(block):
    return pl.ds(pl.multiple_of(block * BS, BS), BS)


def transposed(data_ref, rays_ref, before, target_ref, total_ref, message_refs):
    pair_count, slot_count = rays_ref.shape[:2]
    cols = data_ref.shape[0]
    spots = len(message_refs) * BCAP

    def clear(index, carry):
        total_ref[index] = jnp.zeros((cols, BS), F32)
        return carry

    lax.fori_loop(0, spots, clear, 0, unroll=8)

    def one_pair(pair, carry):
        before(pair)
        data = data_ref[:, lanes(pair)]
        high = data.astype(BF16)
        low = (data - high.astype(F32)).astype(BF16)
        pieces = jnp.concatenate([high, low], axis=0)
        for slot in range(0, slot_count, 2):
            rays = jnp.concatenate([rays_ref[pair, slot], rays_ref[pair, slot + 1]], axis=1)
            part = jnp.dot(pieces, rays, preferred_element_type=F32)
            part = part[:cols] + part[cols:]
            for half in range(2):
                spot = target_ref[pair * slot_count + slot + half]
                total_ref[spot] += part[:, half * BS : (half + 1) * BS]
        return carry

    lax.fori_loop(0, pair_count, one_pair, 0, unroll=True)

    for peer, message_ref in enumerate(message_refs):
        for rank in range(BCAP):
            message_ref[rank * cols : (rank + 1) * cols, :] = total_ref[
                peer * BCAP + rank
            ].astype(BF16)


def start_kernel(peers, me_ref, cells_hbm, counts_hbm, times_hbm, rays_hbm, *refs):
    message_refs = refs[:peers]
    target_ref, total_ref, table_ref, used_ref, cells_ref, counts_ref = refs[peers : peers + 6]
    times_ref, rays_ref, place_ref, sems, ray_sems = refs[peers + 6 :]
    for index, step in enumerate(steps_of(peers)):
        place_ref[me_ref[0] ^ step] = index
    pair_count, slot_count = rays_ref.shape[:2]
    cols = times_ref.shape[0]
    owned = CELL_DEV // BS
    copies = [
        pltpu.make_async_copy(source, dest, sems.at[index])
        for index, (source, dest) in enumerate(
            [(cells_hbm, cells_ref), (counts_hbm, counts_ref), (times_hbm, times_ref)]
        )
    ]
    for copy in copies:
        copy.start()

    def ray_copy(pair):
        return pltpu.make_async_copy(rays_hbm.at[pair], rays_ref.at[pair], ray_sems.at[pair])

    def fetch(pair, carry):
        ray_copy(pair).start()
        return carry

    lax.fori_loop(0, pair_count, fetch, 0)

    def clear(peer, carry):
        used_ref[peer] = 0
        for rank in range(BCAP):
            table_ref[peer * BCAP + rank] = 0
        return carry

    lax.fori_loop(0, peers, clear, 0)
    for copy in copies:
        copy.wait()

    def find_places(pair):
        count = counts_ref[pair]
        for slot in range(slot_count):
            cell = cells_ref[pair, slot]
            owner = place_ref[cell // owned]
            local = cell % owned
            used = used_ref[owner]
            rank = used
            for other in range(BCAP - 1, -1, -1):
                same = (table_ref[owner * BCAP + other] == local) & (other < used)
                rank = jnp.where(same, other, rank)
            spot = owner * BCAP + rank
            table_ref[spot] = local
            used_ref[owner] = jnp.maximum(used, rank + 1)
            target_ref[pair * slot_count + slot] = jnp.where(slot < count, spot, peers * BCAP)

    def before(pair):
        find_places(pair)
        ray_copy(pair).wait()

    transposed(times_ref, rays_ref, before, target_ref, total_ref, message_refs)
    squares = jnp.zeros((cols, BS), F32)
    for pair in range(pair_count):
        part = times_ref[:, pair * BS : (pair + 1) * BS]
        squares += part * part
    tail = squares_tail(squares)
    place = lax.broadcasted_iota(jnp.int32, (TAIL, BS), 0)
    lane = lax.broadcasted_iota(jnp.int32, (TAIL, BS), 1)

    for peer, message_ref in enumerate(message_refs):
        rows = tail
        for rank in range(BCAP):
            asked = table_ref[peer * BCAP + rank].astype(F32)
            rows = jnp.where((place == 3) & (lane == rank), asked, rows)
        message_ref[BCAP * cols :, :] = rows.astype(BF16)


def keep_kernel(target_hbm, own_hbm, rays_hbm, target_ref, own_ref, rays_ref, sems):
    copies = [
        pltpu.make_async_copy(source, dest, sems.at[index])
        for index, (source, dest) in enumerate(
            [(target_hbm, target_ref), (own_hbm, own_ref), (rays_hbm, rays_ref)]
        )
    ]
    for copy in copies:
        copy.start()
    for copy in copies:
        copy.wait()


def pair_kernel(peers, target_ref, *refs):
    fetched_refs = refs[:peers]
    data_ref, beta_ref, rays_ref = refs[peers : peers + 3]
    message_refs = refs[peers + 3 : 2 * peers + 3]
    alpha_ref, raw_ref, total_ref, fetched_ref = refs[2 * peers + 3 :]
    pair_count, slot_count = rays_ref.shape[:2]
    cols = data_ref.shape[0]
    spots = peers * BCAP
    for peer in range(peers):
        fetched_ref[peer] = fetched_refs[peer][: BCAP * cols, :]
    alpha = norm_of_tails(fetched_refs, cols)
    alpha_ref[...] = alpha
    beta = beta_ref[...]
    model_scale = 1.0 / (alpha * beta)
    data_scale = alpha / beta

    def one_pair(pair, squares):
        chosen = []
        for slot in range(slot_count):
            spot = target_ref[pair * slot_count + slot]
            live = spot < spots
            spot = jnp.where(live, spot, 0)
            rows = pl.ds(pl.multiple_of((spot % BCAP) * cols, cols), cols)
            block = fetched_ref[spot // BCAP, rows, :]
            chosen.append(jnp.where(live, block, jnp.zeros_like(block)))
        rays = jnp.concatenate([rays_ref[pair, slot] for slot in range(slot_count)], axis=1)
        product = lax.dot_general(
            rays, jnp.concatenate(chosen, axis=1), (((1,), (1,)), ((), ())),
            preferred_element_type=F32,
        )
        raw = product.T * model_scale - data_ref[:, lanes(pair)] * data_scale
        raw_ref[:, lanes(pair)] = raw
        return squares + raw * raw

    squares = lax.fori_loop(0, pair_count, one_pair, jnp.zeros((cols, BS), F32), unroll=True)
    transposed(raw_ref, rays_ref, lambda pair: None, target_ref, total_ref, message_refs)
    tail = squares_tail(squares).astype(BF16)
    for message_ref in message_refs:
        message_ref[BCAP * cols :, :] = tail


def gathered(arrived_refs, asked_ref, model_ref):
    cols = model_ref.shape[0]
    for peer, arrived_ref in enumerate(arrived_refs):
        for rank in range(BCAP):
            where = lanes(asked_ref[peer, rank])
            model_ref[:, where] += arrived_ref[rank * cols : (rank + 1) * cols, :].astype(F32)


def reply(squares, scale, asked_ref, model_ref, out_refs):
    cols = model_ref.shape[0]
    tail = squares_tail(squares * scale * scale).astype(BF16)
    for peer, out_ref in enumerate(out_refs):
        out_ref[BCAP * cols :, :] = tail
        for rank in range(BCAP):
            block = model_ref[:, lanes(asked_ref[peer, rank])]
            out_ref[rank * cols : (rank + 1) * cols, :] = block.astype(BF16)


def squares_of(model_ref):
    cols, cells = model_ref.shape

    def one_block(block, squares):
        values = model_ref[:, lanes(block)]
        return squares + values * values

    return lax.fori_loop(0, cells // BS, one_block, jnp.zeros((cols, BS), F32), unroll=8)


def first_cell_kernel(peers, *refs):
    arrived_refs, out_refs = refs[:peers], refs[peers + 2 : 2 * peers + 2]
    model_ref, beta_ref = refs[peers : peers + 2]
    asked_ref, table_ref, sem = refs[2 * peers + 2 :]
    cols, cells = model_ref.shape
    for peer in range(peers):
        tail = arrived_refs[peer][BCAP * cols :, :].astype(F32)
        table_ref[peer : peer + 1, :] = tail[3:4].astype(jnp.int32)
    copy = pltpu.make_async_copy(table_ref, asked_ref, sem)
    copy.start()
    beta = norm_of_tails(arrived_refs, cols)
    beta_ref[...] = beta
    model_ref[...] = jnp.zeros((cols, cells), F32)
    copy.wait()
    gathered(arrived_refs, asked_ref, model_ref)
    reply(squares_of(model_ref), 1.0 / beta, asked_ref, model_ref, out_refs)


def start_from(before_ref, scale, model_ref):
    def one_block(block, carry):
        model_ref[:, lanes(block)] = before_ref[:, lanes(block)] * -scale
        return carry

    lax.fori_loop(0, model_ref.shape[1] // BS, one_block, 0, unroll=8)


def cell_kernel(peers, asked_ref, *refs):
    arrived_refs, out_refs = refs[:peers], refs[peers + 5 :]
    before_ref, alpha_ref, beta_before_ref, model_ref, beta_ref = refs[peers : peers + 5]
    beta = norm_of_tails(arrived_refs, model_ref.shape[0])
    beta_ref[...] = beta
    start_from(before_ref, beta * beta / (alpha_ref[...] * beta_before_ref[...]), model_ref)
    gathered(arrived_refs, asked_ref, model_ref)
    reply(squares_of(model_ref), 1.0 / beta, asked_ref, model_ref, out_refs)


def last_cell_kernel(peers, asked_ref, *refs):
    arrived_refs = refs[:peers]
    before_ref, alpha_ref, beta_before_ref, model_ref, beta_ref, out_ref = refs[peers:]
    beta = norm_of_tails(arrived_refs, model_ref.shape[0])
    beta_ref[...] = beta
    start_from(before_ref, beta * beta / (alpha_ref[...] * beta_before_ref[...]), model_ref)
    gathered(arrived_refs, asked_ref, model_ref)
    squares = squares_of(model_ref) / (beta * beta)
    total = jnp.sum(squares, axis=1, keepdims=True)
    row = jnp.sum(jnp.where(diagonal(total.shape[0]), total, 0.0), axis=0, keepdims=True)
    out_ref[...] = jnp.broadcast_to(row, out_ref.shape)


def estimate_kernel(*refs):
    models = refs[:ITERS]
    alphas = [ref[...] for ref in refs[ITERS : 2 * ITERS]]
    betas = [ref[...] for ref in refs[2 * ITERS : 3 * ITERS + 1]]
    estimate_hbm, estimate_ref, sems = refs[3 * ITERS + 1 :]
    cells = estimate_ref.shape[1]
    weights = estimate_weights(betas, alphas)
    blocks = cells // BS // CHUNKS

    def one_block(block, carry):
        where = lanes(block)
        total = weights[0] * models[0][:, where]
        for i in range(1, ITERS):
            total += weights[i] * models[i][:, where]
        estimate_ref[:, where] = total
        return carry

    copies = []
    for chunk in range(CHUNKS):
        lax.fori_loop(chunk * blocks, (chunk + 1) * blocks, one_block, 0, unroll=4)
        where = slice(chunk * blocks * BS, (chunk + 1) * blocks * BS)
        copies.append(
            pltpu.make_async_copy(
                estimate_ref.at[:, where], estimate_hbm.at[:, where], sems.at[chunk]
            )
        )
        copies[-1].start()
    for copy in copies:
        copy.wait()


def estimate_weights(betas, alphas):
    phi_bar = betas[0]
    rho_bar = alphas[0]
    trace = [1.0 / (alphas[0] * betas[0])]
    weight = [jnp.zeros_like(phi_bar)] * ITERS
    for step in range(ITERS):
        beta = betas[step + 1]
        rho = jnp.sqrt(rho_bar * rho_bar + beta * beta)
        cosine = rho_bar / rho
        sine = beta / rho
        gain = cosine * phi_bar / rho
        weight = [
            weight[i] + gain * trace[i] if i < len(trace) else weight[i] for i in range(ITERS)
        ]
        if step + 1 < ITERS:
            alpha = alphas[step + 1]
            theta = sine * alpha
            rho_bar = -cosine * alpha
            phi_bar = sine * phi_bar
            trace = [-(theta / rho) * value for value in trace] + [1.0 / (alpha * beta)]
    return weight


def model_kernel(*refs):
    *share_refs, beta_ref, model_ref, out_hbm, out_ref, sems = refs
    cols, cells = model_ref.shape
    blocks = cells // BS // CHUNKS
    row = sum(ref[...] for ref in share_refs)[0:1]
    column = jnp.sum(jnp.where(diagonal(cols), row, 0.0), axis=1, keepdims=True)
    alpha = jnp.broadcast_to(jnp.sqrt(column + EPS), (cols, BS))
    scale = 1.0 / (alpha * beta_ref[...])

    def one_block(block, carry):
        out_ref[:, lanes(block)] = model_ref[:, lanes(block)] * scale
        return carry

    copies = []
    for chunk in range(CHUNKS):
        lax.fori_loop(chunk * blocks, (chunk + 1) * blocks, one_block, 0, unroll=4)
        where = slice(chunk * blocks * BS, (chunk + 1) * blocks * BS)
        copies.append(
            pltpu.make_async_copy(out_ref.at[:, where], out_hbm.at[:, where], sems.at[chunk])
        )
        copies[-1].start()
    for copy in copies:
        copy.wait()


def call(kernel, name, in_spaces, outs, scratch=(), flops=0, moved=0, limit=16 << 20):
    return pl.pallas_call(
        kernel,
        name=name,
        in_specs=[pl.BlockSpec(memory_space=space) for space in in_spaces],
        out_specs=[pl.BlockSpec(memory_space=space) for _, _, space in outs],
        out_shape=[jax.ShapeDtypeStruct(shape, dtype) for shape, dtype, _ in outs],
        scratch_shapes=list(scratch),
        compiler_params=pltpu.CompilerParams(vmem_limit_bytes=limit),
        cost_estimate=pl.CostEstimate(flops=flops, bytes_accessed=moved, transcendentals=0),
    )


def on_device(ray_blocks, block_cells, block_counts, travel_times):
    pair_count, slot_count = ray_blocks.shape[:2]
    slots = pair_count * slot_count
    peers = lax.axis_size("pair")
    spots = peers * BCAP
    times = travel_times.T
    cols, pairs = times.shape
    messages = [((BCAP * cols + TAIL, BS), BF16, VMEM)] * peers
    ins = [VMEM] * peers
    gathered_blocks = VMEM((peers, BCAP * cols, BS), BF16)
    tile = ((cols, BS), F32, VMEM)
    data = ((cols, pairs), F32, VMEM)
    whole = ((cols, CELL_DEV), F32, VMEM)
    totals = VMEM((spots + 1, cols, BS), F32)
    flops = 2 * slots * BS * BS * cols

    steps = steps_of(peers)

    def exchange(values):
        return [values[0]] + [
            lax.ppermute(value, "pair", [(one, one ^ step) for one in range(peers)])
            for value, step in zip(values[1:], steps[1:])
        ]

    me = lax.axis_index("pair").astype(jnp.int32).reshape(1)
    *outgoing, target = call(
        functools.partial(start_kernel, peers), "start", [SMEM, HBM, HBM, HBM, HBM],
        messages + [((slots,), jnp.int32, SMEM)],
        [
            totals, SMEM((spots,), jnp.int32), SMEM((peers,), jnp.int32),
            SMEM(block_cells.shape, jnp.int32), SMEM(block_counts.shape, jnp.int32),
            VMEM(times.shape, F32), VMEM(ray_blocks.shape, BF16), SMEM((peers,), jnp.int32),
            pltpu.SemaphoreType.DMA((3,)), pltpu.SemaphoreType.DMA((pair_count,)),
        ],
        flops, 6 << 20, 60 << 20,
    )(me, block_cells, block_counts, times, ray_blocks)
    arrived = exchange(outgoing)
    target, arrived[0], ray_blocks = call(
        keep_kernel, "keep", [HBM, HBM, HBM],
        [((slots,), jnp.int32, SMEM), messages[0], (ray_blocks.shape, BF16, VMEM)],
        [pltpu.SemaphoreType.DMA((3,))], 0, 8 << 20, 48 << 20,
    )(target, arrived[0], ray_blocks)
    model, beta, *replies, asked = call(
        functools.partial(first_cell_kernel, peers), "cells_first", ins,
        [whole, tile] + messages + [((peers, BS), jnp.int32, SMEM)],
        [VMEM((peers, BS), jnp.int32), pltpu.SemaphoreType.DMA],
        0, 6 << 20,
    )(*arrived)
    models, betas, alphas = [model], [beta], []
    current = times
    for step in range(ITERS):
        fetched = exchange(replies)
        last = step + 1 == ITERS
        made = call(
            functools.partial(pair_kernel, peers), "pairs_last" if last else "pairs",
            [SMEM] + ins + [VMEM, VMEM, VMEM], messages + [tile] + [data] * (not last),
            [VMEM(data[0], F32)] * last + [totals, gathered_blocks], 2 * flops, 8 << 20,
        )(target, *fetched, current, betas[-1], ray_blocks)
        alphas.append(made[peers])
        current = made[-1]
        arrived = exchange(made[:peers])
        if not last:
            model, beta, *replies = call(
                functools.partial(cell_kernel, peers), "cells", [SMEM] + ins + [VMEM] * 3,
                [whole, tile] + messages, (), 0, 8 << 20,
            )(asked, *arrived, models[-1], alphas[-1], betas[-1])
            models.append(model)
            betas.append(beta)
    model, beta, share = call(
        functools.partial(last_cell_kernel, peers), "cells_last", [SMEM] + ins + [VMEM] * 3,
        [whole, tile, ((8, BS), F32, VMEM)], (), 0, 8 << 20,
    )(asked, *arrived, models[-1], alphas[-1], betas[-1])
    betas.append(beta)
    reach, shares = peers, [share]
    while reach > 1:
        share = sum(shares[1:], shares[0])
        low = max(reach // 4, 1)
        shares = [share] + [
            lax.ppermute(share, "pair", [(one, one ^ step) for one in range(peers)])
            for step in range(low, reach, low)
        ]
        reach = low
    scratch = [VMEM(whole[0], F32), pltpu.SemaphoreType.DMA((CHUNKS,))]
    (estimate,) = call(
        estimate_kernel, "estimate", [VMEM] * (3 * ITERS + 1), [(whole[0], F32, HBM)], scratch,
        0, 6 << 20,
    )(*models, *alphas, *betas)
    (model_vec,) = call(
        model_kernel, "model", [VMEM] * (len(shares) + 2), [(whole[0], F32, HBM)], scratch,
        0, 4 << 20,
    )(*shares, beta, model)
    return (estimate.T, model_vec.T)


def solution(mesh):
    return jax.shard_map(
        on_device,
        mesh=mesh,
        in_specs=(
            P(("groups", "pair"), None, None, None),
            P(("groups", "pair"), None),
            P(("groups", "pair")),
            P(("groups", "pair"), None),
        ),
        out_specs=(P(("groups", "pair"), None), P(("groups", "pair"), None)),
        check_vma=False,
    )
```

```python
import functools

import jax
import jax.numpy as jnp
from jax import lax
from jax.experimental import pallas as pl
from jax.experimental.pallas import tpu as pltpu
from jax.sharding import PartitionSpec as P

CELL_DEV = 8192
BCAP = 4
BS = 128
TAIL = 8
ITERS = 2
EPS = 1e-12
F32 = jnp.float32
BF16 = jnp.bfloat16
VMEM = pltpu.VMEM
SMEM = pltpu.SMEM
HBM = pltpu.HBM
CHUNKS = 8


def steps_of(peers):
    half, quarter = peers // 2, peers // 4
    near = [step for low in range(quarter) for step in (quarter + low, low) if step]
    return [0, half] + [step for low in near for step in (low, half + low)]


def diagonal(cols):
    shape = (cols, BS)
    return lax.broadcasted_iota(jnp.int32, shape, 0) == lax.broadcasted_iota(jnp.int32, shape, 1)


def squares_tail(squares):
    cols = squares.shape[0]
    total = jnp.sum(squares, axis=1, keepdims=True)
    row = jnp.sum(jnp.where(diagonal(cols), total, 0.0), axis=0, keepdims=True)
    high = row.astype(BF16).astype(F32)
    middle = (row - high).astype(BF16).astype(F32)
    low = row - high - middle
    place = lax.broadcasted_iota(jnp.int32, (TAIL, BS), 0)
    return jnp.where(
        place == 0, high, jnp.where(place == 1, middle, jnp.where(place == 2, low, 0.0))
    )


def norm_of_tails(message_refs, cols):
    summed = sum(message_ref[BCAP * cols :, :].astype(F32) for message_ref in message_refs)
    row = summed[0:1] + summed[1:2] + summed[2:3]
    column = jnp.sum(jnp.where(diagonal(cols), row, 0.0), axis=1, keepdims=True)
    return jnp.broadcast_to(jnp.sqrt(column + EPS), (cols, BS))


def lanes(block):
    return pl.ds(pl.multiple_of(block * BS, BS), BS)


def transposed(data_ref, rays_ref, before, target_ref, total_ref, message_refs):
    pair_count, slot_count = rays_ref.shape[:2]
    cols = data_ref.shape[0]
    spots = len(message_refs) * BCAP

    def clear(index, carry):
        total_ref[index] = jnp.zeros((cols, BS), F32)
        return carry

    lax.fori_loop(0, spots, clear, 0, unroll=8)

    def one_pair(pair, carry):
        before(pair)
        data = data_ref[:, lanes(pair)]
        high = data.astype(BF16)
        low = (data - high.astype(F32)).astype(BF16)
        pieces = jnp.concatenate([high, low], axis=0)
        for slot in range(0, slot_count, 2):
            rays = jnp.concatenate([rays_ref[pair, slot], rays_ref[pair, slot + 1]], axis=1)
            part = jnp.dot(pieces, rays, preferred_element_type=F32)
            part = part[:cols] + part[cols:]
            for half in range(2):
                spot = target_ref[pair * slot_count + slot + half]
                total_ref[spot] += part[:, half * BS : (half + 1) * BS]
        return carry

    lax.fori_loop(0, pair_count, one_pair, 0, unroll=True)

    for peer, message_ref in enumerate(message_refs):
        for rank in range(BCAP):
            message_ref[rank * cols : (rank + 1) * cols, :] = total_ref[
                peer * BCAP + rank
            ].astype(BF16)


def start_kernel(peers, me_ref, cells_hbm, counts_hbm, times_hbm, rays_hbm, *refs):
    message_refs = refs[:peers]
    target_ref, total_ref, table_ref, used_ref, cells_ref, counts_ref = refs[peers : peers + 6]
    times_ref, rays_ref, place_ref, sems, ray_sems = refs[peers + 6 :]
    for index, step in enumerate(steps_of(peers)):
        place_ref[me_ref[0] ^ step] = index
    pair_count, slot_count = rays_ref.shape[:2]
    cols = times_ref.shape[0]
    owned = CELL_DEV // BS
    copies = [
        pltpu.make_async_copy(source, dest, sems.at[index])
        for index, (source, dest) in enumerate(
            [(cells_hbm, cells_ref), (counts_hbm, counts_ref), (times_hbm, times_ref)]
        )
    ]
    for copy in copies:
        copy.start()

    def ray_copy(pair):
        return pltpu.make_async_copy(rays_hbm.at[pair], rays_ref.at[pair], ray_sems.at[pair])

    def fetch(pair, carry):
        ray_copy(pair).start()
        return carry

    lax.fori_loop(0, pair_count, fetch, 0)

    def clear(peer, carry):
        used_ref[peer] = 0
        for rank in range(BCAP):
            table_ref[peer * BCAP + rank] = 0
        return carry

    lax.fori_loop(0, peers, clear, 0)
    for copy in copies:
        copy.wait()

    def find_places(pair):
        count = counts_ref[pair]
        for slot in range(slot_count):
            cell = cells_ref[pair, slot]
            owner = place_ref[cell // owned]
            local = cell % owned
            used = used_ref[owner]
            rank = used
            for other in range(BCAP - 1, -1, -1):
                same = (table_ref[owner * BCAP + other] == local) & (other < used)
                rank = jnp.where(same, other, rank)
            spot = owner * BCAP + rank
            table_ref[spot] = local
            used_ref[owner] = jnp.maximum(used, rank + 1)
            target_ref[pair * slot_count + slot] = jnp.where(slot < count, spot, peers * BCAP)

    def before(pair):
        find_places(pair)
        ray_copy(pair).wait()

    transposed(times_ref, rays_ref, before, target_ref, total_ref, message_refs)
    squares = jnp.zeros((cols, BS), F32)
    for pair in range(pair_count):
        part = times_ref[:, pair * BS : (pair + 1) * BS]
        squares += part * part
    tail = squares_tail(squares)
    place = lax.broadcasted_iota(jnp.int32, (TAIL, BS), 0)
    lane = lax.broadcasted_iota(jnp.int32, (TAIL, BS), 1)

    for peer, message_ref in enumerate(message_refs):
        rows = tail
        for rank in range(BCAP):
            asked = table_ref[peer * BCAP + rank].astype(F32)
            rows = jnp.where((place == 3) & (lane == rank), asked, rows)
        message_ref[BCAP * cols :, :] = rows.astype(BF16)


def keep_kernel(target_hbm, own_hbm, rays_hbm, target_ref, own_ref, rays_ref, sems):
    copies = [
        pltpu.make_async_copy(source, dest, sems.at[index])
        for index, (source, dest) in enumerate(
            [(target_hbm, target_ref), (own_hbm, own_ref), (rays_hbm, rays_ref)]
        )
    ]
    for copy in copies:
        copy.start()
    for copy in copies:
        copy.wait()


def pair_kernel(peers, target_ref, *refs):
    fetched_refs = refs[:peers]
    data_ref, beta_ref, rays_ref = refs[peers : peers + 3]
    message_refs = refs[peers + 3 : 2 * peers + 3]
    alpha_ref, raw_ref, total_ref, fetched_ref = refs[2 * peers + 3 :]
    pair_count, slot_count = rays_ref.shape[:2]
    cols = data_ref.shape[0]
    spots = peers * BCAP
    for peer in range(peers):
        fetched_ref[peer] = fetched_refs[peer][: BCAP * cols, :]
    alpha = norm_of_tails(fetched_refs, cols)
    alpha_ref[...] = alpha
    beta = beta_ref[...]
    model_scale = 1.0 / (alpha * beta)
    data_scale = alpha / beta

    def one_pair(pair, squares):
        chosen = []
        for slot in range(slot_count):
            spot = target_ref[pair * slot_count + slot]
            live = spot < spots
            spot = jnp.where(live, spot, 0)
            rows = pl.ds(pl.multiple_of((spot % BCAP) * cols, cols), cols)
            block = fetched_ref[spot // BCAP, rows, :]
            chosen.append(jnp.where(live, block, jnp.zeros_like(block)))
        rays = jnp.concatenate([rays_ref[pair, slot] for slot in range(slot_count)], axis=1)
        product = lax.dot_general(
            rays, jnp.concatenate(chosen, axis=1), (((1,), (1,)), ((), ())),
            preferred_element_type=F32,
        )
        raw = product.T * model_scale - data_ref[:, lanes(pair)] * data_scale
        raw_ref[:, lanes(pair)] = raw
        return squares + raw * raw

    squares = lax.fori_loop(0, pair_count, one_pair, jnp.zeros((cols, BS), F32), unroll=True)
    transposed(raw_ref, rays_ref, lambda pair: None, target_ref, total_ref, message_refs)
    tail = squares_tail(squares).astype(BF16)
    for message_ref in message_refs:
        message_ref[BCAP * cols :, :] = tail


def gathered(arrived_refs, asked_ref, model_ref):
    cols = model_ref.shape[0]
    for peer, arrived_ref in enumerate(arrived_refs):
        for rank in range(BCAP):
            where = lanes(asked_ref[peer, rank])
            model_ref[:, where] += arrived_ref[rank * cols : (rank + 1) * cols, :].astype(F32)


def reply(squares, scale, asked_ref, model_ref, out_refs):
    cols = model_ref.shape[0]
    tail = squares_tail(squares * scale * scale).astype(BF16)
    for peer, out_ref in enumerate(out_refs):
        out_ref[BCAP * cols :, :] = tail
        for rank in range(BCAP):
            block = model_ref[:, lanes(asked_ref[peer, rank])]
            out_ref[rank * cols : (rank + 1) * cols, :] = block.astype(BF16)


def squares_of(model_ref):
    cols, cells = model_ref.shape

    def one_block(block, squares):
        values = model_ref[:, lanes(block)]
        return squares + values * values

    return lax.fori_loop(0, cells // BS, one_block, jnp.zeros((cols, BS), F32), unroll=8)


def first_cell_kernel(peers, *refs):
    arrived_refs, out_refs = refs[:peers], refs[peers + 2 : 2 * peers + 2]
    model_ref, beta_ref = refs[peers : peers + 2]
    asked_ref, table_ref, sem = refs[2 * peers + 2 :]
    cols, cells = model_ref.shape
    for peer in range(peers):
        tail = arrived_refs[peer][BCAP * cols :, :].astype(F32)
        table_ref[peer : peer + 1, :] = tail[3:4].astype(jnp.int32)
    copy = pltpu.make_async_copy(table_ref, asked_ref, sem)
    copy.start()
    beta = norm_of_tails(arrived_refs, cols)
    beta_ref[...] = beta
    model_ref[...] = jnp.zeros((cols, cells), F32)
    copy.wait()
    gathered(arrived_refs, asked_ref, model_ref)
    reply(squares_of(model_ref), 1.0 / beta, asked_ref, model_ref, out_refs)


def start_from(before_ref, scale, model_ref):
    def one_block(block, carry):
        model_ref[:, lanes(block)] = before_ref[:, lanes(block)] * -scale
        return carry

    lax.fori_loop(0, model_ref.shape[1] // BS, one_block, 0, unroll=8)


def cell_kernel(peers, asked_ref, *refs):
    arrived_refs, out_refs = refs[:peers], refs[peers + 5 :]
    before_ref, alpha_ref, beta_before_ref, model_ref, beta_ref = refs[peers : peers + 5]
    beta = norm_of_tails(arrived_refs, model_ref.shape[0])
    beta_ref[...] = beta
    start_from(before_ref, beta * beta / (alpha_ref[...] * beta_before_ref[...]), model_ref)
    gathered(arrived_refs, asked_ref, model_ref)
    reply(squares_of(model_ref), 1.0 / beta, asked_ref, model_ref, out_refs)


def last_cell_kernel(peers, asked_ref, *refs):
    arrived_refs = refs[:peers]
    before_ref, alpha_ref, beta_before_ref, model_ref, beta_ref, out_ref = refs[peers:]
    beta = norm_of_tails(arrived_refs, model_ref.shape[0])
    beta_ref[...] = beta
    start_from(before_ref, beta * beta / (alpha_ref[...] * beta_before_ref[...]), model_ref)
    gathered(arrived_refs, asked_ref, model_ref)
    squares = squares_of(model_ref) / (beta * beta)
    total = jnp.sum(squares, axis=1, keepdims=True)
    row = jnp.sum(jnp.where(diagonal(total.shape[0]), total, 0.0), axis=0, keepdims=True)
    out_ref[...] = jnp.broadcast_to(row, out_ref.shape)


def estimate_kernel(*refs):
    models = refs[:ITERS]
    alphas = [ref[...] for ref in refs[ITERS : 2 * ITERS]]
    betas = [ref[...] for ref in refs[2 * ITERS : 3 * ITERS + 1]]
    estimate_hbm, estimate_ref, sems = refs[3 * ITERS + 1 :]
    cells = estimate_ref.shape[1]
    weights = estimate_weights(betas, alphas)
    blocks = cells // BS // CHUNKS

    def one_block(block, carry):
        where = lanes(block)
        total = weights[0] * models[0][:, where]
        for i in range(1, ITERS):
            total += weights[i] * models[i][:, where]
        estimate_ref[:, where] = total
        return carry

    copies = []
    for chunk in range(CHUNKS):
        lax.fori_loop(chunk * blocks, (chunk + 1) * blocks, one_block, 0, unroll=4)
        where = slice(chunk * blocks * BS, (chunk + 1) * blocks * BS)
        copies.append(
            pltpu.make_async_copy(
                estimate_ref.at[:, where], estimate_hbm.at[:, where], sems.at[chunk]
            )
        )
        copies[-1].start()
    for copy in copies:
        copy.wait()


def estimate_weights(betas, alphas):
    phi_bar = betas[0]
    rho_bar = alphas[0]
    trace = [1.0 / (alphas[0] * betas[0])]
    weight = [jnp.zeros_like(phi_bar)] * ITERS
    for step in range(ITERS):
        beta = betas[step + 1]
        rho = jnp.sqrt(rho_bar * rho_bar + beta * beta)
        cosine = rho_bar / rho
        sine = beta / rho
        gain = cosine * phi_bar / rho
        weight = [
            weight[i] + gain * trace[i] if i < len(trace) else weight[i] for i in range(ITERS)
        ]
        if step + 1 < ITERS:
            alpha = alphas[step + 1]
            theta = sine * alpha
            rho_bar = -cosine * alpha
            phi_bar = sine * phi_bar
            trace = [-(theta / rho) * value for value in trace] + [1.0 / (alpha * beta)]
    return weight


def model_kernel(*refs):
    *share_refs, beta_ref, model_ref, out_hbm, out_ref, sems = refs
    cols, cells = model_ref.shape
    blocks = cells // BS // CHUNKS
    row = sum(ref[...] for ref in share_refs)[0:1]
    column = jnp.sum(jnp.where(diagonal(cols), row, 0.0), axis=1, keepdims=True)
    alpha = jnp.broadcast_to(jnp.sqrt(column + EPS), (cols, BS))
    scale = 1.0 / (alpha * beta_ref[...])

    def one_block(block, carry):
        out_ref[:, lanes(block)] = model_ref[:, lanes(block)] * scale
        return carry

    copies = []
    for chunk in range(CHUNKS):
        lax.fori_loop(chunk * blocks, (chunk + 1) * blocks, one_block, 0, unroll=4)
        where = slice(chunk * blocks * BS, (chunk + 1) * blocks * BS)
        copies.append(
            pltpu.make_async_copy(out_ref.at[:, where], out_hbm.at[:, where], sems.at[chunk])
        )
        copies[-1].start()
    for copy in copies:
        copy.wait()


def call(kernel, name, in_spaces, outs, scratch=(), flops=0, moved=0, limit=16 << 20):
    return pl.pallas_call(
        kernel,
        name=name,
        in_specs=[pl.BlockSpec(memory_space=space) for space in in_spaces],
        out_specs=[pl.BlockSpec(memory_space=space) for _, _, space in outs],
        out_shape=[jax.ShapeDtypeStruct(shape, dtype) for shape, dtype, _ in outs],
        scratch_shapes=list(scratch),
        compiler_params=pltpu.CompilerParams(vmem_limit_bytes=limit),
        cost_estimate=pl.CostEstimate(flops=flops, bytes_accessed=moved, transcendentals=0),
    )


def on_device(ray_blocks, block_cells, block_counts, travel_times):
    pair_count, slot_count = ray_blocks.shape[:2]
    slots = pair_count * slot_count
    peers = lax.axis_size("pair")
    spots = peers * BCAP
    times = travel_times.T
    cols, pairs = times.shape
    messages = [((BCAP * cols + TAIL, BS), BF16, VMEM)] * peers
    ins = [VMEM] * peers
    gathered_blocks = VMEM((peers, BCAP * cols, BS), BF16)
    tile = ((cols, BS), F32, VMEM)
    data = ((cols, pairs), F32, VMEM)
    whole = ((cols, CELL_DEV), F32, VMEM)
    totals = VMEM((spots + 1, cols, BS), F32)
    flops = 2 * slots * BS * BS * cols

    steps = steps_of(peers)

    def exchange(values):
        return [values[0]] + [
            lax.ppermute(value, "pair", [(one, one ^ step) for one in range(peers)])
            for value, step in zip(values[1:], steps[1:])
        ]

    me = lax.axis_index("pair").astype(jnp.int32).reshape(1)
    *outgoing, target = call(
        functools.partial(start_kernel, peers), "start", [SMEM, HBM, HBM, HBM, HBM],
        messages + [((slots,), jnp.int32, SMEM)],
        [
            totals, SMEM((spots,), jnp.int32), SMEM((peers,), jnp.int32),
            SMEM(block_cells.shape, jnp.int32), SMEM(block_counts.shape, jnp.int32),
            VMEM(times.shape, F32), VMEM(ray_blocks.shape, BF16), SMEM((peers,), jnp.int32),
            pltpu.SemaphoreType.DMA((3,)), pltpu.SemaphoreType.DMA((pair_count,)),
        ],
        flops, 6 << 20, 60 << 20,
    )(me, block_cells, block_counts, times, ray_blocks)
    arrived = exchange(outgoing)
    target, arrived[0], ray_blocks = call(
        keep_kernel, "keep", [HBM, HBM, HBM],
        [((slots,), jnp.int32, SMEM), messages[0], (ray_blocks.shape, BF16, VMEM)],
        [pltpu.SemaphoreType.DMA((3,))], 0, 8 << 20, 48 << 20,
    )(target, arrived[0], ray_blocks)
    model, beta, *replies, asked = call(
        functools.partial(first_cell_kernel, peers), "cells_first", ins,
        [whole, tile] + messages + [((peers, BS), jnp.int32, SMEM)],
        [VMEM((peers, BS), jnp.int32), pltpu.SemaphoreType.DMA],
        0, 6 << 20,
    )(*arrived)
    models, betas, alphas = [model], [beta], []
    current = times
    for step in range(ITERS):
        fetched = exchange(replies)
        last = step + 1 == ITERS
        made = call(
            functools.partial(pair_kernel, peers), "pairs_last" if last else "pairs",
            [SMEM] + ins + [VMEM, VMEM, VMEM], messages + [tile] + [data] * (not last),
            [VMEM(data[0], F32)] * last + [totals, gathered_blocks], 2 * flops, 8 << 20,
        )(target, *fetched, current, betas[-1], ray_blocks)
        alphas.append(made[peers])
        current = made[-1]
        arrived = exchange(made[:peers])
        if not last:
            model, beta, *replies = call(
                functools.partial(cell_kernel, peers), "cells", [SMEM] + ins + [VMEM] * 3,
                [whole, tile] + messages, (), 0, 8 << 20,
            )(asked, *arrived, models[-1], alphas[-1], betas[-1])
            models.append(model)
            betas.append(beta)
    model, beta, share = call(
        functools.partial(last_cell_kernel, peers), "cells_last", [SMEM] + ins + [VMEM] * 3,
        [whole, tile, ((8, BS), F32, VMEM)], (), 0, 8 << 20,
    )(asked, *arrived, models[-1], alphas[-1], betas[-1])
    betas.append(beta)
    reach, shares = peers, [share]
    while reach > 1:
        share = sum(shares[1:], shares[0])
        low = max(reach // 4, 1)
        shares = [share] + [
            lax.ppermute(share, "pair", [(one, one ^ step) for one in range(peers)])
            for step in range(low, reach, low)
        ]
        reach = low
    scratch = [VMEM(whole[0], F32), pltpu.SemaphoreType.DMA((CHUNKS,))]
    (estimate,) = call(
        estimate_kernel, "estimate", [VMEM] * (3 * ITERS + 1), [(whole[0], F32, HBM)], scratch,
        0, 6 << 20,
    )(*models, *alphas, *betas)
    (model_vec,) = call(
        model_kernel, "model", [VMEM] * (len(shares) + 2), [(whole[0], F32, HBM)], scratch,
        0, 4 << 20,
    )(*shares, beta, model)
    return (estimate.T, model_vec.T)


def solution(mesh):
    return jax.shard_map(
        on_device,
        mesh=mesh,
        in_specs=(
            P(("groups", "pair"), None, None, None),
            P(("groups", "pair"), None),
            P(("groups", "pair")),
            P(("groups", "pair"), None),
        ),
        out_specs=(P(("groups", "pair"), None), P(("groups", "pair"), None)),
        check_vma=False,
    )
```

```python
import functools

import jax
import jax.numpy as jnp
from jax import lax
from jax.experimental import pallas as pl
from jax.experimental.pallas import tpu as pltpu
from jax.sharding import PartitionSpec as P

CELL_DEV = 8192
BCAP = 4
BS = 128
TAIL = 8
ITERS = 2
EPS = 1e-12
F32 = jnp.float32
BF16 = jnp.bfloat16
VMEM = pltpu.VMEM
SMEM = pltpu.SMEM
HBM = pltpu.HBM
CHUNKS = 8


def steps_of(peers):
    half, quarter = peers // 2, peers // 4
    lows = [low ^ low // 2 for low in range(quarter)]
    near = [step for low in lows for step in (low, quarter + low)][1:]
    return [0, half] + [step for low in near for step in (low, half + low)]


def diagonal(cols):
    shape = (cols, BS)
    return lax.broadcasted_iota(jnp.int32, shape, 0) == lax.broadcasted_iota(jnp.int32, shape, 1)


def squares_tail(squares):
    cols = squares.shape[0]
    total = jnp.sum(squares, axis=1, keepdims=True)
    row = jnp.sum(jnp.where(diagonal(cols), total, 0.0), axis=0, keepdims=True)
    high = row.astype(BF16).astype(F32)
    middle = (row - high).astype(BF16).astype(F32)
    low = row - high - middle
    place = lax.broadcasted_iota(jnp.int32, (TAIL, BS), 0)
    return jnp.where(
        place == 0, high, jnp.where(place == 1, middle, jnp.where(place == 2, low, 0.0))
    )


def norm_of_tails(message_refs, cols):
    summed = sum(message_ref[BCAP * cols :, :].astype(F32) for message_ref in message_refs)
    row = summed[0:1] + summed[1:2] + summed[2:3]
    column = jnp.sum(jnp.where(diagonal(cols), row, 0.0), axis=1, keepdims=True)
    return jnp.broadcast_to(jnp.sqrt(column + EPS), (cols, BS))


def lanes(block):
    return pl.ds(pl.multiple_of(block * BS, BS), BS)


def transposed(data_ref, rays_ref, before, target_ref, total_ref, message_refs):
    pair_count, slot_count = rays_ref.shape[:2]
    cols = data_ref.shape[0]
    spots = len(message_refs) * BCAP

    def clear(index, carry):
        total_ref[index] = jnp.zeros((cols, BS), F32)
        return carry

    lax.fori_loop(0, spots, clear, 0, unroll=8)

    def one_pair(pair, carry):
        before(pair)
        data = data_ref[:, lanes(pair)]
        high = data.astype(BF16)
        low = (data - high.astype(F32)).astype(BF16)
        pieces = jnp.concatenate([high, low], axis=0)
        for slot in range(0, slot_count, 2):
            rays = jnp.concatenate([rays_ref[pair, slot], rays_ref[pair, slot + 1]], axis=1)
            part = jnp.dot(pieces, rays, preferred_element_type=F32)
            part = part[:cols] + part[cols:]
            for half in range(2):
                spot = target_ref[pair * slot_count + slot + half]
                total_ref[spot] += part[:, half * BS : (half + 1) * BS]
        return carry

    lax.fori_loop(0, pair_count, one_pair, 0, unroll=True)

    for peer, message_ref in enumerate(message_refs):
        for rank in range(BCAP):
            message_ref[rank * cols : (rank + 1) * cols, :] = total_ref[
                peer * BCAP + rank
            ].astype(BF16)


def start_kernel(peers, me_ref, cells_hbm, counts_hbm, times_hbm, rays_hbm, *refs):
    message_refs = refs[:peers]
    target_ref, total_ref, table_ref, used_ref, cells_ref, counts_ref = refs[peers : peers + 6]
    times_ref, rays_ref, place_ref, sems, ray_sems = refs[peers + 6 :]
    for index, step in enumerate(steps_of(peers)):
        place_ref[me_ref[0] ^ step] = index
    pair_count, slot_count = rays_ref.shape[:2]
    cols = times_ref.shape[0]
    owned = CELL_DEV // BS
    copies = [
        pltpu.make_async_copy(source, dest, sems.at[index])
        for index, (source, dest) in enumerate(
            [(cells_hbm, cells_ref), (counts_hbm, counts_ref), (times_hbm, times_ref)]
        )
    ]
    for copy in copies:
        copy.start()

    def ray_copy(pair):
        return pltpu.make_async_copy(rays_hbm.at[pair], rays_ref.at[pair], ray_sems.at[pair])

    def fetch(pair, carry):
        ray_copy(pair).start()
        return carry

    lax.fori_loop(0, pair_count, fetch, 0)

    def clear(peer, carry):
        used_ref[peer] = 0
        for rank in range(BCAP):
            table_ref[peer * BCAP + rank] = 0
        return carry

    lax.fori_loop(0, peers, clear, 0)
    for copy in copies:
        copy.wait()

    def find_places(pair):
        count = counts_ref[pair]
        for slot in range(slot_count):
            cell = cells_ref[pair, slot]
            owner = place_ref[cell // owned]
            local = cell % owned
            used = used_ref[owner]
            rank = used
            for other in range(BCAP - 1, -1, -1):
                same = (table_ref[owner * BCAP + other] == local) & (other < used)
                rank = jnp.where(same, other, rank)
            spot = owner * BCAP + rank
            table_ref[spot] = local
            used_ref[owner] = jnp.maximum(used, rank + 1)
            target_ref[pair * slot_count + slot] = jnp.where(slot < count, spot, peers * BCAP)

    def before(pair):
        find_places(pair)
        ray_copy(pair).wait()

    transposed(times_ref, rays_ref, before, target_ref, total_ref, message_refs)
    squares = jnp.zeros((cols, BS), F32)
    for pair in range(pair_count):
        part = times_ref[:, pair * BS : (pair + 1) * BS]
        squares += part * part
    tail = squares_tail(squares)
    place = lax.broadcasted_iota(jnp.int32, (TAIL, BS), 0)
    lane = lax.broadcasted_iota(jnp.int32, (TAIL, BS), 1)

    for peer, message_ref in enumerate(message_refs):
        rows = tail
        for rank in range(BCAP):
            asked = table_ref[peer * BCAP + rank].astype(F32)
            rows = jnp.where((place == 3) & (lane == rank), asked, rows)
        message_ref[BCAP * cols :, :] = rows.astype(BF16)


def keep_kernel(target_hbm, own_hbm, rays_hbm, target_ref, own_ref, rays_ref, sems):
    copies = [
        pltpu.make_async_copy(source, dest, sems.at[index])
        for index, (source, dest) in enumerate(
            [(target_hbm, target_ref), (own_hbm, own_ref), (rays_hbm, rays_ref)]
        )
    ]
    for copy in copies:
        copy.start()
    for copy in copies:
        copy.wait()


def pair_kernel(peers, target_ref, *refs):
    fetched_refs = refs[:peers]
    data_ref, beta_ref, rays_ref = refs[peers : peers + 3]
    message_refs = refs[peers + 3 : 2 * peers + 3]
    alpha_ref, raw_ref, total_ref, fetched_ref = refs[2 * peers + 3 :]
    pair_count, slot_count = rays_ref.shape[:2]
    cols = data_ref.shape[0]
    spots = peers * BCAP
    for peer in range(peers):
        fetched_ref[peer] = fetched_refs[peer][: BCAP * cols, :]
    alpha = norm_of_tails(fetched_refs, cols)
    alpha_ref[...] = alpha
    beta = beta_ref[...]
    model_scale = 1.0 / (alpha * beta)
    data_scale = alpha / beta

    def one_pair(pair, squares):
        chosen = []
        for slot in range(slot_count):
            spot = target_ref[pair * slot_count + slot]
            live = spot < spots
            spot = jnp.where(live, spot, 0)
            rows = pl.ds(pl.multiple_of((spot % BCAP) * cols, cols), cols)
            block = fetched_ref[spot // BCAP, rows, :]
            chosen.append(jnp.where(live, block, jnp.zeros_like(block)))
        rays = jnp.concatenate([rays_ref[pair, slot] for slot in range(slot_count)], axis=1)
        product = lax.dot_general(
            rays, jnp.concatenate(chosen, axis=1), (((1,), (1,)), ((), ())),
            preferred_element_type=F32,
        )
        raw = product.T * model_scale - data_ref[:, lanes(pair)] * data_scale
        raw_ref[:, lanes(pair)] = raw
        return squares + raw * raw

    squares = lax.fori_loop(0, pair_count, one_pair, jnp.zeros((cols, BS), F32), unroll=True)
    transposed(raw_ref, rays_ref, lambda pair: None, target_ref, total_ref, message_refs)
    tail = squares_tail(squares).astype(BF16)
    for message_ref in message_refs:
        message_ref[BCAP * cols :, :] = tail


def gathered(arrived_refs, asked_ref, model_ref):
    cols = model_ref.shape[0]
    for peer, arrived_ref in enumerate(arrived_refs):
        for rank in range(BCAP):
            where = lanes(asked_ref[peer, rank])
            model_ref[:, where] += arrived_ref[rank * cols : (rank + 1) * cols, :].astype(F32)


def reply(squares, scale, asked_ref, model_ref, out_refs):
    cols = model_ref.shape[0]
    tail = squares_tail(squares * scale * scale).astype(BF16)
    for peer, out_ref in enumerate(out_refs):
        out_ref[BCAP * cols :, :] = tail
        for rank in range(BCAP):
            block = model_ref[:, lanes(asked_ref[peer, rank])]
            out_ref[rank * cols : (rank + 1) * cols, :] = block.astype(BF16)


def squares_of(model_ref):
    cols, cells = model_ref.shape

    def one_block(block, squares):
        values = model_ref[:, lanes(block)]
        return squares + values * values

    return lax.fori_loop(0, cells // BS, one_block, jnp.zeros((cols, BS), F32), unroll=32)


def first_cell_kernel(peers, *refs):
    arrived_refs, out_refs = refs[:peers], refs[peers + 2 : 2 * peers + 2]
    model_ref, beta_ref = refs[peers : peers + 2]
    asked_ref, table_ref, sem = refs[2 * peers + 2 :]
    cols, cells = model_ref.shape
    for peer in range(peers):
        tail = arrived_refs[peer][BCAP * cols :, :].astype(F32)
        table_ref[peer : peer + 1, :] = tail[3:4].astype(jnp.int32)
    copy = pltpu.make_async_copy(table_ref, asked_ref, sem)
    copy.start()
    beta = norm_of_tails(arrived_refs, cols)
    beta_ref[...] = beta
    model_ref[...] = jnp.zeros((cols, cells), F32)
    copy.wait()
    gathered(arrived_refs, asked_ref, model_ref)
    reply(squares_of(model_ref), 1.0 / beta, asked_ref, model_ref, out_refs)


def start_from(before_ref, scale, model_ref):
    def one_block(block, carry):
        model_ref[:, lanes(block)] = before_ref[:, lanes(block)] * -scale
        return carry

    lax.fori_loop(0, model_ref.shape[1] // BS, one_block, 0, unroll=32)


def cell_kernel(peers, asked_ref, *refs):
    arrived_refs, out_refs = refs[:peers], refs[peers + 5 :]
    before_ref, alpha_ref, beta_before_ref, model_ref, beta_ref = refs[peers : peers + 5]
    beta = norm_of_tails(arrived_refs, model_ref.shape[0])
    beta_ref[...] = beta
    start_from(before_ref, beta * beta / (alpha_ref[...] * beta_before_ref[...]), model_ref)
    gathered(arrived_refs, asked_ref, model_ref)
    reply(squares_of(model_ref), 1.0 / beta, asked_ref, model_ref, out_refs)


def last_cell_kernel(peers, asked_ref, *refs):
    arrived_refs = refs[:peers]
    before_ref, alpha_ref, beta_before_ref, model_ref, beta_ref, out_ref = refs[peers:]
    beta = norm_of_tails(arrived_refs, model_ref.shape[0])
    beta_ref[...] = beta
    start_from(before_ref, beta * beta / (alpha_ref[...] * beta_before_ref[...]), model_ref)
    gathered(arrived_refs, asked_ref, model_ref)
    squares = squares_of(model_ref) / (beta * beta)
    total = jnp.sum(squares, axis=1, keepdims=True)
    row = jnp.sum(jnp.where(diagonal(total.shape[0]), total, 0.0), axis=0, keepdims=True)
    out_ref[...] = jnp.broadcast_to(row, out_ref.shape)


def estimate_kernel(*refs):
    models = refs[:ITERS]
    alphas = [ref[...] for ref in refs[ITERS : 2 * ITERS]]
    betas = [ref[...] for ref in refs[2 * ITERS : 3 * ITERS + 1]]
    estimate_hbm, estimate_ref, sems = refs[3 * ITERS + 1 :]
    cells = estimate_ref.shape[1]
    weights = estimate_weights(betas, alphas)
    blocks = cells // BS // CHUNKS

    def one_block(block, carry):
        where = lanes(block)
        total = weights[0] * models[0][:, where]
        for i in range(1, ITERS):
            total += weights[i] * models[i][:, where]
        estimate_ref[:, where] = total
        return carry

    copies = []
    for chunk in range(CHUNKS):
        lax.fori_loop(chunk * blocks, (chunk + 1) * blocks, one_block, 0, unroll=True)
        where = slice(chunk * blocks * BS, (chunk + 1) * blocks * BS)
        copies.append(
            pltpu.make_async_copy(
                estimate_ref.at[:, where], estimate_hbm.at[:, where], sems.at[chunk]
            )
        )
        copies[-1].start()
    for copy in copies:
        copy.wait()


def estimate_weights(betas, alphas):
    phi_bar = betas[0]
    rho_bar = alphas[0]
    trace = [1.0 / (alphas[0] * betas[0])]
    weight = [jnp.zeros_like(phi_bar)] * ITERS
    for step in range(ITERS):
        beta = betas[step + 1]
        rho = jnp.sqrt(rho_bar * rho_bar + beta * beta)
        cosine = rho_bar / rho
        sine = beta / rho
        gain = cosine * phi_bar / rho
        weight = [
            weight[i] + gain * trace[i] if i < len(trace) else weight[i] for i in range(ITERS)
        ]
        if step + 1 < ITERS:
            alpha = alphas[step + 1]
            theta = sine * alpha
            rho_bar = -cosine * alpha
            phi_bar = sine * phi_bar
            trace = [-(theta / rho) * value for value in trace] + [1.0 / (alpha * beta)]
    return weight


def model_kernel(*refs):
    *share_refs, beta_ref, model_ref, out_hbm, out_ref, sems = refs
    cols, cells = model_ref.shape
    blocks = cells // BS // CHUNKS
    row = sum(ref[...] for ref in share_refs)[0:1]
    column = jnp.sum(jnp.where(diagonal(cols), row, 0.0), axis=1, keepdims=True)
    alpha = jnp.broadcast_to(jnp.sqrt(column + EPS), (cols, BS))
    scale = 1.0 / (alpha * beta_ref[...])

    def one_block(block, carry):
        out_ref[:, lanes(block)] = model_ref[:, lanes(block)] * scale
        return carry

    copies = []
    for chunk in range(CHUNKS):
        lax.fori_loop(chunk * blocks, (chunk + 1) * blocks, one_block, 0, unroll=True)
        where = slice(chunk * blocks * BS, (chunk + 1) * blocks * BS)
        copies.append(
            pltpu.make_async_copy(out_ref.at[:, where], out_hbm.at[:, where], sems.at[chunk])
        )
        copies[-1].start()
    for copy in copies:
        copy.wait()


def call(kernel, name, in_spaces, outs, scratch=(), flops=0, moved=0, limit=16 << 20):
    return pl.pallas_call(
        kernel,
        name=name,
        in_specs=[pl.BlockSpec(memory_space=space) for space in in_spaces],
        out_specs=[pl.BlockSpec(memory_space=space) for _, _, space in outs],
        out_shape=[jax.ShapeDtypeStruct(shape, dtype) for shape, dtype, _ in outs],
        scratch_shapes=list(scratch),
        compiler_params=pltpu.CompilerParams(vmem_limit_bytes=limit),
        cost_estimate=pl.CostEstimate(flops=flops, bytes_accessed=moved, transcendentals=0),
    )


def on_device(ray_blocks, block_cells, block_counts, travel_times):
    pair_count, slot_count = ray_blocks.shape[:2]
    slots = pair_count * slot_count
    peers = lax.axis_size("pair")
    spots = peers * BCAP
    times = travel_times.T
    cols, pairs = times.shape
    messages = [((BCAP * cols + TAIL, BS), BF16, VMEM)] * peers
    ins = [VMEM] * peers
    gathered_blocks = VMEM((peers, BCAP * cols, BS), BF16)
    tile = ((cols, BS), F32, VMEM)
    data = ((cols, pairs), F32, VMEM)
    whole = ((cols, CELL_DEV), F32, VMEM)
    totals = VMEM((spots + 1, cols, BS), F32)
    flops = 2 * slots * BS * BS * cols

    steps = steps_of(peers)

    def exchange(values):
        return [values[0]] + [
            lax.ppermute(value, "pair", [(one, one ^ step) for one in range(peers)])
            for value, step in zip(values[1:], steps[1:])
        ]

    me = lax.axis_index("pair").astype(jnp.int32).reshape(1)
    *outgoing, target = call(
        functools.partial(start_kernel, peers), "start", [SMEM, HBM, HBM, HBM, HBM],
        messages + [((slots,), jnp.int32, SMEM)],
        [
            totals, SMEM((spots,), jnp.int32), SMEM((peers,), jnp.int32),
            SMEM(block_cells.shape, jnp.int32), SMEM(block_counts.shape, jnp.int32),
            VMEM(times.shape, F32), VMEM(ray_blocks.shape, BF16), SMEM((peers,), jnp.int32),
            pltpu.SemaphoreType.DMA((3,)), pltpu.SemaphoreType.DMA((pair_count,)),
        ],
        flops, 6 << 20, 60 << 20,
    )(me, block_cells, block_counts, times, ray_blocks)
    arrived = exchange(outgoing)
    target, arrived[0], ray_blocks = call(
        keep_kernel, "keep", [HBM, HBM, HBM],
        [((slots,), jnp.int32, SMEM), messages[0], (ray_blocks.shape, BF16, VMEM)],
        [pltpu.SemaphoreType.DMA((3,))], 0, 8 << 20, 48 << 20,
    )(target, arrived[0], ray_blocks)
    model, beta, *replies, asked = call(
        functools.partial(first_cell_kernel, peers), "cells_first", ins,
        [whole, tile] + messages + [((peers, BS), jnp.int32, SMEM)],
        [VMEM((peers, BS), jnp.int32), pltpu.SemaphoreType.DMA],
        0, 6 << 20,
    )(*arrived)
    models, betas, alphas = [model], [beta], []
    current = times
    for step in range(ITERS):
        fetched = exchange(replies)
        last = step + 1 == ITERS
        made = call(
            functools.partial(pair_kernel, peers), "pairs_last" if last else "pairs",
            [SMEM] + ins + [VMEM, VMEM, VMEM], messages + [tile] + [data] * (not last),
            [VMEM(data[0], F32)] * last + [totals, gathered_blocks], 2 * flops, 8 << 20,
        )(target, *fetched, current, betas[-1], ray_blocks)
        alphas.append(made[peers])
        current = made[-1]
        arrived = exchange(made[:peers])
        if not last:
            model, beta, *replies = call(
                functools.partial(cell_kernel, peers), "cells", [SMEM] + ins + [VMEM] * 3,
                [whole, tile] + messages, (), 0, 8 << 20,
            )(asked, *arrived, models[-1], alphas[-1], betas[-1])
            models.append(model)
            betas.append(beta)
    model, beta, share = call(
        functools.partial(last_cell_kernel, peers), "cells_last", [SMEM] + ins + [VMEM] * 3,
        [whole, tile, ((8, BS), F32, VMEM)], (), 0, 8 << 20,
    )(asked, *arrived, models[-1], alphas[-1], betas[-1])
    betas.append(beta)
    reach, shares = peers, [share]
    while reach > 1:
        share = sum(shares[1:], shares[0])
        low = max(reach // 4, 1)
        shares = [share] + [
            lax.ppermute(share, "pair", [(one, one ^ step) for one in range(peers)])
            for step in range(low, reach, low)
        ]
        reach = low
    scratch = [VMEM(whole[0], F32), pltpu.SemaphoreType.DMA((CHUNKS,))]
    (estimate,) = call(
        estimate_kernel, "estimate", [VMEM] * (3 * ITERS + 1), [(whole[0], F32, HBM)], scratch,
        0, 6 << 20,
    )(*models, *alphas, *betas)
    (model_vec,) = call(
        model_kernel, "model", [VMEM] * (len(shares) + 2), [(whole[0], F32, HBM)], scratch,
        0, 4 << 20,
    )(*shares, beta, model)
    return (estimate.T, model_vec.T)


def solution(mesh):
    return jax.shard_map(
        on_device,
        mesh=mesh,
        in_specs=(
            P(("groups", "pair"), None, None, None),
            P(("groups", "pair"), None),
            P(("groups", "pair")),
            P(("groups", "pair"), None),
        ),
        out_specs=(P(("groups", "pair"), None), P(("groups", "pair"), None)),
        check_vma=False,
    )
```

```python
import functools

import jax
import jax.numpy as jnp
from jax import lax
from jax.experimental import pallas as pl
from jax.experimental.pallas import tpu as pltpu
from jax.sharding import PartitionSpec as P

CELL_DEV = 8192
BCAP = 4
BS = 128
TAIL = 8
ITERS = 2
EPS = 1e-12
F32 = jnp.float32
BF16 = jnp.bfloat16
VMEM = pltpu.VMEM
SMEM = pltpu.SMEM
HBM = pltpu.HBM
CHUNKS = 8


def steps_of(peers):
    half, quarter = peers // 2, peers // 4
    near = [step for low in range(quarter) for step in (low, quarter + low)][1:]
    return [0, half] + [step for low in near for step in (low, half + low)]


def diagonal(cols):
    shape = (cols, BS)
    return lax.broadcasted_iota(jnp.int32, shape, 0) == lax.broadcasted_iota(jnp.int32, shape, 1)


def squares_tail(squares):
    cols = squares.shape[0]
    total = jnp.sum(squares, axis=1, keepdims=True)
    row = jnp.sum(jnp.where(diagonal(cols), total, 0.0), axis=0, keepdims=True)
    high = row.astype(BF16).astype(F32)
    middle = (row - high).astype(BF16).astype(F32)
    low = row - high - middle
    place = lax.broadcasted_iota(jnp.int32, (TAIL, BS), 0)
    return jnp.where(
        place == 0, high, jnp.where(place == 1, middle, jnp.where(place == 2, low, 0.0))
    )


def norm_of_tails(message_refs, cols):
    summed = sum(message_ref[BCAP * cols :, :].astype(F32) for message_ref in message_refs)
    row = summed[0:1] + summed[1:2] + summed[2:3]
    column = jnp.sum(jnp.where(diagonal(cols), row, 0.0), axis=1, keepdims=True)
    return jnp.broadcast_to(jnp.sqrt(column + EPS), (cols, BS))


def lanes(block):
    return pl.ds(pl.multiple_of(block * BS, BS), BS)


def transposed(data_ref, rays_ref, begin, before, target_ref, total_ref, message_refs):
    pair_count, slot_count = rays_ref.shape[:2]
    cols = data_ref.shape[0]
    spots = len(message_refs) * BCAP

    def clear(index, carry):
        total_ref[index] = jnp.zeros((cols, BS), F32)
        return carry

    lax.fori_loop(0, spots, clear, 0, unroll=8)
    begin()

    def one_pair(pair, carry):
        before(pair)
        data = data_ref[:, lanes(pair)]
        high = data.astype(BF16)
        low = (data - high.astype(F32)).astype(BF16)
        pieces = jnp.concatenate([high, low], axis=0)
        for slot in range(0, slot_count, 2):
            rays = jnp.concatenate([rays_ref[pair, slot], rays_ref[pair, slot + 1]], axis=1)
            part = jnp.dot(pieces, rays, preferred_element_type=F32)
            part = part[:cols] + part[cols:]
            for half in range(2):
                spot = target_ref[pair * slot_count + slot + half]
                total_ref[spot] += part[:, half * BS : (half + 1) * BS]
        return carry

    lax.fori_loop(0, pair_count, one_pair, 0, unroll=True)

    for peer, message_ref in enumerate(message_refs):
        for rank in range(BCAP):
            message_ref[rank * cols : (rank + 1) * cols, :] = total_ref[
                peer * BCAP + rank
            ].astype(BF16)


def start_kernel(peers, me_ref, cells_hbm, counts_hbm, times_hbm, rays_hbm, *refs):
    message_refs = refs[:peers]
    target_ref, total_ref, table_ref, used_ref, cells_ref, counts_ref = refs[peers : peers + 6]
    times_ref, rays_ref, place_ref, sems, ray_sems = refs[peers + 6 :]
    for index, step in enumerate(steps_of(peers)):
        place_ref[me_ref[0] ^ step] = index
    pair_count, slot_count = rays_ref.shape[:2]
    cols = times_ref.shape[0]
    owned = CELL_DEV // BS
    copies = [
        pltpu.make_async_copy(source, dest, sems.at[index])
        for index, (source, dest) in enumerate(
            [(cells_hbm, cells_ref), (counts_hbm, counts_ref), (times_hbm, times_ref)]
        )
    ]
    for copy in copies:
        copy.start()

    def ray_copy(pair):
        return pltpu.make_async_copy(rays_hbm.at[pair], rays_ref.at[pair], ray_sems.at[pair])

    def fetch(pair, carry):
        ray_copy(pair).start()
        return carry

    lax.fori_loop(0, pair_count, fetch, 0)

    def clear(peer, carry):
        used_ref[peer] = 0
        for rank in range(BCAP):
            table_ref[peer * BCAP + rank] = 0
        return carry

    lax.fori_loop(0, peers, clear, 0)
    def find_places(pair):
        count = counts_ref[pair]
        for slot in range(slot_count):
            cell = cells_ref[pair, slot]
            owner = place_ref[cell // owned]
            local = cell % owned
            used = used_ref[owner]
            rank = used
            for other in range(BCAP - 1, -1, -1):
                same = (table_ref[owner * BCAP + other] == local) & (other < used)
                rank = jnp.where(same, other, rank)
            spot = owner * BCAP + rank
            table_ref[spot] = local
            used_ref[owner] = jnp.maximum(used, rank + 1)
            target_ref[pair * slot_count + slot] = jnp.where(slot < count, spot, peers * BCAP)

    def before(pair):
        find_places(pair)
        ray_copy(pair).wait()

    def begin():
        for copy in copies:
            copy.wait()
        squares = jnp.zeros((cols, BS), F32)
        for pair in range(pair_count):
            values = times_ref[:, pair * BS : (pair + 1) * BS]
            squares += values * values
        tail = squares_tail(squares).astype(BF16)
        for message_ref in message_refs:
            message_ref[BCAP * cols :, :] = tail

    transposed(times_ref, rays_ref, begin, before, target_ref, total_ref, message_refs)
    place = lax.broadcasted_iota(jnp.int32, (TAIL, BS), 0)
    lane = lax.broadcasted_iota(jnp.int32, (TAIL, BS), 1)
    for peer, message_ref in enumerate(message_refs):
        rows = message_ref[BCAP * cols :, :].astype(F32)
        for rank in range(BCAP):
            asked = table_ref[peer * BCAP + rank].astype(F32)
            rows = jnp.where((place == 3) & (lane == rank), asked, rows)
        message_ref[BCAP * cols :, :] = rows.astype(BF16)


def keep_kernel(target_hbm, own_hbm, rays_hbm, target_ref, own_ref, rays_ref, sems):
    copies = [
        pltpu.make_async_copy(source, dest, sems.at[index])
        for index, (source, dest) in enumerate(
            [(target_hbm, target_ref), (own_hbm, own_ref), (rays_hbm, rays_ref)]
        )
    ]
    for copy in copies:
        copy.start()
    for copy in copies:
        copy.wait()


def pair_kernel(peers, target_ref, *refs):
    fetched_refs = refs[:peers]
    data_ref, beta_ref, rays_ref = refs[peers : peers + 3]
    message_refs = refs[peers + 3 : 2 * peers + 3]
    alpha_ref, raw_ref, total_ref, fetched_ref = refs[2 * peers + 3 :]
    pair_count, slot_count = rays_ref.shape[:2]
    cols = data_ref.shape[0]
    spots = peers * BCAP
    for peer in range(peers):
        fetched_ref[peer] = fetched_refs[peer][: BCAP * cols, :]
    alpha = norm_of_tails(fetched_refs, cols)
    alpha_ref[...] = alpha
    beta = beta_ref[...]
    model_scale = 1.0 / (alpha * beta)
    data_scale = alpha / beta

    def one_pair(pair, squares):
        chosen = []
        for slot in range(slot_count):
            spot = target_ref[pair * slot_count + slot]
            live = spot < spots
            spot = jnp.where(live, spot, 0)
            rows = pl.ds(pl.multiple_of((spot % BCAP) * cols, cols), cols)
            block = fetched_ref[spot // BCAP, rows, :]
            chosen.append(jnp.where(live, block, jnp.zeros_like(block)))
        rays = jnp.concatenate([rays_ref[pair, slot] for slot in range(slot_count)], axis=1)
        product = lax.dot_general(
            rays, jnp.concatenate(chosen, axis=1), (((1,), (1,)), ((), ())),
            preferred_element_type=F32,
        )
        raw = product.T * model_scale - data_ref[:, lanes(pair)] * data_scale
        raw_ref[:, lanes(pair)] = raw
        return squares + raw * raw

    squares = lax.fori_loop(0, pair_count, one_pair, jnp.zeros((cols, BS), F32), unroll=True)
    transposed(
        raw_ref, rays_ref, lambda: None, lambda pair: None, target_ref, total_ref, message_refs
    )
    tail = squares_tail(squares).astype(BF16)
    for message_ref in message_refs:
        message_ref[BCAP * cols :, :] = tail


def gathered(arrived_refs, asked_ref, model_ref):
    cols = model_ref.shape[0]
    for peer, arrived_ref in enumerate(arrived_refs):
        for rank in range(BCAP):
            where = lanes(asked_ref[peer, rank])
            model_ref[:, where] += arrived_ref[rank * cols : (rank + 1) * cols, :].astype(F32)


def reply(squares, scale, asked_ref, model_ref, out_refs):
    cols = model_ref.shape[0]
    tail = squares_tail(squares * scale * scale).astype(BF16)
    for peer, out_ref in enumerate(out_refs):
        out_ref[BCAP * cols :, :] = tail
        for rank in range(BCAP):
            block = model_ref[:, lanes(asked_ref[peer, rank])]
            out_ref[rank * cols : (rank + 1) * cols, :] = block.astype(BF16)


def squares_of(model_ref):
    cols, cells = model_ref.shape

    def one_block(block, squares):
        values = model_ref[:, lanes(block)]
        return squares + values * values

    return lax.fori_loop(0, cells // BS, one_block, jnp.zeros((cols, BS), F32), unroll=32)


def first_cell_kernel(peers, *refs):
    arrived_refs, out_refs = refs[:peers], refs[peers + 2 : 2 * peers + 2]
    model_ref, beta_ref = refs[peers : peers + 2]
    asked_ref, table_ref, sem = refs[2 * peers + 2 :]
    cols, cells = model_ref.shape
    for peer in range(peers):
        tail = arrived_refs[peer][BCAP * cols :, :].astype(F32)
        table_ref[peer : peer + 1, :] = tail[3:4].astype(jnp.int32)
    copy = pltpu.make_async_copy(table_ref, asked_ref, sem)
    copy.start()
    beta = norm_of_tails(arrived_refs, cols)
    beta_ref[...] = beta
    model_ref[...] = jnp.zeros((cols, cells), F32)
    copy.wait()
    gathered(arrived_refs, asked_ref, model_ref)
    reply(squares_of(model_ref), 1.0 / beta, asked_ref, model_ref, out_refs)


def start_from(before_ref, scale, model_ref):
    def one_block(block, carry):
        model_ref[:, lanes(block)] = before_ref[:, lanes(block)] * -scale
        return carry

    lax.fori_loop(0, model_ref.shape[1] // BS, one_block, 0, unroll=32)


def cell_kernel(peers, asked_ref, *refs):
    arrived_refs, out_refs = refs[:peers], refs[peers + 5 :]
    before_ref, alpha_ref, beta_before_ref, model_ref, beta_ref = refs[peers : peers + 5]
    beta = norm_of_tails(arrived_refs, model_ref.shape[0])
    beta_ref[...] = beta
    start_from(before_ref, beta * beta / (alpha_ref[...] * beta_before_ref[...]), model_ref)
    gathered(arrived_refs, asked_ref, model_ref)
    reply(squares_of(model_ref), 1.0 / beta, asked_ref, model_ref, out_refs)


def last_cell_kernel(peers, asked_ref, *refs):
    arrived_refs = refs[:peers]
    before_ref, alpha_ref, beta_before_ref, model_ref, beta_ref, out_ref = refs[peers:]
    beta = norm_of_tails(arrived_refs, model_ref.shape[0])
    beta_ref[...] = beta
    start_from(before_ref, beta * beta / (alpha_ref[...] * beta_before_ref[...]), model_ref)
    gathered(arrived_refs, asked_ref, model_ref)
    squares = squares_of(model_ref) / (beta * beta)
    total = jnp.sum(squares, axis=1, keepdims=True)
    row = jnp.sum(jnp.where(diagonal(total.shape[0]), total, 0.0), axis=0, keepdims=True)
    out_ref[...] = jnp.broadcast_to(row, out_ref.shape)


def estimate_kernel(*refs):
    models = refs[:ITERS]
    alphas = [ref[...] for ref in refs[ITERS : 2 * ITERS]]
    betas = [ref[...] for ref in refs[2 * ITERS : 3 * ITERS + 1]]
    estimate_hbm, estimate_ref, sems = refs[3 * ITERS + 1 :]
    cells = estimate_ref.shape[1]
    weights = estimate_weights(betas, alphas)
    blocks = cells // BS // CHUNKS

    def one_block(block, carry):
        where = lanes(block)
        total = weights[0] * models[0][:, where]
        for i in range(1, ITERS):
            total += weights[i] * models[i][:, where]
        estimate_ref[:, where] = total
        return carry

    copies = []
    for chunk in range(CHUNKS):
        lax.fori_loop(chunk * blocks, (chunk + 1) * blocks, one_block, 0, unroll=True)
        where = slice(chunk * blocks * BS, (chunk + 1) * blocks * BS)
        copies.append(
            pltpu.make_async_copy(
                estimate_ref.at[:, where], estimate_hbm.at[:, where], sems.at[chunk]
            )
        )
        copies[-1].start()
    for copy in copies:
        copy.wait()


def estimate_weights(betas, alphas):
    phi_bar = betas[0]
    rho_bar = alphas[0]
    trace = [1.0 / (alphas[0] * betas[0])]
    weight = [jnp.zeros_like(phi_bar)] * ITERS
    for step in range(ITERS):
        beta = betas[step + 1]
        rho = jnp.sqrt(rho_bar * rho_bar + beta * beta)
        cosine = rho_bar / rho
        sine = beta / rho
        gain = cosine * phi_bar / rho
        weight = [
            weight[i] + gain * trace[i] if i < len(trace) else weight[i] for i in range(ITERS)
        ]
        if step + 1 < ITERS:
            alpha = alphas[step + 1]
            theta = sine * alpha
            rho_bar = -cosine * alpha
            phi_bar = sine * phi_bar
            trace = [-(theta / rho) * value for value in trace] + [1.0 / (alpha * beta)]
    return weight


def model_kernel(*refs):
    *share_refs, beta_ref, model_ref, out_hbm, out_ref, sems = refs
    cols, cells = model_ref.shape
    blocks = cells // BS // CHUNKS
    row = sum(ref[...] for ref in share_refs)[0:1]
    column = jnp.sum(jnp.where(diagonal(cols), row, 0.0), axis=1, keepdims=True)
    alpha = jnp.broadcast_to(jnp.sqrt(column + EPS), (cols, BS))
    scale = 1.0 / (alpha * beta_ref[...])

    def one_block(block, carry):
        out_ref[:, lanes(block)] = model_ref[:, lanes(block)] * scale
        return carry

    copies = []
    for chunk in range(CHUNKS):
        lax.fori_loop(chunk * blocks, (chunk + 1) * blocks, one_block, 0, unroll=True)
        where = slice(chunk * blocks * BS, (chunk + 1) * blocks * BS)
        copies.append(
            pltpu.make_async_copy(out_ref.at[:, where], out_hbm.at[:, where], sems.at[chunk])
        )
        copies[-1].start()
    for copy in copies:
        copy.wait()


def call(kernel, name, in_spaces, outs, scratch=(), flops=0, moved=0, limit=16 << 20):
    return pl.pallas_call(
        kernel,
        name=name,
        in_specs=[pl.BlockSpec(memory_space=space) for space in in_spaces],
        out_specs=[pl.BlockSpec(memory_space=space) for _, _, space in outs],
        out_shape=[jax.ShapeDtypeStruct(shape, dtype) for shape, dtype, _ in outs],
        scratch_shapes=list(scratch),
        compiler_params=pltpu.CompilerParams(vmem_limit_bytes=limit),
        cost_estimate=pl.CostEstimate(flops=flops, bytes_accessed=moved, transcendentals=0),
    )


def on_device(ray_blocks, block_cells, block_counts, travel_times):
    pair_count, slot_count = ray_blocks.shape[:2]
    slots = pair_count * slot_count
    peers = lax.axis_size("pair")
    spots = peers * BCAP
    times = travel_times.T
    cols, pairs = times.shape
    messages = [((BCAP * cols + TAIL, BS), BF16, VMEM)] * peers
    ins = [VMEM] * peers
    gathered_blocks = VMEM((peers, BCAP * cols, BS), BF16)
    tile = ((cols, BS), F32, VMEM)
    data = ((cols, pairs), F32, VMEM)
    whole = ((cols, CELL_DEV), F32, VMEM)
    totals = VMEM((spots + 1, cols, BS), F32)
    flops = 2 * slots * BS * BS * cols

    steps = steps_of(peers)

    def exchange(values):
        return [values[0]] + [
            lax.ppermute(value, "pair", [(one, one ^ step) for one in range(peers)])
            for value, step in zip(values[1:], steps[1:])
        ]

    me = lax.axis_index("pair").astype(jnp.int32).reshape(1)
    *outgoing, target = call(
        functools.partial(start_kernel, peers), "start", [SMEM, HBM, HBM, HBM, HBM],
        messages + [((slots,), jnp.int32, SMEM)],
        [
            totals, SMEM((spots,), jnp.int32), SMEM((peers,), jnp.int32),
            SMEM(block_cells.shape, jnp.int32), SMEM(block_counts.shape, jnp.int32),
            VMEM(times.shape, F32), VMEM(ray_blocks.shape, BF16), SMEM((peers,), jnp.int32),
            pltpu.SemaphoreType.DMA((3,)), pltpu.SemaphoreType.DMA((pair_count,)),
        ],
        flops, 6 << 20, 60 << 20,
    )(me, block_cells, block_counts, times, ray_blocks)
    arrived = exchange(outgoing)
    target, arrived[0], ray_blocks = call(
        keep_kernel, "keep", [HBM, HBM, HBM],
        [((slots,), jnp.int32, SMEM), messages[0], (ray_blocks.shape, BF16, VMEM)],
        [pltpu.SemaphoreType.DMA((3,))], 0, 8 << 20, 48 << 20,
    )(target, arrived[0], ray_blocks)
    model, beta, *replies, asked = call(
        functools.partial(first_cell_kernel, peers), "cells_first", ins,
        [whole, tile] + messages + [((peers, BS), jnp.int32, SMEM)],
        [VMEM((peers, BS), jnp.int32), pltpu.SemaphoreType.DMA],
        0, 6 << 20,
    )(*arrived)
    models, betas, alphas = [model], [beta], []
    current = times
    for step in range(ITERS):
        fetched = exchange(replies)
        last = step + 1 == ITERS
        made = call(
            functools.partial(pair_kernel, peers), "pairs_last" if last else "pairs",
            [SMEM] + ins + [VMEM, VMEM, VMEM], messages + [tile] + [data] * (not last),
            [VMEM(data[0], F32)] * last + [totals, gathered_blocks], 2 * flops, 8 << 20,
        )(target, *fetched, current, betas[-1], ray_blocks)
        alphas.append(made[peers])
        current = made[-1]
        arrived = exchange(made[:peers])
        if not last:
            model, beta, *replies = call(
                functools.partial(cell_kernel, peers), "cells", [SMEM] + ins + [VMEM] * 3,
                [whole, tile] + messages, (), 0, 8 << 20,
            )(asked, *arrived, models[-1], alphas[-1], betas[-1])
            models.append(model)
            betas.append(beta)
    model, beta, share = call(
        functools.partial(last_cell_kernel, peers), "cells_last", [SMEM] + ins + [VMEM] * 3,
        [whole, tile, ((8, BS), F32, VMEM)], (), 0, 8 << 20,
    )(asked, *arrived, models[-1], alphas[-1], betas[-1])
    betas.append(beta)
    reach, shares = peers, [share]
    while reach > 1:
        share = sum(shares[1:], shares[0])
        low = max(reach // 4, 1)
        shares = [share] + [
            lax.ppermute(share, "pair", [(one, one ^ step) for one in range(peers)])
            for step in range(low, reach, low)
        ]
        reach = low
    scratch = [VMEM(whole[0], F32), pltpu.SemaphoreType.DMA((CHUNKS,))]
    (estimate,) = call(
        estimate_kernel, "estimate", [VMEM] * (3 * ITERS + 1), [(whole[0], F32, HBM)], scratch,
        0, 6 << 20,
    )(*models, *alphas, *betas)
    (model_vec,) = call(
        model_kernel, "model", [VMEM] * (len(shares) + 2), [(whole[0], F32, HBM)], scratch,
        0, 4 << 20,
    )(*shares, beta, model)
    return (estimate.T, model_vec.T)


def solution(mesh):
    return jax.shard_map(
        on_device,
        mesh=mesh,
        in_specs=(
            P(("groups", "pair"), None, None, None),
            P(("groups", "pair"), None),
            P(("groups", "pair")),
            P(("groups", "pair"), None),
        ),
        out_specs=(P(("groups", "pair"), None), P(("groups", "pair"), None)),
        check_vma=False,
    )
```

```python
import functools

import jax
import jax.numpy as jnp
from jax import lax
from jax.experimental import pallas as pl
from jax.experimental.pallas import tpu as pltpu
from jax.sharding import PartitionSpec as P

CELL_DEV = 8192
BCAP = 4
BS = 128
TAIL = 8
ITERS = 2
EPS = 1e-12
F32 = jnp.float32
BF16 = jnp.bfloat16
VMEM = pltpu.VMEM
SMEM = pltpu.SMEM
HBM = pltpu.HBM
CHUNKS = 8


def steps_of(peers):
    half, quarter = peers // 2, peers // 4
    near = [step for low in range(quarter) for step in (low, quarter + low)][1:]
    return [0] + [step for low in near for step in (low, half + low)] + [half]


def diagonal(cols):
    shape = (cols, BS)
    return lax.broadcasted_iota(jnp.int32, shape, 0) == lax.broadcasted_iota(jnp.int32, shape, 1)


def squares_tail(squares):
    cols = squares.shape[0]
    total = jnp.sum(squares, axis=1, keepdims=True)
    row = jnp.sum(jnp.where(diagonal(cols), total, 0.0), axis=0, keepdims=True)
    high = row.astype(BF16).astype(F32)
    middle = (row - high).astype(BF16).astype(F32)
    low = row - high - middle
    place = lax.broadcasted_iota(jnp.int32, (TAIL, BS), 0)
    return jnp.where(
        place == 0, high, jnp.where(place == 1, middle, jnp.where(place == 2, low, 0.0))
    )


def norm_of_tails(message_refs, cols):
    summed = sum(message_ref[BCAP * cols :, :].astype(F32) for message_ref in message_refs)
    row = summed[0:1] + summed[1:2] + summed[2:3]
    column = jnp.sum(jnp.where(diagonal(cols), row, 0.0), axis=1, keepdims=True)
    return jnp.broadcast_to(jnp.sqrt(column + EPS), (cols, BS))


def lanes(block):
    return pl.ds(pl.multiple_of(block * BS, BS), BS)


def transposed(data_ref, rays_ref, begin, before, target_ref, total_ref, message_refs):
    pair_count, slot_count = rays_ref.shape[:2]
    cols = data_ref.shape[0]
    spots = len(message_refs) * BCAP

    def clear(index, carry):
        total_ref[index] = jnp.zeros((cols, BS), F32)
        return carry

    lax.fori_loop(0, spots, clear, 0, unroll=8)
    begin()

    def one_pair(pair, carry):
        before(pair)
        data = data_ref[:, lanes(pair)]
        high = data.astype(BF16)
        low = (data - high.astype(F32)).astype(BF16)
        pieces = jnp.concatenate([high, low], axis=0)
        for slot in range(0, slot_count, 2):
            rays = jnp.concatenate([rays_ref[pair, slot], rays_ref[pair, slot + 1]], axis=1)
            part = jnp.dot(pieces, rays, preferred_element_type=F32)
            part = part[:cols] + part[cols:]
            for half in range(2):
                spot = target_ref[pair * slot_count + slot + half]
                total_ref[spot] += part[:, half * BS : (half + 1) * BS]
        return carry

    lax.fori_loop(0, pair_count, one_pair, 0, unroll=True)

    for peer, message_ref in enumerate(message_refs):
        for rank in range(BCAP):
            message_ref[rank * cols : (rank + 1) * cols, :] = total_ref[
                peer * BCAP + rank
            ].astype(BF16)


def start_kernel(peers, me_ref, cells_hbm, counts_hbm, times_hbm, rays_hbm, *refs):
    message_refs = refs[:peers]
    target_ref, total_ref, table_ref, used_ref, cells_ref, counts_ref = refs[peers : peers + 6]
    times_ref, rays_ref, place_ref, sems, ray_sems = refs[peers + 6 :]
    for index, step in enumerate(steps_of(peers)):
        place_ref[me_ref[0] ^ step] = index
    pair_count, slot_count = rays_ref.shape[:2]
    cols = times_ref.shape[0]
    owned = CELL_DEV // BS
    copies = [
        pltpu.make_async_copy(source, dest, sems.at[index])
        for index, (source, dest) in enumerate(
            [(cells_hbm, cells_ref), (counts_hbm, counts_ref), (times_hbm, times_ref)]
        )
    ]
    for copy in copies:
        copy.start()

    def ray_copy(pair):
        return pltpu.make_async_copy(rays_hbm.at[pair], rays_ref.at[pair], ray_sems.at[pair])

    def fetch(pair, carry):
        ray_copy(pair).start()
        return carry

    lax.fori_loop(0, pair_count, fetch, 0)

    def clear(peer, carry):
        used_ref[peer] = 0
        for rank in range(BCAP):
            table_ref[peer * BCAP + rank] = 0
        return carry

    lax.fori_loop(0, peers, clear, 0)
    def find_places(pair):
        count = counts_ref[pair]
        for slot in range(slot_count):
            cell = cells_ref[pair, slot]
            owner = place_ref[cell // owned]
            local = cell % owned
            used = used_ref[owner]
            rank = used
            for other in range(BCAP - 1, -1, -1):
                same = (table_ref[owner * BCAP + other] == local) & (other < used)
                rank = jnp.where(same, other, rank)
            spot = owner * BCAP + rank
            table_ref[spot] = local
            used_ref[owner] = jnp.maximum(used, rank + 1)
            target_ref[pair * slot_count + slot] = jnp.where(slot < count, spot, peers * BCAP)

    def before(pair):
        find_places(pair)
        ray_copy(pair).wait()

    def begin():
        for copy in copies:
            copy.wait()
        squares = jnp.zeros((cols, BS), F32)
        for pair in range(pair_count):
            values = times_ref[:, pair * BS : (pair + 1) * BS]
            squares += values * values
        tail = squares_tail(squares).astype(BF16)
        for message_ref in message_refs:
            message_ref[BCAP * cols :, :] = tail

    transposed(times_ref, rays_ref, begin, before, target_ref, total_ref, message_refs)
    place = lax.broadcasted_iota(jnp.int32, (TAIL, BS), 0)
    lane = lax.broadcasted_iota(jnp.int32, (TAIL, BS), 1)
    for peer, message_ref in enumerate(message_refs):
        rows = message_ref[BCAP * cols :, :].astype(F32)
        for rank in range(BCAP):
            asked = table_ref[peer * BCAP + rank].astype(F32)
            rows = jnp.where((place == 3) & (lane == rank), asked, rows)
        message_ref[BCAP * cols :, :] = rows.astype(BF16)


def keep_kernel(target_hbm, own_hbm, rays_hbm, target_ref, own_ref, rays_ref, sems):
    copies = [
        pltpu.make_async_copy(source, dest, sems.at[index])
        for index, (source, dest) in enumerate(
            [(target_hbm, target_ref), (own_hbm, own_ref), (rays_hbm, rays_ref)]
        )
    ]
    for copy in copies:
        copy.start()
    for copy in copies:
        copy.wait()


def pair_kernel(peers, target_ref, *refs):
    fetched_refs = refs[:peers]
    data_ref, beta_ref, rays_ref = refs[peers : peers + 3]
    message_refs = refs[peers + 3 : 2 * peers + 3]
    alpha_ref, raw_ref, total_ref, fetched_ref = refs[2 * peers + 3 :]
    pair_count, slot_count = rays_ref.shape[:2]
    cols = data_ref.shape[0]
    spots = peers * BCAP
    for peer in range(peers):
        fetched_ref[peer] = fetched_refs[peer][: BCAP * cols, :]
    alpha = norm_of_tails(fetched_refs, cols)
    alpha_ref[...] = alpha
    beta = beta_ref[...]
    model_scale = 1.0 / (alpha * beta)
    data_scale = alpha / beta

    def one_pair(pair, squares):
        chosen = []
        for slot in range(slot_count):
            spot = target_ref[pair * slot_count + slot]
            live = spot < spots
            spot = jnp.where(live, spot, 0)
            rows = pl.ds(pl.multiple_of((spot % BCAP) * cols, cols), cols)
            block = fetched_ref[spot // BCAP, rows, :]
            chosen.append(jnp.where(live, block, jnp.zeros_like(block)))
        rays = jnp.concatenate([rays_ref[pair, slot] for slot in range(slot_count)], axis=1)
        product = lax.dot_general(
            rays, jnp.concatenate(chosen, axis=1), (((1,), (1,)), ((), ())),
            preferred_element_type=F32,
        )
        raw = product.T * model_scale - data_ref[:, lanes(pair)] * data_scale
        raw_ref[:, lanes(pair)] = raw
        return squares + raw * raw

    squares = lax.fori_loop(0, pair_count, one_pair, jnp.zeros((cols, BS), F32), unroll=True)
    transposed(
        raw_ref, rays_ref, lambda: None, lambda pair: None, target_ref, total_ref, message_refs
    )
    tail = squares_tail(squares).astype(BF16)
    for message_ref in message_refs:
        message_ref[BCAP * cols :, :] = tail


def gathered(arrived_refs, asked_ref, model_ref):
    cols = model_ref.shape[0]
    for peer, arrived_ref in enumerate(arrived_refs):
        for rank in range(BCAP):
            where = lanes(asked_ref[peer, rank])
            model_ref[:, where] += arrived_ref[rank * cols : (rank + 1) * cols, :].astype(F32)


def reply(squares, scale, asked_ref, model_ref, out_refs):
    cols = model_ref.shape[0]
    tail = squares_tail(squares * scale * scale).astype(BF16)
    for peer, out_ref in enumerate(out_refs):
        out_ref[BCAP * cols :, :] = tail
        for rank in range(BCAP):
            block = model_ref[:, lanes(asked_ref[peer, rank])]
            out_ref[rank * cols : (rank + 1) * cols, :] = block.astype(BF16)


def squares_of(model_ref):
    cols, cells = model_ref.shape

    def one_block(block, squares):
        values = model_ref[:, lanes(block)]
        return squares + values * values

    return lax.fori_loop(0, cells // BS, one_block, jnp.zeros((cols, BS), F32), unroll=32)


def first_cell_kernel(peers, *refs):
    arrived_refs, out_refs = refs[:peers], refs[peers + 2 : 2 * peers + 2]
    model_ref, beta_ref = refs[peers : peers + 2]
    asked_ref, table_ref, sem = refs[2 * peers + 2 :]
    cols, cells = model_ref.shape
    for peer in range(peers):
        tail = arrived_refs[peer][BCAP * cols :, :].astype(F32)
        table_ref[peer : peer + 1, :] = tail[3:4].astype(jnp.int32)
    copy = pltpu.make_async_copy(table_ref, asked_ref, sem)
    copy.start()
    beta = norm_of_tails(arrived_refs, cols)
    beta_ref[...] = beta
    model_ref[...] = jnp.zeros((cols, cells), F32)
    copy.wait()
    gathered(arrived_refs, asked_ref, model_ref)
    reply(squares_of(model_ref), 1.0 / beta, asked_ref, model_ref, out_refs)


def start_from(before_ref, scale, model_ref):
    def one_block(block, carry):
        model_ref[:, lanes(block)] = before_ref[:, lanes(block)] * -scale
        return carry

    lax.fori_loop(0, model_ref.shape[1] // BS, one_block, 0, unroll=32)


def cell_kernel(peers, asked_ref, *refs):
    arrived_refs, out_refs = refs[:peers], refs[peers + 5 :]
    before_ref, alpha_ref, beta_before_ref, model_ref, beta_ref = refs[peers : peers + 5]
    beta = norm_of_tails(arrived_refs, model_ref.shape[0])
    beta_ref[...] = beta
    start_from(before_ref, beta * beta / (alpha_ref[...] * beta_before_ref[...]), model_ref)
    gathered(arrived_refs, asked_ref, model_ref)
    reply(squares_of(model_ref), 1.0 / beta, asked_ref, model_ref, out_refs)


def last_cell_kernel(peers, asked_ref, *refs):
    arrived_refs = refs[:peers]
    before_ref, alpha_ref, beta_before_ref, model_ref, beta_ref, out_ref = refs[peers:]
    beta = norm_of_tails(arrived_refs, model_ref.shape[0])
    beta_ref[...] = beta
    start_from(before_ref, beta * beta / (alpha_ref[...] * beta_before_ref[...]), model_ref)
    gathered(arrived_refs, asked_ref, model_ref)
    squares = squares_of(model_ref) / (beta * beta)
    total = jnp.sum(squares, axis=1, keepdims=True)
    row = jnp.sum(jnp.where(diagonal(total.shape[0]), total, 0.0), axis=0, keepdims=True)
    out_ref[...] = jnp.broadcast_to(row, out_ref.shape)


def estimate_kernel(*refs):
    models = refs[:ITERS]
    alphas = [ref[...] for ref in refs[ITERS : 2 * ITERS]]
    betas = [ref[...] for ref in refs[2 * ITERS : 3 * ITERS + 1]]
    estimate_hbm, estimate_ref, sems = refs[3 * ITERS + 1 :]
    cells = estimate_ref.shape[1]
    weights = estimate_weights(betas, alphas)
    blocks = cells // BS // CHUNKS

    def one_block(block, carry):
        where = lanes(block)
        total = weights[0] * models[0][:, where]
        for i in range(1, ITERS):
            total += weights[i] * models[i][:, where]
        estimate_ref[:, where] = total
        return carry

    copies = []
    for chunk in range(CHUNKS):
        lax.fori_loop(chunk * blocks, (chunk + 1) * blocks, one_block, 0, unroll=True)
        where = slice(chunk * blocks * BS, (chunk + 1) * blocks * BS)
        copies.append(
            pltpu.make_async_copy(
                estimate_ref.at[:, where], estimate_hbm.at[:, where], sems.at[chunk]
            )
        )
        copies[-1].start()
    for copy in copies:
        copy.wait()


def estimate_weights(betas, alphas):
    phi_bar = betas[0]
    rho_bar = alphas[0]
    trace = [1.0 / (alphas[0] * betas[0])]
    weight = [jnp.zeros_like(phi_bar)] * ITERS
    for step in range(ITERS):
        beta = betas[step + 1]
        rho = jnp.sqrt(rho_bar * rho_bar + beta * beta)
        cosine = rho_bar / rho
        sine = beta / rho
        gain = cosine * phi_bar / rho
        weight = [
            weight[i] + gain * trace[i] if i < len(trace) else weight[i] for i in range(ITERS)
        ]
        if step + 1 < ITERS:
            alpha = alphas[step + 1]
            theta = sine * alpha
            rho_bar = -cosine * alpha
            phi_bar = sine * phi_bar
            trace = [-(theta / rho) * value for value in trace] + [1.0 / (alpha * beta)]
    return weight


def model_kernel(*refs):
    *share_refs, beta_ref, model_ref, out_hbm, out_ref, sems = refs
    cols, cells = model_ref.shape
    blocks = cells // BS // CHUNKS
    row = sum(ref[...] for ref in share_refs)[0:1]
    column = jnp.sum(jnp.where(diagonal(cols), row, 0.0), axis=1, keepdims=True)
    alpha = jnp.broadcast_to(jnp.sqrt(column + EPS), (cols, BS))
    scale = 1.0 / (alpha * beta_ref[...])

    def one_block(block, carry):
        out_ref[:, lanes(block)] = model_ref[:, lanes(block)] * scale
        return carry

    copies = []
    for chunk in range(CHUNKS):
        lax.fori_loop(chunk * blocks, (chunk + 1) * blocks, one_block, 0, unroll=True)
        where = slice(chunk * blocks * BS, (chunk + 1) * blocks * BS)
        copies.append(
            pltpu.make_async_copy(out_ref.at[:, where], out_hbm.at[:, where], sems.at[chunk])
        )
        copies[-1].start()
    for copy in copies:
        copy.wait()


def call(kernel, name, in_spaces, outs, scratch=(), flops=0, moved=0, limit=16 << 20):
    return pl.pallas_call(
        kernel,
        name=name,
        in_specs=[pl.BlockSpec(memory_space=space) for space in in_spaces],
        out_specs=[pl.BlockSpec(memory_space=space) for _, _, space in outs],
        out_shape=[jax.ShapeDtypeStruct(shape, dtype) for shape, dtype, _ in outs],
        scratch_shapes=list(scratch),
        compiler_params=pltpu.CompilerParams(vmem_limit_bytes=limit),
        cost_estimate=pl.CostEstimate(flops=flops, bytes_accessed=moved, transcendentals=0),
    )


def on_device(ray_blocks, block_cells, block_counts, travel_times):
    pair_count, slot_count = ray_blocks.shape[:2]
    slots = pair_count * slot_count
    peers = lax.axis_size("pair")
    spots = peers * BCAP
    times = travel_times.T
    cols, pairs = times.shape
    messages = [((BCAP * cols + TAIL, BS), BF16, VMEM)] * peers
    ins = [VMEM] * peers
    gathered_blocks = VMEM((peers, BCAP * cols, BS), BF16)
    tile = ((cols, BS), F32, VMEM)
    data = ((cols, pairs), F32, VMEM)
    whole = ((cols, CELL_DEV), F32, VMEM)
    totals = VMEM((spots + 1, cols, BS), F32)
    flops = 2 * slots * BS * BS * cols

    steps = steps_of(peers)

    def exchange(values):
        return [values[0]] + [
            lax.ppermute(value, "pair", [(one, one ^ step) for one in range(peers)])
            for value, step in zip(values[1:], steps[1:])
        ]

    me = lax.axis_index("pair").astype(jnp.int32).reshape(1)
    *outgoing, target = call(
        functools.partial(start_kernel, peers), "start", [SMEM, HBM, HBM, HBM, HBM],
        messages + [((slots,), jnp.int32, SMEM)],
        [
            totals, SMEM((spots,), jnp.int32), SMEM((peers,), jnp.int32),
            SMEM(block_cells.shape, jnp.int32), SMEM(block_counts.shape, jnp.int32),
            VMEM(times.shape, F32), VMEM(ray_blocks.shape, BF16), SMEM((peers,), jnp.int32),
            pltpu.SemaphoreType.DMA((3,)), pltpu.SemaphoreType.DMA((pair_count,)),
        ],
        flops, 6 << 20, 60 << 20,
    )(me, block_cells, block_counts, times, ray_blocks)
    arrived = exchange(outgoing)
    target, arrived[0], ray_blocks = call(
        keep_kernel, "keep", [HBM, HBM, HBM],
        [((slots,), jnp.int32, SMEM), messages[0], (ray_blocks.shape, BF16, VMEM)],
        [pltpu.SemaphoreType.DMA((3,))], 0, 8 << 20, 48 << 20,
    )(target, arrived[0], ray_blocks)
    model, beta, *replies, asked = call(
        functools.partial(first_cell_kernel, peers), "cells_first", ins,
        [whole, tile] + messages + [((peers, BS), jnp.int32, SMEM)],
        [VMEM((peers, BS), jnp.int32), pltpu.SemaphoreType.DMA],
        0, 6 << 20,
    )(*arrived)
    models, betas, alphas = [model], [beta], []
    current = times
    for step in range(ITERS):
        fetched = exchange(replies)
        last = step + 1 == ITERS
        made = call(
            functools.partial(pair_kernel, peers), "pairs_last" if last else "pairs",
            [SMEM] + ins + [VMEM, VMEM, VMEM], messages + [tile] + [data] * (not last),
            [VMEM(data[0], F32)] * last + [totals, gathered_blocks], 2 * flops, 8 << 20,
        )(target, *fetched, current, betas[-1], ray_blocks)
        alphas.append(made[peers])
        current = made[-1]
        arrived = exchange(made[:peers])
        if not last:
            model, beta, *replies = call(
                functools.partial(cell_kernel, peers), "cells", [SMEM] + ins + [VMEM] * 3,
                [whole, tile] + messages, (), 0, 8 << 20,
            )(asked, *arrived, models[-1], alphas[-1], betas[-1])
            models.append(model)
            betas.append(beta)
    model, beta, share = call(
        functools.partial(last_cell_kernel, peers), "cells_last", [SMEM] + ins + [VMEM] * 3,
        [whole, tile, ((8, BS), F32, VMEM)], (), 0, 8 << 20,
    )(asked, *arrived, models[-1], alphas[-1], betas[-1])
    betas.append(beta)
    reach, shares = peers, [share]
    while reach > 1:
        share = sum(shares[1:], shares[0])
        low = max(reach // 4, 1)
        shares = [share] + [
            lax.ppermute(share, "pair", [(one, one ^ step) for one in range(peers)])
            for step in range(low, reach, low)
        ]
        reach = low
    scratch = [VMEM(whole[0], F32), pltpu.SemaphoreType.DMA((CHUNKS,))]
    (estimate,) = call(
        estimate_kernel, "estimate", [VMEM] * (3 * ITERS + 1), [(whole[0], F32, HBM)], scratch,
        0, 6 << 20,
    )(*models, *alphas, *betas)
    (model_vec,) = call(
        model_kernel, "model", [VMEM] * (len(shares) + 2), [(whole[0], F32, HBM)], scratch,
        0, 4 << 20,
    )(*shares, beta, model)
    return (estimate.T, model_vec.T)


def solution(mesh):
    return jax.shard_map(
        on_device,
        mesh=mesh,
        in_specs=(
            P(("groups", "pair"), None, None, None),
            P(("groups", "pair"), None),
            P(("groups", "pair")),
            P(("groups", "pair"), None),
        ),
        out_specs=(P(("groups", "pair"), None), P(("groups", "pair"), None)),
        check_vma=False,
    )
```
